32 devices in a mesh: batch: 8 (over z, y), tier: 4 (over x, core).
Axes of the slice: x: 2, y: 2, z: 4, core: 2. Of those that a mesh axis runs over, the one named last changes fastest.
Arguments:
- segment: bfloat16 [32, 192, 1024], P('batch', 'tier'), may hold values from -6 to 6
- memory: bfloat16 [32, 192, 1024], P('batch', 'tier'), may hold values from -8 to 8
- compressed: bfloat16 [32, 192, 1024], P('batch', 'tier'), may hold values from -6 to 6
- evicted: int32 [32], P('batch'), may hold values from 48 to 192, as said below
- window_mask: int32 [32, 64], P('batch', 'tier'), may hold values 0 or 1
- cotangent: bfloat16 [32, 192, 1024], P('batch', 'tier'), may hold values from -6 to 6
- w_query: bfloat16 [1024, 1024], P(('batch', 'tier')), may hold values from -0.1875 to 0.1875
- w_key: bfloat16 [1024, 1024], P(('batch', 'tier')), may hold values from -0.1875 to 0.1875
- w_value: bfloat16 [1024, 1024], P(('batch', 'tier')), may hold values from -0.1875 to 0.1875
- w_output: bfloat16 [1024, 1024], P(('batch', 'tier')), may hold values from -0.375 to 0.375
- w_up: bfloat16 [1024, 4096], P(('batch', 'tier')), may hold values from -0.1875 to 0.1875
- b_up: bfloat16 [4096], P(('batch', 'tier')), may hold values from -3 to 3
- w_down: bfloat16 [4096, 1024], P(('batch', 'tier')), may hold values from -0.09375 to 0.09375
- b_down: bfloat16 [1024], P(('batch', 'tier')), may hold values from -3 to 3
- ln_gain: bfloat16 [1024], P(('batch', 'tier')), may hold values from 0.5 to 1.5
- ln_bias: bfloat16 [1024], P(('batch', 'tier')), may hold values from -3 to 3
- w_conv: bfloat16 [3, 1024, 1024], P(None, ('batch', 'tier')), may hold values from -0.109375 to 0.109375
- b_conv: bfloat16 [1024], P(('batch', 'tier')), may hold values from -3 to 3
- slopes: float32 [8], replicated, may hold values from 0.5 to 4
Outputs:
- output: bfloat16 [32, 192, 1024], P('batch', 'tier')
- input_grad: float32 [32, 192, 1024], P('batch', 'tier')
- new_memory: bfloat16 [32, 192, 1024], P('batch', 'tier')
- new_compressed: bfloat16 [32, 192, 1024], P('batch', 'tier')
- grad_query: float32 [1024, 1024], P(('batch', 'tier'))
- grad_key: float32 [1024, 1024], P(('batch', 'tier'))
- grad_value: float32 [1024, 1024], P(('batch', 'tier'))
- grad_output: float32 [1024, 1024], P(('batch', 'tier'))
- grad_up: float32 [1024, 4096], P(('batch', 'tier'))
- grad_up_bias: float32 [4096], P(('batch', 'tier'))
- grad_down: float32 [4096, 1024], P(('batch', 'tier'))
- grad_down_bias: float32 [1024], P(('batch', 'tier'))
- grad_gain: float32 [1024], P(('batch', 'tier'))
- grad_bias: float32 [1024], P(('batch', 'tier'))
- grad_conv: float32 [3, 1024, 1024], P(None, ('batch', 'tier'))
- grad_conv_bias: float32 [1024], P(('batch', 'tier'))
- grad_slopes: float32 [8], replicated
The draws below stay inside these ranges and needn't reach their ends.
Inputs may be any that keep to these rules, and one draw needn't show every extreme that they name: In each aligned block of 4 sequences one has exactly 192 evicted slots.
All inputs are finite; a program needn't handle non-finite values. No bound on the sum of `window_mask` on one device may be relied on, other than what follows from the above.
Results may differ from the reference program's by a relative error of at most 0.015.
Values may be sent and summed in bfloat16 or wider, within the bound.
A program may use at most 192 MiB of HBM per device.

```python
import math
import jax
import jax.numpy as jnp
from jax import lax

D = 1024
HEADS = 8
HDIM = 128
FF = 4096
SEQ_DEV = 4
SEQS = 32
SEG = 192
MEM = 192
CMEM = 192
CTX = 576
NW = 64


def draw_evicted(key, part):
    count_key = jax.random.fold_in(key, 11)
    pick_key = jax.random.fold_in(key, 23)
    counts = jax.random.randint(count_key, (SEQS,), SEG // 4, SEG + 1)
    picks = jax.random.randint(pick_key, (SEQS // SEQ_DEV,), 0, SEQ_DEV)
    seq_index = jnp.arange(SEQS, dtype=jnp.int32)
    chosen = seq_index % SEQ_DEV == jnp.repeat(picks, SEQ_DEV)
    return jnp.where(chosen, SEG, counts).astype(jnp.int32)


def draw_memory(key, part):
    key = jax.random.fold_in(key, 37)
    offset_key = jax.random.fold_in(key, 1)
    noise_key = jax.random.fold_in(key, 2)
    feature_offset = 0.5 * jnp.clip(jax.random.normal(offset_key, (D,), jnp.float32), -4.0, 4.0)
    noise = jnp.clip(jax.random.normal(noise_key, (SEQS, MEM, D), jnp.float32), -5.5, 5.5)
    return (noise + feature_offset[None, None, :]).astype(jnp.bfloat16)


def with_ends(result, rng, low, high):
    place = [jax.random.randint(jax.random.fold_in(rng, axis), (), 0, length) for axis, length in enumerate(result.shape)]
    longest = result.shape.index(max(result.shape))
    neighbour = place[:longest] + [(place[longest] + 1) % result.shape[longest]] + place[longest + 1:]
    return result.at[tuple(place)].set(low).at[tuple(neighbour)].set(high)


def steps_of(stream_key, shape, cuts, smallest, top_value):
    level = 1.0
    for axis_at, blocks in cuts:
        draws = jax.random.uniform(jax.random.fold_in(jax.random.fold_in(stream_key, 6), axis_at), (blocks,), jnp.float32, smallest / len(cuts), top_value / len(cuts))
        level = level * jnp.repeat(jnp.exp(draws), shape[axis_at] // blocks).reshape((-1,) + (1,) * (len(shape) - 1 - axis_at))
    return level


def gaussian(own_key, shape, scale, bound, pieces=(), held_as=jnp.bfloat16):
    drawn = scale * jax.random.normal(own_key, shape, jnp.float32)
    if pieces:
        drawn = drawn * steps_of(own_key, shape, pieces, -0.22, 0.18)
    return jnp.clip(drawn, -bound, bound).astype(held_as)


def setup_inputs(seed: int = 0) -> dict:
    seeds = jax.random.split(jax.random.key(seed), 20)
    return {
        "segment": gaussian(seeds[0], (SEQS, SEG, D), 1.0, 6.0, ((0, 8), (1, 4))),
        "memory": draw_memory(jax.random.fold_in(seeds[19], 71), 0),
        "compressed": gaussian(seeds[2], (SEQS, CMEM, D), 1.0, 6.0, ((0, 8), (1, 4))),
        "evicted": draw_evicted(jax.random.fold_in(seeds[19], 71), 0),
        "window_mask": with_ends((jax.random.randint(seeds[4], (SEQS, NW), 0, 4) < 3).astype(jnp.int32), jax.random.fold_in(seeds[4], 1), 0, 1),
        "cotangent": gaussian(seeds[5], (SEQS, SEG, D), 1.0, 6.0, ((0, 8), (1, 4))),
        "w_query": gaussian(seeds[6], (D, D), D ** -0.5, 0.1875, ((0, 32),)),
        "w_key": gaussian(seeds[7], (D, D), D ** -0.5, 0.1875, ((0, 32),)),
        "w_value": gaussian(seeds[8], (D, D), D ** -0.5, 0.1875, ((0, 32),)),
        "w_output": gaussian(seeds[9], (D, D), (D // 4) ** -0.5, 0.375, ((0, 32),)),
        "w_up": gaussian(seeds[10], (D, FF), D ** -0.5, 0.1875, ((0, 32),)),
        "b_up": gaussian(seeds[11], (FF,), 0.5, 3.0, ((0, 32),)),
        "w_down": gaussian(seeds[12], (FF, D), FF ** -0.5, 0.09375, ((0, 32),)),
        "b_down": gaussian(seeds[13], (D,), 0.5, 3.0, ((0, 32),)),
        "ln_gain": jnp.clip(1.0 + 0.1 * jax.random.normal(seeds[14], (D,), jnp.float32), 0.5, 1.5).astype(jnp.bfloat16),
        "ln_bias": gaussian(seeds[15], (D,), 0.5, 3.0, ((0, 32),)),
        "w_conv": gaussian(seeds[16], (3, D, D), (3 * D) ** -0.5, 0.109375, ((1, 32),)),
        "b_conv": gaussian(seeds[17], (D,), 0.5, 3.0, ((0, 32),)),
        "slopes": jnp.clip(jnp.exp(jax.random.uniform(seeds[18], (HEADS,), jnp.float32, math.log(0.5), math.log(4.0))), 0.5, 4.0),
    }


@jax.custom_vjp
def low(v):
    return lax.optimization_barrier(v.astype(jnp.bfloat16)).astype(jnp.float32)

@jax.custom_vjp
def low_back(v):
    return v

def low_keep(v):
    return (low(v), None)

def low_pass(kept, grad):
    return (grad,)

def back_keep(v):
    return (v, None)

def back_low(kept, grad):
    return (low(grad),)
low.defvjp(low_keep, low_pass)
low_back.defvjp(back_keep, back_low)
masked_value = -1e+30
norm_eps = 1e-05

def product(left, right):
    return jnp.dot(left, right, precision=lax.Precision.HIGHEST, preferred_element_type=jnp.float32)

def layer_norm(resid, ln_gain, ln_bias):
    center = resid - lax.optimization_barrier(jnp.mean(resid, axis=-1, keepdims=True))
    spread = lax.rsqrt(lax.optimization_barrier(jnp.mean(center * center, axis=-1, keepdims=True)) + norm_eps)
    return center * spread * ln_gain + ln_bias

def layer(weights, segment, memory, compressed, live):
    w_query, w_key, w_value, w_output, w_up, b_up, w_down, b_down, ln_gain, ln_bias, w_conv, b_conv, slopes = weights
    context = jnp.concatenate([compressed, memory, segment], axis=0)
    query = low(low_back(product(segment, w_query)))
    keys = low(low_back(product(context, w_key)))
    values = low(low_back(product(context, w_value)))
    head_query = query.reshape(SEG, HEADS, HDIM)
    head_keys = keys.reshape(CTX, HEADS, HDIM)
    head_values = values.reshape(CTX, HEADS, HDIM)
    raw = jnp.einsum('qhd,khd->hqk', head_query, head_keys, precision=lax.Precision.HIGHEST)
    query_pos = jnp.arange(SEG, dtype=jnp.int32) + CMEM + MEM
    key_pos = jnp.arange(CTX, dtype=jnp.int32)
    distance = (query_pos[:, None] - key_pos[None, :]).astype(jnp.float32) * (1.0 / CTX)
    allowed = key_pos[None, :] <= query_pos[:, None]
    scores = low_back(raw) * (1.0 / math.sqrt(HDIM)) - slopes[:, None, None] * distance[None]
    scores = jnp.where(allowed[None], scores, masked_value)
    probs = jax.nn.softmax(scores, axis=-1)
    mixed = jnp.einsum('hqk,khd->qhd', low(probs), head_values, precision=lax.Precision.HIGHEST).reshape(SEG, D)
    mixed = low(low_back(mixed))
    resid = segment + low_back(product(mixed, w_output))
    normed = layer_norm(resid, ln_gain, ln_bias)
    normed_low = low(low_back(normed))
    pre_act = low_back(product(normed_low, w_up)) + b_up
    act_low = low(low_back(jax.nn.gelu(pre_act, approximate=False)))
    final = resid + product(act_low, w_down) + b_down
    windows = memory.reshape(NW, 3 * D)
    conv_out = low_back(product(windows, w_conv.reshape(3 * D, D))) + b_conv
    pooled = lax.optimization_barrier(jnp.mean(memory.reshape(NW, 3, D), axis=1))
    rebuild = 0.5 * jnp.sum(live[:, None] * (conv_out - pooled) ** 2)
    return ((final, rebuild), conv_out)

def reference(segment, memory, compressed, evicted, window_mask, cotangent, w_query, w_key, w_value, w_output, w_up, b_up, w_down, b_down, ln_gain, ln_bias, w_conv, b_conv, slopes):
    weights = tuple((item.astype(jnp.float32) for item in (w_query, w_key, w_value, w_output, w_up, b_up, w_down, b_down, ln_gain, ln_bias, w_conv, b_conv, slopes)))
    window_index = jnp.arange(NW, dtype=jnp.int32)
    slot_index = jnp.arange(CMEM, dtype=jnp.int32)
    memory_index = jnp.arange(MEM, dtype=jnp.int32)
    offset = CMEM - NW

    def one_sequence(totals, items):
        seg_rows, mem_rows, comp_rows, count, masks, cot_rows = items
        seg_float = seg_rows.astype(jnp.float32)
        mem_float = mem_rows.astype(jnp.float32)
        comp_float = comp_rows.astype(jnp.float32)
        mask_float = masks.astype(jnp.float32)
        live = mask_float * (3 * window_index + 3 <= count).astype(jnp.float32)

        def forward(params, inputs):
            return layer(params, inputs, mem_float, comp_float, live)
        outcome, pull, conv_out = jax.vjp(forward, weights, seg_float, has_aux=True)
        grad_weights, grad_segment = pull((cot_rows.astype(outcome[0].dtype), jnp.ones_like(outcome[1])))
        totals = jax.tree.map(jnp.add, totals, grad_weights)
        new_mem = jnp.where((memory_index < count)[:, None], seg_rows, mem_rows)
        padded = jnp.concatenate([jnp.zeros((offset, D), conv_out.dtype), mask_float[:, None] * conv_out], axis=0)
        written = (slot_index >= offset) & (3 * (slot_index - offset) + 3 <= count)
        new_comp = jnp.where(written[:, None], padded.astype(jnp.bfloat16), comp_rows)
        return (totals, (outcome[0].astype(jnp.bfloat16), grad_segment, new_mem, new_comp))
    start = tuple((jnp.zeros_like(item) for item in weights))
    totals, (output, input_grad, new_memory, new_compressed) = lax.scan(one_sequence, start, (segment, memory, compressed, evicted, window_mask, cotangent))
    return (output, input_grad, new_memory, new_compressed, totals[0], totals[1], totals[2], totals[3], totals[4], totals[5], totals[6], totals[7], totals[8], totals[9], totals[10], totals[11], totals[12])
```

```python
import functools
import math

import jax
import jax.numpy as jnp
from jax import lax
from jax.experimental import pallas as pl
from jax.experimental.pallas import tpu as pltpu
from jax.sharding import PartitionSpec as P

norm_eps = 1e-05
MESH = pl.DeviceIdType.MESH
ANY = pl.BlockSpec(memory_space=pl.ANY)
VM = pl.BlockSpec(memory_space=pltpu.VMEM)
f32 = jnp.float32
bf16 = jnp.bfloat16


def remote(src, dst, send, recv, device):
    return pltpu.make_async_remote_copy(
        src_ref=src,
        dst_ref=dst,
        send_sem=send,
        recv_sem=recv,
        device_id=device,
        device_id_type=MESH,
    )


def places(groups):
    b, t = lax.axis_index("batch"), lax.axis_index("tier")
    z, y = b // 2, lax.rem(b, 2)
    zs = [lax.rem(z + d, groups) for d in range(groups)]
    zback = [lax.rem(z + groups - d, groups) for d in range(groups)]
    return b, t, z, y, zs, zback


def greet(groups, tiers, columns):
    b, t, z, y, zs, _ = places(groups)
    barrier = pltpu.get_barrier_semaphore()
    peers = []
    if tiers:
        peers += [(b, t ^ d) for d in (1, 2, 3)]
    if columns:
        peers += [(2 * zz + y, t) for zz in zs[1:]] + [(b ^ 1, t)]
    for peer in peers:
        pl.semaphore_signal(barrier, inc=1, device_id=peer, device_id_type=MESH)
    pl.semaphore_wait(barrier, len(peers))


def gather_kernel(groups, nu, *refs):
    (wa, wu, wc, wd, sm, comp, mem, seg, cot, mk) = refs[:10]
    (WA, WU, WC, WD, SM, CTX, COT, MK) = refs[10:18]
    lsem, ts, tr, zsd, zr, ys, yr, acs, acr = refs[18:]
    G = groups
    b, t, z, y, zs, zback = places(G)
    greet(G, True, True)
    ypeer = (b ^ 1, t)
    local, sends = [], []

    def here(src, dst, i):
        cp = pltpu.make_async_copy(src, dst, lsem.at[i])
        cp.start()
        return cp

    kinds = [(sm, SM), (wa, WA), (wu, WU), (wc, WC)]
    own = []
    for k, (src, dst) in enumerate(kinds):
        mine = src if k == 0 else src.at[t]
        own.append(here(mine, dst.at[b, t], k))
        for d in (1, 2, 3):
            piece = src if k == 0 else src.at[t ^ d]
            cp = remote(piece, dst.at[b, t], ts.at[k, d - 1], tr.at[k, d - 1], (b, t ^ d))
            cp.start()
            sends.append(cp)
    own.append(here(wd, WD.at[b], 4))
    pieces = [
        (comp, lambda q: CTX.at[:, pl.ds(nu * q, nu)]),
        (mem.at[:, 0], lambda q: CTX.at[:, 4 * nu + q]),
        (mem.at[:, 1], lambda q: CTX.at[:, 4 * nu + 4 + q]),
        (mem.at[:, 2], lambda q: CTX.at[:, 4 * nu + 8 + q]),
        (seg, lambda q: CTX.at[:, pl.ds(8 * nu + nu * q, nu)]),
        (mk, lambda q: MK.at[:, q]),
        (cot, lambda q: COT.at[:, pl.ds(nu * q, nu)]),
    ]
    for i, (src, at) in enumerate(pieces):
        own.append(here(src, at(t), 5 + i))
        for j, d in enumerate((1, 2)):
            cp = remote(src, at(t), acs.at[i, j], acr.at[i, j], (b, t ^ d))
            cp.start()
            sends.append(cp)
    table = [SM, WA, WU, WD, WC]
    local_of = [0, 1, 2, 4, 3]
    for k, dst in enumerate(table):
        own[local_of[k]].wait()
        if k != 3:
            kk = local_of[k]
            for d in (1, 2, 3):
                remote(dst.at[b, t], dst.at[b, t ^ d], ts.at[kk, d - 1], tr.at[kk, d - 1], (b, t ^ d)).wait_recv()
        for d in range(1, G):
            cp = remote(dst.at[b], dst.at[b], zsd.at[k, d], zr.at[k, d], (2 * zs[d] + y, t))
            cp.start()
            sends.append(cp)
        cp = remote(dst.at[b], dst.at[b], ys.at[k, 0], yr.at[k, 0], ypeer)
        cp.start()
        sends.append(cp)
    for i, (src, at) in enumerate(pieces):
        remote(at(t ^ 2), at(t ^ 2), acs.at[i, 1], acr.at[i, 1], (b, t ^ 2)).wait_recv()
        cp = remote(at(t ^ 2), at(t ^ 2), acs.at[i, 2], acr.at[i, 2], (b, t ^ 1))
        cp.start()
        sends.append(cp)
    for k, dst in enumerate(table):
        for d in range(1, G):
            at = dst.at[2 * zback[d] + y]
            remote(at, at, zsd.at[k, d], zr.at[k, d], ypeer).wait_recv()
            cp = remote(at, at, ys.at[k, d], yr.at[k, d], ypeer)
            cp.start()
            sends.append(cp)
    for k, dst in enumerate(table):
        for d in range(G):
            at = dst.at[2 * zback[d] + (1 - y)]
            remote(at, at, ys.at[k, d], yr.at[k, d], ypeer).wait_recv()
    for i, (src, at) in enumerate(pieces):
        for j, q in ((0, t ^ 1), (2, t ^ 3)):
            remote(at(q), at(q), acs.at[i, j], acr.at[i, j], (b, t ^ 1)).wait_recv()
    for i in range(len(pieces)):
        own[5 + i].wait()
    for cp in sends:
        cp.wait_send()


def gather_all(nb, nu, wa, wu, wc, wd, sm, comp, mem, seg, cot, mk):
    G = nb // 2
    S, _, U, M = comp.shape
    out = [
        jax.ShapeDtypeStruct((nb,) + wa.shape, bf16),
        jax.ShapeDtypeStruct((nb,) + wu.shape, bf16),
        jax.ShapeDtypeStruct((nb,) + wc.shape, bf16),
        jax.ShapeDtypeStruct((nb,) + wd.shape, bf16),
        jax.ShapeDtypeStruct((nb, 4) + sm.shape, f32),
        jax.ShapeDtypeStruct((S, 12 * nu, U, M), bf16),
        jax.ShapeDtypeStruct((S, 4 * nu, U, M), bf16),
        jax.ShapeDtypeStruct((S, 4) + mk.shape[1:], f32),
    ]
    dma = pltpu.SemaphoreType.DMA
    return pl.pallas_call(
        functools.partial(gather_kernel, G, nu),
        out_shape=out,
        in_specs=[ANY] * 10,
        out_specs=[ANY] * 8,
        scratch_shapes=[
            dma((12,)),
            dma((4, 3)),
            dma((4, 3)),
            dma((5, G)),
            dma((5, G)),
            dma((5, G)),
            dma((5, G)),
            dma((7, 3)),
            dma((7, 3)),
        ],
        compiler_params=pltpu.CompilerParams(collective_id=0, has_side_effects=True),
        name="gather_all",
    )(wa, wu, wc, wd, sm, comp, mem, seg, cot, mk)


def spread_kernel(same, x, o, lsem, ss, rs):
    b, t = lax.axis_index("batch"), lax.axis_index("tier")
    greet(1, True, False)
    cps = []
    for d in (1, 2, 3):
        cp = remote(x if same else x.at[t ^ d], o.at[t], ss.at[d - 1], rs.at[d - 1], (b, t ^ d))
        cp.start()
        cps.append(cp)
    mine = pltpu.make_async_copy(x if same else x.at[t], o.at[t], lsem)
    mine.start()
    mine.wait()
    for d in (1, 2, 3):
        remote(o.at[t ^ d], o.at[t ^ d], ss.at[d - 1], rs.at[d - 1], (b, t ^ d)).wait_recv()
    for cp in cps:
        cp.wait_send()


def spread(x, same, cid):
    dma = pltpu.SemaphoreType.DMA
    shape = ((4,) + x.shape) if same else x.shape
    return pl.pallas_call(
        functools.partial(spread_kernel, same),
        out_shape=jax.ShapeDtypeStruct(shape, x.dtype),
        in_specs=[ANY],
        out_specs=ANY,
        scratch_shapes=[dma, dma((3,)), dma((3,))],
        compiler_params=pltpu.CompilerParams(collective_id=cid, has_side_effects=True),
        name="spread_%d" % cid,
    )(x)


def reduce_kernel(groups, *refs):
    GD, GU, GC, GA, SMG = refs[:5]
    OD, OU, OC, OA, OS = refs[5:10]
    YD, YU, YC, YA, YS, ZD, ZU, ZC, ZA, ZS, TU, TC, TA, MU, MC, MA, ys, yr, zsd, zr, ts, tr = refs[10:]
    G = groups
    b, t, z, y, zs, zback = places(G)
    greet(G, True, True)
    ypeer = (b ^ 1, t)
    sends = []
    kinds = [
        (GD, YD, ZD, OD, None, None),
        (GU, YU, ZU, OU, MU, TU),
        (GC, YC, ZC, OC, MC, TC),
        (GA, YA, ZA, OA, MA, TA),
    ]
    for k, (g, yb, *_) in enumerate(kinds):
        for d in range(G):
            zz = zs[(d + 1) % G]
            cp = remote(g.at[2 * zz + (1 - y)], yb.at[zz], ys.at[k, d], yr.at[k, d], ypeer)
            cp.start()
            sends.append(cp)
    cp = remote(SMG, YS, ys.at[4, 0], yr.at[4, 0], ypeer)
    cp.start()
    sends.append(cp)
    for k, (g, yb, zb, o, m, tb) in enumerate(kinds):
        for d in range(G):
            zz = zs[(d + 1) % G]
            at = yb.at[zz]
            remote(at, at, ys.at[k, d], yr.at[k, d], ypeer).wait_recv()

            def add(i, c, yb=yb, zz=zz, g=g):
                yb[zz, i] = (yb[zz, i].astype(f32) + g[2 * zz + y, i].astype(f32)).astype(bf16)
                return c

            lax.fori_loop(0, yb.shape[1], add, 0)
            if d < G - 1:
                cp = remote(at, zb.at[d], zsd.at[k, d], zr.at[k, d], (2 * zz + y, t))
                cp.start()
                sends.append(cp)
    remote(YS, YS, ys.at[4, 0], yr.at[4, 0], ypeer).wait_recv()
    ZS[z] = SMG[...] + YS[...]
    for d in range(G - 1):
        cp = remote(ZS.at[z], ZS.at[z], zsd.at[4, d], zr.at[4, d], (2 * zs[d + 1] + y, t))
        cp.start()
        sends.append(cp)
    for k, (g, yb, zb, o, m, tb) in enumerate(kinds):
        for d in range(G - 1):
            remote(zb.at[d], zb.at[d], zsd.at[k, d], zr.at[k, d], ypeer).wait_recv()

        def total(i, c, k=k, yb=yb, zb=zb, o=o, m=m):
            acc = yb[z, i].astype(f32)
            for d in range(G - 1):
                acc = acc + zb[d, i].astype(f32)
            if k == 0:
                o[i] = acc
            else:
                m[i] = acc.astype(bf16)
            return c

        lax.fori_loop(0, o.shape[0], total, 0)
        if k:
            for d in (1, 2, 3):
                cp = remote(m.at[t ^ d], tb.at[t], ts.at[k - 1, d - 1], tr.at[k - 1, d - 1], (b, t ^ d))
                cp.start()
                sends.append(cp)
    for d in range(G - 1):
        at = ZS.at[zback[d + 1]]
        remote(at, at, zsd.at[4, d], zr.at[4, d], ypeer).wait_recv()
    acc = ZS[0]
    for zz in range(1, G):
        acc = acc + ZS[zz]
    OS[t] = acc
    for d in (1, 2, 3):
        cp = remote(OS.at[t], OS.at[t], ts.at[3, d - 1], tr.at[3, d - 1], (b, t ^ d))
        cp.start()
        sends.append(cp)
    for k, (g, yb, zb, o, m, tb) in enumerate(kinds):
        if k:
            o[t] = m[t].astype(f32)
            for d in (1, 2, 3):
                at = tb.at[t ^ d]
                remote(at, at, ts.at[k - 1, d - 1], tr.at[k - 1, d - 1], (b, t ^ d)).wait_recv()
                o[t ^ d] = tb[t ^ d].astype(f32)
    for d in (1, 2, 3):
        at = OS.at[t ^ d]
        remote(at, at, ts.at[3, d - 1], tr.at[3, d - 1], (b, t ^ d)).wait_recv()
    for cp in sends:
        cp.wait_send()


def reduce_all(nb, gd, gu, gc, ga, sg):
    G = nb // 2
    dma = pltpu.SemaphoreType.DMA
    shapes = [x.shape[1:] for x in (gd, gu, gc, ga)]
    return pl.pallas_call(
        functools.partial(reduce_kernel, G),
        out_shape=[jax.ShapeDtypeStruct(s, f32) for s in shapes]
        + [jax.ShapeDtypeStruct((4,) + sg.shape, f32)],
        in_specs=[VM] * 5,
        out_specs=[VM] * 5,
        scratch_shapes=[pltpu.VMEM((G,) + s, bf16) for s in shapes]
        + [pltpu.VMEM(sg.shape, f32)]
        + [pltpu.VMEM((G - 1,) + s, bf16) for s in shapes]
        + [pltpu.VMEM((G,) + sg.shape, f32)]
        + [pltpu.VMEM(s, bf16) for s in shapes[1:]]
        + [pltpu.VMEM(s, bf16) for s in shapes[1:]]
        + [dma((5, G)), dma((5, G)), dma((5, G)), dma((5, G)), dma((4, 3)), dma((4, 3))],
        compiler_params=pltpu.CompilerParams(
            collective_id=1, has_side_effects=True, vmem_limit_bytes=48 * 2**20
        ),
        name="reduce_all",
    )(gd, gu, gc, ga, sg)


def dot(a, b):
    return jnp.dot(a, b, preferred_element_type=f32)


def dot_tn(a, b):
    return lax.dot_general(a, b, (((0,), (0,)), ((), ())), preferred_element_type=f32)


def dot_nt(a, b):
    return lax.dot_general(a, b, (((1,), (1,)), ((), ())), preferred_element_type=f32)


def per_device(
    nb,
    segment,
    memory,
    compressed,
    evicted,
    window_mask,
    cotangent,
    w_query,
    w_key,
    w_value,
    w_output,
    w_up,
    b_up,
    w_down,
    b_down,
    ln_gain,
    ln_bias,
    w_conv,
    b_conv,
    slopes,
):
    S, R, M = segment.shape
    heads = slopes.shape[0]
    hd = M // heads
    nt = 4
    rw, rd, rs = w_query.shape[0], w_down.shape[0], b_down.shape[0]
    b, t = lax.axis_index("batch"), lax.axis_index("tier")
    Cw, Fw = M // nt, nb * rd
    nu, W = R // 16, R // 3
    seg_len = nt * R
    T = S * seg_len
    ht = heads // nt
    index = 4 * b + t

    wa = jnp.stack([w_query, w_key, w_value, w_output]).reshape(4, rw, nt, Cw)
    wa = wa.transpose(2, 1, 0, 3).reshape(nt, rw, 4 * Cw)
    wu = w_up.reshape(rw, nb, nt, rd).transpose(2, 0, 1, 3).reshape(nt, rw, Fw)
    wc = w_conv.reshape(3, rw, nt, Cw).transpose(2, 1, 0, 3).reshape(nt, rw, 3 * Cw)
    row0 = jnp.concatenate([ln_gain, ln_bias, b_down, b_conv])
    sm = jnp.zeros((8, 128), f32).at[0, : 4 * rs].set(row0.astype(f32)).at[1, :rd].set(b_up.astype(f32))
    mem = memory.reshape(S, W, 3, M).transpose(0, 2, 1, 3)
    mk = jnp.broadcast_to(window_mask.astype(f32)[:, :, None], (S, W, 128))
    WA, WU, WC, WD, SM, CTX, COT, MK = gather_all(
        nb,
        nu,
        wa,
        wu,
        wc,
        w_down,
        sm,
        compressed.reshape(S, nu, 16, M),
        mem,
        segment.reshape(S, nu, 16, M),
        cotangent.reshape(S, nu, 16, M),
        mk,
    )
    WA = WA.reshape(M, 4 * Cw)
    Wqkv, Wo = WA[:, : 3 * Cw], WA[:, 3 * Cw :]
    WU, WC, WD = WU.reshape(M, Fw), WC.reshape(M, 3 * Cw), WD.reshape(Fw, M)
    gain, bias, bdown, bconv = [SM[:, :, 0, i * rs : (i + 1) * rs].reshape(M) for i in range(4)]
    bup = lax.dynamic_index_in_dim(SM, t, 1, False)[:, 1, :rd].reshape(Fw)
    cols = lambda v: lax.dynamic_slice_in_dim(v, t * Cw, Cw, v.ndim - 1)
    ctx = CTX.reshape(S, 3 * seg_len, M)
    cot = COT.reshape(T, M)
    seg = ctx[:, 2 * seg_len :].reshape(T, M)

    kpos = jnp.concatenate(
        [
            jnp.arange(seg_len),
            seg_len + (3 * jnp.arange(seg_len // 3)[None, :] + jnp.arange(3)[:, None]).reshape(-1),
            2 * seg_len + jnp.arange(seg_len),
        ]
    )
    qpos = 2 * seg_len + jnp.arange(seg_len)
    allowed = kpos[None, :] <= qpos[:, None]
    dist = (qpos[:, None] - kpos[None, :]).astype(f32) * (1.0 / (3 * seg_len))
    slope = lax.dynamic_slice_in_dim(slopes, t * ht, ht)
    scale = 1.0 / math.sqrt(hd)
    q = dot(seg, Wqkv[:, :Cw]).astype(bf16).reshape(S, seg_len, ht, hd)
    kv = dot(ctx.reshape(-1, M), Wqkv[:, Cw:]).astype(bf16).reshape(S, 3 * seg_len, 2, ht, hd)
    kk, vv = kv[:, :, 0], kv[:, :, 1]
    raw = jnp.einsum("sqhd,skhd->shqk", q, kk, preferred_element_type=f32)
    scores = jnp.where(allowed, raw * scale - slope[:, None, None] * dist, -1e30)
    high = jnp.max(scores, axis=-1, keepdims=True)
    e = jnp.exp(scores - high)
    probs = e / jnp.sum(e, axis=-1, keepdims=True)
    probs_low = probs.astype(bf16)
    mixed_t = jnp.einsum("shqk,skhd->sqhd", probs_low, vv, preferred_element_type=f32).astype(bf16)
    MIX = spread(mixed_t.reshape(T, Cw), True, 2)
    mixed = MIX.transpose(1, 0, 2).reshape(T, M)
    resid_t = cols(seg).astype(f32) + dot(mixed, Wo)
    RES = spread(resid_t.astype(bf16), True, 3)
    resid = RES.transpose(1, 0, 2).reshape(T, M).astype(f32)
    center = resid - jnp.mean(resid, axis=-1, keepdims=True)
    spread_ = lax.rsqrt(jnp.mean(center * center, axis=-1, keepdims=True) + norm_eps)
    xhat = center * spread_
    normed = (xhat * gain + bias).astype(bf16)
    pre = dot(normed, WU) + bup
    phi = 0.5 * (1.0 + lax.erf(pre * math.sqrt(0.5)))
    act = (pre * phi).astype(bf16)
    slope_act = phi + pre * jnp.exp(-0.5 * pre * pre) * (1.0 / math.sqrt(2 * math.pi))
    place = lambda v: lax.dynamic_update_slice_in_dim(jnp.zeros((T, M), f32), v, t * Cw, 1)
    out_part = dot(act, WD) + place(resid_t + cols(bdown))
    rows = lambda v: v.astype(bf16).reshape(S, nt, R, M).transpose(1, 0, 2, 3)
    output = jnp.sum(spread(rows(out_part), False, 4).astype(f32), axis=0).astype(bf16)
    gdown = dot_tn(act, cot)
    d_act = dot_nt(cot, WD).astype(bf16)
    d_pre = d_act.astype(f32) * slope_act
    gub = jnp.sum(d_pre, axis=0)
    d_pre_low = d_pre.astype(bf16)
    gup = dot_tn(normed, d_pre_low)
    dn_part = dot_nt(d_pre_low, WU)
    stats = jnp.stack([jnp.mean(dn_part * gain, axis=1), jnp.mean(dn_part * gain * xhat, axis=1)])
    stats = lax.psum(stats, "tier")
    cols_of = lambda v: v.astype(bf16).reshape(T, nt, Cw).transpose(1, 0, 2)
    dn = jnp.sum(spread(cols_of(dn_part), False, 5).astype(f32), axis=0)
    xhat_t = cols(xhat)
    ggain, gbias = jnp.sum(dn * xhat_t, axis=0), jnp.sum(dn, axis=0)
    g = dn * cols(gain)
    cot_t = cols(cot).astype(f32)
    gdb = jnp.sum(cot_t, axis=0)
    d_resid = cot_t + (g - stats[0][:, None] - xhat_t * stats[1][:, None]) * spread_
    d_branch = d_resid.astype(bf16)
    gout = dot_tn(mixed, d_branch)
    dm_part = dot_nt(d_branch, Wo)
    dm = jnp.sum(spread(cols_of(dm_part), False, 6).astype(f32), axis=0).astype(bf16)
    dm = dm.reshape(S, seg_len, ht, hd)
    d_probs = jnp.einsum("sqhd,skhd->shqk", dm, vv, preferred_element_type=f32)
    delta = jnp.sum(probs * d_probs, axis=-1, keepdims=True)
    d_scores = probs * (d_probs - delta)
    gslope = -jnp.sum(d_scores * dist, axis=(0, 2, 3))
    d_raw = (d_scores * scale).astype(bf16)
    dq = jnp.einsum("shqk,skhd->sqhd", d_raw, kk, preferred_element_type=f32).astype(bf16)
    dk = jnp.einsum("shqk,sqhd->skhd", d_raw, q, preferred_element_type=f32).astype(bf16)
    dv = jnp.einsum("shqk,sqhd->skhd", probs_low, dm, preferred_element_type=f32).astype(bf16)
    dq, dk, dv = dq.reshape(T, Cw), dk.reshape(S, -1, Cw), dv.reshape(S, -1, Cw)
    flat = ctx.reshape(-1, M)
    gq = dot_tn(seg, dq)
    gk, gv = dot_tn(flat, dk.reshape(-1, Cw)), dot_tn(flat, dv.reshape(-1, Cw))
    own = lambda v: v[:, 2 * seg_len :].reshape(T, Cw)
    ig_part = dot_nt(jnp.concatenate([dq, own(dk), own(dv)], axis=1), Wqkv) + place(d_resid)
    input_grad = jnp.sum(spread(rows(ig_part), False, 7).astype(f32), axis=0)

    nw = seg_len // 3
    win = ctx[:, seg_len : 2 * seg_len].reshape(S, 3, nw, M)
    win = [win[:, k].reshape(S * nw, M) for k in range(3)]
    conv = sum(dot(win[k], WC[:, k * Cw : (k + 1) * Cw]) for k in range(3)) + cols(bconv)
    pooled = sum(cols(win[k]).astype(f32) for k in range(3)) * (1.0 / 3.0)
    mask = MK.reshape(S, nw, 128)[:, :, :1]
    old = (3 * jnp.arange(nw) + 3)[None, :, None] <= evicted[:, None, None]
    live = jnp.where(old, mask, 0.0).reshape(-1, 1)
    d_conv = live * (conv - pooled)
    gcb = jnp.sum(d_conv, axis=0)
    d_low = d_conv.astype(bf16)
    gconv = jnp.concatenate([dot_tn(win[k], d_low) for k in range(3)], axis=1)
    new_t = (mask.reshape(-1, 1) * conv).astype(bf16)
    NEW = spread(new_t, True, 8).reshape(nt, S, nw, Cw).transpose(1, 2, 0, 3).reshape(S, nw, M)
    slot_offset = seg_len - nw
    local_rows = jnp.arange(R, dtype=jnp.int32) + t * R
    padded = jnp.concatenate([jnp.zeros((S, slot_offset, M), bf16), NEW], axis=1)
    slot_rows = lax.dynamic_slice_in_dim(padded, t * R, R, 1)
    written = (local_rows[None, :] >= slot_offset) & (
        3 * (local_rows[None, :] - slot_offset) + 3 <= evicted[:, None]
    )
    new_compressed = jnp.where(written[..., None], slot_rows, compressed)
    new_memory = jnp.where((local_rows[None, :] < evicted[:, None])[..., None], segment, memory)

    low = lambda v, *s: v.astype(bf16).reshape(s)
    gs = lax.dynamic_update_slice_in_dim(jnp.zeros((128,), f32), gslope, t * ht, 0)
    sg = jnp.concatenate([gub, gdb, ggain, gbias, gcb, gs])
    sg = jnp.concatenate([sg, jnp.zeros((24 * 128 - sg.shape[0],), f32)]).reshape(24, 128)
    OD, OU, OC, OA, OS = reduce_all(
        nb,
        low(gdown, nb, 4, rd // 4, M),
        low(gup, nb, 4, rw, Fw),
        low(gconv, nb, 4, rw, 3 * Cw),
        low(jnp.concatenate([gq, gk, gv, gout], axis=1), nb, 4, rw, 4 * Cw),
        sg,
    )
    OA = OA.reshape(nt, rw, 4, Cw).transpose(2, 1, 0, 3).reshape(4, rw, M)
    OU = OU.reshape(nt, rw, nb, rd).transpose(1, 2, 0, 3).reshape(rw, nb * nt * rd)
    OC = OC.reshape(nt, rw, 3, Cw).transpose(2, 1, 0, 3).reshape(3, rw, M)
    OS = OS.reshape(nt, -1)
    vec = lambda o: lax.dynamic_slice_in_dim(OS[:, o : o + Cw].reshape(M), index * rs, rs)
    gub_out = lax.dynamic_slice(OS, (t, b * rd), (1, rd)).reshape(rd)
    gslopes = jnp.sum(OS[:, Fw + 4 * Cw : Fw + 4 * Cw + heads], axis=0)
    return (
        output,
        input_grad,
        new_memory,
        new_compressed,
        OA[0],
        OA[1],
        OA[2],
        OA[3],
        OU,
        gub_out,
        OD.reshape(rd, M),
        vec(Fw),
        vec(Fw + Cw),
        vec(Fw + 2 * Cw),
        OC,
        vec(Fw + 3 * Cw),
        gslopes,
    )


def solution(mesh):
    both = ("batch", "tier")
    rows = P("batch", "tier", None)
    mat, vec = P(both, None), P(both)
    return jax.shard_map(
        functools.partial(per_device, mesh.shape["batch"]),
        mesh=mesh,
        in_specs=(
            (rows, rows, rows, P("batch"), P("batch", "tier"), rows)
            + (mat, mat, mat, mat, mat, vec, mat, vec, vec, vec)
            + (P(None, both, None), vec, P())
        ),
        out_specs=(
            (rows, rows, rows, rows, mat, mat, mat, mat, mat, vec, mat, vec, vec, vec)
            + (P(None, both, None), vec, P())
        ),
        check_vma=False,
    )
```

```python
import functools
import math

import jax
import jax.numpy as jnp
from jax import lax
from jax.experimental import pallas as pl
from jax.experimental.pallas import tpu as pltpu
from jax.sharding import PartitionSpec as P

norm_eps = 1e-05
MESH = pl.DeviceIdType.MESH
ANY = pl.BlockSpec(memory_space=pl.ANY)
VM = pl.BlockSpec(memory_space=pltpu.VMEM)
f32 = jnp.float32
bf16 = jnp.bfloat16


def remote(src, dst, send, recv, device):
    return pltpu.make_async_remote_copy(
        src_ref=src,
        dst_ref=dst,
        send_sem=send,
        recv_sem=recv,
        device_id=device,
        device_id_type=MESH,
    )


def places(groups):
    b, t = lax.axis_index("batch"), lax.axis_index("tier")
    z, y = b // 2, lax.rem(b, 2)
    zs = [lax.rem(z + d, groups) for d in range(groups)]
    zback = [lax.rem(z + groups - d, groups) for d in range(groups)]
    return b, t, z, y, zs, zback


def greet(groups, tiers, columns):
    b, t, z, y, zs, _ = places(groups)
    barrier = pltpu.get_barrier_semaphore()
    peers = []
    if tiers:
        peers += [(b, t ^ d) for d in (1, 2, 3)]
    if columns:
        peers += [(2 * zz + y, t) for zz in zs[1:]] + [(b ^ 1, t)]
    for peer in peers:
        pl.semaphore_signal(barrier, inc=1, device_id=peer, device_id_type=MESH)
    pl.semaphore_wait(barrier, len(peers))


def gather_kernel(groups, nu, *refs):
    (wa, wu, wc, wd, sm, comp, mem, seg, cot, mk) = refs[:10]
    (WA, WU, WC, WD, SM, CTX, COT, MK) = refs[10:18]
    lsem, ts, tr, zsd, zr, ys, yr, acs, acr = refs[18:]
    G = groups
    b, t, z, y, zs, zback = places(G)
    greet(G, True, True)
    ypeer = (b ^ 1, t)
    local, sends = [], []

    def here(src, dst, i):
        cp = pltpu.make_async_copy(src, dst, lsem.at[i])
        cp.start()
        return cp

    kinds = [(sm, SM), (wa, WA), (wu, WU), (wc, WC)]
    own = []
    for k, (src, dst) in enumerate(kinds):
        mine = src if k == 0 else src.at[t]
        own.append(here(mine, dst.at[b, t], k))
        for d in (1, 2, 3):
            piece = src if k == 0 else src.at[t ^ d]
            cp = remote(piece, dst.at[b, t], ts.at[k, d - 1], tr.at[k, d - 1], (b, t ^ d))
            cp.start()
            sends.append(cp)
    own.append(here(wd, WD.at[b], 4))
    pieces = [
        (comp, lambda q: CTX.at[:, pl.ds(nu * q, nu)]),
        (mem.at[:, 0], lambda q: CTX.at[:, 4 * nu + q]),
        (mem.at[:, 1], lambda q: CTX.at[:, 4 * nu + 4 + q]),
        (mem.at[:, 2], lambda q: CTX.at[:, 4 * nu + 8 + q]),
        (seg, lambda q: CTX.at[:, pl.ds(8 * nu + nu * q, nu)]),
        (mk, lambda q: MK.at[:, q]),
        (cot, lambda q: COT.at[:, pl.ds(nu * q, nu)]),
    ]
    for i, (src, at) in enumerate(pieces):
        own.append(here(src, at(t), 5 + i))
        for j, d in enumerate((1, 2)):
            cp = remote(src, at(t), acs.at[i, j], acr.at[i, j], (b, t ^ d))
            cp.start()
            sends.append(cp)
    table = [SM, WA, WU, WD, WC]
    local_of = [0, 1, 2, 4, 3]
    for k, dst in enumerate(table):
        own[local_of[k]].wait()
        if k != 3:
            kk = local_of[k]
            for d in (1, 2, 3):
                remote(dst.at[b, t], dst.at[b, t ^ d], ts.at[kk, d - 1], tr.at[kk, d - 1], (b, t ^ d)).wait_recv()
        for d in range(1, G):
            cp = remote(dst.at[b], dst.at[b], zsd.at[k, d], zr.at[k, d], (2 * zs[d] + y, t))
            cp.start()
            sends.append(cp)
        cp = remote(dst.at[b], dst.at[b], ys.at[k, 0], yr.at[k, 0], ypeer)
        cp.start()
        sends.append(cp)
    for i, (src, at) in enumerate(pieces):
        remote(at(t ^ 2), at(t ^ 2), acs.at[i, 1], acr.at[i, 1], (b, t ^ 2)).wait_recv()
        cp = remote(at(t ^ 2), at(t ^ 2), acs.at[i, 2], acr.at[i, 2], (b, t ^ 1))
        cp.start()
        sends.append(cp)
    for k, dst in enumerate(table):
        for d in range(1, G):
            at = dst.at[2 * zback[d] + y]
            remote(at, at, zsd.at[k, d], zr.at[k, d], ypeer).wait_recv()
            cp = remote(at, at, ys.at[k, d], yr.at[k, d], ypeer)
            cp.start()
            sends.append(cp)
    for k, dst in enumerate(table):
        for d in range(G):
            at = dst.at[2 * zback[d] + (1 - y)]
            remote(at, at, ys.at[k, d], yr.at[k, d], ypeer).wait_recv()
    for i, (src, at) in enumerate(pieces):
        for j, q in ((0, t ^ 1), (2, t ^ 3)):
            remote(at(q), at(q), acs.at[i, j], acr.at[i, j], (b, t ^ 1)).wait_recv()
    for i in range(len(pieces)):
        own[5 + i].wait()
    for cp in sends:
        cp.wait_send()


def gather_all(nb, nu, wa, wu, wc, wd, sm, comp, mem, seg, cot, mk):
    G = nb // 2
    S, _, U, M = comp.shape
    out = [
        jax.ShapeDtypeStruct((nb,) + wa.shape, bf16),
        jax.ShapeDtypeStruct((nb,) + wu.shape, bf16),
        jax.ShapeDtypeStruct((nb,) + wc.shape, bf16),
        jax.ShapeDtypeStruct((nb,) + wd.shape, bf16),
        jax.ShapeDtypeStruct((nb, 4) + sm.shape, f32),
        jax.ShapeDtypeStruct((S, 12 * nu, U, M), bf16),
        jax.ShapeDtypeStruct((S, 4 * nu, U, M), bf16),
        jax.ShapeDtypeStruct((S, 4) + mk.shape[1:], f32),
    ]
    dma = pltpu.SemaphoreType.DMA
    return pl.pallas_call(
        functools.partial(gather_kernel, G, nu),
        out_shape=out,
        in_specs=[ANY] * 10,
        out_specs=[ANY] * 8,
        scratch_shapes=[
            dma((12,)),
            dma((4, 3)),
            dma((4, 3)),
            dma((5, G)),
            dma((5, G)),
            dma((5, G)),
            dma((5, G)),
            dma((7, 3)),
            dma((7, 3)),
        ],
        compiler_params=pltpu.CompilerParams(collective_id=0, has_side_effects=True),
        name="gather_all",
    )(wa, wu, wc, wd, sm, comp, mem, seg, cot, mk)


def spread_kernel(same, x, o, lsem, ss, rs):
    b, t = lax.axis_index("batch"), lax.axis_index("tier")
    greet(1, True, False)
    cps = []
    for d in (1, 2, 3):
        cp = remote(x if same else x.at[t ^ d], o.at[t], ss.at[d - 1], rs.at[d - 1], (b, t ^ d))
        cp.start()
        cps.append(cp)
    mine = pltpu.make_async_copy(x if same else x.at[t], o.at[t], lsem)
    mine.start()
    mine.wait()
    for d in (1, 2, 3):
        remote(o.at[t ^ d], o.at[t ^ d], ss.at[d - 1], rs.at[d - 1], (b, t ^ d)).wait_recv()
    for cp in cps:
        cp.wait_send()


def spread(x, same, cid):
    dma = pltpu.SemaphoreType.DMA
    shape = ((4,) + x.shape) if same else x.shape
    return pl.pallas_call(
        functools.partial(spread_kernel, same),
        out_shape=jax.ShapeDtypeStruct(shape, x.dtype),
        in_specs=[ANY],
        out_specs=ANY,
        scratch_shapes=[dma, dma((3,)), dma((3,))],
        compiler_params=pltpu.CompilerParams(collective_id=cid, has_side_effects=True),
        name="spread_%d" % cid,
    )(x)


def reduce_kernel(groups, *refs):
    GD, GU, GC, GA, SMG = refs[:5]
    OD, OU, OC, OA, OS = refs[5:10]
    YD, YU, YC, YA, YS, ZD, ZU, ZC, ZA, ZS, TU, TC, TA, MU, MC, MA, ys, yr, zsd, zr, ts, tr = refs[10:]
    G = groups
    b, t, z, y, zs, zback = places(G)
    greet(G, True, True)
    ypeer = (b ^ 1, t)
    sends = []
    kinds = [
        (GD, YD, ZD, OD, None, None),
        (GU, YU, ZU, OU, MU, TU),
        (GC, YC, ZC, OC, MC, TC),
        (GA, YA, ZA, OA, MA, TA),
    ]
    for k, (g, yb, *_) in enumerate(kinds):
        for d in range(G):
            zz = zs[(d + 1) % G]
            cp = remote(g.at[2 * zz + (1 - y)], yb.at[zz], ys.at[k, d], yr.at[k, d], ypeer)
            cp.start()
            sends.append(cp)
    cp = remote(SMG, YS, ys.at[4, 0], yr.at[4, 0], ypeer)
    cp.start()
    sends.append(cp)
    for k, (g, yb, zb, o, m, tb) in enumerate(kinds):
        for d in range(G):
            zz = zs[(d + 1) % G]
            at = yb.at[zz]
            remote(at, at, ys.at[k, d], yr.at[k, d], ypeer).wait_recv()

            def add(i, c, yb=yb, zz=zz, g=g):
                yb[zz, i] = (yb[zz, i].astype(f32) + g[2 * zz + y, i].astype(f32)).astype(bf16)
                return c

            lax.fori_loop(0, yb.shape[1], add, 0)
            if d < G - 1:
                cp = remote(at, zb.at[d], zsd.at[k, d], zr.at[k, d], (2 * zz + y, t))
                cp.start()
                sends.append(cp)
    remote(YS, YS, ys.at[4, 0], yr.at[4, 0], ypeer).wait_recv()
    ZS[z] = SMG[...] + YS[...]
    for d in range(G - 1):
        cp = remote(ZS.at[z], ZS.at[z], zsd.at[4, d], zr.at[4, d], (2 * zs[d + 1] + y, t))
        cp.start()
        sends.append(cp)
    for k, (g, yb, zb, o, m, tb) in enumerate(kinds):
        for d in range(G - 1):
            remote(zb.at[d], zb.at[d], zsd.at[k, d], zr.at[k, d], ypeer).wait_recv()

        def total(i, c, k=k, yb=yb, zb=zb, o=o, m=m):
            acc = yb[z, i].astype(f32)
            for d in range(G - 1):
                acc = acc + zb[d, i].astype(f32)
            if k == 0:
                o[i] = acc
            else:
                m[i] = acc.astype(bf16)
            return c

        lax.fori_loop(0, o.shape[0], total, 0)
        if k:
            for d in (1, 2, 3):
                cp = remote(m.at[t ^ d], tb.at[t], ts.at[k - 1, d - 1], tr.at[k - 1, d - 1], (b, t ^ d))
                cp.start()
                sends.append(cp)
    for d in range(G - 1):
        at = ZS.at[zback[d + 1]]
        remote(at, at, zsd.at[4, d], zr.at[4, d], ypeer).wait_recv()
    acc = ZS[0]
    for zz in range(1, G):
        acc = acc + ZS[zz]
    OS[t] = acc
    for d in (1, 2, 3):
        cp = remote(OS.at[t], OS.at[t], ts.at[3, d - 1], tr.at[3, d - 1], (b, t ^ d))
        cp.start()
        sends.append(cp)
    for k, (g, yb, zb, o, m, tb) in enumerate(kinds):
        if k:
            o[t] = m[t].astype(f32)
            for d in (1, 2, 3):
                at = tb.at[t ^ d]
                remote(at, at, ts.at[k - 1, d - 1], tr.at[k - 1, d - 1], (b, t ^ d)).wait_recv()
                o[t ^ d] = tb[t ^ d].astype(f32)
    for d in (1, 2, 3):
        at = OS.at[t ^ d]
        remote(at, at, ts.at[3, d - 1], tr.at[3, d - 1], (b, t ^ d)).wait_recv()
    for cp in sends:
        cp.wait_send()


def reduce_all(nb, gd, gu, gc, ga, sg):
    G = nb // 2
    dma = pltpu.SemaphoreType.DMA
    shapes = [x.shape[1:] for x in (gd, gu, gc, ga)]
    return pl.pallas_call(
        functools.partial(reduce_kernel, G),
        out_shape=[jax.ShapeDtypeStruct(s, f32) for s in shapes]
        + [jax.ShapeDtypeStruct((4,) + sg.shape, f32)],
        in_specs=[VM] * 5,
        out_specs=[VM] * 5,
        scratch_shapes=[pltpu.VMEM((G,) + s, bf16) for s in shapes]
        + [pltpu.VMEM(sg.shape, f32)]
        + [pltpu.VMEM((G - 1,) + s, bf16) for s in shapes]
        + [pltpu.VMEM((G,) + sg.shape, f32)]
        + [pltpu.VMEM(s, bf16) for s in shapes[1:]]
        + [pltpu.VMEM(s, bf16) for s in shapes[1:]]
        + [dma((5, G)), dma((5, G)), dma((5, G)), dma((5, G)), dma((4, 3)), dma((4, 3))],
        compiler_params=pltpu.CompilerParams(
            collective_id=1, has_side_effects=True, vmem_limit_bytes=48 * 2**20
        ),
        name="reduce_all",
    )(gd, gu, gc, ga, sg)


def dot(a, b):
    return jnp.dot(a, b, preferred_element_type=f32)


def dot_tn(a, b):
    return lax.dot_general(a, b, (((0,), (0,)), ((), ())), preferred_element_type=f32)


def dot_nt(a, b):
    return lax.dot_general(a, b, (((1,), (1,)), ((), ())), preferred_element_type=f32)


def per_device(
    nb,
    segment,
    memory,
    compressed,
    evicted,
    window_mask,
    cotangent,
    w_query,
    w_key,
    w_value,
    w_output,
    w_up,
    b_up,
    w_down,
    b_down,
    ln_gain,
    ln_bias,
    w_conv,
    b_conv,
    slopes,
):
    S, R, M = segment.shape
    heads = slopes.shape[0]
    hd = M // heads
    nt = 4
    rw, rd, rs = w_query.shape[0], w_down.shape[0], b_down.shape[0]
    b, t = lax.axis_index("batch"), lax.axis_index("tier")
    Cw, Fw = M // nt, nb * rd
    nu, W = R // 16, R // 3
    seg_len = nt * R
    T = S * seg_len
    ht = heads // nt
    index = 4 * b + t

    wa = jnp.stack([w_query, w_key, w_value, w_output]).reshape(4, rw, nt, Cw)
    wa = wa.transpose(2, 1, 0, 3).reshape(nt, rw, 4 * Cw)
    wu = w_up.reshape(rw, nb, nt, rd).transpose(2, 0, 1, 3).reshape(nt, rw, Fw)
    wc = w_conv.reshape(3, rw, nt, Cw).transpose(2, 1, 0, 3).reshape(nt, rw, 3 * Cw)
    row0 = jnp.concatenate([ln_gain, ln_bias, b_down, b_conv])
    sm = jnp.zeros((8, 128), f32).at[0, : 4 * rs].set(row0.astype(f32)).at[1, :rd].set(b_up.astype(f32))
    mem = memory.reshape(S, W, 3, M).transpose(0, 2, 1, 3)
    mk = jnp.broadcast_to(window_mask.astype(f32)[:, :, None], (S, W, 128))
    WA, WU, WC, WD, SM, CTX, COT, MK = gather_all(
        nb,
        nu,
        wa,
        wu,
        wc,
        w_down,
        sm,
        compressed.reshape(S, nu, 16, M),
        mem,
        segment.reshape(S, nu, 16, M),
        cotangent.reshape(S, nu, 16, M),
        mk,
    )
    WA = WA.reshape(M, 4 * Cw)
    Wqkv, Wo = WA[:, : 3 * Cw], WA[:, 3 * Cw :]
    WU, WC, WD = WU.reshape(M, Fw), WC.reshape(M, 3 * Cw), WD.reshape(Fw, M)
    gain, bias, bdown, bconv = [SM[:, :, 0, i * rs : (i + 1) * rs].reshape(M) for i in range(4)]
    bup = lax.dynamic_index_in_dim(SM, t, 1, False)[:, 1, :rd].reshape(Fw)
    cols = lambda v: lax.dynamic_slice_in_dim(v, t * Cw, Cw, v.ndim - 1)
    ctx = CTX.reshape(S, 3 * seg_len, M)
    cot = COT.reshape(T, M)
    seg = ctx[:, 2 * seg_len :].reshape(T, M)

    kpos = jnp.concatenate(
        [
            jnp.arange(seg_len),
            seg_len + (3 * jnp.arange(seg_len // 3)[None, :] + jnp.arange(3)[:, None]).reshape(-1),
            2 * seg_len + jnp.arange(seg_len),
        ]
    )
    qpos = 2 * seg_len + jnp.arange(seg_len)
    allowed = kpos[None, :] <= qpos[:, None]
    dist = (qpos[:, None] - kpos[None, :]).astype(f32) * (1.0 / (3 * seg_len))
    slope = lax.dynamic_slice_in_dim(slopes, t * ht, ht)
    scale = 1.0 / math.sqrt(hd)
    q = dot(seg, Wqkv[:, :Cw]).astype(bf16).reshape(S, seg_len, ht, hd)
    kv = dot(ctx.reshape(-1, M), Wqkv[:, Cw:]).astype(bf16).reshape(S, 3 * seg_len, 2, ht, hd)
    kk, vv = kv[:, :, 0], kv[:, :, 1]
    raw = jnp.einsum("sqhd,skhd->shqk", q, kk, preferred_element_type=f32)
    scores = jnp.where(allowed, raw * scale - slope[:, None, None] * dist, -1e30)
    high = jnp.max(scores, axis=-1, keepdims=True)
    e = jnp.exp(scores - high)
    probs = e / jnp.sum(e, axis=-1, keepdims=True)
    probs_low = probs.astype(bf16)
    mixed_t = jnp.einsum("shqk,skhd->sqhd", probs_low, vv, preferred_element_type=f32).astype(bf16)
    MIX = spread(mixed_t.reshape(T, Cw), True, 2)
    mixed = MIX.transpose(1, 0, 2).reshape(T, M)
    resid_t = cols(seg).astype(f32) + dot(mixed, Wo)
    RES = spread(resid_t.astype(bf16), True, 3)
    resid = RES.transpose(1, 0, 2).reshape(T, M).astype(f32)
    center = resid - jnp.mean(resid, axis=-1, keepdims=True)
    spread_ = lax.rsqrt(jnp.mean(center * center, axis=-1, keepdims=True) + norm_eps)
    xhat = center * spread_
    normed = (xhat * gain + bias).astype(bf16)
    pre = dot(normed, WU) + bup
    phi = 0.5 * (1.0 + lax.erf(pre * math.sqrt(0.5)))
    act = (pre * phi).astype(bf16)
    slope_act = phi + pre * jnp.exp(-0.5 * pre * pre) * (1.0 / math.sqrt(2 * math.pi))
    place = lambda v: lax.dynamic_update_slice_in_dim(jnp.zeros((T, M), f32), v, t * Cw, 1)
    out_part = dot(act, WD) + place(resid_t + cols(bdown))
    rows = lambda v: v.astype(bf16).reshape(S, nt, R, M).transpose(1, 0, 2, 3)
    output = jnp.sum(spread(rows(out_part), False, 4).astype(f32), axis=0).astype(bf16)
    gdown = dot_tn(act, cot)
    d_act = dot_nt(cot, WD).astype(bf16)
    d_pre = d_act.astype(f32) * slope_act
    gub = jnp.sum(d_pre, axis=0)
    d_pre_low = d_pre.astype(bf16)
    gup = dot_tn(normed, d_pre_low)
    dn_part = dot_nt(d_pre_low, WU)
    stats = jnp.stack([jnp.mean(dn_part * gain, axis=1), jnp.mean(dn_part * gain * xhat, axis=1)])
    stats = lax.psum(stats, "tier")
    cols_of = lambda v: v.astype(bf16).reshape(T, nt, Cw).transpose(1, 0, 2)
    dn = jnp.sum(spread(cols_of(dn_part), False, 5).astype(f32), axis=0)
    xhat_t = cols(xhat)
    ggain, gbias = jnp.sum(dn * xhat_t, axis=0), jnp.sum(dn, axis=0)
    g = dn * cols(gain)
    cot_t = cols(cot).astype(f32)
    gdb = jnp.sum(cot_t, axis=0)
    d_resid = cot_t + (g - stats[0][:, None] - xhat_t * stats[1][:, None]) * spread_
    d_branch = d_resid.astype(bf16)
    gout = dot_tn(mixed, d_branch)
    dm_part = dot_nt(d_branch, Wo)
    dm = jnp.sum(spread(cols_of(dm_part), False, 6).astype(f32), axis=0).astype(bf16)
    dm = dm.reshape(S, seg_len, ht, hd)
    d_probs = jnp.einsum("sqhd,skhd->shqk", dm, vv, preferred_element_type=f32)
    delta = jnp.sum(probs * d_probs, axis=-1, keepdims=True)
    d_scores = probs * (d_probs - delta)
    gslope = -jnp.sum(d_scores * dist, axis=(0, 2, 3))
    d_raw = (d_scores * scale).astype(bf16)
    dq = jnp.einsum("shqk,skhd->sqhd", d_raw, kk, preferred_element_type=f32).astype(bf16)
    dk = jnp.einsum("shqk,sqhd->skhd", d_raw, q, preferred_element_type=f32).astype(bf16)
    dv = jnp.einsum("shqk,sqhd->skhd", probs_low, dm, preferred_element_type=f32).astype(bf16)
    dq, dk, dv = dq.reshape(T, Cw), dk.reshape(S, -1, Cw), dv.reshape(S, -1, Cw)
    flat = ctx.reshape(-1, M)
    gq = dot_tn(seg, dq)
    gk, gv = dot_tn(flat, dk.reshape(-1, Cw)), dot_tn(flat, dv.reshape(-1, Cw))
    own = lambda v: v[:, 2 * seg_len :].reshape(T, Cw)
    ig_part = dot_nt(jnp.concatenate([dq, own(dk), own(dv)], axis=1), Wqkv) + place(d_resid)
    input_grad = jnp.sum(spread(rows(ig_part), False, 7).astype(f32), axis=0)

    nw = seg_len // 3
    win = ctx[:, seg_len : 2 * seg_len].reshape(S, 3, nw, M)
    win = [win[:, k].reshape(S * nw, M) for k in range(3)]
    conv = sum(dot(win[k], WC[:, k * Cw : (k + 1) * Cw]) for k in range(3)) + cols(bconv)
    pooled = sum(cols(win[k]).astype(f32) for k in range(3)) * (1.0 / 3.0)
    mask = MK.reshape(S, nw, 128)[:, :, :1]
    old = (3 * jnp.arange(nw) + 3)[None, :, None] <= evicted[:, None, None]
    live = jnp.where(old, mask, 0.0).reshape(-1, 1)
    d_conv = live * (conv - pooled)
    gcb = jnp.sum(d_conv, axis=0)
    d_low = d_conv.astype(bf16)
    gconv = jnp.concatenate([dot_tn(win[k], d_low) for k in range(3)], axis=1)
    new_t = (mask.reshape(-1, 1) * conv).astype(bf16)
    NEW = spread(new_t, True, 8).reshape(nt, S, nw, Cw).transpose(1, 2, 0, 3).reshape(S, nw, M)
    slot_offset = seg_len - nw
    local_rows = jnp.arange(R, dtype=jnp.int32) + t * R
    padded = jnp.concatenate([jnp.zeros((S, slot_offset, M), bf16), NEW], axis=1)
    slot_rows = lax.dynamic_slice_in_dim(padded, t * R, R, 1)
    written = (local_rows[None, :] >= slot_offset) & (
        3 * (local_rows[None, :] - slot_offset) + 3 <= evicted[:, None]
    )
    new_compressed = jnp.where(written[..., None], slot_rows, compressed)
    new_memory = jnp.where((local_rows[None, :] < evicted[:, None])[..., None], segment, memory)

    low = lambda v, *s: v.astype(bf16).reshape(s)
    gs = lax.dynamic_update_slice_in_dim(jnp.zeros((128,), f32), gslope, t * ht, 0)
    sg = jnp.concatenate([gub, gdb, ggain, gbias, gcb, gs])
    sg = jnp.concatenate([sg, jnp.zeros((24 * 128 - sg.shape[0],), f32)]).reshape(24, 128)
    OD, OU, OC, OA, OS = reduce_all(
        nb,
        low(gdown, nb, 4, rd // 4, M),
        low(gup, nb, 4, rw, Fw),
        low(gconv, nb, 4, rw, 3 * Cw),
        low(jnp.concatenate([gq, gk, gv, gout], axis=1), nb, 4, rw, 4 * Cw),
        sg,
    )
    OA = OA.reshape(nt, rw, 4, Cw).transpose(2, 1, 0, 3).reshape(4, rw, M)
    OU = OU.reshape(nt, rw, nb, rd).transpose(1, 2, 0, 3).reshape(rw, nb * nt * rd)
    OC = OC.reshape(nt, rw, 3, Cw).transpose(2, 1, 0, 3).reshape(3, rw, M)
    OS = OS.reshape(nt, -1)
    vec = lambda o: lax.dynamic_slice_in_dim(OS[:, o : o + Cw].reshape(M), index * rs, rs)
    gub_out = lax.dynamic_slice(OS, (t, b * rd), (1, rd)).reshape(rd)
    gslopes = jnp.sum(OS[:, Fw + 4 * Cw : Fw + 4 * Cw + heads], axis=0)
    return (
        output,
        input_grad,
        new_memory,
        new_compressed,
        OA[0],
        OA[1],
        OA[2],
        OA[3],
        OU,
        gub_out,
        OD.reshape(rd, M),
        vec(Fw),
        vec(Fw + Cw),
        vec(Fw + 2 * Cw),
        OC,
        vec(Fw + 3 * Cw),
        gslopes,
    )


class Names:
    def __init__(self, names, refs):
        for name, ref in zip(names, refs):
            setattr(self, name, ref)


def layer_kernel(names, shape, *refs):
    r = Names(names, refs)
    nb, nu, S, ht, hd, M, Cw, rw, rd = shape
    G, bq = nb // 2, nb // 4
    L = 16 * 4 * nu
    C3 = 3 * L
    nw = L // 3
    Fw = nb * rd
    scale = 1.0 / math.sqrt(hd)
    b, t, z, y, zs, zback = places(G)
    ypeer = (b ^ 1, t)
    tc = pl.ds(pl.multiple_of(t * Cw, Cw), Cw)
    sends = []

    def put(cp):
        cp.start()
        sends.append(cp)

    def each(n, body):
        lax.fori_loop(0, n, lambda i, c: (body(i), c)[1], 0)

    def ex_send(e, s, src, dst):
        for d in (1, 2, 3):
            remote(src(t ^ d), dst(d), r.es.at[e, s, d - 1], r.er.at[e, s, d - 1], (b, t ^ d)).start()

    def ex_wait(e, s, dst):
        for d in (1, 2, 3):
            at = dst(d)
            remote(at, at, r.es.at[e, s, d - 1], r.er.at[e, s, d - 1], (b, t ^ d)).wait_recv()

    def ex_sent(e, src):
        def one(s):
            for d in (1, 2, 3):
                at = src(t ^ d, s)
                remote(at, at, r.es.at[e, s, d - 1], r.er.at[e, s, d - 1], (b, t ^ d)).wait_send()

        each(S, one)

    greet(G, True, True)

    def here(src, dst, i):
        cp = pltpu.make_async_copy(src, dst, r.lsem.at[i])
        cp.start()
        return cp

    kinds = {"S": (r.sm, r.SM, 0), "A": (r.wa, r.WA, 1), "U": (r.wu, r.WU, 2), "C": (r.wc, r.WC, 3), "D": (r.wd, r.WD, 4)}
    own = {}

    def tier_start(n):
        src, dst, k = kinds[n]
        own[n] = here(src if n == "S" else src.at[t], dst.at[b, t], k)
        for d in (1, 2, 3):
            piece = src if n == "S" else src.at[t ^ d]
            put(remote(piece, dst.at[b, t], r.ts.at[k, d - 1], r.tr.at[k, d - 1], (b, t ^ d)))

    def tier_wait(n):
        src, dst, k = kinds[n]
        own[n].wait()
        if n != "D":
            for d in (1, 2, 3):
                at = dst.at[b, t ^ d]
                remote(at, at, r.ts.at[k, d - 1], r.tr.at[k, d - 1], (b, t ^ d)).wait_recv()

    def z_send(n):
        src, dst, k = kinds[n]
        for d in range(1, G):
            put(remote(dst.at[b], dst.at[b], r.zsd.at[k, d], r.zr.at[k, d], (2 * zs[d] + y, t)))

    def y_send(n):
        src, dst, k = kinds[n]
        put(remote(dst.at[b], dst.at[b], r.ys.at[k, 0], r.yr.at[k, 0], ypeer))

    def y_forward(n):
        src, dst, k = kinds[n]
        for d in range(1, G):
            at = dst.at[2 * zback[d] + y]
            remote(at, at, r.zsd.at[k, d], r.zr.at[k, d], ypeer).wait_recv()
            put(remote(at, at, r.ys.at[k, d], r.yr.at[k, d], ypeer))

    def y_wait(n):
        src, dst, k = kinds[n]
        for d in range(G):
            at = dst.at[2 * zback[d] + (1 - y)]
            remote(at, at, r.ys.at[k, d], r.yr.at[k, d], ypeer).wait_recv()

    pieces = [
        (r.seg, lambda q: r.CTX.at[:, pl.ds(8 * nu + nu * q, nu)]),
        (r.comp, lambda q: r.CTX.at[:, pl.ds(nu * q, nu)]),
        (r.mem.at[:, 0], lambda q: r.CTX.at[:, 4 * nu + q]),
        (r.mem.at[:, 1], lambda q: r.CTX.at[:, 4 * nu + 4 + q]),
        (r.mem.at[:, 2], lambda q: r.CTX.at[:, 4 * nu + 8 + q]),
        (r.cot, lambda q: r.COT.at[:, pl.ds(nu * q, nu)]),
        (r.mk, lambda q: r.MK.at[:, q]),
    ]

    tier_start("A")
    own["D"] = here(r.wd, r.WD.at[b], 4)
    tier_start("U")
    acts = []
    for i, (src, at) in enumerate(pieces):
        acts.append(here(src, at(t), 5 + i))
        for j, d in enumerate((1, 2)):
            put(remote(src, at(t), r.acs.at[i, j], r.acr.at[i, j], (b, t ^ d)))
    tier_start("C")
    tier_start("S")
    tier_wait("A")
    z_send("A")
    y_send("A")
    tier_wait("D")
    y_send("D")
    tier_wait("U")
    z_send("U")
    y_send("U")

    row = lax.broadcasted_iota(jnp.int32, (L, C3), 0) + 2 * L
    col = lax.broadcasted_iota(jnp.int32, (L, C3), 1)
    inner = col - L
    k1 = (inner >= nw).astype(jnp.int32)
    k2 = (inner >= 2 * nw).astype(jnp.int32)
    win = inner - nw * (k1 + k2)
    pos = jnp.where((col >= L) & (col < 2 * L), L + 3 * win + k1 + k2, col)
    r.DIST[...] = jnp.where(pos <= row, (row - pos).astype(f32) * (1.0 / C3), 1e30)
    r.SMG[...] = jnp.zeros_like(r.SMG)

    y_forward("A")
    z_send("D")
    for i, (src, at) in enumerate(pieces):
        remote(at(t ^ 2), at(t ^ 2), r.acs.at[i, 1], r.acr.at[i, 1], (b, t ^ 2)).wait_recv()
        put(remote(at(t ^ 2), at(t ^ 2), r.acs.at[i, 2], r.acr.at[i, 2], (b, t ^ 1)))
    for i, (src, at) in enumerate(pieces):
        for j, q in ((0, t ^ 1), (2, t ^ 3)):
            remote(at(q), at(q), r.acs.at[i, j], r.acr.at[i, j], (b, t ^ 1)).wait_recv()
        acts[i].wait()
    y_wait("A")

    def seg_rows(s):
        return r.CTX[s, 8 * nu : 12 * nu].reshape(L, M)

    def project(s):
        rows = r.CTX[s].reshape(C3, M)
        kv = jnp.dot(rows, r.WA[:, :, :, Cw : 3 * Cw].reshape(M, 2 * Cw), preferred_element_type=f32)
        r.KV[s] = kv.astype(bf16)
        q = jnp.dot(seg_rows(s), r.WA[:, :, :, :Cw].reshape(M, Cw), preferred_element_type=f32)
        r.Q[s] = q.astype(bf16)

    each(S, project)
    tier_wait("S")
    z_send("S")
    y_send("S")

    def attend(s):
        for h in range(ht):
            c = slice(h * hd, (h + 1) * hd)
            raw = dot_nt(r.Q[s, :, c], r.KV[s, :, c])
            slope = r.sl[pl.ds(t * ht + h, 1), :][:, :1]
            scores = raw * scale - slope * r.DIST[...]
            e = jnp.exp(scores - jnp.max(scores, axis=1, keepdims=True))
            p = e * (1.0 / jnp.sum(e, axis=1, keepdims=True))
            r.PR[s, h] = p
            v = r.KV[s, :, Cw + h * hd : Cw + (h + 1) * hd]
            r.MIX[t, s, :, c] = jnp.dot(p.astype(bf16), v, preferred_element_type=f32).astype(bf16)
        ex_send(0, s, lambda q: r.MIX.at[t, s], lambda d: r.MIX.at[t, s])

    each(S, attend)
    y_forward("U")
    tier_wait("C")
    z_send("C")

    def wo(q):
        return r.WA[bq * q : bq * (q + 1), :, :, 3 * Cw :].reshape(Cw, Cw)

    def residual(s):
        ex_wait(0, s, lambda d: r.MIX.at[t ^ d, s])
        acc = r.CTX[s, 8 * nu : 12 * nu, :, tc].reshape(L, Cw).astype(f32)
        for q in range(4):
            acc = acc + jnp.dot(r.MIX[q, s], wo(q), preferred_element_type=f32)
        r.RT[s] = acc
        r.RES[t, s] = acc.astype(bf16)
        ex_send(1, s, lambda q: r.RES.at[t, s], lambda d: r.RES.at[t, s])

    each(S, residual)
    y_forward("S")
    y_wait("S")
    for q in range(4):
        block = r.SM[bq * q, 0, 0:8]
        for bb in range(bq * q, bq * (q + 1)):
            for tt in range(4):
                if bb != bq * q or tt:
                    block = block + r.SM[bb, tt, 0:8]
        for i in range(8):
            at = q * Cw + 128 * (i % 2)
            r.VV[i // 2 : i // 2 + 1, at : at + 128] = block[i : i + 1]
    for bb in range(nb):
        r.VV[4:5, bb * rd : (bb + 1) * rd] = r.SM[bb, t, 8:9, :rd]
    y_wait("U")

    def xhat_of(s, q):
        return (r.RES[q, s].astype(f32) - r.MU[s, :, :1]) * r.INV[s, :, :1]

    def feed(s):
        ex_wait(1, s, lambda d: r.RES.at[t ^ d, s])
        parts = [r.RES[q, s].astype(f32) for q in range(4)]
        mu = sum(jnp.sum(x, axis=1, keepdims=True) for x in parts) * (1.0 / M)
        var = sum(jnp.sum((x - mu) * (x - mu), axis=1, keepdims=True) for x in parts) * (1.0 / M)
        inv = lax.rsqrt(var + norm_eps)
        r.MU[s] = jnp.broadcast_to(mu, (L, 128))
        r.INV[s] = jnp.broadcast_to(inv, (L, 128))
        for q in range(4):
            c = slice(q * Cw, (q + 1) * Cw)
            r.NRM[s, :, c] = (((parts[q] - mu) * inv) * r.VV[0:1, c] + r.VV[1:2, c]).astype(bf16)
        fb = Fw // 4
        for j in range(4):
            c = slice(j * fb, (j + 1) * fb)
            pre = jnp.dot(r.NRM[s], r.WU[:, :, :, c].reshape(M, fb), preferred_element_type=f32) + r.VV[4:5, c]
            phi = 0.5 + 0.5 * lax.erf(pre * math.sqrt(0.5))
            r.ACT[s, :, c] = (pre * phi).astype(bf16)
            r.GP[s, :, c] = (phi + pre * (jnp.exp(-0.5 * pre * pre) * (1.0 / math.sqrt(2 * math.pi)))).astype(bf16)

    each(S, feed)

    grads = [(r.GD, r.YD, r.ZD), (r.GU, r.YU, r.ZU), (r.GC, r.YC, r.ZC), (r.GA, r.YA, r.ZA)]

    def to_y(k, zz):
        g, yb, zb = grads[k]
        remote(g.at[2 * zz + (1 - y)], yb.at[zz], r.gys.at[k, zz], r.gyr.at[k, zz], ypeer).start()

    def mid(k):
        g, yb, zb = grads[k]
        for d in range(G):
            zz = zs[(d + 1) % G]
            at = yb.at[zz]
            remote(at, at, r.gys.at[k, zz], r.gyr.at[k, zz], ypeer).wait_recv()

            def add(i, zz=zz):
                yb[zz, i] = (yb[zz, i].astype(f32) + g[2 * zz + y, i].astype(f32)).astype(bf16)

            each(yb.shape[1], add)
            if d < G - 1:
                put(remote(at, zb.at[d], r.gzs.at[k, d], r.gzr.at[k, d], (2 * zz + y, t)))

    def fin(k, store):
        g, yb, zb = grads[k]
        for d in range(G - 1):
            remote(zb.at[d], zb.at[d], r.gzs.at[k, d], r.gzr.at[k, d], ypeer).wait_recv()

        def total(i):
            acc = yb[z, i].astype(f32)
            for d in range(G - 1):
                acc = acc + zb[d, i].astype(f32)
            store(i, acc)

        each(4, total)

    fb = Fw // 4

    def grad_down(j):
        c = pl.ds(pl.multiple_of(j * fb, fb), fb)
        rows = r.ACT[:, :, c].reshape(S * L, fb)
        g = dot_tn(rows, r.COT[...].reshape(S * L, M)).astype(bf16)
        r.GD[pl.ds(j * bq, bq)] = g.reshape(bq, 4, rd // 4, M)
        for i in range(bq // 2):
            to_y(0, j * (bq // 2) + i)

    each(4, grad_down)
    y_forward("D")
    y_send("C")
    y_wait("D")

    def back_feed(s):
        cot = r.COT[s].reshape(L, M)
        for j in range(4):
            c = slice(j * fb, (j + 1) * fb)
            wd = r.WD[bq * j : bq * (j + 1)].reshape(fb, M)
            d_act = dot_nt(cot, wd).astype(bf16).astype(f32)
            d_pre = d_act * r.GP[s, :, c].astype(f32)
            total = jnp.sum(d_pre, axis=0, keepdims=True)
            for i in range(fb // 128):
                at = j * (fb // 128) + i
                r.SMG[at : at + 1] += total[:, 128 * i : 128 * (i + 1)]
            r.GP[s, :, c] = d_pre.astype(bf16)
        m1 = jnp.zeros((L, 1), f32)
        m2 = jnp.zeros((L, 1), f32)
        for q in range(4):
            c = slice(q * Cw, (q + 1) * Cw)
            dn = dot_nt(r.GP[s], r.WU[bq * q : bq * (q + 1)].reshape(Cw, Fw))
            g = dn * r.VV[0:1, c]
            m1 = m1 + jnp.sum(g, axis=1, keepdims=True)
            m2 = m2 + jnp.sum(g * xhat_of(s, q), axis=1, keepdims=True)
            r.DNP[q, s] = dn.astype(bf16)
        lane = lax.broadcasted_iota(jnp.int32, (L, 128), 1)
        both = jnp.where(lane == 0, m1, jnp.where(lane == 1, m2, 0.0)) * (1.0 / M)
        pick = (
            lax.broadcasted_iota(jnp.int32, (8, 128), 0) == lax.broadcasted_iota(jnp.int32, (8, 128), 1)
        ).astype(f32)
        r.ST[t, s] = lax.dot_general(
            pick, both, (((1,), (1,)), ((), ())), precision=lax.Precision.HIGHEST, preferred_element_type=f32
        )
        ex_send(2, s, lambda q: r.DNP.at[q, s], lambda d: r.DNR.at[d - 1, s])
        ex_send(3, s, lambda q: r.ST.at[t, s], lambda d: r.ST.at[t, s])

    each(S, back_feed)

    def grad_up(j):
        c = pl.ds(pl.multiple_of(j * Cw, Cw), Cw)
        rows = r.NRM[:, :, c].reshape(S * L, Cw)
        g = dot_tn(rows, r.GP[...].reshape(S * L, Fw)).astype(bf16)
        r.GU[pl.ds(j * bq, bq)] = g.reshape(bq, 4, rw, Fw)
        for i in range(bq // 2):
            to_y(1, j * (bq // 2) + i)

    each(4, grad_up)
    mid(0)

    def back_norm(s):
        ex_wait(2, s, lambda d: r.DNR.at[d - 1, s])
        ex_wait(3, s, lambda d: r.ST.at[t ^ d, s])
        dn = r.DNP[t, s].astype(f32)
        for d in range(3):
            dn = dn + r.DNR[d, s].astype(f32)
        st = r.ST[0, s] + r.ST[1, s] + r.ST[2, s] + r.ST[3, s]
        side = lax.broadcasted_iota(jnp.int32, (8, 128), 0)
        col_of = lambda i: lax.dot_general(
            st,
            (side == i).astype(f32),
            (((0,), (0,)), ((), ())),
            precision=lax.Precision.HIGHEST,
            preferred_element_type=f32,
        )[:, :1]
        m1, m2 = col_of(0), col_of(1)
        inv = r.INV[s, :, :1]
        xhat = (r.RES[t, s].astype(f32) - r.MU[s, :, :1]) * inv
        cot = r.COT[s, :, :, tc].reshape(L, Cw).astype(f32)
        for i, v in enumerate((cot, dn * xhat, dn)):
            total = jnp.sum(v, axis=0, keepdims=True)
            for k in range(Cw // 128):
                at = Fw // 128 + i * (Cw // 128) + k
                r.SMG[at : at + 1] += total[:, 128 * k : 128 * (k + 1)]
        d_resid = cot + (dn * r.VV[0:1, tc] - m1 - xhat * m2) * inv
        r.DR[s] = d_resid
        db = d_resid.astype(bf16)
        r.DB[s] = db
        for q in range(4):
            r.DMP[q, s] = dot_nt(db, wo(q)).astype(bf16)
        ex_send(4, s, lambda q: r.DMP.at[q, s], lambda d: r.DMR.at[d - 1, s])

    each(S, back_norm)
    for q in range(4):
        g = dot_tn(r.MIX[q].reshape(S * L, Cw), r.DB[...].reshape(S * L, Cw))
        r.GA[bq * q : bq * (q + 1), :, :, 3 * Cw :] = g.astype(bf16).reshape(bq, 4, rw, Cw)

    def out_rows(s):
        for q in range(4):
            c = slice(q * Cw, (q + 1) * Cw)
            o = jnp.dot(r.ACT[s], r.WD[:, :, c].reshape(Fw, Cw), preferred_element_type=f32)
            mine = (t == q).astype(f32)
            o = o + mine * (r.RT[s] + r.VV[2:3, c])
            r.OP[s, :, :, c] = o.astype(bf16).reshape(4 * nu, 16, Cw)
        ex_send(5, s, lambda q: r.OP.at[s, pl.ds(nu * q, nu)], lambda d: r.OR.at[d - 1, s])

    each(S, out_rows)

    y_forward("C")
    y_wait("C")

    def windows(k):
        return r.CTX[:, 4 * nu + 4 * k : 4 * nu + 4 * (k + 1)].reshape(S * nw, M)

    conv = r.VV[3:4, tc]
    pooled = 0.0
    for k in range(3):
        wk = r.WC[:, :, :, k * Cw : (k + 1) * Cw].reshape(M, Cw)
        conv = conv + jnp.dot(windows(k), wk, preferred_element_type=f32)
        pooled = pooled + r.CTX[:, 4 * nu + 4 * k : 4 * nu + 4 * (k + 1), :, tc].reshape(S * nw, Cw).astype(f32)
    mask = r.MK[...].reshape(S * nw, 128)[:, :1]
    done = 3 * lax.broadcasted_iota(jnp.int32, (nw, 128), 0) + 3
    live = jnp.concatenate(
        [(done.astype(f32) <= r.ev[s, 0:1, :]).astype(f32)[:, :1] for s in range(S)], axis=0
    ) * mask
    r.NEW[t] = (mask * conv).astype(bf16)
    for d in (1, 2, 3):
        put(remote(r.NEW.at[t], r.NEW.at[t], r.ts.at[5, d - 1], r.tr.at[5, d - 1], (b, t ^ d)))
    d_conv = live * (conv - pooled * (1.0 / 3.0))
    total = jnp.sum(d_conv, axis=0, keepdims=True)
    for k in range(Cw // 128):
        at = Fw // 128 + 3 * (Cw // 128) + k
        r.SMG[at : at + 1] = total[:, 128 * k : 128 * (k + 1)]
    r.DC[...] = d_conv.astype(bf16)
    for k in range(3):
        g = dot_tn(windows(k), r.DC[...])
        r.GC[:, :, :, k * Cw : (k + 1) * Cw] = g.astype(bf16).reshape(nb, 4, rw, Cw)
    for zz in range(G):
        to_y(2, zz)
    mid(1)

    slope_row = Fw // 128 + 4 * (Cw // 128)

    def back_attend(s):
        ex_wait(4, s, lambda d: r.DMR.at[d - 1, s])
        dm = r.DMP[t, s].astype(f32)
        for d in range(3):
            dm = dm + r.DMR[d, s].astype(f32)
        dm = dm.astype(bf16)
        lane = lax.broadcasted_iota(jnp.int32, (1, 128), 1)
        for h in range(ht):
            c = slice(h * hd, (h + 1) * hd)
            cv = slice(Cw + h * hd, Cw + (h + 1) * hd)
            p = r.PR[s, h]
            dp = dot_nt(dm[:, c], r.KV[s, :, cv])
            delta = jnp.sum(p * dp, axis=1, keepdims=True)
            ds = p * (dp - delta)
            part = jnp.sum(jnp.sum(ds * r.DIST[...], axis=0, keepdims=True), axis=1, keepdims=True)
            r.SMG[slope_row : slope_row + 1] -= jnp.where(lane == t * ht + h, part, 0.0)
            dr = (ds * scale).astype(bf16)
            dq = jnp.dot(dr, r.KV[s, :, c], preferred_element_type=f32).astype(bf16)
            dk = dot_tn(dr, r.Q[s, :, c]).astype(bf16)
            dv = dot_tn(p.astype(bf16), dm[:, c]).astype(bf16)
            r.Q[s, :, c] = dq
            r.KV[s, :, c] = dk
            r.KV[s, :, cv] = dv

    each(S, back_attend)

    def grad_proj(j):
        c = pl.ds(pl.multiple_of(j * Cw, Cw), Cw)
        gq = jnp.zeros((Cw, Cw), f32)
        gkv = jnp.zeros((Cw, 2 * Cw), f32)
        for s in range(S):
            gq = gq + dot_tn(r.CTX[s, 8 * nu : 12 * nu, :, c].reshape(L, Cw), r.Q[s])
            gkv = gkv + dot_tn(r.CTX[s, :, :, c].reshape(C3, Cw), r.KV[s])
        rows = pl.ds(j * bq, bq)
        r.GA[rows, :, :, :Cw] = gq.astype(bf16).reshape(bq, 4, rw, Cw)
        r.GA[rows, :, :, Cw : 3 * Cw] = gkv.astype(bf16).reshape(bq, 4, rw, 2 * Cw)
        for i in range(bq // 2):
            to_y(3, j * (bq // 2) + i)

    each(4, grad_proj)
    put(remote(r.SMG, r.YS, r.gys.at[4, 0], r.gyr.at[4, 0], ypeer))
    ex_sent(5, lambda q, s: r.OP.at[s, pl.ds(nu * q, nu)])

    def own_out(s):
        ex_wait(5, s, lambda d: r.OR.at[d - 1, s])
        acc = r.OP[s, pl.ds(nu * t, nu)].astype(f32)
        for d in range(3):
            acc = acc + r.OR[d, s].astype(f32)
        r.out[s] = acc.astype(bf16)

    each(S, own_out)

    def input_rows(s):
        x = jnp.concatenate([r.Q[s], r.KV[s, 2 * L :]], axis=1)
        for q in range(4):
            c = slice(q * Cw, (q + 1) * Cw)
            w = r.WA[bq * q : bq * (q + 1), :, :, : 3 * Cw].reshape(Cw, 3 * Cw)
            o = dot_nt(x, w) + (t == q).astype(f32) * r.DR[s]
            r.OP[s, :, :, c] = o.astype(bf16).reshape(4 * nu, 16, Cw)
        ex_send(6, s, lambda q: r.OP.at[s, pl.ds(nu * q, nu)], lambda d: r.IR.at[d - 1, s])

    each(S, input_rows)

    mid(2)

    def keep(o):
        def store(i, acc):
            o[i] = acc

        return store

    def hold(m):
        def store(i, acc):
            m[i] = acc.astype(bf16)

        return store

    def tier_back(k, m, tb):
        for d in (1, 2, 3):
            put(remote(m.at[t ^ d], tb.at[t], r.gts.at[k, d - 1], r.gtr.at[k, d - 1], (b, t ^ d)))

    fin(0, keep(r.od))
    fin(1, hold(r.MU_))
    tier_back(0, r.MU_, r.TU)
    remote(r.YS, r.YS, r.gys.at[4, 0], r.gyr.at[4, 0], ypeer).wait_recv()
    r.ZS[z] = r.SMG[...] + r.YS[...]
    for d in range(G - 1):
        put(remote(r.ZS.at[z], r.ZS.at[z], r.gzs.at[4, d], r.gzr.at[4, d], (2 * zs[d + 1] + y, t)))
    mid(3)
    fin(2, hold(r.MC_))
    tier_back(1, r.MC_, r.TC)
    for d in range(G - 1):
        at = r.ZS.at[zback[d + 1]]
        remote(at, at, r.gzs.at[4, d], r.gzr.at[4, d], ypeer).wait_recv()
    acc = r.ZS[0]
    for zz in range(1, G):
        acc = acc + r.ZS[zz]
    r.os[t] = acc
    for d in (1, 2, 3):
        put(remote(r.os.at[t], r.os.at[t], r.gts.at[3, d - 1], r.gtr.at[3, d - 1], (b, t ^ d)))

    def own_input(s):
        ex_wait(6, s, lambda d: r.IR.at[d - 1, s])
        acc = r.OP[s, pl.ds(nu * t, nu)].astype(f32)
        for d in range(3):
            acc = acc + r.IR[d, s].astype(f32)
        r.ig[s] = acc

    each(S, own_input)
    fin(3, hold(r.MA_))
    tier_back(2, r.MA_, r.TA)
    for k, (m, tb, o) in enumerate(((r.MU_, r.TU, r.ou), (r.MC_, r.TC, r.oc), (r.MA_, r.TA, r.oa))):
        o[t] = m[t].astype(f32)
        for d in (1, 2, 3):
            at = tb.at[t ^ d]
            remote(at, at, r.gts.at[k, d - 1], r.gtr.at[k, d - 1], (b, t ^ d)).wait_recv()
            o[t ^ d] = tb[t ^ d].astype(f32)
    for d in (1, 2, 3):
        at = r.os.at[t ^ d]
        remote(at, at, r.gts.at[3, d - 1], r.gtr.at[3, d - 1], (b, t ^ d)).wait_recv()
        at = r.NEW.at[t ^ d]
        remote(at, at, r.ts.at[5, d - 1], r.tr.at[5, d - 1], (b, t ^ d)).wait_recv()
    r.new[...] = r.NEW[...]

    for cp in sends:
        cp.wait_send()
    for k, (g, yb, zb) in enumerate(grads):
        for zz in range(G):
            remote(yb.at[zz], yb.at[zz], r.gys.at[k, zz], r.gyr.at[k, zz], ypeer).wait_send()
    ex_sent(0, lambda q, s: r.MIX.at[t, s])
    ex_sent(1, lambda q, s: r.RES.at[t, s])
    ex_sent(2, lambda q, s: r.DNP.at[q, s])
    ex_sent(3, lambda q, s: r.ST.at[t, s])
    ex_sent(4, lambda q, s: r.DMP.at[q, s])
    ex_sent(6, lambda q, s: r.OP.at[s, pl.ds(nu * q, nu)])


def whole_layer(nb, nu, ht, hd, wa, wu, wc, wd, sm, comp, mem, seg, cot, mk, ev, sl):
    S, _, _, M = comp.shape
    _, rw, _ = wa.shape
    rd = wd.shape[0]
    G, Cw, Fw, L = nb // 2, M // 4, nb * rd, 64 * nu
    dma = pltpu.SemaphoreType.DMA
    V = lambda shape, dtype=bf16: pltpu.VMEM(shape, dtype)
    D4, A4, U4, C4 = (4, rd // 4, M), (4, rw, 4 * Cw), (4, rw, Fw), (4, rw, 3 * Cw)
    ins = dict(wa=wa, wu=wu, wc=wc, wd=wd, sm=sm, comp=comp, mem=mem, seg=seg, cot=cot, mk=mk, ev=ev, sl=sl)
    outs = dict(
        out=((S, nu, 16, M), bf16),
        ig=((S, nu, 16, M), f32),
        new=((4, S * L // 3, Cw), bf16),
        od=(D4, f32),
        ou=(U4, f32),
        oc=(C4, f32),
        oa=(A4, f32),
        os=((4, 24, 128), f32),
    )
    scratch = dict(
        WA=V((nb,) + A4),
        WU=V((nb,) + U4),
        WC=V((nb,) + C4),
        WD=V((nb, rd, M)),
        SM=V((nb, 4, 16, 128), f32),
        CTX=V((S, 12 * nu, 16, M)),
        COT=V((S, 4 * nu, 16, M)),
        MK=V((S, 4, L // 12, 128), f32),
        DIST=V((L, 3 * L), f32),
        VV=V((8, max(M, Fw)), f32),
        SMG=V((24, 128), f32),
        Q=V((S, L, Cw)),
        KV=V((S, 3 * L, 2 * Cw)),
        PR=V((S, ht, L, 3 * L), f32),
        MIX=V((4, S, L, Cw)),
        RT=V((S, L, Cw), f32),
        RES=V((4, S, L, Cw)),
        MU=V((S, L, 128), f32),
        INV=V((S, L, 128), f32),
        NRM=V((S, L, M)),
        ACT=V((S, L, Fw)),
        GP=V((S, L, Fw)),
        DNP=V((4, S, L, Cw)),
        DNR=V((3, S, L, Cw)),
        ST=V((4, S, 8, L), f32),
        DR=V((S, L, Cw), f32),
        DB=V((S, L, Cw)),
        DMP=V((4, S, L, Cw)),
        DMR=V((3, S, L, Cw)),
        OP=V((S, 4 * nu, 16, M)),
        OR=V((3, S, nu, 16, M)),
        IR=V((3, S, nu, 16, M)),
        NEW=V((4, S * L // 3, Cw)),
        DC=V((S * L // 3, Cw)),
        GD=V((nb,) + D4),
        GU=V((nb,) + U4),
        GC=V((nb,) + C4),
        GA=V((nb,) + A4),
        YD=V((G,) + D4),
        YU=V((G,) + U4),
        YC=V((G,) + C4),
        YA=V((G,) + A4),
        ZD=V((G - 1,) + D4),
        ZU=V((G - 1,) + U4),
        ZC=V((G - 1,) + C4),
        ZA=V((G - 1,) + A4),
        YS=V((24, 128), f32),
        ZS=V((G, 24, 128), f32),
        MU_=V(U4),
        MC_=V(C4),
        MA_=V(A4),
        TU=V(U4),
        TC=V(C4),
        TA=V(A4),
        lsem=dma((12,)),
        ts=dma((6, 3)),
        tr=dma((6, 3)),
        zsd=dma((5, G)),
        zr=dma((5, G)),
        ys=dma((5, G)),
        yr=dma((5, G)),
        acs=dma((7, 3)),
        acr=dma((7, 3)),
        es=dma((7, S, 3)),
        er=dma((7, S, 3)),
        gys=dma((5, G)),
        gyr=dma((5, G)),
        gzs=dma((5, G)),
        gzr=dma((5, G)),
        gts=dma((4, 3)),
        gtr=dma((4, 3)),
    )
    names = list(ins) + list(outs) + list(scratch)
    near = ("ev", "sl")
    return pl.pallas_call(
        functools.partial(layer_kernel, names, (nb, nu, S, ht, hd, M, Cw, rw, rd)),
        out_shape=[jax.ShapeDtypeStruct(s, d) for s, d in outs.values()],
        in_specs=[VM if n in near else ANY for n in ins],
        out_specs=[VM] * len(outs),
        scratch_shapes=list(scratch.values()),
        compiler_params=pltpu.CompilerParams(
            collective_id=9, has_side_effects=True, vmem_limit_bytes=63 * 2**20
        ),
        name="whole_layer",
    )(*ins.values())


def prepared(nb, segment, memory, compressed, evicted, window_mask, cotangent, w, b_up, vectors, w_up, w_conv, slopes):
    S, R, M = segment.shape
    rw, rd, rs = w[0].shape[0], b_up.shape[0], vectors[0].shape[0]
    b, t = lax.axis_index("batch"), lax.axis_index("tier")
    Cw, nu, W = M // 4, R // 16, R // 3
    wa = jnp.stack(w).reshape(4, rw, 4, Cw).transpose(2, 1, 0, 3).reshape(4, rw, 4 * Cw)
    wu = w_up.reshape(rw, nb, 4, rd).transpose(2, 0, 1, 3).reshape(4, rw, nb * rd)
    wc = w_conv.reshape(3, rw, 4, Cw).transpose(2, 1, 0, 3).reshape(4, rw, 3 * Cw)
    four = jnp.stack(vectors).astype(f32)
    four = lax.dynamic_update_slice(jnp.zeros((4, Cw), f32), four, (0, lax.rem(rs * (4 * b + t), Cw)))
    low = jnp.zeros((8, 128), f32).at[0, :rd].set(b_up.astype(f32))
    sm = jnp.concatenate([four.reshape(8, 128), low], axis=0)
    mem = memory.reshape(S, W, 3, M).transpose(0, 2, 1, 3)
    mk = jnp.broadcast_to(window_mask.astype(f32)[:, :, None], (S, W, 128))
    ev = jnp.broadcast_to(evicted.astype(f32)[:, None, None], (S, 8, 128))
    sl = jnp.broadcast_to(slopes[:, None], (slopes.shape[0], 128))
    cut = lambda v: v.reshape(S, nu, 16, M)
    return wa, wu, wc, sm, cut(compressed), mem, cut(segment), cut(cotangent), mk, ev, sl


def per_device_fused(
    nb,
    segment,
    memory,
    compressed,
    evicted,
    window_mask,
    cotangent,
    w_query,
    w_key,
    w_value,
    w_output,
    w_up,
    b_up,
    w_down,
    b_down,
    ln_gain,
    ln_bias,
    w_conv,
    b_conv,
    slopes,
):
    S, R, M = segment.shape
    heads = slopes.shape[0]
    rw, rd, rs = w_query.shape[0], w_down.shape[0], b_down.shape[0]
    b, t = lax.axis_index("batch"), lax.axis_index("tier")
    Cw, Fw, seg_len = M // 4, nb * rd, 4 * R
    index = 4 * b + t
    wa, wu, wc, sm, comp, mem, seg, cot, mk, ev, sl = prepared(
        nb,
        segment,
        memory,
        compressed,
        evicted,
        window_mask,
        cotangent,
        (w_query, w_key, w_value, w_output),
        b_up,
        (ln_gain, ln_bias, b_down, b_conv),
        w_up,
        w_conv,
        slopes,
    )
    out, ig, NEW, OD, OU, OC, OA, OS = whole_layer(
        nb, R // 16, heads // 4, M // heads, wa, wu, wc, w_down, sm, comp, mem, seg, cot, mk, ev, sl
    )
    nw = seg_len // 3
    NEW = NEW.reshape(4, S, nw, Cw).transpose(1, 2, 0, 3).reshape(S, nw, M)
    slot_offset = seg_len - nw
    local_rows = jnp.arange(R, dtype=jnp.int32) + t * R
    padded = jnp.concatenate([jnp.zeros((S, slot_offset, M), bf16), NEW], axis=1)
    slot_rows = lax.dynamic_slice_in_dim(padded, t * R, R, 1)
    written = (local_rows[None, :] >= slot_offset) & (
        3 * (local_rows[None, :] - slot_offset) + 3 <= evicted[:, None]
    )
    new_compressed = jnp.where(written[..., None], slot_rows, compressed)
    new_memory = jnp.where((local_rows[None, :] < evicted[:, None])[..., None], segment, memory)
    OA = OA.reshape(4, rw, 4, Cw).transpose(2, 1, 0, 3).reshape(4, rw, M)
    OU = OU.reshape(4, rw, nb, rd).transpose(1, 2, 0, 3).reshape(rw, nb * 4 * rd)
    OC = OC.reshape(4, rw, 3, Cw).transpose(2, 1, 0, 3).reshape(3, rw, M)
    OS = OS.reshape(4, -1)
    vec = lambda o: lax.dynamic_slice_in_dim(OS[:, o : o + Cw].reshape(M), index * rs, rs)
    gub_out = lax.dynamic_slice(OS, (t, b * rd), (1, rd)).reshape(rd)
    gslopes = jnp.sum(OS[:, Fw + 4 * Cw : Fw + 4 * Cw + heads], axis=0)
    return (
        out.reshape(S, R, M),
        ig.reshape(S, R, M),
        new_memory,
        new_compressed,
        OA[0],
        OA[1],
        OA[2],
        OA[3],
        OU,
        gub_out,
        OD.reshape(rd, M),
        vec(Fw),
        vec(Fw + Cw),
        vec(Fw + 2 * Cw),
        OC,
        vec(Fw + 3 * Cw),
        gslopes,
    )


def solution(mesh):
    both = ("batch", "tier")
    rows = P("batch", "tier", None)
    mat, vec = P(both, None), P(both)
    nb = mesh.shape["batch"]

    def body(*args):
        fused = args[6].shape[0] % 16 == 0 and args[12].shape[0] == 128
        return (per_device_fused if fused else per_device)(nb, *args)

    return jax.shard_map(
        body,
        mesh=mesh,
        in_specs=(
            (rows, rows, rows, P("batch"), P("batch", "tier"), rows)
            + (mat, mat, mat, mat, mat, vec, mat, vec, vec, vec)
            + (P(None, both, None), vec, P())
        ),
        out_specs=(
            (rows, rows, rows, rows, mat, mat, mat, mat, mat, vec, mat, vec, vec, vec)
            + (P(None, both, None), vec, P())
        ),
        check_vma=False,
    )
```

```python
import functools
import math

import jax
import jax.numpy as jnp
from jax import lax
from jax.experimental import pallas as pl
from jax.experimental.pallas import tpu as pltpu
from jax.sharding import PartitionSpec as P

norm_eps = 1e-05
MESH = pl.DeviceIdType.MESH
ANY = pl.BlockSpec(memory_space=pl.ANY)
VM = pl.BlockSpec(memory_space=pltpu.VMEM)
SM = pl.BlockSpec(memory_space=pltpu.SMEM)
f32 = jnp.float32
bf16 = jnp.bfloat16


def remote(src, dst, send, recv, device):
    return pltpu.make_async_remote_copy(
        src_ref=src,
        dst_ref=dst,
        send_sem=send,
        recv_sem=recv,
        device_id=device,
        device_id_type=MESH,
    )


def places(groups):
    b, t = lax.axis_index("batch"), lax.axis_index("tier")
    z, y = b // 2, lax.rem(b, 2)
    zs = [lax.rem(z + d, groups) for d in range(groups)]
    zback = [lax.rem(z + groups - d, groups) for d in range(groups)]
    return b, t, z, y, zs, zback


def greet(groups, tiers, columns):
    b, t, z, y, zs, _ = places(groups)
    barrier = pltpu.get_barrier_semaphore()
    peers = []
    if tiers:
        peers += [(b, t ^ d) for d in (1, 2, 3)]
    if columns:
        peers += [(2 * zz + y, t) for zz in zs[1:]] + [(b ^ 1, t)]
    for peer in peers:
        pl.semaphore_signal(barrier, inc=1, device_id=peer, device_id_type=MESH)
    pl.semaphore_wait(barrier, len(peers))


def gather_kernel(groups, nu, *refs):
    (wa, wu, wc, wd, sm, comp, mem, seg, cot, mk) = refs[:10]
    (WA, WU, WC, WD, SM, CTX, COT, MK) = refs[10:18]
    lsem, ts, tr, zsd, zr, ys, yr, acs, acr = refs[18:]
    G = groups
    b, t, z, y, zs, zback = places(G)
    greet(G, True, True)
    ypeer = (b ^ 1, t)
    local, sends = [], []

    def here(src, dst, i):
        cp = pltpu.make_async_copy(src, dst, lsem.at[i])
        cp.start()
        return cp

    kinds = [(sm, SM), (wa, WA), (wu, WU), (wc, WC)]
    own = []
    for k, (src, dst) in enumerate(kinds):
        mine = src if k == 0 else src.at[t]
        own.append(here(mine, dst.at[b, t], k))
        for d in (1, 2, 3):
            piece = src if k == 0 else src.at[t ^ d]
            cp = remote(piece, dst.at[b, t], ts.at[k, d - 1], tr.at[k, d - 1], (b, t ^ d))
            cp.start()
            sends.append(cp)
    own.append(here(wd, WD.at[b], 4))
    pieces = [
        (comp, lambda q: CTX.at[:, pl.ds(nu * q, nu)]),
        (mem.at[:, 0], lambda q: CTX.at[:, 4 * nu + q]),
        (mem.at[:, 1], lambda q: CTX.at[:, 4 * nu + 4 + q]),
        (mem.at[:, 2], lambda q: CTX.at[:, 4 * nu + 8 + q]),
        (seg, lambda q: CTX.at[:, pl.ds(8 * nu + nu * q, nu)]),
        (mk, lambda q: MK.at[:, q]),
        (cot, lambda q: COT.at[:, pl.ds(nu * q, nu)]),
    ]
    for i, (src, at) in enumerate(pieces):
        own.append(here(src, at(t), 5 + i))
        for j, d in enumerate((1, 2)):
            cp = remote(src, at(t), acs.at[i, j], acr.at[i, j], (b, t ^ d))
            cp.start()
            sends.append(cp)
    table = [SM, WA, WU, WD, WC]
    local_of = [0, 1, 2, 4, 3]
    for k, dst in enumerate(table):
        own[local_of[k]].wait()
        if k != 3:
            kk = local_of[k]
            for d in (1, 2, 3):
                remote(dst.at[b, t], dst.at[b, t ^ d], ts.at[kk, d - 1], tr.at[kk, d - 1], (b, t ^ d)).wait_recv()
        for d in range(1, G):
            cp = remote(dst.at[b], dst.at[b], zsd.at[k, d], zr.at[k, d], (2 * zs[d] + y, t))
            cp.start()
            sends.append(cp)
        cp = remote(dst.at[b], dst.at[b], ys.at[k, 0], yr.at[k, 0], ypeer)
        cp.start()
        sends.append(cp)
    for i, (src, at) in enumerate(pieces):
        remote(at(t ^ 2), at(t ^ 2), acs.at[i, 1], acr.at[i, 1], (b, t ^ 2)).wait_recv()
        cp = remote(at(t ^ 2), at(t ^ 2), acs.at[i, 2], acr.at[i, 2], (b, t ^ 1))
        cp.start()
        sends.append(cp)
    for k, dst in enumerate(table):
        for d in range(1, G):
            at = dst.at[2 * zback[d] + y]
            remote(at, at, zsd.at[k, d], zr.at[k, d], ypeer).wait_recv()
            cp = remote(at, at, ys.at[k, d], yr.at[k, d], ypeer)
            cp.start()
            sends.append(cp)
    for k, dst in enumerate(table):
        for d in range(G):
            at = dst.at[2 * zback[d] + (1 - y)]
            remote(at, at, ys.at[k, d], yr.at[k, d], ypeer).wait_recv()
    for i, (src, at) in enumerate(pieces):
        for j, q in ((0, t ^ 1), (2, t ^ 3)):
            remote(at(q), at(q), acs.at[i, j], acr.at[i, j], (b, t ^ 1)).wait_recv()
    for i in range(len(pieces)):
        own[5 + i].wait()
    for cp in sends:
        cp.wait_send()


def gather_all(nb, nu, wa, wu, wc, wd, sm, comp, mem, seg, cot, mk):
    G = nb // 2
    S, _, U, M = comp.shape
    out = [
        jax.ShapeDtypeStruct((nb,) + wa.shape, bf16),
        jax.ShapeDtypeStruct((nb,) + wu.shape, bf16),
        jax.ShapeDtypeStruct((nb,) + wc.shape, bf16),
        jax.ShapeDtypeStruct((nb,) + wd.shape, bf16),
        jax.ShapeDtypeStruct((nb, 4) + sm.shape, f32),
        jax.ShapeDtypeStruct((S, 12 * nu, U, M), bf16),
        jax.ShapeDtypeStruct((S, 4 * nu, U, M), bf16),
        jax.ShapeDtypeStruct((S, 4) + mk.shape[1:], f32),
    ]
    dma = pltpu.SemaphoreType.DMA
    return pl.pallas_call(
        functools.partial(gather_kernel, G, nu),
        out_shape=out,
        in_specs=[ANY] * 10,
        out_specs=[ANY] * 8,
        scratch_shapes=[
            dma((12,)),
            dma((4, 3)),
            dma((4, 3)),
            dma((5, G)),
            dma((5, G)),
            dma((5, G)),
            dma((5, G)),
            dma((7, 3)),
            dma((7, 3)),
        ],
        compiler_params=pltpu.CompilerParams(collective_id=0, has_side_effects=True),
        name="gather_all",
    )(wa, wu, wc, wd, sm, comp, mem, seg, cot, mk)


def spread_kernel(same, x, o, lsem, ss, rs):
    b, t = lax.axis_index("batch"), lax.axis_index("tier")
    greet(1, True, False)
    cps = []
    for d in (1, 2, 3):
        cp = remote(x if same else x.at[t ^ d], o.at[t], ss.at[d - 1], rs.at[d - 1], (b, t ^ d))
        cp.start()
        cps.append(cp)
    mine = pltpu.make_async_copy(x if same else x.at[t], o.at[t], lsem)
    mine.start()
    mine.wait()
    for d in (1, 2, 3):
        remote(o.at[t ^ d], o.at[t ^ d], ss.at[d - 1], rs.at[d - 1], (b, t ^ d)).wait_recv()
    for cp in cps:
        cp.wait_send()


def spread(x, same, cid):
    dma = pltpu.SemaphoreType.DMA
    shape = ((4,) + x.shape) if same else x.shape
    return pl.pallas_call(
        functools.partial(spread_kernel, same),
        out_shape=jax.ShapeDtypeStruct(shape, x.dtype),
        in_specs=[ANY],
        out_specs=ANY,
        scratch_shapes=[dma, dma((3,)), dma((3,))],
        compiler_params=pltpu.CompilerParams(collective_id=cid, has_side_effects=True),
        name="spread_%d" % cid,
    )(x)


def reduce_kernel(groups, *refs):
    GD, GU, GC, GA, SMG = refs[:5]
    OD, OU, OC, OA, OS = refs[5:10]
    YD, YU, YC, YA, YS, ZD, ZU, ZC, ZA, ZS, TU, TC, TA, MU, MC, MA, ys, yr, zsd, zr, ts, tr = refs[10:]
    G = groups
    b, t, z, y, zs, zback = places(G)
    greet(G, True, True)
    ypeer = (b ^ 1, t)
    sends = []
    kinds = [
        (GD, YD, ZD, OD, None, None),
        (GU, YU, ZU, OU, MU, TU),
        (GC, YC, ZC, OC, MC, TC),
        (GA, YA, ZA, OA, MA, TA),
    ]
    for k, (g, yb, *_) in enumerate(kinds):
        for d in range(G):
            zz = zs[(d + 1) % G]
            cp = remote(g.at[2 * zz + (1 - y)], yb.at[zz], ys.at[k, d], yr.at[k, d], ypeer)
            cp.start()
            sends.append(cp)
    cp = remote(SMG, YS, ys.at[4, 0], yr.at[4, 0], ypeer)
    cp.start()
    sends.append(cp)
    for k, (g, yb, zb, o, m, tb) in enumerate(kinds):
        for d in range(G):
            zz = zs[(d + 1) % G]
            at = yb.at[zz]
            remote(at, at, ys.at[k, d], yr.at[k, d], ypeer).wait_recv()

            def add(i, c, yb=yb, zz=zz, g=g):
                yb[zz, i] = (yb[zz, i].astype(f32) + g[2 * zz + y, i].astype(f32)).astype(bf16)
                return c

            lax.fori_loop(0, yb.shape[1], add, 0)
            if d < G - 1:
                cp = remote(at, zb.at[d], zsd.at[k, d], zr.at[k, d], (2 * zz + y, t))
                cp.start()
                sends.append(cp)
    remote(YS, YS, ys.at[4, 0], yr.at[4, 0], ypeer).wait_recv()
    ZS[z] = SMG[...] + YS[...]
    for d in range(G - 1):
        cp = remote(ZS.at[z], ZS.at[z], zsd.at[4, d], zr.at[4, d], (2 * zs[d + 1] + y, t))
        cp.start()
        sends.append(cp)
    for k, (g, yb, zb, o, m, tb) in enumerate(kinds):
        for d in range(G - 1):
            remote(zb.at[d], zb.at[d], zsd.at[k, d], zr.at[k, d], ypeer).wait_recv()

        def total(i, c, k=k, yb=yb, zb=zb, o=o, m=m):
            acc = yb[z, i].astype(f32)
            for d in range(G - 1):
                acc = acc + zb[d, i].astype(f32)
            if k == 0:
                o[i] = acc
            else:
                m[i] = acc.astype(bf16)
            return c

        lax.fori_loop(0, o.shape[0], total, 0)
        if k:
            for d in (1, 2, 3):
                cp = remote(m.at[t ^ d], tb.at[t], ts.at[k - 1, d - 1], tr.at[k - 1, d - 1], (b, t ^ d))
                cp.start()
                sends.append(cp)
    for d in range(G - 1):
        at = ZS.at[zback[d + 1]]
        remote(at, at, zsd.at[4, d], zr.at[4, d], ypeer).wait_recv()
    acc = ZS[0]
    for zz in range(1, G):
        acc = acc + ZS[zz]
    OS[t] = acc
    for d in (1, 2, 3):
        cp = remote(OS.at[t], OS.at[t], ts.at[3, d - 1], tr.at[3, d - 1], (b, t ^ d))
        cp.start()
        sends.append(cp)
    for k, (g, yb, zb, o, m, tb) in enumerate(kinds):
        if k:
            o[t] = m[t].astype(f32)
            for d in (1, 2, 3):
                at = tb.at[t ^ d]
                remote(at, at, ts.at[k - 1, d - 1], tr.at[k - 1, d - 1], (b, t ^ d)).wait_recv()
                o[t ^ d] = tb[t ^ d].astype(f32)
    for d in (1, 2, 3):
        at = OS.at[t ^ d]
        remote(at, at, ts.at[3, d - 1], tr.at[3, d - 1], (b, t ^ d)).wait_recv()
    for cp in sends:
        cp.wait_send()


def reduce_all(nb, gd, gu, gc, ga, sg):
    G = nb // 2
    dma = pltpu.SemaphoreType.DMA
    shapes = [x.shape[1:] for x in (gd, gu, gc, ga)]
    return pl.pallas_call(
        functools.partial(reduce_kernel, G),
        out_shape=[jax.ShapeDtypeStruct(s, f32) for s in shapes]
        + [jax.ShapeDtypeStruct((4,) + sg.shape, f32)],
        in_specs=[VM] * 5,
        out_specs=[VM] * 5,
        scratch_shapes=[pltpu.VMEM((G,) + s, bf16) for s in shapes]
        + [pltpu.VMEM(sg.shape, f32)]
        + [pltpu.VMEM((G - 1,) + s, bf16) for s in shapes]
        + [pltpu.VMEM((G,) + sg.shape, f32)]
        + [pltpu.VMEM(s, bf16) for s in shapes[1:]]
        + [pltpu.VMEM(s, bf16) for s in shapes[1:]]
        + [dma((5, G)), dma((5, G)), dma((5, G)), dma((5, G)), dma((4, 3)), dma((4, 3))],
        compiler_params=pltpu.CompilerParams(
            collective_id=1, has_side_effects=True, vmem_limit_bytes=48 * 2**20
        ),
        name="reduce_all",
    )(gd, gu, gc, ga, sg)


def dot(a, b):
    return jnp.dot(a, b, preferred_element_type=f32)


def dot_tn(a, b):
    return lax.dot_general(a, b, (((0,), (0,)), ((), ())), preferred_element_type=f32)


def dot_nt(a, b):
    return lax.dot_general(a, b, (((1,), (1,)), ((), ())), preferred_element_type=f32)


def per_device(
    nb,
    segment,
    memory,
    compressed,
    evicted,
    window_mask,
    cotangent,
    w_query,
    w_key,
    w_value,
    w_output,
    w_up,
    b_up,
    w_down,
    b_down,
    ln_gain,
    ln_bias,
    w_conv,
    b_conv,
    slopes,
):
    S, R, M = segment.shape
    heads = slopes.shape[0]
    hd = M // heads
    nt = 4
    rw, rd, rs = w_query.shape[0], w_down.shape[0], b_down.shape[0]
    b, t = lax.axis_index("batch"), lax.axis_index("tier")
    Cw, Fw = M // nt, nb * rd
    nu, W = R // 16, R // 3
    seg_len = nt * R
    T = S * seg_len
    ht = heads // nt
    index = 4 * b + t

    wa = jnp.stack([w_query, w_key, w_value, w_output]).reshape(4, rw, nt, Cw)
    wa = wa.transpose(2, 1, 0, 3).reshape(nt, rw, 4 * Cw)
    wu = w_up.reshape(rw, nb, nt, rd).transpose(2, 0, 1, 3).reshape(nt, rw, Fw)
    wc = w_conv.reshape(3, rw, nt, Cw).transpose(2, 1, 0, 3).reshape(nt, rw, 3 * Cw)
    row0 = jnp.concatenate([ln_gain, ln_bias, b_down, b_conv])
    sm = jnp.zeros((8, 128), f32).at[0, : 4 * rs].set(row0.astype(f32)).at[1, :rd].set(b_up.astype(f32))
    mem = memory.reshape(S, W, 3, M).transpose(0, 2, 1, 3)
    mk = jnp.broadcast_to(window_mask.astype(f32)[:, :, None], (S, W, 128))
    WA, WU, WC, WD, SM, CTX, COT, MK = gather_all(
        nb,
        nu,
        wa,
        wu,
        wc,
        w_down,
        sm,
        compressed.reshape(S, nu, 16, M),
        mem,
        segment.reshape(S, nu, 16, M),
        cotangent.reshape(S, nu, 16, M),
        mk,
    )
    WA = WA.reshape(M, 4 * Cw)
    Wqkv, Wo = WA[:, : 3 * Cw], WA[:, 3 * Cw :]
    WU, WC, WD = WU.reshape(M, Fw), WC.reshape(M, 3 * Cw), WD.reshape(Fw, M)
    gain, bias, bdown, bconv = [SM[:, :, 0, i * rs : (i + 1) * rs].reshape(M) for i in range(4)]
    bup = lax.dynamic_index_in_dim(SM, t, 1, False)[:, 1, :rd].reshape(Fw)
    cols = lambda v: lax.dynamic_slice_in_dim(v, t * Cw, Cw, v.ndim - 1)
    ctx = CTX.reshape(S, 3 * seg_len, M)
    cot = COT.reshape(T, M)
    seg = ctx[:, 2 * seg_len :].reshape(T, M)

    kpos = jnp.concatenate(
        [
            jnp.arange(seg_len),
            seg_len + (3 * jnp.arange(seg_len // 3)[None, :] + jnp.arange(3)[:, None]).reshape(-1),
            2 * seg_len + jnp.arange(seg_len),
        ]
    )
    qpos = 2 * seg_len + jnp.arange(seg_len)
    allowed = kpos[None, :] <= qpos[:, None]
    dist = (qpos[:, None] - kpos[None, :]).astype(f32) * (1.0 / (3 * seg_len))
    slope = lax.dynamic_slice_in_dim(slopes, t * ht, ht)
    scale = 1.0 / math.sqrt(hd)
    q = dot(seg, Wqkv[:, :Cw]).astype(bf16).reshape(S, seg_len, ht, hd)
    kv = dot(ctx.reshape(-1, M), Wqkv[:, Cw:]).astype(bf16).reshape(S, 3 * seg_len, 2, ht, hd)
    kk, vv = kv[:, :, 0], kv[:, :, 1]
    raw = jnp.einsum("sqhd,skhd->shqk", q, kk, preferred_element_type=f32)
    scores = jnp.where(allowed, raw * scale - slope[:, None, None] * dist, -1e30)
    high = jnp.max(scores, axis=-1, keepdims=True)
    e = jnp.exp(scores - high)
    probs = e / jnp.sum(e, axis=-1, keepdims=True)
    probs_low = probs.astype(bf16)
    mixed_t = jnp.einsum("shqk,skhd->sqhd", probs_low, vv, preferred_element_type=f32).astype(bf16)
    MIX = spread(mixed_t.reshape(T, Cw), True, 2)
    mixed = MIX.transpose(1, 0, 2).reshape(T, M)
    resid_t = cols(seg).astype(f32) + dot(mixed, Wo)
    RES = spread(resid_t.astype(bf16), True, 3)
    resid = RES.transpose(1, 0, 2).reshape(T, M).astype(f32)
    center = resid - jnp.mean(resid, axis=-1, keepdims=True)
    spread_ = lax.rsqrt(jnp.mean(center * center, axis=-1, keepdims=True) + norm_eps)
    xhat = center * spread_
    normed = (xhat * gain + bias).astype(bf16)
    pre = dot(normed, WU) + bup
    phi = 0.5 * (1.0 + lax.erf(pre * math.sqrt(0.5)))
    act = (pre * phi).astype(bf16)
    slope_act = phi + pre * jnp.exp(-0.5 * pre * pre) * (1.0 / math.sqrt(2 * math.pi))
    place = lambda v: lax.dynamic_update_slice_in_dim(jnp.zeros((T, M), f32), v, t * Cw, 1)
    out_part = dot(act, WD) + place(resid_t + cols(bdown))
    rows = lambda v: v.astype(bf16).reshape(S, nt, R, M).transpose(1, 0, 2, 3)
    output = jnp.sum(spread(rows(out_part), False, 4).astype(f32), axis=0).astype(bf16)
    gdown = dot_tn(act, cot)
    d_act = dot_nt(cot, WD).astype(bf16)
    d_pre = d_act.astype(f32) * slope_act
    gub = jnp.sum(d_pre, axis=0)
    d_pre_low = d_pre.astype(bf16)
    gup = dot_tn(normed, d_pre_low)
    dn_part = dot_nt(d_pre_low, WU)
    stats = jnp.stack([jnp.mean(dn_part * gain, axis=1), jnp.mean(dn_part * gain * xhat, axis=1)])
    stats = lax.psum(stats, "tier")
    cols_of = lambda v: v.astype(bf16).reshape(T, nt, Cw).transpose(1, 0, 2)
    dn = jnp.sum(spread(cols_of(dn_part), False, 5).astype(f32), axis=0)
    xhat_t = cols(xhat)
    ggain, gbias = jnp.sum(dn * xhat_t, axis=0), jnp.sum(dn, axis=0)
    g = dn * cols(gain)
    cot_t = cols(cot).astype(f32)
    gdb = jnp.sum(cot_t, axis=0)
    d_resid = cot_t + (g - stats[0][:, None] - xhat_t * stats[1][:, None]) * spread_
    d_branch = d_resid.astype(bf16)
    gout = dot_tn(mixed, d_branch)
    dm_part = dot_nt(d_branch, Wo)
    dm = jnp.sum(spread(cols_of(dm_part), False, 6).astype(f32), axis=0).astype(bf16)
    dm = dm.reshape(S, seg_len, ht, hd)
    d_probs = jnp.einsum("sqhd,skhd->shqk", dm, vv, preferred_element_type=f32)
    delta = jnp.sum(probs * d_probs, axis=-1, keepdims=True)
    d_scores = probs * (d_probs - delta)
    gslope = -jnp.sum(d_scores * dist, axis=(0, 2, 3))
    d_raw = (d_scores * scale).astype(bf16)
    dq = jnp.einsum("shqk,skhd->sqhd", d_raw, kk, preferred_element_type=f32).astype(bf16)
    dk = jnp.einsum("shqk,sqhd->skhd", d_raw, q, preferred_element_type=f32).astype(bf16)
    dv = jnp.einsum("shqk,sqhd->skhd", probs_low, dm, preferred_element_type=f32).astype(bf16)
    dq, dk, dv = dq.reshape(T, Cw), dk.reshape(S, -1, Cw), dv.reshape(S, -1, Cw)
    flat = ctx.reshape(-1, M)
    gq = dot_tn(seg, dq)
    gk, gv = dot_tn(flat, dk.reshape(-1, Cw)), dot_tn(flat, dv.reshape(-1, Cw))
    own = lambda v: v[:, 2 * seg_len :].reshape(T, Cw)
    ig_part = dot_nt(jnp.concatenate([dq, own(dk), own(dv)], axis=1), Wqkv) + place(d_resid)
    input_grad = jnp.sum(spread(rows(ig_part), False, 7).astype(f32), axis=0)

    nw = seg_len // 3
    win = ctx[:, seg_len : 2 * seg_len].reshape(S, 3, nw, M)
    win = [win[:, k].reshape(S * nw, M) for k in range(3)]
    conv = sum(dot(win[k], WC[:, k * Cw : (k + 1) * Cw]) for k in range(3)) + cols(bconv)
    pooled = sum(cols(win[k]).astype(f32) for k in range(3)) * (1.0 / 3.0)
    mask = MK.reshape(S, nw, 128)[:, :, :1]
    old = (3 * jnp.arange(nw) + 3)[None, :, None] <= evicted[:, None, None]
    live = jnp.where(old, mask, 0.0).reshape(-1, 1)
    d_conv = live * (conv - pooled)
    gcb = jnp.sum(d_conv, axis=0)
    d_low = d_conv.astype(bf16)
    gconv = jnp.concatenate([dot_tn(win[k], d_low) for k in range(3)], axis=1)
    new_t = (mask.reshape(-1, 1) * conv).astype(bf16)
    NEW = spread(new_t, True, 8).reshape(nt, S, nw, Cw).transpose(1, 2, 0, 3).reshape(S, nw, M)
    slot_offset = seg_len - nw
    local_rows = jnp.arange(R, dtype=jnp.int32) + t * R
    padded = jnp.concatenate([jnp.zeros((S, slot_offset, M), bf16), NEW], axis=1)
    slot_rows = lax.dynamic_slice_in_dim(padded, t * R, R, 1)
    written = (local_rows[None, :] >= slot_offset) & (
        3 * (local_rows[None, :] - slot_offset) + 3 <= evicted[:, None]
    )
    new_compressed = jnp.where(written[..., None], slot_rows, compressed)
    new_memory = jnp.where((local_rows[None, :] < evicted[:, None])[..., None], segment, memory)

    low = lambda v, *s: v.astype(bf16).reshape(s)
    gs = lax.dynamic_update_slice_in_dim(jnp.zeros((128,), f32), gslope, t * ht, 0)
    sg = jnp.concatenate([gub, gdb, ggain, gbias, gcb, gs])
    sg = jnp.concatenate([sg, jnp.zeros((24 * 128 - sg.shape[0],), f32)]).reshape(24, 128)
    OD, OU, OC, OA, OS = reduce_all(
        nb,
        low(gdown, nb, 4, rd // 4, M),
        low(gup, nb, 4, rw, Fw),
        low(gconv, nb, 4, rw, 3 * Cw),
        low(jnp.concatenate([gq, gk, gv, gout], axis=1), nb, 4, rw, 4 * Cw),
        sg,
    )
    OA = OA.reshape(nt, rw, 4, Cw).transpose(2, 1, 0, 3).reshape(4, rw, M)
    OU = OU.reshape(nt, rw, nb, rd).transpose(1, 2, 0, 3).reshape(rw, nb * nt * rd)
    OC = OC.reshape(nt, rw, 3, Cw).transpose(2, 1, 0, 3).reshape(3, rw, M)
    OS = OS.reshape(nt, -1)
    vec = lambda o: lax.dynamic_slice_in_dim(OS[:, o : o + Cw].reshape(M), index * rs, rs)
    gub_out = lax.dynamic_slice(OS, (t, b * rd), (1, rd)).reshape(rd)
    gslopes = jnp.sum(OS[:, Fw + 4 * Cw : Fw + 4 * Cw + heads], axis=0)
    return (
        output,
        input_grad,
        new_memory,
        new_compressed,
        OA[0],
        OA[1],
        OA[2],
        OA[3],
        OU,
        gub_out,
        OD.reshape(rd, M),
        vec(Fw),
        vec(Fw + Cw),
        vec(Fw + 2 * Cw),
        OC,
        vec(Fw + 3 * Cw),
        gslopes,
    )


class Names:
    def __init__(self, names, refs):
        for name, ref in zip(names, refs):
            setattr(self, name, ref)


def layer_kernel(names, shape, *refs):
    r = Names(names, refs)
    nb, nu, S, ht, hd, M, Cw, rw, rd, rs = shape
    R = 16 * nu
    G, bq = nb // 2, nb // 4
    L = 16 * 4 * nu
    C3 = 3 * L
    nw = L // 3
    Fw = nb * rd
    scale = 1.0 / math.sqrt(hd)
    b, t, z, y, zs, zback = places(G)
    mate, ends = z ^ 1, (z == 0) | (z == G - 1)
    ypeer = (b ^ 1, t)
    tc = pl.ds(pl.multiple_of(t * Cw, Cw), Cw)
    sends = []

    def got(ref, sem):
        pltpu.make_async_copy(ref, ref, sem).wait()

    def left_all(ref, sem):
        sends.append((ref, sem))

    def each(n, body, between=None):
        def step(i, c):
            body(i)
            for at, then in (between or {}).items():
                pl.when(i == at)(then)
            return c

        lax.fori_loop(0, n, step, 0)

    def ex_send(e, sem, src, dst):
        for d in (1, 2, 3):
            remote(src(t ^ d), dst(d), r.es.at[e], sem, (b, t ^ d)).start()

    def spread_send(e, s, arr):
        at = arr.at[t, s]
        for d in (1, 2):
            remote(at, at, r.es.at[e], r.er.at[e, s, d - 1], (b, t ^ d)).start()

    def spread_pass(e, s, arr):
        at = arr.at[t ^ 2, s]
        got(at, r.er.at[e, s, 1])
        remote(at, at, r.es.at[e], r.er.at[e, s, 0], (b, t ^ 1)).start()

    def spread_wait(e, s, arr):
        @pl.when(s < S - 1)
        def _():
            spread_pass(e, s + 1, arr)

        got(arr.at[0:2, s], r.er.at[e, s, 0])

    def fold_send(e, s, out, into):
        for i, d in enumerate((1, 3)):
            remote(out.at[t ^ d, s], into.at[i, s], r.es.at[e], r.er.at[e, s, i], (b, t ^ 1)).start()

    def fold_pass(e, s, out, into):
        at = into.at[1, s]
        got(at, r.er.at[e, s, 1])
        out[t ^ 2, s] = (out[t ^ 2, s].astype(f32) + at[...].astype(f32)).astype(bf16)
        remote(out.at[t ^ 2, s], into.at[2, s], r.es.at[e], r.er.at[e, s, 0], (b, t ^ 2)).start()

    def fold_late(e, s, out, into):
        @pl.when(s > 0)
        def _():
            fold_pass(e, s - 1, out, into)

    def folded(e, s, out, into):
        got(into.at[0:2, s], r.er.at[e, s, 0])
        return out[t, s].astype(f32) + into[0, s].astype(f32) + into[2, s].astype(f32)

    def here(src, dst, i):
        cp = pltpu.make_async_copy(src, dst, r.lsem.at[i])
        cp.start()
        return cp

    wide = lambda at, size: pl.ds(pl.multiple_of(at, 128), size)
    mats = (r.w_query, r.w_key, r.w_value, r.w_output)
    whole = {"S": r.SM, "A": r.WA, "U": r.WU, "C": r.WC}
    index = {"S": 0, "A": 1, "U": 2, "C": 3}

    def cuts(n, q):
        if n == "S":
            return [(r.SM.at[b, t], r.SM.at[b, t])]
        if n == "A":
            return [(w.at[:, wide(Cw * q, Cw)], r.WA.at[b, t, :, i * Cw : (i + 1) * Cw]) for i, w in enumerate(mats)]
        if n == "U":
            return [
                (r.w_up.at[:, wide((4 * i + q) * rd, rd)], r.WU.at[b, t, :, i * rd : (i + 1) * rd]) for i in range(nb)
            ]
        return [(r.w_conv.at[i, :, wide(Cw * q, Cw)], r.WC.at[b, t, :, i * Cw : (i + 1) * Cw]) for i in range(3)]

    def tier_start(n):
        i = index[n]
        if n != "S":
            for src, dst in cuts(n, t):
                here(src, dst, i)
        for d in (1, 2, 3):
            for src, dst in cuts(n, t ^ d):
                remote(src, dst, r.ts.at[i], r.tr.at[i], (b, t ^ d)).start()
        left_all(whole[n].at[b, 0:3], r.ts.at[i])

    def tier_wait(n):
        i = index[n]
        if n != "S":
            got(whole[n].at[b, t], r.lsem.at[i])
        got(whole[n].at[b, 0:3], r.tr.at[i])

    def if_(cond, body):
        pl.when(cond)(body)

    right, left = (2 * z + 2 + y, t), (2 * z - 2 + y, t)
    parts = {"S": [(r.SM, 0, 0, 4, 0)], "C": [(r.WC, 1, 0, 4, 1)], "X": [(r.WC, 2, 0, 4, 2)]}
    for i, (n, w, size) in enumerate((("A", r.WA, 2), ("U", r.WU, 2), ("D", r.WD, rd // 2))):
        parts[n] = [(w, 3 + 2 * i + h, h * size, size, 3 + i) for h in (0, 1)]

    def chunk_of(n, part, zz, col=None):
        w, k, at, size, _ = part
        col = ((1 - y) if n == "X" else y) if col is None else col
        return w.at[2 * zz + col, pl.ds(at, size)]

    def hop(part, at, j, way):
        k = part[1]
        peer, past = (right, z < G - 1) if way == 0 else (left, z > 0)
        return past, remote(at, at, r.zs.at[part[4]], r.zr.at[way, k, j], peer)

    def own_z(n):
        for part in parts[n]:
            for way in (0, 1):
                past, cp = hop(part, chunk_of(n, part, z), 0, way)
                if_(past, cp.start)

    def own_y(n):
        for part in parts[n]:
            at, k = chunk_of(n, part, z), part[4]
            remote(at, at, r.ys.at[k], r.yr.at[k], ypeer).start()

    def arrivals(n, step, js):
        for j in js:
            for part in parts[n]:
                for way in (0, 1):
                    zz = z - j if way == 0 else z + j
                    step(part, j, way, zz, chunk_of(n, part, zz), zz >= 0 if way == 0 else zz < G)

    def onward(n, *js):
        def step(part, j, way, zz, at, there):
            k = part[1]

            def body():
                got(at, r.zr.at[way, k, j - 1])
                if j < G - 1:
                    past, cp = hop(part, at, j, way)
                    if_(past, cp.start)
                if n not in "CX":
                    remote(at, at, r.ys.at[part[4]], r.yr.at[part[4]], ypeer).start()

            if_(there, body)

        arrivals(n, step, js or range(1, G))

    def all_sent(n):
        w, k = parts[n][0][0], parts[n][0][4]
        if_(ends, lambda: got(w.at[0:1], r.zs.at[k]))
        if_(~ends, lambda: got(w.at[0:5], r.zs.at[k]))
        if n != "X":
            got(w.at[0 : 1 if n == "C" else G], r.ys.at[k])

    def y_wait(n):
        w, k = parts[n][0][0], parts[n][0][4]
        got(w.at[0 : 1 if n == "C" else G], r.yr.at[k])

    def small_start():
        lane = lax.broadcasted_iota(jnp.int32, (8, 128), 1)
        side = lax.broadcasted_iota(jnp.int32, (8, 128), 0)
        spot = lax.rem(4 * b + t, Cw // rs)
        half, group = spot // (128 // rs), lax.rem(spot, 128 // rs)
        for q, v in enumerate((r.gain, r.bias, r.bdown, r.bconv)):
            r.SMG[q : q + 1, :rs] = v[...].astype(f32)
        r.SMG[4:5, :rd] = r.bup[...].astype(f32)
        acc = jnp.zeros((8, 128), f32)
        for q in range(4):
            turned = pltpu.roll(jnp.broadcast_to(r.SMG[q : q + 1], (8, 128)), rs * group, 1)
            mine = (side == 2 * q + half) & (lane >= rs * group) & (lane < rs * (group + 1))
            acc = jnp.where(mine, turned, acc)
        r.SM[b, t, 0:8] = acc
        r.SM[b, t, 8:16] = jnp.broadcast_to(r.SMG[4:5], (8, 128))
        tier_start("S")

    def memory_rows():
        W = R // 3
        to, frm = (lax.broadcasted_iota(jnp.int32, (R, R), axis) for axis in (0, 1))
        tap = (to >= W).astype(jnp.int32) + (to >= 2 * W).astype(jnp.int32)
        order = (frm == 3 * (to - W * tap) + tap).astype(bf16)
        for s in range(S):
            rows = jnp.dot(order, r.mem[s], preferred_element_type=f32).astype(bf16)
            for i in range(3):
                r.CTX[s, 4 * nu + 4 * i + t] = rows[W * i : W * (i + 1)]
            square = lambda axis: lax.broadcasted_iota(jnp.int32, (R // 3, R // 3), axis)
            line = jnp.broadcast_to(r.mask[s : s + 1].astype(f32), (R // 3, R // 3))
            col = jnp.sum(jnp.where(square(0) == square(1), line, 0.0), axis=1, keepdims=True)
            r.MK[s, t] = jnp.broadcast_to(col, (R // 3, 128))

    def rows_of(src, buf, first):
        at = lambda q: buf.at[:, pl.ds(first + nu * q, nu)]
        parts = [(src.at[:, 16 * i : 16 * i + 16], buf.at[:, first + nu * t + i]) for i in range(nu)]
        return parts, at, True

    def held(at):
        return [(at(t), at(t))], at, False

    pieces = [
        rows_of(r.seg, r.CTX, 8 * nu),
        rows_of(r.comp, r.CTX, 0),
        held(lambda q: r.CTX.at[:, 4 * nu + q]),
        held(lambda q: r.CTX.at[:, 4 * nu + 4 + q]),
        held(lambda q: r.CTX.at[:, 4 * nu + 8 + q]),
        rows_of(r.cot, r.COT, 0),
        held(lambda q: r.MK.at[:, q]),
    ]

    group = lambda i: 0 if i < 5 else i - 4
    grouped = [(r.CTX, 3 * nu), (r.COT, nu), (r.MK, 1)]

    def act_start(*which):
        for i in which:
            cut, at, far = pieces[i]
            g = group(i)
            for src, dst in cut:
                if far:
                    here(src, dst, 4 + g)
                remote(src, dst, r.acs.at[g], r.acc.at[g], (b, t ^ 1)).start()
                remote(src, dst, r.acs.at[g], r.acx.at[i], (b, t ^ 2)).start()

    def act_forward(*which):
        for i in which:
            at = pieces[i][1](t ^ 2)
            got(at, r.acx.at[i])
            remote(at, at, r.acs.at[group(i)], r.acf.at[group(i)], (b, t ^ 1)).start()

    def act_wait(g):
        buf, n = grouped[g]
        got(buf.at[:, 0:n], r.acc.at[g])
        got(buf.at[:, 0:n], r.acf.at[g])
        if g < 2:
            got(buf.at[:, 0 : n if g else 2 * nu], r.lsem.at[4 + g])

    def act_sent():
        for g, (buf, n) in enumerate(grouped):
            got(buf.at[:, 0 : 3 * n], r.acs.at[g])

    def table():
        row = lax.broadcasted_iota(jnp.int32, (L, C3), 0) + 2 * L
        col = lax.broadcasted_iota(jnp.int32, (L, C3), 1)
        inner = col - L
        k1 = (inner >= nw).astype(jnp.int32)
        k2 = (inner >= 2 * nw).astype(jnp.int32)
        win = inner - nw * (k1 + k2)
        pos = jnp.where((col >= L) & (col < 2 * L), L + 3 * win + k1 + k2, col)
        r.DIST[...] = jnp.where(pos <= row, (row - pos).astype(f32) * (1.0 / C3), 1e30)
        r.SMG[...] = jnp.zeros_like(r.SMG)

    def seg_rows(s):
        return r.CTX[s, 8 * nu : 12 * nu].reshape(L, M)

    def project(s):
        rows = r.CTX[s].reshape(C3, M)
        kv = jnp.dot(rows, r.WA[:, :, :, Cw : 3 * Cw].reshape(M, 2 * Cw), preferred_element_type=f32)
        r.KV[s] = kv.astype(bf16)
        q = jnp.dot(seg_rows(s), r.WA[:, :, :, :Cw].reshape(M, Cw), preferred_element_type=f32)
        r.Q[s] = q.astype(bf16)


    def attend(s):
        for h in range(ht):
            c = slice(h * hd, (h + 1) * hd)
            raw = dot_nt(r.Q[s, :, c], r.KV[s, :, c])
            scores = raw * scale - r.slopes[t * ht + h] * r.DIST[...]
            e = jnp.exp(scores - jnp.max(scores, axis=1, keepdims=True))
            p = e * (1.0 / jnp.sum(e, axis=1, keepdims=True))
            r.PR[s, h] = p
            v = r.KV[s, :, Cw + h * hd : Cw + (h + 1) * hd]
            r.MIX[t, s, :, c] = jnp.dot(p.astype(bf16), v, preferred_element_type=f32).astype(bf16)
        spread_send(0, s, r.MIX)


    def wo(q):
        return r.WA[bq * q : bq * (q + 1), :, :, 3 * Cw :].reshape(Cw, Cw)

    def residual(s):
        spread_wait(0, s, r.MIX)
        acc = r.CTX[s, 8 * nu : 12 * nu, :, tc].reshape(L, Cw).astype(f32)
        for q in range(4):
            acc = acc + jnp.dot(r.MIX[q, s], wo(q), preferred_element_type=f32)
        r.RT[s] = acc
        r.RES[t, s] = acc.astype(bf16)
        spread_send(1, s, r.RES)

    def vectors():
        for q in range(4):
            block = r.SM[bq * q, 0, 0:8]
            for bb in range(bq * q, bq * (q + 1)):
                for tt in range(4):
                    if bb != bq * q or tt:
                        block = block + r.SM[bb, tt, 0:8]
            for i in range(8):
                at = q * Cw + 128 * (i % 2)
                r.VV[i // 2 : i // 2 + 1, at : at + 128] = block[i : i + 1]
        for bb in range(nb):
            r.VV[4:5, bb * rd : (bb + 1) * rd] = r.SM[bb, t, 8:9, :rd]

    def xhat_of(s, q):
        return (r.RES[q, s].astype(f32) - r.MU[s, :, :1]) * r.MU[s, :, 1:2]

    def feed(s):
        spread_wait(1, s, r.RES)
        parts = [r.RES[q, s].astype(f32) for q in range(4)]
        mu = sum(jnp.sum(x, axis=1, keepdims=True) for x in parts) * (1.0 / M)
        var = sum(jnp.sum((x - mu) * (x - mu), axis=1, keepdims=True) for x in parts) * (1.0 / M)
        inv = lax.rsqrt(var + norm_eps)
        lane = lax.broadcasted_iota(jnp.int32, (L, 128), 1)
        r.MU[s] = jnp.where(lane == 0, mu, inv)
        for q in range(4):
            c = slice(q * Cw, (q + 1) * Cw)
            rows = ((parts[q] - mu) * inv) * r.VV[0:1, c] + r.VV[1:2, c]
            r.NRM[s, :, :, c] = rows.astype(bf16).reshape(4 * nu, 16, Cw)
        fb = Fw // 4
        for j in range(4):
            c = slice(j * fb, (j + 1) * fb)
            pre = jnp.dot(r.NRM[s].reshape(L, M), r.WU[:, :, :, c].reshape(M, fb), preferred_element_type=f32) + r.VV[4:5, c]
            phi = 0.5 + 0.5 * lax.erf(pre * math.sqrt(0.5))
            r.ACT[s, :, c] = (pre * phi).astype(bf16)
            r.GP[s, :, c] = (phi + pre * (jnp.exp(-0.5 * pre * pre) * (1.0 / math.sqrt(2 * math.pi)))).astype(bf16)


    def turn(j):
        low = lax.rem(G - j, G)
        inner = jnp.where(z == 1, low, G - 1 - low)
        return jnp.where(z == 0, G - 1 - j, jnp.where(z == G - 1, j, inner))

    grads = [(r.GD, r.YD, r.ZD), (r.GU, r.YU, r.ZU), (r.GC, r.YC, r.ZC), (r.GA, r.YA, r.ZA)]

    def to_y(k, zz):
        g, yb, zb = grads[k]
        remote(g.at[2 * zz + (1 - y)], yb.at[zz], r.gys.at[k], r.gyr.at[k, zz], ypeer).start()

    def plus(into, *others):
        def add(i):
            acc = into[i].astype(f32)
            for o in others:
                acc = acc + o[i].astype(f32)
            into[i] = acc.astype(bf16)

        each(into.shape[0], add)

    def pass_on(i, at, zb, o, sem):
        @pl.when((o != mate) & ~ends)
        def _():
            slot = lax.rem(o, 2)
            got(zb.at[slot], r.gzr.at[sem, slot])
            plus(at, zb.at[slot])

        to = jnp.where(ends, mate, o)
        slot = jnp.where(o == mate, 2, jnp.where(ends, lax.rem(o, 2), 3))
        remote(at, zb.at[slot], r.gzs.at[sem], r.gzr.at[sem, jnp.minimum(slot, 2)], (2 * to + y, t)).start()

    def mid(k, *steps):
        g, yb, zb = grads[k]
        for i in steps or range(G - 1):
            o = turn(i)
            at = yb.at[o]
            got(at, r.gyr.at[k, o])
            plus(at, g.at[2 * o + y])
            pass_on(i, at, zb, o, k)

    def mid_c(*steps):
        for i in steps or range(G - 1):
            o = turn(i)
            for c, col in enumerate((1 - y, y)):
                pass_on(i, r.GC.at[2 * o + col], r.ZC.at[c], o, (2, 4)[c])

    def arrived(zb, sem):
        got(zb.at[2:4], r.gzr.at[sem, 2])

    def summed(at, zb, more, store):
        def total(i):
            acc = at[i].astype(f32)
            for o in [zb.at[2], zb.at[3]] + more:
                acc = acc + o[i].astype(f32)
            store(i, acc)

        each(4, total)

    def fin(k, store):
        g, yb, zb = grads[k]
        at = yb.at[z]
        got(at, r.gyr.at[k, z])
        arrived(zb, k)
        summed(at, zb, [g.at[2 * z + y]], store)

    def cross_c():
        arrived(r.ZC.at[0], 2)
        other = r.GC.at[2 * z + 1 - y]

        def store(i, acc):
            other[i] = acc.astype(bf16)

        summed(other, r.ZC.at[0], [], store)
        remote(other, r.YC, r.gys.at[2], r.gyr.at[2, 0], ypeer).start()

    def fin_c(store):
        got(r.YC, r.gyr.at[2, 0])
        arrived(r.ZC.at[1], 4)
        summed(r.GC.at[2 * z + y], r.ZC.at[1], [r.YC], store)

    def reduced_sent():
        for k, (g, yb, zb) in enumerate(grads):
            got(g.at[0 : 1 if k == 2 else G], r.gys.at[k])
            for sem in (2, 4) if k == 2 else (k,):
                got(g.at[0:3], r.gzs.at[sem])

    fb = Fw // 4

    def grad_down(i):
        j = turn(i)
        c = pl.ds(pl.multiple_of(j * fb, fb), fb)
        rows = r.ACT[:, :, c].reshape(S * L, fb)
        g = dot_tn(rows, r.COT[...].reshape(S * L, M)).astype(bf16)
        r.GD[pl.ds(j * bq, bq)] = g.reshape(bq, 4, rd // 4, M)
        to_y(0, j)


    def back_feed(s):
        cot = r.COT[s].reshape(L, M)
        for j in range(4):
            c = slice(j * fb, (j + 1) * fb)
            wd = r.WD[bq * j : bq * (j + 1)].reshape(fb, M)
            d_act = dot_nt(cot, wd).astype(bf16).astype(f32)
            d_pre = d_act * r.GP[s, :, c].astype(f32)
            total = jnp.sum(d_pre, axis=0, keepdims=True)
            for i in range(fb // 128):
                at = j * (fb // 128) + i
                r.SMG[at : at + 1] += total[:, 128 * i : 128 * (i + 1)]
            r.GP[s, :, c] = d_pre.astype(bf16)
        m1 = jnp.zeros((L, 1), f32)
        m2 = jnp.zeros((L, 1), f32)
        for q in range(4):
            c = slice(q * Cw, (q + 1) * Cw)
            dn = dot_nt(r.GP[s], r.WU[bq * q : bq * (q + 1)].reshape(Cw, Fw))
            g = dn * r.VV[0:1, c]
            m1 = m1 + jnp.sum(g, axis=1, keepdims=True)
            m2 = m2 + jnp.sum(g * xhat_of(s, q), axis=1, keepdims=True)
            r.DNP[q, s] = dn.astype(bf16)
        lane = lax.broadcasted_iota(jnp.int32, (L, 128), 1)
        both = jnp.where(lane == 0, m1, jnp.where(lane == 1, m2, 0.0)) * (1.0 / M)
        pick = (
            lax.broadcasted_iota(jnp.int32, (8, 128), 0) == lax.broadcasted_iota(jnp.int32, (8, 128), 1)
        ).astype(f32)
        r.ST[t, s] = lax.dot_general(
            pick, both, (((1,), (1,)), ((), ())), precision=lax.Precision.HIGHEST, preferred_element_type=f32
        )
        fold_send(2, s, r.DNP, r.DNR)
        ex_send(3, r.er.at[3, s, 0], lambda q: r.ST.at[t, s], lambda d: r.ST.at[t, s])
        fold_late(2, s, r.DNP, r.DNR)


    def grad_up(i):
        j = turn(i)
        c = pl.ds(pl.multiple_of(j * Cw, Cw), Cw)
        rows = r.NRM[:, :, :, c].reshape(S * L, Cw)
        g = dot_tn(rows, r.GP[...].reshape(S * L, Fw)).astype(bf16)
        r.GU[pl.ds(j * bq, bq)] = g.reshape(bq, 4, rw, Fw)
        to_y(1, j)


    def back_norm(s):
        dn = folded(2, s, r.DNP, r.DNR)
        got(r.ST.at[0:3, s], r.er.at[3, s, 0])
        st = r.ST[0, s] + r.ST[1, s] + r.ST[2, s] + r.ST[3, s]
        side = lax.broadcasted_iota(jnp.int32, (8, 128), 0)
        col_of = lambda i: lax.dot_general(
            st,
            (side == i).astype(f32),
            (((0,), (0,)), ((), ())),
            precision=lax.Precision.HIGHEST,
            preferred_element_type=f32,
        )[:, :1]
        m1, m2 = col_of(0), col_of(1)
        inv = r.MU[s, :, 1:2]
        xhat = (r.RES[t, s].astype(f32) - r.MU[s, :, :1]) * inv
        cot = r.COT[s, :, :, tc].reshape(L, Cw).astype(f32)
        for i, v in enumerate((cot, dn * xhat, dn)):
            total = jnp.sum(v, axis=0, keepdims=True)
            for k in range(Cw // 128):
                at = Fw // 128 + i * (Cw // 128) + k
                r.SMG[at : at + 1] += total[:, 128 * k : 128 * (k + 1)]
        d_resid = cot + (dn * r.VV[0:1, tc] - m1 - xhat * m2) * inv
        r.DR[s] = d_resid
        db = d_resid.astype(bf16)
        r.DB[s] = db
        for q in range(4):
            r.DMP[q, s] = dot_nt(db, wo(q)).astype(bf16)
        fold_send(4, s, r.DMP, r.DMR)
        fold_late(4, s, r.DMP, r.DMR)

    def grad_out():
        for q in range(4):
            g = dot_tn(r.MIX[q].reshape(S * L, Cw), r.DB[...].reshape(S * L, Cw))
            r.GA[bq * q : bq * (q + 1), :, :, 3 * Cw :] = g.astype(bf16).reshape(bq, 4, rw, Cw)

    def out_rows(s):
        for q in range(4):
            c = slice(q * Cw, (q + 1) * Cw)
            o = jnp.dot(r.ACT[s], r.WD[:, :, c].reshape(Fw, Cw), preferred_element_type=f32)
            mine = (t == q).astype(f32)
            o = o + mine * (r.RT[s] + r.VV[2:3, c])
            r.OP[s, :, :, c] = o.astype(bf16).reshape(4 * nu, 16, Cw)
        ex_send(5, r.eo.at[0], lambda q: r.OP.at[s, pl.ds(nu * q, nu)], lambda d: r.OR.at[d - 1, s])


    def windows(k):
        return r.CTX[:, 4 * nu + 4 * k : 4 * nu + 4 * (k + 1)].reshape(S * nw, M)

    def compress():
        conv = r.VV[3:4, tc]
        pooled = 0.0
        for k in range(3):
            wk = r.WC[:, :, :, k * Cw : (k + 1) * Cw].reshape(M, Cw)
            conv = conv + jnp.dot(windows(k), wk, preferred_element_type=f32)
            pooled = pooled + r.CTX[:, 4 * nu + 4 * k : 4 * nu + 4 * (k + 1), :, tc].reshape(S * nw, Cw).astype(f32)
        mask = r.MK[...].reshape(S * nw, 128)[:, :1]
        done = 3 * lax.broadcasted_iota(jnp.int32, (nw, 128), 0) + 3
        live = jnp.concatenate(
            [(done <= r.evicted[s]).astype(f32)[:, :1] for s in range(S)], axis=0
        ) * mask
        r.NEW[t] = (mask * conv).astype(bf16)
        d_conv = live * (conv - pooled * (1.0 / 3.0))
        total = jnp.sum(d_conv, axis=0, keepdims=True)
        for k in range(Cw // 128):
            at = Fw // 128 + 3 * (Cw // 128) + k
            r.SMG[at : at + 1] = total[:, 128 * k : 128 * (k + 1)]
        r.DC[...] = d_conv.astype(bf16)
        for k in range(3):
            g = dot_tn(windows(k), r.DC[...])
            r.GC[:, :, :, k * Cw : (k + 1) * Cw] = g.astype(bf16).reshape(nb, 4, rw, Cw)

    slope_row = Fw // 128 + 4 * (Cw // 128)

    def back_attend(s):
        dm = folded(4, s, r.DMP, r.DMR).astype(bf16)
        lane = lax.broadcasted_iota(jnp.int32, (1, 128), 1)
        for h in range(ht):
            c = slice(h * hd, (h + 1) * hd)
            cv = slice(Cw + h * hd, Cw + (h + 1) * hd)
            p = r.PR[s, h]
            dp = dot_nt(dm[:, c], r.KV[s, :, cv])
            delta = jnp.sum(p * dp, axis=1, keepdims=True)
            ds = p * (dp - delta)
            part = jnp.sum(jnp.sum(ds * r.DIST[...], axis=0, keepdims=True), axis=1, keepdims=True)
            r.SMG[slope_row : slope_row + 1] -= jnp.where(lane == t * ht + h, part, 0.0)
            dr = (ds * scale).astype(bf16)
            dq = jnp.dot(dr, r.KV[s, :, c], preferred_element_type=f32).astype(bf16)
            dk = dot_tn(dr, r.Q[s, :, c]).astype(bf16)
            dv = dot_tn(p.astype(bf16), dm[:, c]).astype(bf16)
            r.Q[s, :, c] = dq
            r.KV[s, :, c] = dk
            r.KV[s, :, cv] = dv


    def grad_proj(i):
        j = turn(i)
        c = pl.ds(pl.multiple_of(j * Cw, Cw), Cw)
        gq = jnp.zeros((Cw, Cw), f32)
        gkv = jnp.zeros((Cw, 2 * Cw), f32)
        for s in range(S):
            gq = gq + dot_tn(r.CTX[s, 8 * nu : 12 * nu, :, c].reshape(L, Cw), r.Q[s])
            gkv = gkv + dot_tn(r.CTX[s, :, :, c].reshape(C3, Cw), r.KV[s])
        rows = pl.ds(j * bq, bq)
        r.GA[rows, :, :, :Cw] = gq.astype(bf16).reshape(bq, 4, rw, Cw)
        r.GA[rows, :, :, Cw : 3 * Cw] = gkv.astype(bf16).reshape(bq, 4, rw, 2 * Cw)
        to_y(3, j)

    def own_out(s):
        acc = r.OP[s, pl.ds(nu * t, nu)].astype(f32)
        for d in range(3):
            acc = acc + r.OR[d, s].astype(f32)
        r.OR[0, s] = acc.astype(bf16)


    def input_rows(s):
        x = jnp.concatenate([r.Q[s], r.KV[s, 2 * L :]], axis=1)
        for q in range(4):
            c = slice(q * Cw, (q + 1) * Cw)
            w = r.WA[bq * q : bq * (q + 1), :, :, : 3 * Cw].reshape(Cw, 3 * Cw)
            o = dot_nt(x, w) + (t == q).astype(f32) * r.DR[s]
            r.NRM[s, :, :, c] = o.astype(bf16).reshape(4 * nu, 16, Cw)
        ex_send(6, r.eo.at[1], lambda q: r.NRM.at[s, pl.ds(nu * q, nu)], lambda d: r.IR.at[d - 1, s])


    def keep(o):
        def store(i, acc):
            o[pl.ds(i * (rd // 4), rd // 4)] = acc

        return store

    def hold(m):
        def store(i, acc):
            m[i] = acc.astype(bf16)

        return store

    def tier_back(k, m, tb):
        for d in (1, 2, 3):
            remote(m.at[t ^ d], tb.at[t], r.gts.at[k], r.gtr.at[k], (b, t ^ d)).start()
        left_all(tb.at[0:3], r.gts.at[k])

    def small_y():
        remote(r.SMG, r.YS, r.ss.at[0], r.sr.at[0], ypeer).start()
        left_all(r.SMG, r.ss.at[0])

    def small_z():
        got(r.YS, r.sr.at[0])
        r.ZS[z] = r.SMG[...] + r.YS[...]
        for d in range(1, G):
            remote(r.ZS.at[z], r.ZS.at[z], r.ss.at[1], r.sr.at[1], (2 * zs[d] + y, t)).start()
        left_all(r.ZS.at[0 : G - 1], r.ss.at[1])

    def small_tier():
        got(r.ZS.at[0 : G - 1], r.sr.at[1])
        acc = r.ZS[0]
        for zz in range(1, G):
            acc = acc + r.ZS[zz]
        r.os[t] = acc
        for d in (1, 2, 3):
            remote(r.os.at[t], r.os.at[t], r.gts.at[3], r.gtr.at[3], (b, t ^ d)).start()
        left_all(r.os.at[0:3], r.gts.at[3])

    def own_input(s):
        acc = r.NRM[s, pl.ds(nu * t, nu)].astype(f32)
        for d in range(3):
            acc = acc + r.IR[d, s].astype(f32)
        r.IG[s] = acc

    mineU, mineC, mineA = (g.at[2 * z + y] for g in (r.GU, r.GC, r.GA))
    def give(i, src, dst):
        pltpu.make_async_copy(src, dst, r.osem.at[i]).start()

    def rows_out(i, src, dst):
        for j in range(nu):
            give(i, src.at[:, j], dst.at[:, 16 * j : 16 * j + 16])

    backs = ((mineU, r.TU, r.OU, r.ou), (mineC, r.TC, r.OC, r.oc), (mineA, r.TA, r.OA, r.oa))

    def lay(k, o, q, rows):
        if k == 0:
            for i in range(nb):
                o[:, wide((4 * i + q) * rd, rd)] = rows[:, i * rd : (i + 1) * rd].astype(f32)
        else:
            for i in range(o.shape[0]):
                o[i, :, wide(q * Cw, Cw)] = rows[:, i * Cw : (i + 1) * Cw].astype(f32)

    def tier_out(k):
        m, tb, o, far = backs[k]
        lay(k, o, t, m[t])
        got(tb.at[0:3], r.gtr.at[k])
        for d in (1, 2, 3):
            lay(k, o, t ^ d, tb[t ^ d])
        give(k, o, far)

    def given():
        for i, (src, dst) in enumerate(((r.OU, r.ou), (r.OC, r.oc), (r.OA, r.oa), (r.OD, r.od), (r.NEW, r.new))):
            pltpu.make_async_copy(src, dst, r.osem.at[i]).wait()
        for i, (src, dst) in ((5, (r.OR.at[0], r.out)), (6, (r.IG, r.ig))):
            for j in range(nu):
                pltpu.make_async_copy(src.at[:, j], dst.at[:, 16 * j : 16 * j + 16], r.osem.at[i]).wait()

    def small_out():
        got(r.os.at[0:3], r.gtr.at[3])

    def new_send():
        for d in (1, 2, 3):
            remote(r.NEW.at[t], r.NEW.at[t], r.ts.at[4], r.tr.at[4], (b, t ^ d)).start()
        left_all(r.NEW.at[0:3], r.ts.at[4])

    def new_out():
        got(r.NEW.at[0:3], r.tr.at[4])
        give(4, r.NEW, r.new)

    def drain():
        for n in parts:
            all_sent(n)
        for ref, sem in sends:
            got(ref, sem)
        act_sent()
        reduced_sent()
        for e, ref in enumerate((r.MIX, r.RES, r.DNP, r.ST, r.DMP, r.OR, r.IR)):
            got(ref.at[0:3], r.es.at[e])
        given()

    def out_come():
        got(r.OR, r.eo.at[0])

    def in_come():
        got(r.IR, r.eo.at[1])

    greet(G, True, True)
    here(r.wd, r.WD.at[b], 0)
    tier_start("A")
    tier_start("C")
    small_start()
    tier_start("U")
    act_start(0, 1)
    memory_rows()
    act_start(2, 3, 4, 5, 6)
    got(r.WD.at[b], r.lsem.at[0])
    own_z("D")
    own_y("D")
    tier_wait("A")
    own_z("A")
    own_y("A")
    tier_wait("C")
    own_y("C")
    tier_wait("S")
    own_z("S")
    own_y("S")
    table()
    onward("A", 1)
    onward("S", 1)
    onward("A", 2)
    onward("S", 2)
    tier_wait("U")
    own_z("U")
    onward("A", 3)
    own_y("U")
    onward("S", 3)
    y_wait("C")
    onward("U", 1)
    act_forward(0, 1, 2, 3, 4)
    act_wait(0)
    y_wait("A")
    each(S, project, {0: lambda: onward("U", 2), 1: lambda: onward("D", 1)})
    own_z("C")
    own_z("X")
    each(S, attend, {1: lambda: onward("U", 3)})
    spread_pass(0, 0, r.MIX)
    each(S, residual)
    onward("D", 2)
    y_wait("S")
    vectors()
    onward("C", 1)
    act_forward(5, 6)
    y_wait("U")
    spread_pass(1, 0, r.RES)
    each(S, feed, {1: lambda: onward("X", 1), 3: lambda: onward("D", 3)})
    act_wait(1)
    act_wait(2)
    each(4, grad_down, {1: lambda: onward("C", 2)})
    onward("X", 2)
    y_wait("D")
    each(S, back_feed, {0: lambda: onward("C", 3), 1: lambda: mid(0, 0), 2: lambda: onward("X", 3)})
    fold_pass(2, S - 1, r.DNP, r.DNR)
    compress()
    mid_c(0)
    mid(0, 1)
    each(4, grad_up)
    each(S, back_norm)
    fold_pass(4, S - 1, r.DMP, r.DMR)
    mid_c(1)
    mid(0, 2)
    grad_out()
    each(S, back_attend, {1: lambda: mid_c(2)})
    small_y()
    mid(1, 0)
    each(4, grad_proj)
    each(S, out_rows)
    mid(1, 1)
    each(S, input_rows)
    new_send()
    mid(1, 2)
    mid(3, 0)
    cross_c()
    fin(0, keep(r.OD))
    give(3, r.OD, r.od)
    small_z()
    mid(3, 1)
    fin(1, hold(mineU))
    tier_back(0, mineU, r.TU)
    mid(3, 2)
    small_tier()
    fin_c(hold(mineC))
    tier_back(1, mineC, r.TC)
    out_come()
    each(S, own_out)
    rows_out(5, r.OR.at[0], r.out)
    in_come()
    each(S, own_input)
    rows_out(6, r.IG, r.ig)
    new_out()
    tier_out(0)
    tier_out(1)
    small_out()
    fin(3, hold(mineA))
    tier_back(2, mineA, r.TA)
    tier_out(2)
    drain()

def whole_layer(nb, ht, hd, arrays):
    S, R, M = arrays["seg"].shape
    rw, rd, rs = arrays["w_query"].shape[0], arrays["wd"].shape[0], M // (4 * nb)
    nu = R // 16
    G, Cw, Fw, L = nb // 2, M // 4, nb * rd, 64 * nu
    dma = pltpu.SemaphoreType.DMA
    V = lambda shape, dtype=bf16: pltpu.VMEM(shape, dtype)
    D4, A4, U4, C4 = (4, rd // 4, M), (4, rw, 4 * Cw), (4, rw, Fw), (4, rw, 3 * Cw)
    ins = arrays
    outs = dict(
        out=((S, R, M), bf16),
        ig=((S, R, M), f32),
        new=((4, S * L // 3, Cw), bf16),
        od=((rd, M), f32),
        ou=((rw, 4 * Fw), f32),
        oc=((3, rw, M), f32),
        oa=((4, rw, M), f32),
        os=((4, 24, 128), f32),
    )
    scratch = dict(
        WA=V((nb,) + A4),
        WU=V((nb,) + U4),
        WC=V((nb,) + C4),
        WD=V((nb, rd, M)),
        SM=V((nb, 4, 16, 128), f32),
        CTX=V((S, 12 * nu, 16, M)),
        COT=V((S, 4 * nu, 16, M)),
        MK=V((S, 4, L // 12, 128), f32),
        DIST=V((L, 3 * L), f32),
        VV=V((8, max(M, Fw)), f32),
        SMG=V((24, 128), f32),
        Q=V((S, L, Cw)),
        KV=V((S, 3 * L, 2 * Cw)),
        PR=V((S, ht, L, 3 * L), f32),
        MIX=V((4, S, L, Cw)),
        RT=V((S, L, Cw), f32),
        RES=V((4, S, L, Cw)),
        MU=V((S, L, 128), f32),
        NRM=V((S, 4 * nu, 16, M)),
        ACT=V((S, L, Fw)),
        GP=V((S, L, Fw)),
        DNP=V((4, S, L, Cw)),
        DNR=V((3, S, L, Cw)),
        ST=V((4, S, 8, L), f32),
        DR=V((S, L, Cw), f32),
        DB=V((S, L, Cw)),
        DMP=V((4, S, L, Cw)),
        DMR=V((3, S, L, Cw)),
        OP=V((S, 4 * nu, 16, M)),
        OR=V((3, S, nu, 16, M)),
        IR=V((3, S, nu, 16, M)),
        DC=V((S * L // 3, Cw)),
        GD=V((nb,) + D4),
        GU=V((nb,) + U4),
        GC=V((nb,) + C4),
        GA=V((nb,) + A4),
        YD=V((G,) + D4),
        YU=V((G,) + U4),
        YC=V(C4),
        YA=V((G,) + A4),
        ZD=V((4,) + D4),
        ZU=V((4,) + U4),
        ZC=V((2, 4) + C4),
        ZA=V((4,) + A4),
        YS=V((24, 128), f32),
        ZS=V((G, 24, 128), f32),
        TU=V(U4),
        TC=V(C4),
        TA=V(A4),
        NEW=V((4, S * L // 3, Cw)),
        IG=V((S, nu, 16, M), f32),
        OD=V((rd, M), f32),
        OU=V((rw, 4 * Fw), f32),
        OC=V((3, rw, M), f32),
        OA=V((4, rw, M), f32),
        osem=dma((7,)),
        lsem=dma((6,)),
        ts=dma((5,)),
        tr=dma((5,)),
        zs=dma((6,)),
        zr=dma((2, 9, G - 1)),
        ys=dma((6,)),
        yr=dma((6,)),
        acs=dma((3,)),
        acc=dma((3,)),
        acf=dma((3,)),
        acx=dma((7,)),
        es=dma((7,)),
        er=dma((5, S, 2)),
        eo=dma((2,)),
        gys=dma((4,)),
        gyr=dma((4, G)),
        gzs=dma((5,)),
        gzr=dma((5, 3)),
        ss=dma((2,)),
        sr=dma((2,)),
        gts=dma((4,)),
        gtr=dma((4,)),
    )
    names = list(ins) + list(outs) + list(scratch)
    near = dict(gain=VM, bias=VM, bdown=VM, bconv=VM, bup=VM, mem=VM, mask=VM, evicted=SM, slopes=SM)
    return pl.pallas_call(
        functools.partial(layer_kernel, names, (nb, nu, S, ht, hd, M, Cw, rw, rd, rs)),
        out_shape=[jax.ShapeDtypeStruct(s, d) for s, d in outs.values()],
        in_specs=[near.get(n, ANY) for n in ins],
        out_specs=[VM if n == "os" else ANY for n in outs],
        scratch_shapes=list(scratch.values()),
        compiler_params=pltpu.CompilerParams(
            collective_id=9, has_side_effects=True, vmem_limit_bytes=63 * 2**20
        ),
        name="whole_layer",
    )(*ins.values())


def finish_kernel(names, shape, *refs):
    r = Names(names, refs)
    r.bufs = refs[len(names) :]
    nb, rs, rd, Fw, Cw, heads = shape
    S, R, M = r.seg.shape
    b, t = lax.axis_index("batch"), lax.axis_index("tier")
    moves = [(r.out, r.o_out), (r.ig, r.o_ig), (r.od, r.o_od), (r.ou, r.o_ou), (r.oc, r.o_oc)]
    moves += [(r.oa.at[i], o) for i, o in enumerate((r.o_q, r.o_k, r.o_v, r.o_o))]
    into, onto = [], []
    for i, (src, dst) in enumerate(moves):
        n = src.shape[0]
        cut = 4 if n % 4 == 0 else 1
        for j in range(cut):
            rows = pl.ds(j * (n // cut), n // cut)
            buf = r.bufs[i].at[rows]
            into.append(pltpu.make_async_copy(src.at[rows], buf, r.sem.at[len(into)]))
            onto.append(pltpu.make_async_copy(buf, dst.at[rows], r.sem.at[64 + len(onto)]))
    for cp in into:
        cp.start()
    nw = 4 * R // 3
    slots = 4 * R - nw
    place = lax.broadcasted_iota(jnp.int32, (R, 1), 0) + R * t
    for s in range(S):
        r.o_mem[s] = jnp.where(place < r.evicted[s], r.seg[s], r.mem[s])
        r.o_comp[s] = r.comp[s]
    for tier in range(4):
        first = max(slots - R * tier, 0)
        if first < R:

            @pl.when(t == tier)
            def _(tier=tier, first=first):
                w = R * tier + first - slots
                side = lax.broadcasted_iota(jnp.int32, (R - first, 1), 0)
                for s in range(S):
                    written = 3 * (side + w) + 3 <= r.evicted[s]
                    for q in range(4):
                        c = slice(q * Cw, (q + 1) * Cw)
                        rows = r.new[q, s * nw + w : s * nw + w + R - first]
                        r.o_comp[s, first:, c] = jnp.where(written, rows, r.comp[s, first:, c])
    spot = 4 * b + t
    block, inner = spot // (Cw // rs), lax.rem(spot, Cw // rs)
    half, group = inner // (128 // rs), lax.rem(inner, 128 // rs)
    for i, o in enumerate((r.o_down, r.o_gain, r.o_bias, r.o_conv)):
        row = r.os[block, pl.ds(Fw // 128 + (Cw // 128) * i + half, 1), :]
        turned = pltpu.roll(jnp.broadcast_to(row, (8, 128)), lax.rem(128 - rs * group, 128), 1)
        o[...] = turned[0:1, :rs]
    r.o_up[...] = r.os[t, pl.ds(b, 1), :rd]
    at = Fw // 128 + 4 * (Cw // 128)
    total = r.os[0, at : at + 1]
    for q in range(1, 4):
        total = total + r.os[q, at : at + 1]
    r.o_slopes[...] = total[:, :heads]
    for cp, then in zip(into, onto):
        cp.wait()
        then.start()
    for cp in onto:
        cp.wait()


def finish(nb, heads, arrays):
    S, R, M = arrays["seg"].shape
    rw, rd, rs = arrays["oa"].shape[1], arrays["od"].shape[0], M // (4 * nb)
    Cw, Fw = M // 4, nb * rd
    rows, mat, vec = (S, R, M), (rw, M), (1, rs)
    outs = dict(
        o_out=(rows, bf16, ANY),
        o_ig=(rows, f32, ANY),
        o_mem=(rows, bf16, VM),
        o_comp=(rows, bf16, VM),
        o_q=(mat, f32, ANY),
        o_k=(mat, f32, ANY),
        o_v=(mat, f32, ANY),
        o_o=(mat, f32, ANY),
        o_ou=((rw, 4 * Fw), f32, ANY),
        o_up=((1, rd), f32, VM),
        o_od=((rd, M), f32, ANY),
        o_down=(vec, f32, VM),
        o_gain=(vec, f32, VM),
        o_bias=(vec, f32, VM),
        o_oc=((3, rw, M), f32, ANY),
        o_conv=(vec, f32, VM),
        o_slopes=((1, heads), f32, VM),
    )
    moved = ("o_out", "o_ig", "o_od", "o_ou", "o_oc", "o_q", "o_k", "o_v", "o_o")
    near = dict(seg=VM, mem=VM, comp=VM, new=VM, os=VM, evicted=SM)
    return pl.pallas_call(
        functools.partial(
            finish_kernel, list(arrays) + list(outs) + ["sem"], (nb, rs, rd, Fw, Cw, heads)
        ),
        out_shape=[jax.ShapeDtypeStruct(s, d) for s, d, _ in outs.values()],
        in_specs=[near.get(n, ANY) for n in arrays],
        out_specs=[o[2] for o in outs.values()],
        scratch_shapes=[pltpu.SemaphoreType.DMA((128,))]
        + [pltpu.VMEM(outs[n][0], outs[n][1]) for n in moved],
        compiler_params=pltpu.CompilerParams(vmem_limit_bytes=63 * 2**20),
        name="finish",
    )(*arrays.values())


def per_device_fused(
    nb,
    segment,
    memory,
    compressed,
    evicted,
    window_mask,
    cotangent,
    w_query,
    w_key,
    w_value,
    w_output,
    w_up,
    b_up,
    w_down,
    b_down,
    ln_gain,
    ln_bias,
    w_conv,
    b_conv,
    slopes,
):
    S, R, M = segment.shape
    heads = slopes.shape[0]
    line = lambda v: v.reshape(1, -1)
    names = ("out", "ig", "new", "od", "ou", "oc", "oa", "os")
    made = whole_layer(
        nb,
        heads // 4,
        M // heads,
        dict(
            w_query=w_query,
            w_key=w_key,
            w_value=w_value,
            w_output=w_output,
            w_up=w_up,
            w_conv=w_conv,
            wd=w_down,
            comp=compressed,
            seg=segment,
            cot=cotangent,
            mem=memory,
            gain=line(ln_gain),
            bias=line(ln_bias),
            bdown=line(b_down),
            bconv=line(b_conv),
            bup=line(b_up),
            mask=window_mask,
            evicted=evicted,
            slopes=slopes,
        ),
    )
    arrays = dict(zip(names, made), seg=segment, mem=memory, comp=compressed, evicted=evicted)
    outs = finish(nb, heads, arrays)
    flat = (9, 11, 12, 13, 15, 16)
    return tuple(o.reshape(-1) if i in flat else o for i, o in enumerate(outs))


def solution(mesh):
    both = ("batch", "tier")
    rows = P("batch", "tier", None)
    mat, vec = P(both, None), P(both)
    nb = mesh.shape["batch"]

    def body(*args):
        fused = args[6].shape[0] % 16 == 0 and args[12].shape[0] == 128
        return (per_device_fused if fused else per_device)(nb, *args)

    return jax.shard_map(
        body,
        mesh=mesh,
        in_specs=(
            (rows, rows, rows, P("batch"), P("batch", "tier"), rows)
            + (mat, mat, mat, mat, mat, vec, mat, vec, vec, vec)
            + (P(None, both, None), vec, P())
        ),
        out_specs=(
            (rows, rows, rows, rows, mat, mat, mat, mat, mat, vec, mat, vec, vec, vec)
            + (P(None, both, None), vec, P())
        ),
        check_vma=False,
    )
```

```python
import functools
import math

import jax
import jax.numpy as jnp
from jax import lax
from jax.experimental import pallas as pl
from jax.experimental.pallas import tpu as pltpu
from jax.sharding import PartitionSpec as P

norm_eps = 1e-05
MESH = pl.DeviceIdType.MESH
ANY = pl.BlockSpec(memory_space=pl.ANY)
VM = pl.BlockSpec(memory_space=pltpu.VMEM)
SM = pl.BlockSpec(memory_space=pltpu.SMEM)
f32 = jnp.float32
bf16 = jnp.bfloat16


def remote(src, dst, send, recv, device):
    return pltpu.make_async_remote_copy(
        src_ref=src,
        dst_ref=dst,
        send_sem=send,
        recv_sem=recv,
        device_id=device,
        device_id_type=MESH,
    )


def places(groups):
    b, t = lax.axis_index("batch"), lax.axis_index("tier")
    z, y = b // 2, lax.rem(b, 2)
    zs = [lax.rem(z + d, groups) for d in range(groups)]
    zback = [lax.rem(z + groups - d, groups) for d in range(groups)]
    return b, t, z, y, zs, zback


def greet(groups, tiers, columns):
    b, t, z, y, zs, _ = places(groups)
    barrier = pltpu.get_barrier_semaphore()
    peers = []
    if tiers:
        peers += [(b, t ^ d) for d in (1, 2, 3)]
    if columns:
        peers += [(2 * zz + y, t) for zz in zs[1:]] + [(b ^ 1, t)]
    for peer in peers:
        pl.semaphore_signal(barrier, inc=1, device_id=peer, device_id_type=MESH)
    pl.semaphore_wait(barrier, len(peers))


def gather_kernel(groups, nu, *refs):
    (wa, wu, wc, wd, sm, comp, mem, seg, cot, mk) = refs[:10]
    (WA, WU, WC, WD, SM, CTX, COT, MK) = refs[10:18]
    lsem, ts, tr, zsd, zr, ys, yr, acs, acr = refs[18:]
    G = groups
    b, t, z, y, zs, zback = places(G)
    greet(G, True, True)
    ypeer = (b ^ 1, t)
    local, sends = [], []

    def here(src, dst, i):
        cp = pltpu.make_async_copy(src, dst, lsem.at[i])
        cp.start()
        return cp

    kinds = [(sm, SM), (wa, WA), (wu, WU), (wc, WC)]
    own = []
    for k, (src, dst) in enumerate(kinds):
        mine = src if k == 0 else src.at[t]
        own.append(here(mine, dst.at[b, t], k))
        for d in (1, 2, 3):
            piece = src if k == 0 else src.at[t ^ d]
            cp = remote(piece, dst.at[b, t], ts.at[k, d - 1], tr.at[k, d - 1], (b, t ^ d))
            cp.start()
            sends.append(cp)
    own.append(here(wd, WD.at[b], 4))
    pieces = [
        (comp, lambda q: CTX.at[:, pl.ds(nu * q, nu)]),
        (mem.at[:, 0], lambda q: CTX.at[:, 4 * nu + q]),
        (mem.at[:, 1], lambda q: CTX.at[:, 4 * nu + 4 + q]),
        (mem.at[:, 2], lambda q: CTX.at[:, 4 * nu + 8 + q]),
        (seg, lambda q: CTX.at[:, pl.ds(8 * nu + nu * q, nu)]),
        (mk, lambda q: MK.at[:, q]),
        (cot, lambda q: COT.at[:, pl.ds(nu * q, nu)]),
    ]
    for i, (src, at) in enumerate(pieces):
        own.append(here(src, at(t), 5 + i))
        for j, d in enumerate((1, 2)):
            cp = remote(src, at(t), acs.at[i, j], acr.at[i, j], (b, t ^ d))
            cp.start()
            sends.append(cp)
    table = [SM, WA, WU, WD, WC]
    local_of = [0, 1, 2, 4, 3]
    for k, dst in enumerate(table):
        own[local_of[k]].wait()
        if k != 3:
            kk = local_of[k]
            for d in (1, 2, 3):
                remote(dst.at[b, t], dst.at[b, t ^ d], ts.at[kk, d - 1], tr.at[kk, d - 1], (b, t ^ d)).wait_recv()
        for d in range(1, G):
            cp = remote(dst.at[b], dst.at[b], zsd.at[k, d], zr.at[k, d], (2 * zs[d] + y, t))
            cp.start()
            sends.append(cp)
        cp = remote(dst.at[b], dst.at[b], ys.at[k, 0], yr.at[k, 0], ypeer)
        cp.start()
        sends.append(cp)
    for i, (src, at) in enumerate(pieces):
        remote(at(t ^ 2), at(t ^ 2), acs.at[i, 1], acr.at[i, 1], (b, t ^ 2)).wait_recv()
        cp = remote(at(t ^ 2), at(t ^ 2), acs.at[i, 2], acr.at[i, 2], (b, t ^ 1))
        cp.start()
        sends.append(cp)
    for k, dst in enumerate(table):
        for d in range(1, G):
            at = dst.at[2 * zback[d] + y]
            remote(at, at, zsd.at[k, d], zr.at[k, d], ypeer).wait_recv()
            cp = remote(at, at, ys.at[k, d], yr.at[k, d], ypeer)
            cp.start()
            sends.append(cp)
    for k, dst in enumerate(table):
        for d in range(G):
            at = dst.at[2 * zback[d] + (1 - y)]
            remote(at, at, ys.at[k, d], yr.at[k, d], ypeer).wait_recv()
    for i, (src, at) in enumerate(pieces):
        for j, q in ((0, t ^ 1), (2, t ^ 3)):
            remote(at(q), at(q), acs.at[i, j], acr.at[i, j], (b, t ^ 1)).wait_recv()
    for i in range(len(pieces)):
        own[5 + i].wait()
    for cp in sends:
        cp.wait_send()


def gather_all(nb, nu, wa, wu, wc, wd, sm, comp, mem, seg, cot, mk):
    G = nb // 2
    S, _, U, M = comp.shape
    out = [
        jax.ShapeDtypeStruct((nb,) + wa.shape, bf16),
        jax.ShapeDtypeStruct((nb,) + wu.shape, bf16),
        jax.ShapeDtypeStruct((nb,) + wc.shape, bf16),
        jax.ShapeDtypeStruct((nb,) + wd.shape, bf16),
        jax.ShapeDtypeStruct((nb, 4) + sm.shape, f32),
        jax.ShapeDtypeStruct((S, 12 * nu, U, M), bf16),
        jax.ShapeDtypeStruct((S, 4 * nu, U, M), bf16),
        jax.ShapeDtypeStruct((S, 4) + mk.shape[1:], f32),
    ]
    dma = pltpu.SemaphoreType.DMA
    return pl.pallas_call(
        functools.partial(gather_kernel, G, nu),
        out_shape=out,
        in_specs=[ANY] * 10,
        out_specs=[ANY] * 8,
        scratch_shapes=[
            dma((12,)),
            dma((4, 3)),
            dma((4, 3)),
            dma((5, G)),
            dma((5, G)),
            dma((5, G)),
            dma((5, G)),
            dma((7, 3)),
            dma((7, 3)),
        ],
        compiler_params=pltpu.CompilerParams(collective_id=0, has_side_effects=True),
        name="gather_all",
    )(wa, wu, wc, wd, sm, comp, mem, seg, cot, mk)


def spread_kernel(same, x, o, lsem, ss, rs):
    b, t = lax.axis_index("batch"), lax.axis_index("tier")
    greet(1, True, False)
    cps = []
    for d in (1, 2, 3):
        cp = remote(x if same else x.at[t ^ d], o.at[t], ss.at[d - 1], rs.at[d - 1], (b, t ^ d))
        cp.start()
        cps.append(cp)
    mine = pltpu.make_async_copy(x if same else x.at[t], o.at[t], lsem)
    mine.start()
    mine.wait()
    for d in (1, 2, 3):
        remote(o.at[t ^ d], o.at[t ^ d], ss.at[d - 1], rs.at[d - 1], (b, t ^ d)).wait_recv()
    for cp in cps:
        cp.wait_send()


def spread(x, same, cid):
    dma = pltpu.SemaphoreType.DMA
    shape = ((4,) + x.shape) if same else x.shape
    return pl.pallas_call(
        functools.partial(spread_kernel, same),
        out_shape=jax.ShapeDtypeStruct(shape, x.dtype),
        in_specs=[ANY],
        out_specs=ANY,
        scratch_shapes=[dma, dma((3,)), dma((3,))],
        compiler_params=pltpu.CompilerParams(collective_id=cid, has_side_effects=True),
        name="spread_%d" % cid,
    )(x)


def reduce_kernel(groups, *refs):
    GD, GU, GC, GA, SMG = refs[:5]
    OD, OU, OC, OA, OS = refs[5:10]
    YD, YU, YC, YA, YS, ZD, ZU, ZC, ZA, ZS, TU, TC, TA, MU, MC, MA, ys, yr, zsd, zr, ts, tr = refs[10:]
    G = groups
    b, t, z, y, zs, zback = places(G)
    greet(G, True, True)
    ypeer = (b ^ 1, t)
    sends = []
    kinds = [
        (GD, YD, ZD, OD, None, None),
        (GU, YU, ZU, OU, MU, TU),
        (GC, YC, ZC, OC, MC, TC),
        (GA, YA, ZA, OA, MA, TA),
    ]
    for k, (g, yb, *_) in enumerate(kinds):
        for d in range(G):
            zz = zs[(d + 1) % G]
            cp = remote(g.at[2 * zz + (1 - y)], yb.at[zz], ys.at[k, d], yr.at[k, d], ypeer)
            cp.start()
            sends.append(cp)
    cp = remote(SMG, YS, ys.at[4, 0], yr.at[4, 0], ypeer)
    cp.start()
    sends.append(cp)
    for k, (g, yb, zb, o, m, tb) in enumerate(kinds):
        for d in range(G):
            zz = zs[(d + 1) % G]
            at = yb.at[zz]
            remote(at, at, ys.at[k, d], yr.at[k, d], ypeer).wait_recv()

            def add(i, c, yb=yb, zz=zz, g=g):
                yb[zz, i] = (yb[zz, i].astype(f32) + g[2 * zz + y, i].astype(f32)).astype(bf16)
                return c

            lax.fori_loop(0, yb.shape[1], add, 0)
            if d < G - 1:
                cp = remote(at, zb.at[d], zsd.at[k, d], zr.at[k, d], (2 * zz + y, t))
                cp.start()
                sends.append(cp)
    remote(YS, YS, ys.at[4, 0], yr.at[4, 0], ypeer).wait_recv()
    ZS[z] = SMG[...] + YS[...]
    for d in range(G - 1):
        cp = remote(ZS.at[z], ZS.at[z], zsd.at[4, d], zr.at[4, d], (2 * zs[d + 1] + y, t))
        cp.start()
        sends.append(cp)
    for k, (g, yb, zb, o, m, tb) in enumerate(kinds):
        for d in range(G - 1):
            remote(zb.at[d], zb.at[d], zsd.at[k, d], zr.at[k, d], ypeer).wait_recv()

        def total(i, c, k=k, yb=yb, zb=zb, o=o, m=m):
            acc = yb[z, i].astype(f32)
            for d in range(G - 1):
                acc = acc + zb[d, i].astype(f32)
            if k == 0:
                o[i] = acc
            else:
                m[i] = acc.astype(bf16)
            return c

        lax.fori_loop(0, o.shape[0], total, 0)
        if k:
            for d in (1, 2, 3):
                cp = remote(m.at[t ^ d], tb.at[t], ts.at[k - 1, d - 1], tr.at[k - 1, d - 1], (b, t ^ d))
                cp.start()
                sends.append(cp)
    for d in range(G - 1):
        at = ZS.at[zback[d + 1]]
        remote(at, at, zsd.at[4, d], zr.at[4, d], ypeer).wait_recv()
    acc = ZS[0]
    for zz in range(1, G):
        acc = acc + ZS[zz]
    OS[t] = acc
    for d in (1, 2, 3):
        cp = remote(OS.at[t], OS.at[t], ts.at[3, d - 1], tr.at[3, d - 1], (b, t ^ d))
        cp.start()
        sends.append(cp)
    for k, (g, yb, zb, o, m, tb) in enumerate(kinds):
        if k:
            o[t] = m[t].astype(f32)
            for d in (1, 2, 3):
                at = tb.at[t ^ d]
                remote(at, at, ts.at[k - 1, d - 1], tr.at[k - 1, d - 1], (b, t ^ d)).wait_recv()
                o[t ^ d] = tb[t ^ d].astype(f32)
    for d in (1, 2, 3):
        at = OS.at[t ^ d]
        remote(at, at, ts.at[3, d - 1], tr.at[3, d - 1], (b, t ^ d)).wait_recv()
    for cp in sends:
        cp.wait_send()


def reduce_all(nb, gd, gu, gc, ga, sg):
    G = nb // 2
    dma = pltpu.SemaphoreType.DMA
    shapes = [x.shape[1:] for x in (gd, gu, gc, ga)]
    return pl.pallas_call(
        functools.partial(reduce_kernel, G),
        out_shape=[jax.ShapeDtypeStruct(s, f32) for s in shapes]
        + [jax.ShapeDtypeStruct((4,) + sg.shape, f32)],
        in_specs=[VM] * 5,
        out_specs=[VM] * 5,
        scratch_shapes=[pltpu.VMEM((G,) + s, bf16) for s in shapes]
        + [pltpu.VMEM(sg.shape, f32)]
        + [pltpu.VMEM((G - 1,) + s, bf16) for s in shapes]
        + [pltpu.VMEM((G,) + sg.shape, f32)]
        + [pltpu.VMEM(s, bf16) for s in shapes[1:]]
        + [pltpu.VMEM(s, bf16) for s in shapes[1:]]
        + [dma((5, G)), dma((5, G)), dma((5, G)), dma((5, G)), dma((4, 3)), dma((4, 3))],
        compiler_params=pltpu.CompilerParams(
            collective_id=1, has_side_effects=True, vmem_limit_bytes=48 * 2**20
        ),
        name="reduce_all",
    )(gd, gu, gc, ga, sg)


def dot(a, b):
    return jnp.dot(a, b, preferred_element_type=f32)


def dot_tn(a, b):
    return lax.dot_general(a, b, (((0,), (0,)), ((), ())), preferred_element_type=f32)


def dot_nt(a, b):
    return lax.dot_general(a, b, (((1,), (1,)), ((), ())), preferred_element_type=f32)


def per_device(
    nb,
    segment,
    memory,
    compressed,
    evicted,
    window_mask,
    cotangent,
    w_query,
    w_key,
    w_value,
    w_output,
    w_up,
    b_up,
    w_down,
    b_down,
    ln_gain,
    ln_bias,
    w_conv,
    b_conv,
    slopes,
):
    S, R, M = segment.shape
    heads = slopes.shape[0]
    hd = M // heads
    nt = 4
    rw, rd, rs = w_query.shape[0], w_down.shape[0], b_down.shape[0]
    b, t = lax.axis_index("batch"), lax.axis_index("tier")
    Cw, Fw = M // nt, nb * rd
    nu, W = R // 16, R // 3
    seg_len = nt * R
    T = S * seg_len
    ht = heads // nt
    index = 4 * b + t

    wa = jnp.stack([w_query, w_key, w_value, w_output]).reshape(4, rw, nt, Cw)
    wa = wa.transpose(2, 1, 0, 3).reshape(nt, rw, 4 * Cw)
    wu = w_up.reshape(rw, nb, nt, rd).transpose(2, 0, 1, 3).reshape(nt, rw, Fw)
    wc = w_conv.reshape(3, rw, nt, Cw).transpose(2, 1, 0, 3).reshape(nt, rw, 3 * Cw)
    row0 = jnp.concatenate([ln_gain, ln_bias, b_down, b_conv])
    sm = jnp.zeros((8, 128), f32).at[0, : 4 * rs].set(row0.astype(f32)).at[1, :rd].set(b_up.astype(f32))
    mem = memory.reshape(S, W, 3, M).transpose(0, 2, 1, 3)
    mk = jnp.broadcast_to(window_mask.astype(f32)[:, :, None], (S, W, 128))
    WA, WU, WC, WD, SM, CTX, COT, MK = gather_all(
        nb,
        nu,
        wa,
        wu,
        wc,
        w_down,
        sm,
        compressed.reshape(S, nu, 16, M),
        mem,
        segment.reshape(S, nu, 16, M),
        cotangent.reshape(S, nu, 16, M),
        mk,
    )
    WA = WA.reshape(M, 4 * Cw)
    Wqkv, Wo = WA[:, : 3 * Cw], WA[:, 3 * Cw :]
    WU, WC, WD = WU.reshape(M, Fw), WC.reshape(M, 3 * Cw), WD.reshape(Fw, M)
    gain, bias, bdown, bconv = [SM[:, :, 0, i * rs : (i + 1) * rs].reshape(M) for i in range(4)]
    bup = lax.dynamic_index_in_dim(SM, t, 1, False)[:, 1, :rd].reshape(Fw)
    cols = lambda v: lax.dynamic_slice_in_dim(v, t * Cw, Cw, v.ndim - 1)
    ctx = CTX.reshape(S, 3 * seg_len, M)
    cot = COT.reshape(T, M)
    seg = ctx[:, 2 * seg_len :].reshape(T, M)

    kpos = jnp.concatenate(
        [
            jnp.arange(seg_len),
            seg_len + (3 * jnp.arange(seg_len // 3)[None, :] + jnp.arange(3)[:, None]).reshape(-1),
            2 * seg_len + jnp.arange(seg_len),
        ]
    )
    qpos = 2 * seg_len + jnp.arange(seg_len)
    allowed = kpos[None, :] <= qpos[:, None]
    dist = (qpos[:, None] - kpos[None, :]).astype(f32) * (1.0 / (3 * seg_len))
    slope = lax.dynamic_slice_in_dim(slopes, t * ht, ht)
    scale = 1.0 / math.sqrt(hd)
    q = dot(seg, Wqkv[:, :Cw]).astype(bf16).reshape(S, seg_len, ht, hd)
    kv = dot(ctx.reshape(-1, M), Wqkv[:, Cw:]).astype(bf16).reshape(S, 3 * seg_len, 2, ht, hd)
    kk, vv = kv[:, :, 0], kv[:, :, 1]
    raw = jnp.einsum("sqhd,skhd->shqk", q, kk, preferred_element_type=f32)
    scores = jnp.where(allowed, raw * scale - slope[:, None, None] * dist, -1e30)
    high = jnp.max(scores, axis=-1, keepdims=True)
    e = jnp.exp(scores - high)
    probs = e / jnp.sum(e, axis=-1, keepdims=True)
    probs_low = probs.astype(bf16)
    mixed_t = jnp.einsum("shqk,skhd->sqhd", probs_low, vv, preferred_element_type=f32).astype(bf16)
    MIX = spread(mixed_t.reshape(T, Cw), True, 2)
    mixed = MIX.transpose(1, 0, 2).reshape(T, M)
    resid_t = cols(seg).astype(f32) + dot(mixed, Wo)
    RES = spread(resid_t.astype(bf16), True, 3)
    resid = RES.transpose(1, 0, 2).reshape(T, M).astype(f32)
    center = resid - jnp.mean(resid, axis=-1, keepdims=True)
    spread_ = lax.rsqrt(jnp.mean(center * center, axis=-1, keepdims=True) + norm_eps)
    xhat = center * spread_
    normed = (xhat * gain + bias).astype(bf16)
    pre = dot(normed, WU) + bup
    phi = 0.5 * (1.0 + lax.erf(pre * math.sqrt(0.5)))
    act = (pre * phi).astype(bf16)
    slope_act = phi + pre * jnp.exp(-0.5 * pre * pre) * (1.0 / math.sqrt(2 * math.pi))
    place = lambda v: lax.dynamic_update_slice_in_dim(jnp.zeros((T, M), f32), v, t * Cw, 1)
    out_part = dot(act, WD) + place(resid_t + cols(bdown))
    rows = lambda v: v.astype(bf16).reshape(S, nt, R, M).transpose(1, 0, 2, 3)
    output = jnp.sum(spread(rows(out_part), False, 4).astype(f32), axis=0).astype(bf16)
    gdown = dot_tn(act, cot)
    d_act = dot_nt(cot, WD).astype(bf16)
    d_pre = d_act.astype(f32) * slope_act
    gub = jnp.sum(d_pre, axis=0)
    d_pre_low = d_pre.astype(bf16)
    gup = dot_tn(normed, d_pre_low)
    dn_part = dot_nt(d_pre_low, WU)
    stats = jnp.stack([jnp.mean(dn_part * gain, axis=1), jnp.mean(dn_part * gain * xhat, axis=1)])
    stats = lax.psum(stats, "tier")
    cols_of = lambda v: v.astype(bf16).reshape(T, nt, Cw).transpose(1, 0, 2)
    dn = jnp.sum(spread(cols_of(dn_part), False, 5).astype(f32), axis=0)
    xhat_t = cols(xhat)
    ggain, gbias = jnp.sum(dn * xhat_t, axis=0), jnp.sum(dn, axis=0)
    g = dn * cols(gain)
    cot_t = cols(cot).astype(f32)
    gdb = jnp.sum(cot_t, axis=0)
    d_resid = cot_t + (g - stats[0][:, None] - xhat_t * stats[1][:, None]) * spread_
    d_branch = d_resid.astype(bf16)
    gout = dot_tn(mixed, d_branch)
    dm_part = dot_nt(d_branch, Wo)
    dm = jnp.sum(spread(cols_of(dm_part), False, 6).astype(f32), axis=0).astype(bf16)
    dm = dm.reshape(S, seg_len, ht, hd)
    d_probs = jnp.einsum("sqhd,skhd->shqk", dm, vv, preferred_element_type=f32)
    delta = jnp.sum(probs * d_probs, axis=-1, keepdims=True)
    d_scores = probs * (d_probs - delta)
    gslope = -jnp.sum(d_scores * dist, axis=(0, 2, 3))
    d_raw = (d_scores * scale).astype(bf16)
    dq = jnp.einsum("shqk,skhd->sqhd", d_raw, kk, preferred_element_type=f32).astype(bf16)
    dk = jnp.einsum("shqk,sqhd->skhd", d_raw, q, preferred_element_type=f32).astype(bf16)
    dv = jnp.einsum("shqk,sqhd->skhd", probs_low, dm, preferred_element_type=f32).astype(bf16)
    dq, dk, dv = dq.reshape(T, Cw), dk.reshape(S, -1, Cw), dv.reshape(S, -1, Cw)
    flat = ctx.reshape(-1, M)
    gq = dot_tn(seg, dq)
    gk, gv = dot_tn(flat, dk.reshape(-1, Cw)), dot_tn(flat, dv.reshape(-1, Cw))
    own = lambda v: v[:, 2 * seg_len :].reshape(T, Cw)
    ig_part = dot_nt(jnp.concatenate([dq, own(dk), own(dv)], axis=1), Wqkv) + place(d_resid)
    input_grad = jnp.sum(spread(rows(ig_part), False, 7).astype(f32), axis=0)

    nw = seg_len // 3
    win = ctx[:, seg_len : 2 * seg_len].reshape(S, 3, nw, M)
    win = [win[:, k].reshape(S * nw, M) for k in range(3)]
    conv = sum(dot(win[k], WC[:, k * Cw : (k + 1) * Cw]) for k in range(3)) + cols(bconv)
    pooled = sum(cols(win[k]).astype(f32) for k in range(3)) * (1.0 / 3.0)
    mask = MK.reshape(S, nw, 128)[:, :, :1]
    old = (3 * jnp.arange(nw) + 3)[None, :, None] <= evicted[:, None, None]
    live = jnp.where(old, mask, 0.0).reshape(-1, 1)
    d_conv = live * (conv - pooled)
    gcb = jnp.sum(d_conv, axis=0)
    d_low = d_conv.astype(bf16)
    gconv = jnp.concatenate([dot_tn(win[k], d_low) for k in range(3)], axis=1)
    new_t = (mask.reshape(-1, 1) * conv).astype(bf16)
    NEW = spread(new_t, True, 8).reshape(nt, S, nw, Cw).transpose(1, 2, 0, 3).reshape(S, nw, M)
    slot_offset = seg_len - nw
    local_rows = jnp.arange(R, dtype=jnp.int32) + t * R
    padded = jnp.concatenate([jnp.zeros((S, slot_offset, M), bf16), NEW], axis=1)
    slot_rows = lax.dynamic_slice_in_dim(padded, t * R, R, 1)
    written = (local_rows[None, :] >= slot_offset) & (
        3 * (local_rows[None, :] - slot_offset) + 3 <= evicted[:, None]
    )
    new_compressed = jnp.where(written[..., None], slot_rows, compressed)
    new_memory = jnp.where((local_rows[None, :] < evicted[:, None])[..., None], segment, memory)

    low = lambda v, *s: v.astype(bf16).reshape(s)
    gs = lax.dynamic_update_slice_in_dim(jnp.zeros((128,), f32), gslope, t * ht, 0)
    sg = jnp.concatenate([gub, gdb, ggain, gbias, gcb, gs])
    sg = jnp.concatenate([sg, jnp.zeros((24 * 128 - sg.shape[0],), f32)]).reshape(24, 128)
    OD, OU, OC, OA, OS = reduce_all(
        nb,
        low(gdown, nb, 4, rd // 4, M),
        low(gup, nb, 4, rw, Fw),
        low(gconv, nb, 4, rw, 3 * Cw),
        low(jnp.concatenate([gq, gk, gv, gout], axis=1), nb, 4, rw, 4 * Cw),
        sg,
    )
    OA = OA.reshape(nt, rw, 4, Cw).transpose(2, 1, 0, 3).reshape(4, rw, M)
    OU = OU.reshape(nt, rw, nb, rd).transpose(1, 2, 0, 3).reshape(rw, nb * nt * rd)
    OC = OC.reshape(nt, rw, 3, Cw).transpose(2, 1, 0, 3).reshape(3, rw, M)
    OS = OS.reshape(nt, -1)
    vec = lambda o: lax.dynamic_slice_in_dim(OS[:, o : o + Cw].reshape(M), index * rs, rs)
    gub_out = lax.dynamic_slice(OS, (t, b * rd), (1, rd)).reshape(rd)
    gslopes = jnp.sum(OS[:, Fw + 4 * Cw : Fw + 4 * Cw + heads], axis=0)
    return (
        output,
        input_grad,
        new_memory,
        new_compressed,
        OA[0],
        OA[1],
        OA[2],
        OA[3],
        OU,
        gub_out,
        OD.reshape(rd, M),
        vec(Fw),
        vec(Fw + Cw),
        vec(Fw + 2 * Cw),
        OC,
        vec(Fw + 3 * Cw),
        gslopes,
    )


class Names:
    def __init__(self, names, refs):
        for name, ref in zip(names, refs):
            setattr(self, name, ref)


def layer_kernel(names, shape, *refs):
    r = Names(names, refs)
    nb, nu, S, ht, hd, M, Cw, rw, rd, rs = shape
    R = 16 * nu
    ct = r.OC.shape[0] - r.GB.shape[-1] // Cw
    G, bq = nb // 2, nb // 4
    L = 16 * 4 * nu
    C3 = 3 * L
    nw = L // 3
    Fw = nb * rd
    scale = 1.0 / math.sqrt(hd)
    b, t, z, y, zs, zback = places(G)
    mate, ends = z ^ 1, (z == 0) | (z == G - 1)
    ypeer = (b ^ 1, t)
    tc = pl.ds(pl.multiple_of(t * Cw, Cw), Cw)
    sends = []

    def got(ref, sem):
        pltpu.make_async_copy(ref, ref, sem).wait()

    def left_all(ref, sem):
        sends.append((ref, sem))

    def each(n, body, between=None):
        def step(i, c):
            body(i)
            for at, then in (between or {}).items():
                pl.when(i == at)(then)
            return c

        lax.fori_loop(0, n, step, 0)

    def ex_send(e, sem, src, dst):
        for d in (1, 2, 3):
            remote(src(t ^ d), dst(d), r.es.at[e], sem, (b, t ^ d)).start()

    def spread_send(e, s, arr):
        at = arr.at[t, s]
        for d in (1, 2):
            remote(at, at, r.es.at[e], r.er.at[e, s, d - 1], (b, t ^ d)).start()

    def spread_pass(e, s, arr):
        at = arr.at[t ^ 2, s]
        got(at, r.er.at[e, s, 1])
        remote(at, at, r.es.at[e], r.er.at[e, s, 0], (b, t ^ 1)).start()

    def spread_wait(e, s, arr):
        @pl.when(s < S - 1)
        def _():
            spread_pass(e, s + 1, arr)

        got(arr.at[0:2, s], r.er.at[e, s, 0])

    folds = {
        2: (lambda q, s: r.DNP.at[q, s], r.DNR),
        4: (lambda q, s: r.DMP.at[q, s], r.DMR),
        5: (lambda q, s: r.OP.at[s, pl.ds(nu * q, nu)], r.OR),
        6: (lambda q, s: r.NRM.at[s, pl.ds(nu * q, nu)], r.IR),
    }

    def fold_send(e, s):
        out, into = folds[e]
        for i, d in enumerate((1, 3)):
            remote(out(t ^ d, s), into.at[i, s], r.es.at[e], r.er.at[e, s, i], (b, t ^ 1)).start()

    def fold_pass(e, s):
        out, into = folds[e]
        at, far = into.at[1, s], out(t ^ 2, s)
        got(at, r.er.at[e, s, 1])
        far[...] = (far[...].astype(f32) + at[...].astype(f32)).astype(bf16)
        remote(far, into.at[2, s], r.es.at[e], r.er.at[e, s, 0], (b, t ^ 2)).start()

    def fold_late(e, s):
        @pl.when(s > 0)
        def _():
            fold_pass(e, s - 1)

    def folded(e, s):
        out, into = folds[e]
        got(into.at[0:2, s], r.er.at[e, s, 0])
        return out(t, s)[...].astype(f32) + into[0, s].astype(f32) + into[2, s].astype(f32)

    def here(src, dst, i):
        cp = pltpu.make_async_copy(src, dst, r.lsem.at[i])
        cp.start()
        return cp

    wide = lambda at, size: pl.ds(pl.multiple_of(at, 128), size)
    mats = (r.w_query, r.w_key, r.w_value, r.w_output)
    whole = {"S": r.SM, "A": r.WA, "U": r.WU, "C": r.WC}
    index = {"S": 0, "A": 1, "U": 2, "C": 3}

    def cuts(n, q):
        if n == "S":
            return [(r.SM.at[b, t], r.SM.at[b, t])]
        if n == "A":
            return [(w.at[:, wide(Cw * q, Cw)], r.WA.at[b, t, :, i * Cw : (i + 1) * Cw]) for i, w in enumerate(mats)]
        if n == "U":
            return [
                (r.w_up.at[:, wide((4 * i + q) * rd, rd)], r.WU.at[b, t, :, i * rd : (i + 1) * rd]) for i in range(nb)
            ]
        return [(r.w_conv.at[i, :, wide(Cw * q, Cw)], r.WC.at[b, t, :, i * Cw : (i + 1) * Cw]) for i in range(3)]

    def tier_own(n):
        for src, dst in cuts(n, t):
            here(src, dst, index[n])

    def tier_start(n):
        i = index[n]
        for d in (1, 2, 3):
            for src, dst in cuts(n, t ^ d):
                remote(src, dst, r.ts.at[i], r.tr.at[i], (b, t ^ d)).start()
        left_all(whole[n].at[b, 0:3], r.ts.at[i])

    def tier_wait(n):
        i = index[n]
        if n != "S":
            got(whole[n].at[b, t], r.lsem.at[i])
        got(whole[n].at[b, 0:3], r.tr.at[i])

    def if_(cond, body):
        pl.when(cond)(body)

    right, left = (2 * z + 2 + y, t), (2 * z - 2 + y, t)
    parts = {"S": [(r.SM, 0, 0, 4, 0)], "C": [(r.WC, 1, 0, 4, 1)], "X": [(r.WC, 2, 0, 4, 2)]}
    for i, (n, w, size) in enumerate((("A", r.WA, 2), ("U", r.WU, 2), ("D", r.WD, rd // 2))):
        parts[n] = [(w, 3 + 2 * i + h, h * size, size, 3 + i) for h in (0, 1)]

    def chunk_of(n, part, zz, col=None):
        w, k, at, size, _ = part
        col = ((1 - y) if n == "X" else y) if col is None else col
        return w.at[2 * zz + col, pl.ds(at, size)]

    def hop(part, at, j, way):
        k = part[1]
        peer, past = (right, z < G - 1) if way == 0 else (left, z > 0)
        return past, remote(at, at, r.zs.at[part[4]], r.zr.at[way, k, j], peer)

    def own_z(n):
        for part in parts[n]:
            for way in (0, 1):
                past, cp = hop(part, chunk_of(n, part, z), 0, way)
                if_(past, cp.start)

    def own_y(n):
        for part in parts[n]:
            at, k = chunk_of(n, part, z), part[4]
            remote(at, at, r.ys.at[k], r.yr.at[k], ypeer).start()

    def arrivals(n, step, js):
        for j in js:
            for part in parts[n]:
                for way in (0, 1):
                    zz = z - j if way == 0 else z + j
                    step(part, j, way, zz, chunk_of(n, part, zz), zz >= 0 if way == 0 else zz < G)

    def onward(n, *js):
        def step(part, j, way, zz, at, there):
            k = part[1]

            def body():
                got(at, r.zr.at[way, k, j - 1])
                if j < G - 1:
                    past, cp = hop(part, at, j, way)
                    if_(past, cp.start)
                if n not in "CX":
                    remote(at, at, r.ys.at[part[4]], r.yr.at[part[4]], ypeer).start()

            if_(there, body)

        arrivals(n, step, js or range(1, G))

    def all_sent(n):
        w, k = parts[n][0][0], parts[n][0][4]
        if_(ends, lambda: got(w.at[0:1], r.zs.at[k]))
        if_(~ends, lambda: got(w.at[0:5], r.zs.at[k]))
        if n != "X":
            got(w.at[0 : 1 if n == "C" else G], r.ys.at[k])

    def y_wait(n):
        w, k = parts[n][0][0], parts[n][0][4]
        got(w.at[0 : 1 if n == "C" else G], r.yr.at[k])

    def small_start():
        lane = lax.broadcasted_iota(jnp.int32, (8, 128), 1)
        side = lax.broadcasted_iota(jnp.int32, (8, 128), 0)
        spot = lax.rem(4 * b + t, Cw // rs)
        half, group = spot // (128 // rs), lax.rem(spot, 128 // rs)
        for q, v in enumerate((r.gain, r.bias, r.bdown, r.bconv)):
            r.SMG[q : q + 1, :rs] = v[...].astype(f32)
        r.SMG[4:5, :rd] = r.bup[...].astype(f32)
        acc = jnp.zeros((8, 128), f32)
        for q in range(4):
            turned = pltpu.roll(jnp.broadcast_to(r.SMG[q : q + 1], (8, 128)), rs * group, 1)
            mine = (side == 2 * q + half) & (lane >= rs * group) & (lane < rs * (group + 1))
            acc = jnp.where(mine, turned, acc)
        r.SM[b, t, 0:8] = acc
        r.SM[b, t, 8:16] = jnp.broadcast_to(r.SMG[4:5], (8, 128))
        tier_start("S")

    def memory_rows():
        W = R // 3
        to, frm = (lax.broadcasted_iota(jnp.int32, (R, R), axis) for axis in (0, 1))
        tap = (to >= W).astype(jnp.int32) + (to >= 2 * W).astype(jnp.int32)
        order = (frm == 3 * (to - W * tap) + tap).astype(bf16)
        for s in range(S):
            rows = jnp.dot(order, r.MEMV[s], preferred_element_type=f32).astype(bf16)
            for i in range(3):
                r.CTX[s, 4 * nu + 4 * i + t] = rows[W * i : W * (i + 1)]
            square = lambda axis: lax.broadcasted_iota(jnp.int32, (R // 3, R // 3), axis)
            line = jnp.broadcast_to(r.mask[s : s + 1].astype(f32), (R // 3, R // 3))
            col = jnp.sum(jnp.where(square(0) == square(1), line, 0.0), axis=1, keepdims=True)
            r.MK[s, t] = jnp.broadcast_to(col, (R // 3, 128))

    def rows_of(src, buf, first):
        at = lambda q: buf.at[:, pl.ds(first + nu * q, nu)]
        parts = [(src.at[:, 16 * i : 16 * i + 16], buf.at[:, first + nu * t + i]) for i in range(nu)]
        return parts, at, True

    def held(at):
        return [(at(t), at(t))], at, False

    pieces = [
        rows_of(r.seg, r.CTX, 8 * nu),
        rows_of(r.comp, r.CTX, 0),
        held(lambda q: r.CTX.at[:, 4 * nu + q]),
        held(lambda q: r.CTX.at[:, 4 * nu + 4 + q]),
        held(lambda q: r.CTX.at[:, 4 * nu + 8 + q]),
        rows_of(r.cot, r.COT, 0),
        held(lambda q: r.MK.at[:, q]),
    ]

    group = lambda i: 0 if i < 5 else i - 4
    grouped = [(r.CTX, 3 * nu), (r.COT, nu), (r.MK, 1)]

    def act_own():
        for i, (cut, at, far) in enumerate(pieces):
            if far:
                for src, dst in cut:
                    here(src, dst, 4 + group(i))

    def act_start(*which):
        for i in which:
            cut, at, far = pieces[i]
            g = group(i)
            for src, dst in cut:
                remote(src, dst, r.acs.at[g], r.acc.at[g], (b, t ^ 1)).start()
                remote(src, dst, r.acs.at[g], r.acx.at[i], (b, t ^ 2)).start()

    def act_forward(*which):
        for i in which:
            at = pieces[i][1](t ^ 2)
            got(at, r.acx.at[i])
            remote(at, at, r.acs.at[group(i)], r.acf.at[group(i)], (b, t ^ 1)).start()

    def act_wait(g):
        buf, n = grouped[g]
        got(buf.at[:, 0:n], r.acc.at[g])
        got(buf.at[:, 0:n], r.acf.at[g])
        if g < 2:
            got(buf.at[:, 0 : n if g else 2 * nu], r.lsem.at[4 + g])

    def act_sent():
        for g, (buf, n) in enumerate(grouped):
            got(buf.at[:, 0 : 3 * n], r.acs.at[g])

    def table():
        row = lax.broadcasted_iota(jnp.int32, (L, C3), 0) + 2 * L
        col = lax.broadcasted_iota(jnp.int32, (L, C3), 1)
        inner = col - L
        k1 = (inner >= nw).astype(jnp.int32)
        k2 = (inner >= 2 * nw).astype(jnp.int32)
        win = inner - nw * (k1 + k2)
        pos = jnp.where((col >= L) & (col < 2 * L), L + 3 * win + k1 + k2, col)
        r.DIST[...] = jnp.where(pos <= row, (row - pos).astype(f32) * (1.0 / C3), 1e30)
        r.SMG[...] = jnp.zeros_like(r.SMG)

    def seg_rows(s):
        return r.CTX[s, 8 * nu : 12 * nu].reshape(L, M)

    def project(s):
        rows = r.CTX[s].reshape(C3, M)
        kv = jnp.dot(rows, r.WA[:, :, :, Cw : 3 * Cw].reshape(M, 2 * Cw), preferred_element_type=f32)
        r.KV[s] = kv.astype(bf16)
        q = jnp.dot(seg_rows(s), r.WA[:, :, :, :Cw].reshape(M, Cw), preferred_element_type=f32)
        r.Q[s] = q.astype(bf16)


    def attend(s):
        for h in range(ht):
            c = slice(h * hd, (h + 1) * hd)
            raw = dot_nt(r.Q[s, :, c], r.KV[s, :, c])
            scores = raw * scale - r.slopes[t * ht + h] * r.DIST[...]
            e = jnp.exp(scores - jnp.max(scores, axis=1, keepdims=True))
            p = e * (1.0 / jnp.sum(e, axis=1, keepdims=True))
            r.PR[s, h] = p
            v = r.KV[s, :, Cw + h * hd : Cw + (h + 1) * hd]
            r.MIX[t, s, :, c] = jnp.dot(p.astype(bf16), v, preferred_element_type=f32).astype(bf16)
        spread_send(0, s, r.MIX)


    def wo(q):
        return r.WA[bq * q : bq * (q + 1), :, :, 3 * Cw :].reshape(Cw, Cw)

    def residual(s):
        spread_wait(0, s, r.MIX)
        acc = r.CTX[s, 8 * nu : 12 * nu, :, tc].reshape(L, Cw).astype(f32)
        for q in range(4):
            acc = acc + jnp.dot(r.MIX[q, s], wo(q), preferred_element_type=f32)
        r.RT[s] = acc
        r.RES[t, s] = acc.astype(bf16)
        spread_send(1, s, r.RES)

    def vectors():
        for q in range(4):
            block = r.SM[bq * q, 0, 0:8]
            for bb in range(bq * q, bq * (q + 1)):
                for tt in range(4):
                    if bb != bq * q or tt:
                        block = block + r.SM[bb, tt, 0:8]
            for i in range(8):
                at = q * Cw + 128 * (i % 2)
                r.VV[i // 2 : i // 2 + 1, at : at + 128] = block[i : i + 1]
        for bb in range(nb):
            r.VV[4:5, bb * rd : (bb + 1) * rd] = r.SM[bb, t, 8:9, :rd]

    def xhat_of(s, q):
        return (r.RES[q, s].astype(f32) - r.MU[s, :, :1]) * r.MU[s, :, 1:2]

    def feed(s):
        spread_wait(1, s, r.RES)
        parts = [r.RES[q, s].astype(f32) for q in range(4)]
        mu = sum(jnp.sum(x, axis=1, keepdims=True) for x in parts) * (1.0 / M)
        var = sum(jnp.sum((x - mu) * (x - mu), axis=1, keepdims=True) for x in parts) * (1.0 / M)
        inv = lax.rsqrt(var + norm_eps)
        lane = lax.broadcasted_iota(jnp.int32, (L, 128), 1)
        r.MU[s] = jnp.where(lane == 0, mu, inv)
        for q in range(4):
            c = slice(q * Cw, (q + 1) * Cw)
            rows = ((parts[q] - mu) * inv) * r.VV[0:1, c] + r.VV[1:2, c]
            r.NRM[s, :, :, c] = rows.astype(bf16).reshape(4 * nu, 16, Cw)
        fb = Fw // 4
        for j in range(4):
            c = slice(j * fb, (j + 1) * fb)
            pre = jnp.dot(r.NRM[s].reshape(L, M), r.WU[:, :, :, c].reshape(M, fb), preferred_element_type=f32) + r.VV[4:5, c]
            phi = 0.5 + 0.5 * lax.erf(pre * math.sqrt(0.5))
            r.ACT[s, :, c] = (pre * phi).astype(bf16)
            r.GP[s, :, c] = (phi + pre * (jnp.exp(-0.5 * pre * pre) * (1.0 / math.sqrt(2 * math.pi)))).astype(bf16)


    def turn(j):
        low = lax.rem(G - j, G)
        inner = jnp.where(z == 1, low, G - 1 - low)
        return jnp.where(z == 0, G - 1 - j, jnp.where(z == G - 1, j, inner))

    grads = [(r.GD, r.YD, r.ZD), (r.GU, r.YU, r.ZU), (r.GB, r.YB, r.ZB), (r.WU, r.YA, r.ZA)]

    def to_y(k, zz):
        g, yb, zb = grads[k]
        remote(g.at[2 * zz + (1 - y)], yb.at[zz], r.gys.at[k], r.gyr.at[k, zz], ypeer).start()

    def plus(into, *others):
        def add(i):
            acc = into[i].astype(f32)
            for o in others:
                acc = acc + o[i].astype(f32)
            into[i] = acc.astype(bf16)

        each(into.shape[0], add)

    def pass_on(i, at, zb, o, sem):
        @pl.when((o != mate) & ~ends)
        def _():
            slot = lax.rem(o, 2)
            got(zb.at[slot], r.gzr.at[sem, slot])
            plus(at, zb.at[slot])

        to = jnp.where(ends, mate, o)
        slot = jnp.where(o == mate, 2, jnp.where(ends, lax.rem(o, 2), 3))
        remote(at, zb.at[slot], r.gzs.at[sem], r.gzr.at[sem, jnp.minimum(slot, 2)], (2 * to + y, t)).start()

    def mid(k, *steps):
        g, yb, zb = grads[k]
        for i in steps or range(G - 1):
            o = turn(i)
            at = yb.at[o]
            got(at, r.gyr.at[k, o])
            plus(at, g.at[2 * o + y])
            pass_on(i, at, zb, o, k)

    def mid_c(*steps):
        for i in steps or range(G - 1):
            o = turn(i)
            for c, col in enumerate((1 - y, y)):
                pass_on(i, r.GC.at[2 * o + col], r.ZC.at[c], o, 4 + c)

    def arrived(zb, sem):
        got(zb.at[2:4], r.gzr.at[sem, 2])

    def summed(at, zb, more, store):
        def total(i):
            acc = at[i].astype(f32)
            for o in [zb.at[2], zb.at[3]] + more:
                acc = acc + o[i].astype(f32)
            store(i, acc)

        each(4, total)

    def fin(k, store):
        g, yb, zb = grads[k]
        at = yb.at[z]
        got(at, r.gyr.at[k, z])
        arrived(zb, k)
        summed(at, zb, [g.at[2 * z + y]], store)

    def cross_c():
        arrived(r.ZC.at[0], 4)
        other = r.GC.at[2 * z + 1 - y]

        def store(i, acc):
            other[i] = acc.astype(bf16)

        summed(other, r.ZC.at[0], [], store)
        remote(other, r.YC, r.gys.at[4], r.gyr.at[4, 0], ypeer).start()

    def fin_c(store):
        got(r.YC, r.gyr.at[4, 0])
        arrived(r.ZC.at[1], 5)
        summed(r.GC.at[2 * z + y], r.ZC.at[1], [r.YC], store)

    def reduced_sent():
        for k, (g, yb, zb) in enumerate(grads):
            got(g.at[0:G], r.gys.at[k])
            got(g.at[0:3], r.gzs.at[k])
        got(r.YC, r.gys.at[4])
        for sem in (4, 5):
            got(r.GC.at[0:3], r.gzs.at[sem])

    fb = Fw // 4

    def grad_down(i):
        j = turn(i)
        c = pl.ds(pl.multiple_of(j * fb, fb), fb)
        rows = r.ACT[:, :, c].reshape(S * L, fb)
        g = dot_tn(rows, r.COT[...].reshape(S * L, M)).astype(bf16)
        r.GD[pl.ds(j * bq, bq)] = g.reshape(bq, 4, rd // 4, M)
        to_y(0, j)


    def back_feed(s):
        cot = r.COT[s].reshape(L, M)
        for j in range(4):
            c = slice(j * fb, (j + 1) * fb)
            wd = r.WD[bq * j : bq * (j + 1)].reshape(fb, M)
            d_act = dot_nt(cot, wd).astype(bf16).astype(f32)
            d_pre = d_act * r.GP[s, :, c].astype(f32)
            total = jnp.sum(d_pre, axis=0, keepdims=True)
            for i in range(fb // 128):
                at = j * (fb // 128) + i
                r.SMG[at : at + 1] += total[:, 128 * i : 128 * (i + 1)]
            r.GP[s, :, c] = d_pre.astype(bf16)
        m1 = jnp.zeros((L, 1), f32)
        m2 = jnp.zeros((L, 1), f32)
        for q in range(4):
            c = slice(q * Cw, (q + 1) * Cw)
            dn = dot_nt(r.GP[s], r.WU[bq * q : bq * (q + 1)].reshape(Cw, Fw))
            g = dn * r.VV[0:1, c]
            m1 = m1 + jnp.sum(g, axis=1, keepdims=True)
            m2 = m2 + jnp.sum(g * xhat_of(s, q), axis=1, keepdims=True)
            r.DNP[q, s] = dn.astype(bf16)
        lane = lax.broadcasted_iota(jnp.int32, (L, 128), 1)
        both = jnp.where(lane == 0, m1, jnp.where(lane == 1, m2, 0.0)) * (1.0 / M)
        pick = (
            lax.broadcasted_iota(jnp.int32, (8, 128), 0) == lax.broadcasted_iota(jnp.int32, (8, 128), 1)
        ).astype(f32)
        r.ST[t, s] = lax.dot_general(
            pick, both, (((1,), (1,)), ((), ())), precision=lax.Precision.HIGHEST, preferred_element_type=f32
        )
        fold_send(2, s)
        ex_send(3, r.er.at[3, s, 0], lambda q: r.ST.at[t, s], lambda d: r.ST.at[t, s])
        fold_late(2, s)


    def grad_up(i):
        j = turn(i)
        c = pl.ds(pl.multiple_of(j * Cw, Cw), Cw)
        rows = r.NRM[:, :, :, c].reshape(S * L, Cw)
        g = dot_tn(rows, r.GP[...].reshape(S * L, Fw)).astype(bf16)
        r.GU[pl.ds(j * bq, bq)] = g.reshape(bq, 4, rw, Fw)
        to_y(1, j)


    def back_norm(s):
        dn = folded(2, s)
        got(r.ST.at[0:3, s], r.er.at[3, s, 0])
        st = r.ST[0, s] + r.ST[1, s] + r.ST[2, s] + r.ST[3, s]
        side = lax.broadcasted_iota(jnp.int32, (8, 128), 0)
        col_of = lambda i: lax.dot_general(
            st,
            (side == i).astype(f32),
            (((0,), (0,)), ((), ())),
            precision=lax.Precision.HIGHEST,
            preferred_element_type=f32,
        )[:, :1]
        m1, m2 = col_of(0), col_of(1)
        inv = r.MU[s, :, 1:2]
        xhat = (r.RES[t, s].astype(f32) - r.MU[s, :, :1]) * inv
        cot = r.COT[s, :, :, tc].reshape(L, Cw).astype(f32)
        for i, v in enumerate((cot, dn * xhat, dn)):
            total = jnp.sum(v, axis=0, keepdims=True)
            for k in range(Cw // 128):
                at = Fw // 128 + i * (Cw // 128) + k
                r.SMG[at : at + 1] += total[:, 128 * k : 128 * (k + 1)]
        d_resid = cot + (dn * r.VV[0:1, tc] - m1 - xhat * m2) * inv
        r.DR[s] = d_resid
        db = d_resid.astype(bf16)
        r.DB[s] = db
        for q in range(4):
            r.DMP[q, s] = dot_nt(db, wo(q)).astype(bf16)
        fold_send(4, s)
        fold_late(4, s)

    def grad_out():
        for q in range(4):
            g = dot_tn(r.MIX[q].reshape(S * L, Cw), r.DB[...].reshape(S * L, Cw))
            r.GA[bq * q : bq * (q + 1), :, :, 3 * Cw :] = g.astype(bf16).reshape(bq, 4, rw, Cw)

    def out_rows(s):
        for q in range(4):
            c = slice(q * Cw, (q + 1) * Cw)
            o = jnp.dot(r.ACT[s], r.WD[:, :, c].reshape(Fw, Cw), preferred_element_type=f32)
            mine = (t == q).astype(f32)
            o = o + mine * (r.RT[s] + r.VV[2:3, c])
            r.OP[s, :, :, c] = o.astype(bf16).reshape(4 * nu, 16, Cw)
        fold_send(5, s)
        fold_late(5, s)


    def windows(k):
        return r.CTX[:, 4 * nu + 4 * k : 4 * nu + 4 * (k + 1)].reshape(S * nw, M)

    def compress():
        conv = r.VV[3:4, tc]
        pooled = 0.0
        for k in range(3):
            wk = r.WC[:, :, :, k * Cw : (k + 1) * Cw].reshape(M, Cw)
            conv = conv + jnp.dot(windows(k), wk, preferred_element_type=f32)
            pooled = pooled + r.CTX[:, 4 * nu + 4 * k : 4 * nu + 4 * (k + 1), :, tc].reshape(S * nw, Cw).astype(f32)
        mask = r.MK[...].reshape(S * nw, 128)[:, :1]
        done = 3 * lax.broadcasted_iota(jnp.int32, (nw, 128), 0) + 3
        live = jnp.concatenate(
            [(done <= r.evicted[s]).astype(f32)[:, :1] for s in range(S)], axis=0
        ) * mask
        r.NEW[t] = (mask * conv).astype(bf16).reshape(S, nw, Cw)
        d_conv = live * (conv - pooled * (1.0 / 3.0))
        total = jnp.sum(d_conv, axis=0, keepdims=True)
        for k in range(Cw // 128):
            at = Fw // 128 + 3 * (Cw // 128) + k
            r.SMG[at : at + 1] = total[:, 128 * k : 128 * (k + 1)]
        r.DC[...] = d_conv.astype(bf16)
        for k in range(3):
            g = dot_tn(windows(k), r.DC[...])
            far, at = (r.GC, k) if k < ct else (r.GB, k - ct)
            far[:, :, :, at * Cw : (at + 1) * Cw] = g.astype(bf16).reshape(nb, 4, rw, Cw)

    slope_row = Fw // 128 + 4 * (Cw // 128)

    def back_attend(s):
        dm = folded(4, s).astype(bf16)
        lane = lax.broadcasted_iota(jnp.int32, (1, 128), 1)
        for h in range(ht):
            c = slice(h * hd, (h + 1) * hd)
            cv = slice(Cw + h * hd, Cw + (h + 1) * hd)
            p = r.PR[s, h]
            dp = dot_nt(dm[:, c], r.KV[s, :, cv])
            delta = jnp.sum(p * dp, axis=1, keepdims=True)
            ds = p * (dp - delta)
            part = jnp.sum(jnp.sum(ds * r.DIST[...], axis=0, keepdims=True), axis=1, keepdims=True)
            r.SMG[slope_row : slope_row + 1] -= jnp.where(lane == t * ht + h, part, 0.0)
            dr = (ds * scale).astype(bf16)
            dq = jnp.dot(dr, r.KV[s, :, c], preferred_element_type=f32).astype(bf16)
            dk = dot_tn(dr, r.Q[s, :, c]).astype(bf16)
            dv = dot_tn(p.astype(bf16), dm[:, c]).astype(bf16)
            r.Q[s, :, c] = dq
            r.KV[s, :, c] = dk
            r.KV[s, :, cv] = dv


    def grad_proj(i):
        j = turn(i)
        c = pl.ds(pl.multiple_of(j * Cw, Cw), Cw)
        gq = jnp.zeros((Cw, Cw), f32)
        gkv = jnp.zeros((Cw, 2 * Cw), f32)
        for s in range(S):
            gq = gq + dot_tn(r.CTX[s, 8 * nu : 12 * nu, :, c].reshape(L, Cw), r.Q[s])
            gkv = gkv + dot_tn(r.CTX[s, :, :, c].reshape(C3, Cw), r.KV[s])
        rows = pl.ds(j * bq, bq)
        r.GA[rows, :, :, :Cw] = gq.astype(bf16).reshape(bq, 4, rw, Cw)
        r.GA[rows, :, :, Cw : 3 * Cw] = gkv.astype(bf16).reshape(bq, 4, rw, 2 * Cw)
        for d in (1, 2, 3):
            remote(r.GA.at[rows, t ^ d], r.WU.at[rows, t], r.xs.at[0], r.xr.at[j], (b, t ^ d)).start()
        r.WU[rows, t] = r.GA[rows, t]

    def proj_y(*steps):
        for i in steps:
            j = turn(i)
            got(r.WU.at[pl.ds(j * bq, bq), 0:3], r.xr.at[j])
            to_y(3, j)

    def own_out(s):
        r.OR[1, s] = folded(5, s).astype(bf16)

    def input_rows(s):
        x = jnp.concatenate([r.Q[s], r.KV[s, 2 * L :]], axis=1)
        for q in range(4):
            c = slice(q * Cw, (q + 1) * Cw)
            w = r.WA[bq * q : bq * (q + 1), :, :, : 3 * Cw].reshape(Cw, 3 * Cw)
            o = dot_nt(x, w) + (t == q).astype(f32) * r.DR[s]
            r.NRM[s, :, :, c] = o.astype(bf16).reshape(4 * nu, 16, Cw)
        fold_send(6, s)
        fold_late(6, s)


    def keep(o):
        def store(i, acc):
            o[pl.ds(i * (rd // 4), rd // 4)] = acc

        return store

    def across(q, acc):
        for i in range(4):
            r.OA[i, :, wide(q * Cw, Cw)] = acc[:, i * Cw : (i + 1) * Cw]

    def hold(m):
        def store(i, acc):
            m[i] = acc.astype(bf16)

        return store

    def tier_back(k, m, tb):
        for d in (1, 2, 3):
            remote(m.at[t ^ d], tb.at[t], r.gts.at[k], r.gtr.at[k], (b, t ^ d)).start()
        left_all(tb.at[0:3], r.gts.at[k])

    def small_y():
        remote(r.SMG, r.YS, r.ss.at[0], r.sr.at[0], ypeer).start()
        left_all(r.SMG, r.ss.at[0])

    def small_z():
        got(r.YS, r.sr.at[0])
        r.ZS[z] = r.SMG[...] + r.YS[...]
        for d in range(1, G):
            remote(r.ZS.at[z], r.ZS.at[z], r.ss.at[1], r.sr.at[1], (2 * zs[d] + y, t)).start()
        left_all(r.ZS.at[0 : G - 1], r.ss.at[1])

    def small_tier():
        got(r.ZS.at[0 : G - 1], r.sr.at[1])
        acc = r.ZS[0]
        for zz in range(1, G):
            acc = acc + r.ZS[zz]
        r.os[t] = acc
        for d in (1, 2, 3):
            remote(r.os.at[t], r.os.at[t], r.gts.at[3], r.gtr.at[3], (b, t ^ d)).start()
        left_all(r.os.at[0:3], r.gts.at[3])

    def own_input(s):
        r.IG[s] = folded(6, s)

    mineU, mineC, mineA, mineB = (g.at[2 * z + y] for g in (r.GU, r.GC, r.GA, r.GB))
    def give(i, src, dst):
        pltpu.make_async_copy(src, dst, r.osem.at[i]).start()

    def rows_out(i, src, dst):
        for j in range(nu):
            give(i, src.at[:, j], dst.at[:, 16 * j : 16 * j + 16])

    backs = (
        (mineU, r.TU, r.OU, r.ou),
        (mineC, r.TC, r.OC.at[0:ct], r.oc.at[0:ct]),
        None,
        None,
        (mineB, r.TB, r.OC.at[ct:3], r.oc.at[ct:3]),
    )
    places_out = (0, 1, 2, None, 7)

    def lay(k, o, q, rows):
        if k == 0:
            for i in range(nb):
                o[:, wide((4 * i + q) * rd, rd)] = rows[:, i * rd : (i + 1) * rd].astype(f32)
        else:
            for i in range(o.shape[0]):
                o[i, :, wide(q * Cw, Cw)] = rows[:, i * Cw : (i + 1) * Cw].astype(f32)

    def tier_out(k):
        m, tb, o, far = backs[k]
        lay(k, o, t, m[t])
        got(tb.at[0:3], r.gtr.at[k])
        for d in (1, 2, 3):
            lay(k, o, t ^ d, tb[t ^ d])
        give(places_out[k], o, far)

    def given():
        for i, (src, dst) in ((0, (r.OU, r.ou)), (2, (r.OA, r.oa)), (3, (r.OD, r.od))):
            pltpu.make_async_copy(src, dst, r.osem.at[i]).wait()
        for i, (src, dst) in ((1, (r.OC.at[0:ct], r.oc.at[0:ct])), (7, (r.OC.at[ct:3], r.oc.at[ct:3]))):
            pltpu.make_async_copy(src, dst, r.osem.at[i]).wait()
        for i, (src, dst) in ((5, (r.OR.at[1], r.out)), (6, (r.IG, r.ig)), (4, (r.OR.at[0], r.om)), (8, (r.OR.at[2], r.ocm))):
            for j in range(nu):
                pltpu.make_async_copy(src.at[:, j], dst.at[:, 16 * j : 16 * j + 16], r.osem.at[i]).wait()

    def small_out():
        got(r.os.at[0:3], r.gtr.at[3])

    slots = L - nw
    windows_of = [(q, max(R * q - slots, 0), R - max(slots - R * q, 0)) for q in range(4) if slots < R * (q + 1)]

    def new_send():
        for q, at, n in windows_of:
            part = r.NEW.at[t, :, at : at + n]
            if_(t != q, remote(part, part, r.ns.at[0], r.ns.at[1], (b, q)).start)

    def new_sent():
        for q, at, n in windows_of:
            if_(t != q, lambda: got(r.NEW.at[0, :, at : at + n], r.ns.at[0]))

    def new_out():
        for q, at, n in windows_of:
            if_(t == q, lambda: got(r.NEW.at[0:3, :, at : at + n], r.ns.at[1]))

    def memories():
        side = lax.broadcasted_iota(jnp.int32, (16, 1), 0)
        for s in range(S):
            for i in range(nu):
                fresh = side + (R * t + 16 * i) < r.evicted[s]
                r.OR[0, s, i] = jnp.where(fresh, r.CTX[s, 8 * nu + nu * t + i], r.MEMV[s, 16 * i : 16 * i + 16])
                r.OR[2, s, i] = r.CTX[s, nu * t + i]
        for q, at, n in windows_of:

            @pl.when(t == q)
            def _(at=at, n=n):
                for i in range((R - n) // 16, nu):
                    w = at + 16 * i - (R - n)
                    for s in range(S):
                        written = 3 * (side + w) + 3 <= r.evicted[s]
                        for p in range(4):
                            c = slice(p * Cw, (p + 1) * Cw)
                            old = r.CTX[s, nu * t + i, :, c]
                            r.OR[2, s, i, :, c] = jnp.where(written, r.NEW[p, s, w : w + 16], old)

    def drain():
        for n in parts:
            if n != "U":
                all_sent(n)
        got(r.GA.at[:, 0:3], r.xs.at[0])
        for ref, sem in sends:
            got(ref, sem)
        act_sent()
        new_sent()
        reduced_sent()
        for e, ref in enumerate((r.MIX, r.RES, r.DNP, r.ST, r.DMP, r.OR, r.IR)):
            got(ref.at[0:3], r.es.at[e])
        given()

    here(r.wd, r.WD.at[b], 0)
    here(r.mem, r.MEMV, 6)
    for n in ("A", "C", "U"):
        tier_own(n)
    act_own()
    greet(G, True, True)
    tier_start("A")
    tier_start("C")
    small_start()
    tier_start("U")
    act_start(0, 1)
    got(r.MEMV, r.lsem.at[6])
    memory_rows()
    act_start(2, 3, 4, 5, 6)
    got(r.WD.at[b], r.lsem.at[0])
    own_z("D")
    own_y("D")
    tier_wait("A")
    own_z("A")
    own_y("A")
    tier_wait("C")
    own_y("C")
    tier_wait("S")
    own_z("S")
    own_y("S")
    table()
    onward("A", 1)
    onward("S", 1)
    onward("A", 2)
    onward("S", 2)
    tier_wait("U")
    own_z("U")
    onward("A", 3)
    own_y("U")
    onward("S", 3)
    y_wait("C")
    onward("U", 1)
    act_forward(0, 1, 2, 3, 4)
    act_wait(0)
    y_wait("A")
    each(S, project, {0: lambda: onward("U", 2), 1: lambda: onward("D", 1)})
    own_z("C")
    own_z("X")
    each(S, attend, {1: lambda: onward("U", 3)})
    spread_pass(0, 0, r.MIX)
    each(S, residual)
    onward("D", 2)
    y_wait("S")
    vectors()
    onward("C", 1)
    act_forward(5, 6)
    y_wait("U")
    spread_pass(1, 0, r.RES)
    each(S, feed, {1: lambda: onward("X", 1), 3: lambda: onward("D", 3)})
    act_wait(1)
    act_wait(2)
    each(4, grad_down, {1: lambda: onward("C", 2)})
    onward("X", 2)
    y_wait("D")
    each(S, back_feed, {0: lambda: onward("C", 3), 1: lambda: mid(0, 0), 2: lambda: onward("X", 3), 3: lambda: mid(0, 1)})
    fold_pass(2, S - 1)
    compress()
    mid_c(0)
    each(4, grad_up)
    each(G, lambda i: to_y(2, turn(i)))
    all_sent("U")
    each(S, back_norm, {2: lambda: mid(0, 2)})
    fold_pass(4, S - 1)
    mid_c(1)
    grad_out()
    each(S, back_attend, {1: lambda: mid_c(2), 2: lambda: mid(1, 0)})
    small_y()
    each(4, grad_proj, {1: lambda: mid(1, 1)})
    proj_y(0)
    mid(1, 2)
    each(S, out_rows)
    proj_y(1)
    fold_pass(5, S - 1)
    each(S, input_rows)
    proj_y(2)
    fold_pass(6, S - 1)
    cross_c()
    new_send()
    mid(2, 0)
    proj_y(3)
    fin(0, keep(r.OD))
    give(3, r.OD, r.od)
    mid(2, 1)
    mid(2, 2)
    fin(1, hold(mineU))
    tier_back(0, mineU, r.TU)
    mid(3, 0)
    small_z()
    each(S, own_out)
    rows_out(5, r.OR.at[1], r.out)
    mid(3, 1)
    fin(2, hold(mineB))
    tier_back(4, mineB, r.TB)
    small_tier()
    new_out()
    memories()
    rows_out(4, r.OR.at[0], r.om)
    rows_out(8, r.OR.at[2], r.ocm)
    mid(3, 2)
    fin_c(hold(mineC))
    tier_back(1, mineC, r.TC)
    each(S, own_input)
    rows_out(6, r.IG, r.ig)
    tier_out(0)
    tier_out(4)
    small_out()
    tier_out(1)
    fin(3, across)
    give(2, r.OA, r.oa)
    drain()

def whole_layer(nb, ht, hd, arrays):
    S, R, M = arrays["seg"].shape
    rw, rd, rs = arrays["w_query"].shape[0], arrays["wd"].shape[0], M // (4 * nb)
    nu = R // 16
    G, Cw, Fw, L = nb // 2, M // 4, nb * rd, 64 * nu
    dma = pltpu.SemaphoreType.DMA
    V = lambda shape, dtype=bf16: pltpu.VMEM(shape, dtype)
    ct = 1
    D4, A4, U4, C4 = (4, rd // 4, M), (4, rw, 4 * Cw), (4, rw, Fw), (4, rw, 3 * Cw)
    ins = arrays
    outs = dict(
        out=((S, R, M), bf16),
        ig=((S, R, M), f32),
        om=((S, R, M), bf16),
        ocm=((S, R, M), bf16),
        od=((rd, M), f32),
        ou=((rw, 4 * Fw), f32),
        oc=((3, rw, M), f32),
        oa=((4, rw, M), f32),
        os=((4, 24, 128), f32),
    )
    scratch = dict(
        WA=V((nb,) + A4),
        WU=V((nb,) + U4),
        WC=V((nb,) + C4),
        WD=V((nb, rd, M)),
        SM=V((nb, 4, 16, 128), f32),
        CTX=V((S, 12 * nu, 16, M)),
        COT=V((S, 4 * nu, 16, M)),
        MK=V((S, 4, L // 12, 128), f32),
        DIST=V((L, 3 * L), f32),
        VV=V((8, max(M, Fw)), f32),
        SMG=V((24, 128), f32),
        Q=V((S, L, Cw)),
        KV=V((S, 3 * L, 2 * Cw)),
        PR=V((S, ht, L, 3 * L), f32),
        MIX=V((4, S, L, Cw)),
        RT=V((S, L, Cw), f32),
        RES=V((4, S, L, Cw)),
        MU=V((S, L, 128), f32),
        NRM=V((S, 4 * nu, 16, M)),
        ACT=V((S, L, Fw)),
        GP=V((S, L, Fw)),
        DNP=V((4, S, L, Cw)),
        DNR=V((3, S, L, Cw)),
        ST=V((4, S, 8, L), f32),
        DR=V((S, L, Cw), f32),
        DB=V((S, L, Cw)),
        DMP=V((4, S, L, Cw)),
        DMR=V((3, S, L, Cw)),
        OP=V((S, 4 * nu, 16, M)),
        OR=V((3, S, nu, 16, M)),
        IR=V((3, S, nu, 16, M)),
        DC=V((S * L // 3, Cw)),
        GD=V((nb,) + D4),
        GU=V((nb,) + U4),
        GC=V((nb, 4, rw, ct * Cw)),
        GB=V((nb, 4, rw, (3 - ct) * Cw)),
        GA=V((nb,) + A4),
        YD=V((G,) + D4),
        YU=V((G,) + U4),
        YC=V((4, rw, ct * Cw)),
        YB=V((G, 4, rw, (3 - ct) * Cw)),
        YA=V((G,) + A4),
        ZD=V((4,) + D4),
        ZU=V((4,) + U4),
        ZC=V((2, 4, 4, rw, ct * Cw)),
        ZB=V((4, 4, rw, (3 - ct) * Cw)),
        ZA=V((4,) + A4),
        YS=V((24, 128), f32),
        ZS=V((G, 24, 128), f32),
        TU=V(U4),
        TC=V((4, rw, ct * Cw)),
        TB=V((4, rw, (3 - ct) * Cw)),
        NEW=V((4, S, L // 3, Cw)),
        IG=V((S, nu, 16, M), f32),
        OD=V((rd, M), f32),
        OU=V((rw, 4 * Fw), f32),
        OC=V((3, rw, M), f32),
        OA=V((4, rw, M), f32),
        MEMV=V((S, R, M)),
        osem=dma((9,)),
        lsem=dma((7,)),
        ts=dma((4,)),
        tr=dma((4,)),
        zs=dma((6,)),
        zr=dma((2, 9, G - 1)),
        ys=dma((6,)),
        yr=dma((6,)),
        acs=dma((3,)),
        acc=dma((3,)),
        acf=dma((3,)),
        acx=dma((7,)),
        es=dma((7,)),
        er=dma((7, S, 2)),
        ns=dma((2,)),
        gys=dma((5,)),
        gyr=dma((5, G)),
        gzs=dma((6,)),
        gzr=dma((6, 3)),
        ss=dma((2,)),
        sr=dma((2,)),
        xs=dma((1,)),
        xr=dma((G,)),
        gts=dma((5,)),
        gtr=dma((5,)),
    )
    names = list(ins) + list(outs) + list(scratch)
    near = dict(gain=VM, bias=VM, bdown=VM, bconv=VM, bup=VM, mask=VM, evicted=SM, slopes=SM)
    return pl.pallas_call(
        functools.partial(layer_kernel, names, (nb, nu, S, ht, hd, M, Cw, rw, rd, rs)),
        out_shape=[jax.ShapeDtypeStruct(s, d) for s, d in outs.values()],
        in_specs=[near.get(n, ANY) for n in ins],
        out_specs=[VM if n == "os" else ANY for n in outs],
        scratch_shapes=list(scratch.values()),
        compiler_params=pltpu.CompilerParams(
            collective_id=9, has_side_effects=True, vmem_limit_bytes=63 * 2**20
        ),
        name="whole_layer",
    )(*ins.values())


def finish_kernel(names, shape, *refs):
    r = Names(names, refs)
    nb, rs, rd, Fw, Cw, heads = shape
    b, t = lax.axis_index("batch"), lax.axis_index("tier")
    moves = [(r.out, r.o_out), (r.ig, r.o_ig), (r.od, r.o_od), (r.ou, r.o_ou), (r.oc, r.o_oc)]
    moves += [(r.oa.at[i], o) for i, o in enumerate((r.o_q, r.o_k, r.o_v, r.o_o))]
    moves += [(r.om, r.o_mem), (r.ocm, r.o_comp)]
    bufs = refs[len(names) :]
    into = [pltpu.make_async_copy(src, buf, r.sem.at[i]) for i, ((src, _), buf) in enumerate(zip(moves, bufs))]
    n = len(moves)
    onto = [pltpu.make_async_copy(buf, dst, r.sem.at[n + i]) for i, ((_, dst), buf) in enumerate(zip(moves, bufs))]
    for cp in into:
        cp.start()
    spot = 4 * b + t
    block, inner = spot // (Cw // rs), lax.rem(spot, Cw // rs)
    half, group = inner // (128 // rs), lax.rem(inner, 128 // rs)
    for i, o in enumerate((r.o_down, r.o_gain, r.o_bias, r.o_conv)):
        row = r.os[block, pl.ds(Fw // 128 + (Cw // 128) * i + half, 1), :]
        turned = pltpu.roll(jnp.broadcast_to(row, (8, 128)), lax.rem(128 - rs * group, 128), 1)
        o[...] = turned[0:1, :rs]
    r.o_up[...] = r.os[t, pl.ds(b, 1), :rd]
    at = Fw // 128 + 4 * (Cw // 128)
    total = r.os[0, at : at + 1]
    for q in range(1, 4):
        total = total + r.os[q, at : at + 1]
    r.o_slopes[...] = total[:, :heads]
    for cp, then in zip(into, onto):
        cp.wait()
        then.start()
    for cp in onto:
        cp.wait()


def finish(nb, heads, arrays):
    S, R, M = arrays["out"].shape
    rw, rd, rs = arrays["oa"].shape[1], arrays["od"].shape[0], M // (4 * nb)
    Cw, Fw = M // 4, nb * rd
    rows, mat, vec = (S, R, M), (rw, M), (1, rs)
    outs = dict(
        o_out=(rows, bf16, ANY),
        o_ig=(rows, f32, ANY),
        o_mem=(rows, bf16, ANY),
        o_comp=(rows, bf16, ANY),
        o_q=(mat, f32, ANY),
        o_k=(mat, f32, ANY),
        o_v=(mat, f32, ANY),
        o_o=(mat, f32, ANY),
        o_ou=((rw, 4 * Fw), f32, ANY),
        o_up=((1, rd), f32, VM),
        o_od=((rd, M), f32, ANY),
        o_down=(vec, f32, VM),
        o_gain=(vec, f32, VM),
        o_bias=(vec, f32, VM),
        o_oc=((3, rw, M), f32, ANY),
        o_conv=(vec, f32, VM),
        o_slopes=((1, heads), f32, VM),
    )
    moved = ("o_out", "o_ig", "o_od", "o_ou", "o_oc", "o_q", "o_k", "o_v", "o_o", "o_mem", "o_comp")
    return pl.pallas_call(
        functools.partial(
            finish_kernel, list(arrays) + list(outs) + ["sem"], (nb, rs, rd, Fw, Cw, heads)
        ),
        out_shape=[jax.ShapeDtypeStruct(s, d) for s, d, _ in outs.values()],
        in_specs=[VM if n == "os" else ANY for n in arrays],
        out_specs=[o[2] for o in outs.values()],
        scratch_shapes=[pltpu.SemaphoreType.DMA((2 * len(moved),))]
        + [pltpu.VMEM(outs[n][0], outs[n][1]) for n in moved],
        compiler_params=pltpu.CompilerParams(vmem_limit_bytes=63 * 2**20),
        name="finish",
    )(*arrays.values())


def per_device_fused(
    nb,
    segment,
    memory,
    compressed,
    evicted,
    window_mask,
    cotangent,
    w_query,
    w_key,
    w_value,
    w_output,
    w_up,
    b_up,
    w_down,
    b_down,
    ln_gain,
    ln_bias,
    w_conv,
    b_conv,
    slopes,
):
    S, R, M = segment.shape
    heads = slopes.shape[0]
    line = lambda v: v.reshape(1, -1)
    names = ("out", "ig", "om", "ocm", "od", "ou", "oc", "oa", "os")
    made = whole_layer(
        nb,
        heads // 4,
        M // heads,
        dict(
            w_query=w_query,
            w_key=w_key,
            w_value=w_value,
            w_output=w_output,
            w_up=w_up,
            w_conv=w_conv,
            wd=w_down,
            comp=compressed,
            seg=segment,
            cot=cotangent,
            mem=memory,
            gain=line(ln_gain),
            bias=line(ln_bias),
            bdown=line(b_down),
            bconv=line(b_conv),
            bup=line(b_up),
            mask=window_mask,
            evicted=evicted,
            slopes=slopes,
        ),
    )
    outs = finish(nb, heads, dict(zip(names, made)))
    flat = (9, 11, 12, 13, 15, 16)
    return tuple(o.reshape(-1) if i in flat else o for i, o in enumerate(outs))


def solution(mesh):
    both = ("batch", "tier")
    rows = P("batch", "tier", None)
    mat, vec = P(both, None), P(both)
    nb = mesh.shape["batch"]

    def body(*args):
        fused = args[6].shape[0] % 16 == 0 and args[12].shape[0] == 128
        return (per_device_fused if fused else per_device)(nb, *args)

    return jax.shard_map(
        body,
        mesh=mesh,
        in_specs=(
            (rows, rows, rows, P("batch"), P("batch", "tier"), rows)
            + (mat, mat, mat, mat, mat, vec, mat, vec, vec, vec)
            + (P(None, both, None), vec, P())
        ),
        out_specs=(
            (rows, rows, rows, rows, mat, mat, mat, mat, mat, vec, mat, vec, vec, vec)
            + (P(None, both, None), vec, P())
        ),
        check_vma=False,
    )
```

```python
import functools
import math

import jax
import jax.numpy as jnp
from jax import lax
from jax.experimental import pallas as pl
from jax.experimental.pallas import tpu as pltpu
from jax.sharding import PartitionSpec as P

norm_eps = 1e-05
MESH = pl.DeviceIdType.MESH
ANY = pl.BlockSpec(memory_space=pl.ANY)
VM = pl.BlockSpec(memory_space=pltpu.VMEM)
SM = pl.BlockSpec(memory_space=pltpu.SMEM)
f32 = jnp.float32
bf16 = jnp.bfloat16


def remote(src, dst, send, recv, device):
    return pltpu.make_async_remote_copy(
        src_ref=src,
        dst_ref=dst,
        send_sem=send,
        recv_sem=recv,
        device_id=device,
        device_id_type=MESH,
    )


def places(groups):
    b, t = lax.axis_index("batch"), lax.axis_index("tier")
    z, y = b // 2, lax.rem(b, 2)
    zs = [lax.rem(z + d, groups) for d in range(groups)]
    zback = [lax.rem(z + groups - d, groups) for d in range(groups)]
    return b, t, z, y, zs, zback


def greet(groups, tiers, columns):
    b, t, z, y, zs, _ = places(groups)
    barrier = pltpu.get_barrier_semaphore()
    peers = []
    if tiers:
        peers += [(b, t ^ d) for d in (1, 2, 3)]
    if columns:
        peers += [(2 * zz + y, t) for zz in zs[1:]] + [(b ^ 1, t)]
    for peer in peers:
        pl.semaphore_signal(barrier, inc=1, device_id=peer, device_id_type=MESH)
    pl.semaphore_wait(barrier, len(peers))


def gather_kernel(groups, nu, *refs):
    (wa, wu, wc, wd, sm, comp, mem, seg, cot, mk) = refs[:10]
    (WA, WU, WC, WD, SM, CTX, COT, MK) = refs[10:18]
    lsem, ts, tr, zsd, zr, ys, yr, acs, acr = refs[18:]
    G = groups
    b, t, z, y, zs, zback = places(G)
    greet(G, True, True)
    ypeer = (b ^ 1, t)
    local, sends = [], []

    def here(src, dst, i):
        cp = pltpu.make_async_copy(src, dst, lsem.at[i])
        cp.start()
        return cp

    kinds = [(sm, SM), (wa, WA), (wu, WU), (wc, WC)]
    own = []
    for k, (src, dst) in enumerate(kinds):
        mine = src if k == 0 else src.at[t]
        own.append(here(mine, dst.at[b, t], k))
        for d in (1, 2, 3):
            piece = src if k == 0 else src.at[t ^ d]
            cp = remote(piece, dst.at[b, t], ts.at[k, d - 1], tr.at[k, d - 1], (b, t ^ d))
            cp.start()
            sends.append(cp)
    own.append(here(wd, WD.at[b], 4))
    pieces = [
        (comp, lambda q: CTX.at[:, pl.ds(nu * q, nu)]),
        (mem.at[:, 0], lambda q: CTX.at[:, 4 * nu + q]),
        (mem.at[:, 1], lambda q: CTX.at[:, 4 * nu + 4 + q]),
        (mem.at[:, 2], lambda q: CTX.at[:, 4 * nu + 8 + q]),
        (seg, lambda q: CTX.at[:, pl.ds(8 * nu + nu * q, nu)]),
        (mk, lambda q: MK.at[:, q]),
        (cot, lambda q: COT.at[:, pl.ds(nu * q, nu)]),
    ]
    for i, (src, at) in enumerate(pieces):
        own.append(here(src, at(t), 5 + i))
        for j, d in enumerate((1, 2)):
            cp = remote(src, at(t), acs.at[i, j], acr.at[i, j], (b, t ^ d))
            cp.start()
            sends.append(cp)
    table = [SM, WA, WU, WD, WC]
    local_of = [0, 1, 2, 4, 3]
    for k, dst in enumerate(table):
        own[local_of[k]].wait()
        if k != 3:
            kk = local_of[k]
            for d in (1, 2, 3):
                remote(dst.at[b, t], dst.at[b, t ^ d], ts.at[kk, d - 1], tr.at[kk, d - 1], (b, t ^ d)).wait_recv()
        for d in range(1, G):
            cp = remote(dst.at[b], dst.at[b], zsd.at[k, d], zr.at[k, d], (2 * zs[d] + y, t))
            cp.start()
            sends.append(cp)
        cp = remote(dst.at[b], dst.at[b], ys.at[k, 0], yr.at[k, 0], ypeer)
        cp.start()
        sends.append(cp)
    for i, (src, at) in enumerate(pieces):
        remote(at(t ^ 2), at(t ^ 2), acs.at[i, 1], acr.at[i, 1], (b, t ^ 2)).wait_recv()
        cp = remote(at(t ^ 2), at(t ^ 2), acs.at[i, 2], acr.at[i, 2], (b, t ^ 1))
        cp.start()
        sends.append(cp)
    for k, dst in enumerate(table):
        for d in range(1, G):
            at = dst.at[2 * zback[d] + y]
            remote(at, at, zsd.at[k, d], zr.at[k, d], ypeer).wait_recv()
            cp = remote(at, at, ys.at[k, d], yr.at[k, d], ypeer)
            cp.start()
            sends.append(cp)
    for k, dst in enumerate(table):
        for d in range(G):
            at = dst.at[2 * zback[d] + (1 - y)]
            remote(at, at, ys.at[k, d], yr.at[k, d], ypeer).wait_recv()
    for i, (src, at) in enumerate(pieces):
        for j, q in ((0, t ^ 1), (2, t ^ 3)):
            remote(at(q), at(q), acs.at[i, j], acr.at[i, j], (b, t ^ 1)).wait_recv()
    for i in range(len(pieces)):
        own[5 + i].wait()
    for cp in sends:
        cp.wait_send()


def gather_all(nb, nu, wa, wu, wc, wd, sm, comp, mem, seg, cot, mk):
    G = nb // 2
    S, _, U, M = comp.shape
    out = [
        jax.ShapeDtypeStruct((nb,) + wa.shape, bf16),
        jax.ShapeDtypeStruct((nb,) + wu.shape, bf16),
        jax.ShapeDtypeStruct((nb,) + wc.shape, bf16),
        jax.ShapeDtypeStruct((nb,) + wd.shape, bf16),
        jax.ShapeDtypeStruct((nb, 4) + sm.shape, f32),
        jax.ShapeDtypeStruct((S, 12 * nu, U, M), bf16),
        jax.ShapeDtypeStruct((S, 4 * nu, U, M), bf16),
        jax.ShapeDtypeStruct((S, 4) + mk.shape[1:], f32),
    ]
    dma = pltpu.SemaphoreType.DMA
    return pl.pallas_call(
        functools.partial(gather_kernel, G, nu),
        out_shape=out,
        in_specs=[ANY] * 10,
        out_specs=[ANY] * 8,
        scratch_shapes=[
            dma((12,)),
            dma((4, 3)),
            dma((4, 3)),
            dma((5, G)),
            dma((5, G)),
            dma((5, G)),
            dma((5, G)),
            dma((7, 3)),
            dma((7, 3)),
        ],
        compiler_params=pltpu.CompilerParams(collective_id=0, has_side_effects=True),
        name="gather_all",
    )(wa, wu, wc, wd, sm, comp, mem, seg, cot, mk)


def spread_kernel(same, x, o, lsem, ss, rs):
    b, t = lax.axis_index("batch"), lax.axis_index("tier")
    greet(1, True, False)
    cps = []
    for d in (1, 2, 3):
        cp = remote(x if same else x.at[t ^ d], o.at[t], ss.at[d - 1], rs.at[d - 1], (b, t ^ d))
        cp.start()
        cps.append(cp)
    mine = pltpu.make_async_copy(x if same else x.at[t], o.at[t], lsem)
    mine.start()
    mine.wait()
    for d in (1, 2, 3):
        remote(o.at[t ^ d], o.at[t ^ d], ss.at[d - 1], rs.at[d - 1], (b, t ^ d)).wait_recv()
    for cp in cps:
        cp.wait_send()


def spread(x, same, cid):
    dma = pltpu.SemaphoreType.DMA
    shape = ((4,) + x.shape) if same else x.shape
    return pl.pallas_call(
        functools.partial(spread_kernel, same),
        out_shape=jax.ShapeDtypeStruct(shape, x.dtype),
        in_specs=[ANY],
        out_specs=ANY,
        scratch_shapes=[dma, dma((3,)), dma((3,))],
        compiler_params=pltpu.CompilerParams(collective_id=cid, has_side_effects=True),
        name="spread_%d" % cid,
    )(x)


def reduce_kernel(groups, *refs):
    GD, GU, GC, GA, SMG = refs[:5]
    OD, OU, OC, OA, OS = refs[5:10]
    YD, YU, YC, YA, YS, ZD, ZU, ZC, ZA, ZS, TU, TC, TA, MU, MC, MA, ys, yr, zsd, zr, ts, tr = refs[10:]
    G = groups
    b, t, z, y, zs, zback = places(G)
    greet(G, True, True)
    ypeer = (b ^ 1, t)
    sends = []
    kinds = [
        (GD, YD, ZD, OD, None, None),
        (GU, YU, ZU, OU, MU, TU),
        (GC, YC, ZC, OC, MC, TC),
        (GA, YA, ZA, OA, MA, TA),
    ]
    for k, (g, yb, *_) in enumerate(kinds):
        for d in range(G):
            zz = zs[(d + 1) % G]
            cp = remote(g.at[2 * zz + (1 - y)], yb.at[zz], ys.at[k, d], yr.at[k, d], ypeer)
            cp.start()
            sends.append(cp)
    cp = remote(SMG, YS, ys.at[4, 0], yr.at[4, 0], ypeer)
    cp.start()
    sends.append(cp)
    for k, (g, yb, zb, o, m, tb) in enumerate(kinds):
        for d in range(G):
            zz = zs[(d + 1) % G]
            at = yb.at[zz]
            remote(at, at, ys.at[k, d], yr.at[k, d], ypeer).wait_recv()

            def add(i, c, yb=yb, zz=zz, g=g):
                yb[zz, i] = (yb[zz, i].astype(f32) + g[2 * zz + y, i].astype(f32)).astype(bf16)
                return c

            lax.fori_loop(0, yb.shape[1], add, 0)
            if d < G - 1:
                cp = remote(at, zb.at[d], zsd.at[k, d], zr.at[k, d], (2 * zz + y, t))
                cp.start()
                sends.append(cp)
    remote(YS, YS, ys.at[4, 0], yr.at[4, 0], ypeer).wait_recv()
    ZS[z] = SMG[...] + YS[...]
    for d in range(G - 1):
        cp = remote(ZS.at[z], ZS.at[z], zsd.at[4, d], zr.at[4, d], (2 * zs[d + 1] + y, t))
        cp.start()
        sends.append(cp)
    for k, (g, yb, zb, o, m, tb) in enumerate(kinds):
        for d in range(G - 1):
            remote(zb.at[d], zb.at[d], zsd.at[k, d], zr.at[k, d], ypeer).wait_recv()

        def total(i, c, k=k, yb=yb, zb=zb, o=o, m=m):
            acc = yb[z, i].astype(f32)
            for d in range(G - 1):
                acc = acc + zb[d, i].astype(f32)
            if k == 0:
                o[i] = acc
            else:
                m[i] = acc.astype(bf16)
            return c

        lax.fori_loop(0, o.shape[0], total, 0)
        if k:
            for d in (1, 2, 3):
                cp = remote(m.at[t ^ d], tb.at[t], ts.at[k - 1, d - 1], tr.at[k - 1, d - 1], (b, t ^ d))
                cp.start()
                sends.append(cp)
    for d in range(G - 1):
        at = ZS.at[zback[d + 1]]
        remote(at, at, zsd.at[4, d], zr.at[4, d], ypeer).wait_recv()
    acc = ZS[0]
    for zz in range(1, G):
        acc = acc + ZS[zz]
    OS[t] = acc
    for d in (1, 2, 3):
        cp = remote(OS.at[t], OS.at[t], ts.at[3, d - 1], tr.at[3, d - 1], (b, t ^ d))
        cp.start()
        sends.append(cp)
    for k, (g, yb, zb, o, m, tb) in enumerate(kinds):
        if k:
            o[t] = m[t].astype(f32)
            for d in (1, 2, 3):
                at = tb.at[t ^ d]
                remote(at, at, ts.at[k - 1, d - 1], tr.at[k - 1, d - 1], (b, t ^ d)).wait_recv()
                o[t ^ d] = tb[t ^ d].astype(f32)
    for d in (1, 2, 3):
        at = OS.at[t ^ d]
        remote(at, at, ts.at[3, d - 1], tr.at[3, d - 1], (b, t ^ d)).wait_recv()
    for cp in sends:
        cp.wait_send()


def reduce_all(nb, gd, gu, gc, ga, sg):
    G = nb // 2
    dma = pltpu.SemaphoreType.DMA
    shapes = [x.shape[1:] for x in (gd, gu, gc, ga)]
    return pl.pallas_call(
        functools.partial(reduce_kernel, G),
        out_shape=[jax.ShapeDtypeStruct(s, f32) for s in shapes]
        + [jax.ShapeDtypeStruct((4,) + sg.shape, f32)],
        in_specs=[VM] * 5,
        out_specs=[VM] * 5,
        scratch_shapes=[pltpu.VMEM((G,) + s, bf16) for s in shapes]
        + [pltpu.VMEM(sg.shape, f32)]
        + [pltpu.VMEM((G - 1,) + s, bf16) for s in shapes]
        + [pltpu.VMEM((G,) + sg.shape, f32)]
        + [pltpu.VMEM(s, bf16) for s in shapes[1:]]
        + [pltpu.VMEM(s, bf16) for s in shapes[1:]]
        + [dma((5, G)), dma((5, G)), dma((5, G)), dma((5, G)), dma((4, 3)), dma((4, 3))],
        compiler_params=pltpu.CompilerParams(
            collective_id=1, has_side_effects=True, vmem_limit_bytes=48 * 2**20
        ),
        name="reduce_all",
    )(gd, gu, gc, ga, sg)


def dot(a, b):
    return jnp.dot(a, b, preferred_element_type=f32)


def dot_tn(a, b):
    return lax.dot_general(a, b, (((0,), (0,)), ((), ())), preferred_element_type=f32)


def dot_nt(a, b):
    return lax.dot_general(a, b, (((1,), (1,)), ((), ())), preferred_element_type=f32)


def per_device(
    nb,
    segment,
    memory,
    compressed,
    evicted,
    window_mask,
    cotangent,
    w_query,
    w_key,
    w_value,
    w_output,
    w_up,
    b_up,
    w_down,
    b_down,
    ln_gain,
    ln_bias,
    w_conv,
    b_conv,
    slopes,
):
    S, R, M = segment.shape
    heads = slopes.shape[0]
    hd = M // heads
    nt = 4
    rw, rd, rs = w_query.shape[0], w_down.shape[0], b_down.shape[0]
    b, t = lax.axis_index("batch"), lax.axis_index("tier")
    Cw, Fw = M // nt, nb * rd
    nu, W = R // 16, R // 3
    seg_len = nt * R
    T = S * seg_len
    ht = heads // nt
    index = 4 * b + t

    wa = jnp.stack([w_query, w_key, w_value, w_output]).reshape(4, rw, nt, Cw)
    wa = wa.transpose(2, 1, 0, 3).reshape(nt, rw, 4 * Cw)
    wu = w_up.reshape(rw, nb, nt, rd).transpose(2, 0, 1, 3).reshape(nt, rw, Fw)
    wc = w_conv.reshape(3, rw, nt, Cw).transpose(2, 1, 0, 3).reshape(nt, rw, 3 * Cw)
    row0 = jnp.concatenate([ln_gain, ln_bias, b_down, b_conv])
    sm = jnp.zeros((8, 128), f32).at[0, : 4 * rs].set(row0.astype(f32)).at[1, :rd].set(b_up.astype(f32))
    mem = memory.reshape(S, W, 3, M).transpose(0, 2, 1, 3)
    mk = jnp.broadcast_to(window_mask.astype(f32)[:, :, None], (S, W, 128))
    WA, WU, WC, WD, SM, CTX, COT, MK = gather_all(
        nb,
        nu,
        wa,
        wu,
        wc,
        w_down,
        sm,
        compressed.reshape(S, nu, 16, M),
        mem,
        segment.reshape(S, nu, 16, M),
        cotangent.reshape(S, nu, 16, M),
        mk,
    )
    WA = WA.reshape(M, 4 * Cw)
    Wqkv, Wo = WA[:, : 3 * Cw], WA[:, 3 * Cw :]
    WU, WC, WD = WU.reshape(M, Fw), WC.reshape(M, 3 * Cw), WD.reshape(Fw, M)
    gain, bias, bdown, bconv = [SM[:, :, 0, i * rs : (i + 1) * rs].reshape(M) for i in range(4)]
    bup = lax.dynamic_index_in_dim(SM, t, 1, False)[:, 1, :rd].reshape(Fw)
    cols = lambda v: lax.dynamic_slice_in_dim(v, t * Cw, Cw, v.ndim - 1)
    ctx = CTX.reshape(S, 3 * seg_len, M)
    cot = COT.reshape(T, M)
    seg = ctx[:, 2 * seg_len :].reshape(T, M)

    kpos = jnp.concatenate(
        [
            jnp.arange(seg_len),
            seg_len + (3 * jnp.arange(seg_len // 3)[None, :] + jnp.arange(3)[:, None]).reshape(-1),
            2 * seg_len + jnp.arange(seg_len),
        ]
    )
    qpos = 2 * seg_len + jnp.arange(seg_len)
    allowed = kpos[None, :] <= qpos[:, None]
    dist = (qpos[:, None] - kpos[None, :]).astype(f32) * (1.0 / (3 * seg_len))
    slope = lax.dynamic_slice_in_dim(slopes, t * ht, ht)
    scale = 1.0 / math.sqrt(hd)
    q = dot(seg, Wqkv[:, :Cw]).astype(bf16).reshape(S, seg_len, ht, hd)
    kv = dot(ctx.reshape(-1, M), Wqkv[:, Cw:]).astype(bf16).reshape(S, 3 * seg_len, 2, ht, hd)
    kk, vv = kv[:, :, 0], kv[:, :, 1]
    raw = jnp.einsum("sqhd,skhd->shqk", q, kk, preferred_element_type=f32)
    scores = jnp.where(allowed, raw * scale - slope[:, None, None] * dist, -1e30)
    high = jnp.max(scores, axis=-1, keepdims=True)
    e = jnp.exp(scores - high)
    probs = e / jnp.sum(e, axis=-1, keepdims=True)
    probs_low = probs.astype(bf16)
    mixed_t = jnp.einsum("shqk,skhd->sqhd", probs_low, vv, preferred_element_type=f32).astype(bf16)
    MIX = spread(mixed_t.reshape(T, Cw), True, 2)
    mixed = MIX.transpose(1, 0, 2).reshape(T, M)
    resid_t = cols(seg).astype(f32) + dot(mixed, Wo)
    RES = spread(resid_t.astype(bf16), True, 3)
    resid = RES.transpose(1, 0, 2).reshape(T, M).astype(f32)
    center = resid - jnp.mean(resid, axis=-1, keepdims=True)
    spread_ = lax.rsqrt(jnp.mean(center * center, axis=-1, keepdims=True) + norm_eps)
    xhat = center * spread_
    normed = (xhat * gain + bias).astype(bf16)
    pre = dot(normed, WU) + bup
    phi = 0.5 * (1.0 + lax.erf(pre * math.sqrt(0.5)))
    act = (pre * phi).astype(bf16)
    slope_act = phi + pre * jnp.exp(-0.5 * pre * pre) * (1.0 / math.sqrt(2 * math.pi))
    place = lambda v: lax.dynamic_update_slice_in_dim(jnp.zeros((T, M), f32), v, t * Cw, 1)
    out_part = dot(act, WD) + place(resid_t + cols(bdown))
    rows = lambda v: v.astype(bf16).reshape(S, nt, R, M).transpose(1, 0, 2, 3)
    output = jnp.sum(spread(rows(out_part), False, 4).astype(f32), axis=0).astype(bf16)
    gdown = dot_tn(act, cot)
    d_act = dot_nt(cot, WD).astype(bf16)
    d_pre = d_act.astype(f32) * slope_act
    gub = jnp.sum(d_pre, axis=0)
    d_pre_low = d_pre.astype(bf16)
    gup = dot_tn(normed, d_pre_low)
    dn_part = dot_nt(d_pre_low, WU)
    stats = jnp.stack([jnp.mean(dn_part * gain, axis=1), jnp.mean(dn_part * gain * xhat, axis=1)])
    stats = lax.psum(stats, "tier")
    cols_of = lambda v: v.astype(bf16).reshape(T, nt, Cw).transpose(1, 0, 2)
    dn = jnp.sum(spread(cols_of(dn_part), False, 5).astype(f32), axis=0)
    xhat_t = cols(xhat)
    ggain, gbias = jnp.sum(dn * xhat_t, axis=0), jnp.sum(dn, axis=0)
    g = dn * cols(gain)
    cot_t = cols(cot).astype(f32)
    gdb = jnp.sum(cot_t, axis=0)
    d_resid = cot_t + (g - stats[0][:, None] - xhat_t * stats[1][:, None]) * spread_
    d_branch = d_resid.astype(bf16)
    gout = dot_tn(mixed, d_branch)
    dm_part = dot_nt(d_branch, Wo)
    dm = jnp.sum(spread(cols_of(dm_part), False, 6).astype(f32), axis=0).astype(bf16)
    dm = dm.reshape(S, seg_len, ht, hd)
    d_probs = jnp.einsum("sqhd,skhd->shqk", dm, vv, preferred_element_type=f32)
    delta = jnp.sum(probs * d_probs, axis=-1, keepdims=True)
    d_scores = probs * (d_probs - delta)
    gslope = -jnp.sum(d_scores * dist, axis=(0, 2, 3))
    d_raw = (d_scores * scale).astype(bf16)
    dq = jnp.einsum("shqk,skhd->sqhd", d_raw, kk, preferred_element_type=f32).astype(bf16)
    dk = jnp.einsum("shqk,sqhd->skhd", d_raw, q, preferred_element_type=f32).astype(bf16)
    dv = jnp.einsum("shqk,sqhd->skhd", probs_low, dm, preferred_element_type=f32).astype(bf16)
    dq, dk, dv = dq.reshape(T, Cw), dk.reshape(S, -1, Cw), dv.reshape(S, -1, Cw)
    flat = ctx.reshape(-1, M)
    gq = dot_tn(seg, dq)
    gk, gv = dot_tn(flat, dk.reshape(-1, Cw)), dot_tn(flat, dv.reshape(-1, Cw))
    own = lambda v: v[:, 2 * seg_len :].reshape(T, Cw)
    ig_part = dot_nt(jnp.concatenate([dq, own(dk), own(dv)], axis=1), Wqkv) + place(d_resid)
    input_grad = jnp.sum(spread(rows(ig_part), False, 7).astype(f32), axis=0)

    nw = seg_len // 3
    win = ctx[:, seg_len : 2 * seg_len].reshape(S, 3, nw, M)
    win = [win[:, k].reshape(S * nw, M) for k in range(3)]
    conv = sum(dot(win[k], WC[:, k * Cw : (k + 1) * Cw]) for k in range(3)) + cols(bconv)
    pooled = sum(cols(win[k]).astype(f32) for k in range(3)) * (1.0 / 3.0)
    mask = MK.reshape(S, nw, 128)[:, :, :1]
    old = (3 * jnp.arange(nw) + 3)[None, :, None] <= evicted[:, None, None]
    live = jnp.where(old, mask, 0.0).reshape(-1, 1)
    d_conv = live * (conv - pooled)
    gcb = jnp.sum(d_conv, axis=0)
    d_low = d_conv.astype(bf16)
    gconv = jnp.concatenate([dot_tn(win[k], d_low) for k in range(3)], axis=1)
    new_t = (mask.reshape(-1, 1) * conv).astype(bf16)
    NEW = spread(new_t, True, 8).reshape(nt, S, nw, Cw).transpose(1, 2, 0, 3).reshape(S, nw, M)
    slot_offset = seg_len - nw
    local_rows = jnp.arange(R, dtype=jnp.int32) + t * R
    padded = jnp.concatenate([jnp.zeros((S, slot_offset, M), bf16), NEW], axis=1)
    slot_rows = lax.dynamic_slice_in_dim(padded, t * R, R, 1)
    written = (local_rows[None, :] >= slot_offset) & (
        3 * (local_rows[None, :] - slot_offset) + 3 <= evicted[:, None]
    )
    new_compressed = jnp.where(written[..., None], slot_rows, compressed)
    new_memory = jnp.where((local_rows[None, :] < evicted[:, None])[..., None], segment, memory)

    low = lambda v, *s: v.astype(bf16).reshape(s)
    gs = lax.dynamic_update_slice_in_dim(jnp.zeros((128,), f32), gslope, t * ht, 0)
    sg = jnp.concatenate([gub, gdb, ggain, gbias, gcb, gs])
    sg = jnp.concatenate([sg, jnp.zeros((24 * 128 - sg.shape[0],), f32)]).reshape(24, 128)
    OD, OU, OC, OA, OS = reduce_all(
        nb,
        low(gdown, nb, 4, rd // 4, M),
        low(gup, nb, 4, rw, Fw),
        low(gconv, nb, 4, rw, 3 * Cw),
        low(jnp.concatenate([gq, gk, gv, gout], axis=1), nb, 4, rw, 4 * Cw),
        sg,
    )
    OA = OA.reshape(nt, rw, 4, Cw).transpose(2, 1, 0, 3).reshape(4, rw, M)
    OU = OU.reshape(nt, rw, nb, rd).transpose(1, 2, 0, 3).reshape(rw, nb * nt * rd)
    OC = OC.reshape(nt, rw, 3, Cw).transpose(2, 1, 0, 3).reshape(3, rw, M)
    OS = OS.reshape(nt, -1)
    vec = lambda o: lax.dynamic_slice_in_dim(OS[:, o : o + Cw].reshape(M), index * rs, rs)
    gub_out = lax.dynamic_slice(OS, (t, b * rd), (1, rd)).reshape(rd)
    gslopes = jnp.sum(OS[:, Fw + 4 * Cw : Fw + 4 * Cw + heads], axis=0)
    return (
        output,
        input_grad,
        new_memory,
        new_compressed,
        OA[0],
        OA[1],
        OA[2],
        OA[3],
        OU,
        gub_out,
        OD.reshape(rd, M),
        vec(Fw),
        vec(Fw + Cw),
        vec(Fw + 2 * Cw),
        OC,
        vec(Fw + 3 * Cw),
        gslopes,
    )


class Names:
    def __init__(self, names, refs):
        for name, ref in zip(names, refs):
            setattr(self, name, ref)


def layer_kernel(names, shape, *refs):
    r = Names(names, refs)
    nb, nu, S, ht, hd, M, Cw, rw, rd, rs = shape
    R = 16 * nu
    ct = r.OC.shape[0] - r.GB.shape[-1] // Cw
    G, bq = nb // 2, nb // 4
    L = 16 * 4 * nu
    C3 = 3 * L
    nw = L // 3
    Fw = nb * rd
    scale = 1.0 / math.sqrt(hd)
    b, t, z, y, zs, zback = places(G)
    mate, ends = z ^ 1, (z == 0) | (z == G - 1)
    ypeer = (b ^ 1, t)
    tc = pl.ds(pl.multiple_of(t * Cw, Cw), Cw)
    sends = []

    def got(ref, sem):
        pltpu.make_async_copy(ref, ref, sem).wait()

    def left_all(ref, sem):
        sends.append((ref, sem))

    def each(n, body, between=None):
        def step(i, c):
            body(i)
            for at, then in (between or {}).items():
                pl.when(i == at)(then)
            return c

        lax.fori_loop(0, n, step, 0)

    def ex_send(e, sem, src, dst):
        for d in (1, 2, 3):
            remote(src(t ^ d), dst(d), r.es.at[e], sem, (b, t ^ d)).start()

    def spread_send(e, s, arr):
        at = arr.at[t, s]
        for d in (1, 2):
            remote(at, at, r.es.at[e], r.er.at[e, s, d - 1], (b, t ^ d)).start()

    def spread_pass(e, s, arr):
        at = arr.at[t ^ 2, s]
        got(at, r.er.at[e, s, 1])
        remote(at, at, r.es.at[e], r.er.at[e, s, 0], (b, t ^ 1)).start()

    def spread_wait(e, s, arr):
        @pl.when(s < S - 1)
        def _():
            spread_pass(e, s + 1, arr)

        got(arr.at[0:2, s], r.er.at[e, s, 0])

    folds = {
        2: (lambda q, s: r.DNP.at[q, s], r.DNR),
        4: (lambda q, s: r.DMP.at[q, s], r.DMR),
        5: (lambda q, s: r.OP.at[s, pl.ds(nu * q, nu)], r.OR),
        6: (lambda q, s: r.NRM.at[s, pl.ds(nu * q, nu)], r.IR),
    }

    def fold_send(e, s):
        out, into = folds[e]
        for i, d in enumerate((1, 3)):
            remote(out(t ^ d, s), into.at[i, s], r.es.at[e], r.er.at[e, s, i], (b, t ^ 1)).start()

    def fold_pass(e, s):
        out, into = folds[e]
        at, far = into.at[1, s], out(t ^ 2, s)
        got(at, r.er.at[e, s, 1])
        far[...] = (far[...].astype(f32) + at[...].astype(f32)).astype(bf16)
        remote(far, into.at[2, s], r.es.at[e], r.er.at[e, s, 0], (b, t ^ 2)).start()

    def fold_late(e, s):
        @pl.when(s > 0)
        def _():
            fold_pass(e, s - 1)

    def folded(e, s):
        out, into = folds[e]
        got(into.at[0:2, s], r.er.at[e, s, 0])
        return out(t, s)[...].astype(f32) + into[0, s].astype(f32) + into[2, s].astype(f32)

    def here(src, dst, i):
        cp = pltpu.make_async_copy(src, dst, r.lsem.at[i])
        cp.start()
        return cp

    wide = lambda at, size: pl.ds(pl.multiple_of(at, 128), size)
    mats = (r.w_query, r.w_key, r.w_value, r.w_output)
    whole = {"S": r.SM, "A": r.WA, "U": r.WU, "C": r.WC}
    index = {"S": 0, "A": 1, "U": 2, "C": 3}

    def cuts(n, q):
        if n == "S":
            return [(r.SM.at[b, t], r.SM.at[b, t])]
        if n == "A":
            return [(w.at[:, wide(Cw * q, Cw)], r.WA.at[b, t, :, i * Cw : (i + 1) * Cw]) for i, w in enumerate(mats)]
        if n == "U":
            return [
                (r.w_up.at[:, wide((4 * i + q) * rd, rd)], r.WU.at[b, t, :, i * rd : (i + 1) * rd]) for i in range(nb)
            ]
        return [(r.w_conv.at[i, :, wide(Cw * q, Cw)], r.WC.at[b, t, :, i * Cw : (i + 1) * Cw]) for i in range(3)]

    def tier_own(n):
        for src, dst in cuts(n, t):
            here(src, dst, index[n])

    def tier_start(n):
        i = index[n]
        for d in (1, 2, 3):
            for src, dst in cuts(n, t ^ d):
                remote(src, dst, r.ts.at[i], r.tr.at[i], (b, t ^ d)).start()
        left_all(whole[n].at[b, 0:3], r.ts.at[i])

    def tier_wait(n):
        i = index[n]
        if n != "S":
            got(whole[n].at[b, t], r.lsem.at[i])
        got(whole[n].at[b, 0:3], r.tr.at[i])

    def if_(cond, body):
        pl.when(cond)(body)

    right, left = (2 * z + 2 + y, t), (2 * z - 2 + y, t)
    parts = {"S": [(r.SM, 0, 0, 4, 0)], "C": [(r.WC, 1, 0, 4, 1)], "X": [(r.WC, 2, 0, 4, 2)]}
    for i, (n, w, size) in enumerate((("A", r.WA, 2), ("U", r.WU, 2), ("D", r.WD, rd // 2))):
        parts[n] = [(w, 3 + 2 * i + h, h * size, size, 3 + i) for h in (0, 1)]

    def chunk_of(n, part, zz, col=None):
        w, k, at, size, _ = part
        col = ((1 - y) if n == "X" else y) if col is None else col
        return w.at[2 * zz + col, pl.ds(at, size)]

    def hop(part, at, zz, way):
        k = part[1]
        peer, past = (right, z < G - 1) if way == 0 else (left, z > 0)
        return past, remote(at, at, r.zs.at[part[4]], r.zr.at[k, zz - way], peer)

    def own_z(n):
        for part in parts[n]:
            for way in (0, 1):
                past, cp = hop(part, chunk_of(n, part, z), z, way)
                if_(past, cp.start)

    def own_y(n):
        for part in parts[n]:
            at, k = chunk_of(n, part, z), part[4]
            remote(at, at, r.ys.at[k], r.yr.at[k], ypeer).start()

    def arrivals(n, step, js):
        for j in js:
            for part in parts[n]:
                for way in (0, 1):
                    zz = z - j if way == 0 else z + j
                    step(part, j, way, zz, chunk_of(n, part, zz), zz >= 0 if way == 0 else zz < G)

    def onward(n, *js, cross=True):
        def step(part, j, way, zz, at, there):
            k = part[1]

            def body():
                got(at, r.zr.at[k, zz - way])
                if j < G - 1:
                    past, cp = hop(part, at, zz, way)
                    if_(past, cp.start)
                if n not in "CX" and cross:
                    remote(at, at, r.ys.at[part[4]], r.yr.at[part[4]], ypeer).start()

            if_(there, body)

        arrivals(n, step, js or range(1, G))

    def over(n, *js):
        def step(part, j, way, zz, at, there):
            if_(there, remote(at, at, r.ys.at[part[4]], r.yr.at[part[4]], ypeer).start)

        arrivals(n, step, js)

    def all_sent(n):
        w, k = parts[n][0][0], parts[n][0][4]
        if_(ends, lambda: got(w.at[0:1], r.zs.at[k]))
        if_(~ends, lambda: got(w.at[0:5], r.zs.at[k]))
        if n != "X":
            got(w.at[0 : 1 if n == "C" else G], r.ys.at[k])

    def y_wait(n):
        w, k = parts[n][0][0], parts[n][0][4]
        got(w.at[0 : 1 if n == "C" else G], r.yr.at[k])

    def small_start():
        r.SM[b, t] = jnp.zeros((8, 128), f32)
        for q, v in enumerate((r.gain, r.bias, r.bdown, r.bconv, r.bup)):
            r.SM[b, t, q : q + 1, : v.shape[1]] = v[...].astype(f32)
        tier_start("S")

    def memory_rows():
        W = R // 3
        to, frm = (lax.broadcasted_iota(jnp.int32, (R, R), axis) for axis in (0, 1))
        tap = (to >= W).astype(jnp.int32) + (to >= 2 * W).astype(jnp.int32)
        order = (frm == 3 * (to - W * tap) + tap).astype(bf16)
        for s in range(S):
            rows = jnp.dot(order, r.MEMV[s], preferred_element_type=f32).astype(bf16)
            for i in range(3):
                r.CTX[s, 4 * nu + 4 * i + t] = rows[W * i : W * (i + 1)]
            square = lambda axis: lax.broadcasted_iota(jnp.int32, (R // 3, R // 3), axis)
            line = jnp.broadcast_to(r.mask[s : s + 1].astype(f32), (R // 3, R // 3))
            col = jnp.sum(jnp.where(square(0) == square(1), line, 0.0), axis=1, keepdims=True)
            r.MK[s, t] = jnp.broadcast_to(col, (R // 3, 128))

    def rows_of(src, buf, first):
        at = lambda q: buf.at[:, pl.ds(first + nu * q, nu)]
        parts = [(src.at[:, 16 * i : 16 * i + 16], buf.at[:, first + nu * t + i]) for i in range(nu)]
        return parts, at, True

    def held(at):
        return [(at(t), at(t))], at, False

    pieces = [
        rows_of(r.seg, r.CTX, 8 * nu),
        rows_of(r.comp, r.CTX, 0),
        held(lambda q: r.CTX.at[:, 4 * nu + q]),
        held(lambda q: r.CTX.at[:, 4 * nu + 4 + q]),
        held(lambda q: r.CTX.at[:, 4 * nu + 8 + q]),
        rows_of(r.cot, r.COT, 0),
        held(lambda q: r.MK.at[:, q]),
    ]

    group = lambda i: 0 if i < 5 else i - 4
    grouped = [(r.CTX, 3 * nu), (r.COT, nu), (r.MK, 1)]

    def act_own():
        for i, (cut, at, far) in enumerate(pieces):
            if far:
                for src, dst in cut:
                    here(src, dst, 4 + group(i))

    def act_start(*which):
        for i in which:
            cut, at, far = pieces[i]
            g = group(i)
            for src, dst in cut:
                remote(src, dst, r.acs.at[g], r.acc.at[g], (b, t ^ 1)).start()
                remote(src, dst, r.acs.at[g], r.acx.at[i], (b, t ^ 2)).start()

    def act_forward(*which):
        for i in which:
            at = pieces[i][1](t ^ 2)
            got(at, r.acx.at[i])
            remote(at, at, r.acs.at[group(i)], r.acf.at[group(i)], (b, t ^ 1)).start()

    def act_wait(g):
        buf, n = grouped[g]
        got(buf.at[:, 0:n], r.acc.at[g])
        got(buf.at[:, 0:n], r.acf.at[g])
        if g < 2:
            got(buf.at[:, 0 : n if g else 2 * nu], r.lsem.at[4 + g])

    def act_sent():
        for g, (buf, n) in enumerate(grouped):
            got(buf.at[:, 0 : 3 * n], r.acs.at[g])

    def table():
        row = lax.broadcasted_iota(jnp.int32, (L, C3), 0) + 2 * L
        col = lax.broadcasted_iota(jnp.int32, (L, C3), 1)
        inner = col - L
        k1 = (inner >= nw).astype(jnp.int32)
        k2 = (inner >= 2 * nw).astype(jnp.int32)
        win = inner - nw * (k1 + k2)
        pos = jnp.where((col >= L) & (col < 2 * L), L + 3 * win + k1 + k2, col)
        r.DIST[...] = jnp.where(pos <= row, (row - pos).astype(f32) * (1.0 / C3), 1e30)
        r.SMG[...] = jnp.zeros_like(r.SMG)

    def seg_rows(s):
        return r.CTX[s, 8 * nu : 12 * nu].reshape(L, M)

    def project(s):
        rows = r.CTX[s].reshape(C3, M)
        kv = jnp.dot(rows, r.WA[:, :, :, Cw : 3 * Cw].reshape(M, 2 * Cw), preferred_element_type=f32)
        r.KV[s] = kv.astype(bf16)
        q = jnp.dot(seg_rows(s), r.WA[:, :, :, :Cw].reshape(M, Cw), preferred_element_type=f32)
        r.Q[s] = q.astype(bf16)


    def attend(s):
        for h in range(ht):
            c = slice(h * hd, (h + 1) * hd)
            raw = dot_nt(r.Q[s, :, c], r.KV[s, :, c])
            scores = raw * scale - r.slopes[t * ht + h] * r.DIST[...]
            e = jnp.exp(scores - jnp.max(scores, axis=1, keepdims=True))
            p = e * (1.0 / jnp.sum(e, axis=1, keepdims=True))
            r.PR[s, h] = p
            v = r.KV[s, :, Cw + h * hd : Cw + (h + 1) * hd]
            r.MIX[t, s, :, c] = jnp.dot(p.astype(bf16), v, preferred_element_type=f32).astype(bf16)
        spread_send(0, s, r.MIX)


    def wo(q):
        return r.WA[bq * q : bq * (q + 1), :, :, 3 * Cw :].reshape(Cw, Cw)

    def residual(s):
        spread_wait(0, s, r.MIX)
        acc = r.CTX[s, 8 * nu : 12 * nu, :, tc].reshape(L, Cw).astype(f32)
        for q in range(4):
            acc = acc + jnp.dot(r.MIX[q, s], wo(q), preferred_element_type=f32)
        r.RT[s] = acc
        r.RES[t, s] = acc.astype(bf16)
        spread_send(1, s, r.RES)

    def vectors():
        lane = lax.broadcasted_iota(jnp.int32, (8, 128), 1)
        for at in range(0, M, 128):
            block = jnp.zeros((8, 128), f32)
            for i in range(128 // rs):
                spot = at // rs + i
                turned = pltpu.roll(r.SM[spot // 4, spot % 4], rs * i, 1)
                block = jnp.where((lane >= rs * i) & (lane < rs * (i + 1)), turned, block)
            r.VV[0:4, at : at + 128] = block[0:4]
        for bb in range(nb):
            r.VV[4:5, bb * rd : (bb + 1) * rd] = r.SM[bb, t, 4:5, :rd]

    def xhat_of(s, q):
        return (r.RES[q, s].astype(f32) - r.MU[s, :, :1]) * r.MU[s, :, 1:2]

    def feed(s):
        spread_wait(1, s, r.RES)
        parts = [r.RES[q, s].astype(f32) for q in range(4)]
        mu = sum(jnp.sum(x, axis=1, keepdims=True) for x in parts) * (1.0 / M)
        var = sum(jnp.sum((x - mu) * (x - mu), axis=1, keepdims=True) for x in parts) * (1.0 / M)
        inv = lax.rsqrt(var + norm_eps)
        lane = lax.broadcasted_iota(jnp.int32, (L, 128), 1)
        r.MU[s] = jnp.where(lane == 0, mu, inv)
        for q in range(4):
            c = slice(q * Cw, (q + 1) * Cw)
            rows = ((parts[q] - mu) * inv) * r.VV[0:1, c] + r.VV[1:2, c]
            r.NRM[s, :, :, c] = rows.astype(bf16).reshape(4 * nu, 16, Cw)
        fb = Fw // 4
        for j in range(4):
            c = slice(j * fb, (j + 1) * fb)
            pre = jnp.dot(r.NRM[s].reshape(L, M), r.WU[:, :, :, c].reshape(M, fb), preferred_element_type=f32) + r.VV[4:5, c]
            phi = 0.5 + 0.5 * lax.erf(pre * math.sqrt(0.5))
            r.ACT[s, :, c] = (pre * phi).astype(bf16)
            r.GP[s, :, c] = (phi + pre * (jnp.exp(-0.5 * pre * pre) * (1.0 / math.sqrt(2 * math.pi)))).astype(bf16)


    def turn(j):
        low = lax.rem(G - j, G)
        inner = jnp.where(z == 1, low, G - 1 - low)
        return jnp.where(z == 0, G - 1 - j, jnp.where(z == G - 1, j, inner))

    grads = [(r.GD, r.YD, r.ZD), (r.GU, r.YU, r.ZU), (r.GB, r.YB, r.ZB), (r.WU, r.YA, r.ZA)]

    def to_y(k, zz):
        g, yb, zb = grads[k]
        remote(g.at[2 * zz + (1 - y)], yb.at[zz], r.gys.at[k], r.gyr.at[k, zz], ypeer).start()

    def plus(into, *others):
        def add(i):
            acc = into[i].astype(f32)
            for o in others:
                acc = acc + o[i].astype(f32)
            into[i] = acc.astype(bf16)

        each(into.shape[0], add)

    def pass_on(i, at, zb, o, sem):
        @pl.when((o != mate) & ~ends)
        def _():
            slot = lax.rem(o, 2)
            got(zb.at[slot], r.gzr.at[sem, slot])
            plus(at, zb.at[slot])

        to = jnp.where(ends, mate, o)
        slot = jnp.where(o == mate, 2, jnp.where(ends, lax.rem(o, 2), 3))
        remote(at, zb.at[slot], r.gzs.at[sem], r.gzr.at[sem, jnp.minimum(slot, 2)], (2 * to + y, t)).start()

    def mid(k, *steps):
        g, yb, zb = grads[k]
        for i in steps or range(G - 1):
            o = turn(i)
            at = yb.at[o]
            got(at, r.gyr.at[k, o])
            plus(at, g.at[2 * o + y])
            pass_on(i, at, zb, o, k)

    def mid_c(*steps):
        for i in steps or range(G - 1):
            o = turn(i)
            for c, col in enumerate((1 - y, y)):
                pass_on(i, r.GC.at[2 * o + col], r.ZC.at[c], o, 4 + c)

    def arrived(zb, sem):
        got(zb.at[2:4], r.gzr.at[sem, 2])

    def summed(at, zb, more, store):
        def total(i):
            acc = at[i].astype(f32)
            for o in [zb.at[2], zb.at[3]] + more:
                acc = acc + o[i].astype(f32)
            store(i, acc)

        each(4, total)

    def fin(k, store):
        g, yb, zb = grads[k]
        at = yb.at[z]
        got(at, r.gyr.at[k, z])
        arrived(zb, k)
        summed(at, zb, [g.at[2 * z + y]], store)

    def cross_c():
        arrived(r.ZC.at[0], 4)
        other = r.GC.at[2 * z + 1 - y]

        def store(i, acc):
            other[i] = acc.astype(bf16)

        summed(other, r.ZC.at[0], [], store)
        remote(other, r.YC, r.gys.at[4], r.gyr.at[4, 0], ypeer).start()

    def fin_c(store):
        got(r.YC, r.gyr.at[4, 0])
        arrived(r.ZC.at[1], 5)
        summed(r.GC.at[2 * z + y], r.ZC.at[1], [r.YC], store)

    def reduced_sent():
        for k, (g, yb, zb) in enumerate(grads):
            got(g.at[0:G], r.gys.at[k])
            got(g.at[0:3], r.gzs.at[k])
        got(r.YC, r.gys.at[4])
        for sem in (4, 5):
            got(r.GC.at[0:3], r.gzs.at[sem])

    fb = Fw // 4

    def grad_down(i):
        j = turn(i)
        c = pl.ds(pl.multiple_of(j * fb, fb), fb)
        rows = r.ACT[:, :, c].reshape(S * L, fb)
        g = dot_tn(rows, r.COT[...].reshape(S * L, M)).astype(bf16)
        r.GD[pl.ds(j * bq, bq)] = g.reshape(bq, 4, rd // 4, M)
        to_y(0, j)


    def back_feed(s):
        cot = r.COT[s].reshape(L, M)
        for j in range(4):
            c = slice(j * fb, (j + 1) * fb)
            wd = r.WD[bq * j : bq * (j + 1)].reshape(fb, M)
            d_act = dot_nt(cot, wd).astype(bf16).astype(f32)
            d_pre = d_act * r.GP[s, :, c].astype(f32)
            total = jnp.sum(d_pre, axis=0, keepdims=True)
            for i in range(fb // 128):
                at = j * (fb // 128) + i
                r.SMG[at : at + 1] += total[:, 128 * i : 128 * (i + 1)]
            r.GP[s, :, c] = d_pre.astype(bf16)
        m1 = jnp.zeros((L, 1), f32)
        m2 = jnp.zeros((L, 1), f32)
        for q in range(4):
            c = slice(q * Cw, (q + 1) * Cw)
            dn = dot_nt(r.GP[s], r.WU[bq * q : bq * (q + 1)].reshape(Cw, Fw))
            g = dn * r.VV[0:1, c]
            m1 = m1 + jnp.sum(g, axis=1, keepdims=True)
            m2 = m2 + jnp.sum(g * xhat_of(s, q), axis=1, keepdims=True)
            r.DNP[q, s] = dn.astype(bf16)
        lane = lax.broadcasted_iota(jnp.int32, (L, 128), 1)
        both = jnp.where(lane == 0, m1, jnp.where(lane == 1, m2, 0.0)) * (1.0 / M)
        pick = (
            lax.broadcasted_iota(jnp.int32, (8, 128), 0) == lax.broadcasted_iota(jnp.int32, (8, 128), 1)
        ).astype(f32)
        r.ST[t, s] = lax.dot_general(
            pick, both, (((1,), (1,)), ((), ())), precision=lax.Precision.HIGHEST, preferred_element_type=f32
        )
        fold_send(2, s)
        ex_send(3, r.er.at[3, s, 0], lambda q: r.ST.at[t, s], lambda d: r.ST.at[t, s])
        fold_late(2, s)


    def grad_up(i):
        j = turn(i)
        c = pl.ds(pl.multiple_of(j * Cw, Cw), Cw)
        rows = r.NRM[:, :, :, c].reshape(S * L, Cw)
        g = dot_tn(rows, r.GP[...].reshape(S * L, Fw)).astype(bf16)
        r.GU[pl.ds(j * bq, bq)] = g.reshape(bq, 4, rw, Fw)
        to_y(1, j)


    def back_norm(s):
        dn = folded(2, s)
        got(r.ST.at[0:3, s], r.er.at[3, s, 0])
        st = r.ST[0, s] + r.ST[1, s] + r.ST[2, s] + r.ST[3, s]
        side = lax.broadcasted_iota(jnp.int32, (8, 128), 0)
        col_of = lambda i: lax.dot_general(
            st,
            (side == i).astype(f32),
            (((0,), (0,)), ((), ())),
            precision=lax.Precision.HIGHEST,
            preferred_element_type=f32,
        )[:, :1]
        m1, m2 = col_of(0), col_of(1)
        inv = r.MU[s, :, 1:2]
        xhat = (r.RES[t, s].astype(f32) - r.MU[s, :, :1]) * inv
        cot = r.COT[s, :, :, tc].reshape(L, Cw).astype(f32)
        for i, v in enumerate((cot, dn * xhat, dn)):
            total = jnp.sum(v, axis=0, keepdims=True)
            for k in range(Cw // 128):
                at = Fw // 128 + i * (Cw // 128) + k
                r.SMG[at : at + 1] += total[:, 128 * k : 128 * (k + 1)]
        d_resid = cot + (dn * r.VV[0:1, tc] - m1 - xhat * m2) * inv
        r.DR[s] = d_resid
        db = d_resid.astype(bf16)
        r.DB[s] = db
        for q in range(4):
            r.DMP[q, s] = dot_nt(db, wo(q)).astype(bf16)
        fold_send(4, s)
        fold_late(4, s)

    def grad_out():
        for q in range(4):
            g = dot_tn(r.MIX[q].reshape(S * L, Cw), r.DB[...].reshape(S * L, Cw))
            r.GA[bq * q : bq * (q + 1), :, :, 3 * Cw :] = g.astype(bf16).reshape(bq, 4, rw, Cw)

    def out_rows(s):
        for q in range(4):
            c = slice(q * Cw, (q + 1) * Cw)
            o = jnp.dot(r.ACT[s], r.WD[:, :, c].reshape(Fw, Cw), preferred_element_type=f32)
            mine = (t == q).astype(f32)
            o = o + mine * (r.RT[s] + r.VV[2:3, c])
            r.OP[s, :, :, c] = o.astype(bf16).reshape(4 * nu, 16, Cw)
        fold_send(5, s)
        fold_late(5, s)


    def windows(k):
        return r.CTX[:, 4 * nu + 4 * k : 4 * nu + 4 * (k + 1)].reshape(S * nw, M)

    def compress():
        conv = r.VV[3:4, tc]
        pooled = 0.0
        for k in range(3):
            wk = r.WC[:, :, :, k * Cw : (k + 1) * Cw].reshape(M, Cw)
            conv = conv + jnp.dot(windows(k), wk, preferred_element_type=f32)
            pooled = pooled + r.CTX[:, 4 * nu + 4 * k : 4 * nu + 4 * (k + 1), :, tc].reshape(S * nw, Cw).astype(f32)
        mask = r.MK[...].reshape(S * nw, 128)[:, :1]
        done = 3 * lax.broadcasted_iota(jnp.int32, (nw, 128), 0) + 3
        live = jnp.concatenate(
            [(done <= r.evicted[s]).astype(f32)[:, :1] for s in range(S)], axis=0
        ) * mask
        r.NEW[t] = (mask * conv).astype(bf16).reshape(S, nw, Cw)
        d_conv = live * (conv - pooled * (1.0 / 3.0))
        total = jnp.sum(d_conv, axis=0, keepdims=True)
        for k in range(Cw // 128):
            at = Fw // 128 + 3 * (Cw // 128) + k
            r.SMG[at : at + 1] = total[:, 128 * k : 128 * (k + 1)]
        r.DC[...] = d_conv.astype(bf16)
        for k in range(3):
            g = dot_tn(windows(k), r.DC[...])
            far, at = (r.GC, k) if k < ct else (r.GB, k - ct)
            far[:, :, :, at * Cw : (at + 1) * Cw] = g.astype(bf16).reshape(nb, 4, rw, Cw)

    slope_row = Fw // 128 + 4 * (Cw // 128)

    def back_attend(s):
        dm = folded(4, s).astype(bf16)
        lane = lax.broadcasted_iota(jnp.int32, (1, 128), 1)
        for h in range(ht):
            c = slice(h * hd, (h + 1) * hd)
            cv = slice(Cw + h * hd, Cw + (h + 1) * hd)
            p = r.PR[s, h]
            dp = dot_nt(dm[:, c], r.KV[s, :, cv])
            delta = jnp.sum(p * dp, axis=1, keepdims=True)
            ds = p * (dp - delta)
            part = jnp.sum(jnp.sum(ds * r.DIST[...], axis=0, keepdims=True), axis=1, keepdims=True)
            r.SMG[slope_row : slope_row + 1] -= jnp.where(lane == t * ht + h, part, 0.0)
            dr = (ds * scale).astype(bf16)
            dq = jnp.dot(dr, r.KV[s, :, c], preferred_element_type=f32).astype(bf16)
            dk = dot_tn(dr, r.Q[s, :, c]).astype(bf16)
            dv = dot_tn(p.astype(bf16), dm[:, c]).astype(bf16)
            r.Q[s, :, c] = dq
            r.KV[s, :, c] = dk
            r.KV[s, :, cv] = dv


    def grad_proj(i):
        j = turn(i)
        c = pl.ds(pl.multiple_of(j * Cw, Cw), Cw)
        gq = jnp.zeros((Cw, Cw), f32)
        gkv = jnp.zeros((Cw, 2 * Cw), f32)
        for s in range(S):
            gq = gq + dot_tn(r.CTX[s, 8 * nu : 12 * nu, :, c].reshape(L, Cw), r.Q[s])
            gkv = gkv + dot_tn(r.CTX[s, :, :, c].reshape(C3, Cw), r.KV[s])
        rows = pl.ds(j * bq, bq)
        r.GA[rows, :, :, :Cw] = gq.astype(bf16).reshape(bq, 4, rw, Cw)
        r.GA[rows, :, :, Cw : 3 * Cw] = gkv.astype(bf16).reshape(bq, 4, rw, 2 * Cw)
        for d in (1, 2, 3):
            remote(r.GA.at[rows, t ^ d], r.WU.at[rows, t], r.xs.at[0], r.xr.at[j], (b, t ^ d)).start()
        r.WU[rows, t] = r.GA[rows, t]

    def proj_y(*steps):
        for i in steps:
            j = turn(i)
            got(r.WU.at[pl.ds(j * bq, bq), 0:3], r.xr.at[j])
            to_y(3, j)

    def own_out(s):
        r.OR[1, s] = folded(5, s).astype(bf16)

    def input_rows(s):
        x = jnp.concatenate([r.Q[s], r.KV[s, 2 * L :]], axis=1)
        for q in range(4):
            c = slice(q * Cw, (q + 1) * Cw)
            w = r.WA[bq * q : bq * (q + 1), :, :, : 3 * Cw].reshape(Cw, 3 * Cw)
            o = dot_nt(x, w) + (t == q).astype(f32) * r.DR[s]
            r.NRM[s, :, :, c] = o.astype(bf16).reshape(4 * nu, 16, Cw)
        fold_send(6, s)
        fold_late(6, s)


    def keep(o):
        def store(i, acc):
            o[pl.ds(i * (rd // 4), rd // 4)] = acc

        return store

    def across(q, acc):
        for i in range(4):
            r.OA[i, :, wide(q * Cw, Cw)] = acc[:, i * Cw : (i + 1) * Cw]

    def hold(m):
        def store(i, acc):
            m[i] = acc.astype(bf16)

        return store

    def tier_back(k, m, tb):
        for d in (1, 2, 3):
            remote(m.at[t ^ d], tb.at[t], r.gts.at[k], r.gtr.at[k], (b, t ^ d)).start()
        left_all(tb.at[0:3], r.gts.at[k])

    def small_y():
        remote(r.SMG, r.YS, r.ss.at[0], r.sr.at[0], ypeer).start()
        left_all(r.SMG, r.ss.at[0])

    def small_z():
        got(r.YS, r.sr.at[0])
        r.ZS[z] = r.SMG[...] + r.YS[...]
        for d in range(1, G):
            remote(r.ZS.at[z], r.ZS.at[z], r.ss.at[1], r.sr.at[1], (2 * zs[d] + y, t)).start()
        left_all(r.ZS.at[0 : G - 1], r.ss.at[1])

    def small_tier():
        got(r.ZS.at[0 : G - 1], r.sr.at[1])
        acc = r.ZS[0]
        for zz in range(1, G):
            acc = acc + r.ZS[zz]
        r.os[t] = acc
        for d in (1, 2, 3):
            remote(r.os.at[t], r.os.at[t], r.gts.at[3], r.gtr.at[3], (b, t ^ d)).start()
        left_all(r.os.at[0:3], r.gts.at[3])

    def own_input(s):
        r.IG[s] = folded(6, s)

    mineU, mineC, mineA, mineB = (g.at[2 * z + y] for g in (r.GU, r.GC, r.GA, r.GB))
    def give(i, src, dst):
        pltpu.make_async_copy(src, dst, r.osem.at[i]).start()

    def rows_out(i, src, dst):
        for j in range(nu):
            give(i, src.at[:, j], dst.at[:, 16 * j : 16 * j + 16])

    backs = (
        (mineU, r.TU, r.OU, r.ou),
        (mineC, r.TC, r.OC.at[0:ct], r.oc.at[0:ct]),
        None,
        None,
        (mineB, r.TB, r.OC.at[ct:3], r.oc.at[ct:3]),
    )
    places_out = (0, 1, 2, None, 7)

    def lay(k, o, q, rows):
        if k == 0:
            for i in range(nb):
                o[:, wide((4 * i + q) * rd, rd)] = rows[:, i * rd : (i + 1) * rd].astype(f32)
        else:
            for i in range(o.shape[0]):
                o[i, :, wide(q * Cw, Cw)] = rows[:, i * Cw : (i + 1) * Cw].astype(f32)

    def tier_out(k):
        m, tb, o, far = backs[k]
        lay(k, o, t, m[t])
        got(tb.at[0:3], r.gtr.at[k])
        for d in (1, 2, 3):
            lay(k, o, t ^ d, tb[t ^ d])
        give(places_out[k], o, far)

    def given():
        for i, (src, dst) in ((0, (r.OU, r.ou)), (2, (r.OA, r.oa)), (3, (r.OD, r.od))):
            pltpu.make_async_copy(src, dst, r.osem.at[i]).wait()
        for i, (src, dst) in ((1, (r.OC.at[0:ct], r.oc.at[0:ct])), (7, (r.OC.at[ct:3], r.oc.at[ct:3]))):
            pltpu.make_async_copy(src, dst, r.osem.at[i]).wait()
        for i, (src, dst) in ((5, (r.OR.at[1], r.out)), (6, (r.IG, r.ig)), (4, (r.OR.at[0], r.om)), (8, (r.OR.at[2], r.ocm))):
            for j in range(nu):
                pltpu.make_async_copy(src.at[:, j], dst.at[:, 16 * j : 16 * j + 16], r.osem.at[i]).wait()

    def small_out():
        got(r.os.at[0:3], r.gtr.at[3])

    slots = L - nw
    windows_of = [(q, max(R * q - slots, 0), R - max(slots - R * q, 0)) for q in range(4) if slots < R * (q + 1)]

    def new_send():
        for q, at, n in windows_of:
            part = r.NEW.at[t, :, at : at + n]
            if_(t != q, remote(part, part, r.ns.at[0], r.ns.at[1], (b, q)).start)

    def new_sent():
        for q, at, n in windows_of:
            if_(t != q, lambda: got(r.NEW.at[0, :, at : at + n], r.ns.at[0]))

    def new_out():
        for q, at, n in windows_of:
            if_(t == q, lambda: got(r.NEW.at[0:3, :, at : at + n], r.ns.at[1]))

    def memories():
        side = lax.broadcasted_iota(jnp.int32, (16, 1), 0)
        for s in range(S):
            for i in range(nu):
                fresh = side + (R * t + 16 * i) < r.evicted[s]
                r.OR[0, s, i] = jnp.where(fresh, r.CTX[s, 8 * nu + nu * t + i], r.MEMV[s, 16 * i : 16 * i + 16])
                r.OR[2, s, i] = r.CTX[s, nu * t + i]
        for q, at, n in windows_of:

            @pl.when(t == q)
            def _(at=at, n=n):
                for i in range((R - n) // 16, nu):
                    w = at + 16 * i - (R - n)
                    for s in range(S):
                        written = 3 * (side + w) + 3 <= r.evicted[s]
                        for p in range(4):
                            c = slice(p * Cw, (p + 1) * Cw)
                            old = r.CTX[s, nu * t + i, :, c]
                            r.OR[2, s, i, :, c] = jnp.where(written, r.NEW[p, s, w : w + 16], old)

    def drain():
        for n in parts:
            if n != "U":
                all_sent(n)
        got(r.GA.at[:, 0:3], r.xs.at[0])
        for ref, sem in sends:
            got(ref, sem)
        act_sent()
        new_sent()
        reduced_sent()
        for e, ref in enumerate((r.MIX, r.RES, r.DNP, r.ST, r.DMP, r.OR, r.IR)):
            got(ref.at[0:3], r.es.at[e])
        given()

    here(r.wd, r.WD.at[b], 0)
    here(r.mem, r.MEMV, 6)
    for n in ("A", "C", "U"):
        tier_own(n)
    act_own()
    greet(G, True, True)
    tier_start("A")
    tier_start("C")
    small_start()
    tier_start("U")
    act_start(0, 1)
    got(r.MEMV, r.lsem.at[6])
    memory_rows()
    act_start(2, 3, 4, 5, 6)
    got(r.WD.at[b], r.lsem.at[0])
    own_z("D")
    own_y("D")
    tier_wait("A")
    own_z("A")
    own_y("A")
    tier_wait("C")
    own_y("C")
    tier_wait("S")
    own_z("S")
    own_y("S")
    table()
    onward("A", 1)
    onward("S", 1)
    onward("A", 2)
    onward("S", 2)
    tier_wait("U")
    own_z("U")
    onward("A", 3)
    own_y("U")
    onward("S", 3)
    y_wait("C")
    onward("U", 1)
    act_forward(0, 1, 2, 3, 4)
    act_wait(0)
    y_wait("A")
    each(S, project, {0: lambda: onward("U", 2), 1: lambda: onward("D", 1, cross=False)})
    own_z("C")
    each(S, attend, {1: lambda: onward("U", 3)})
    over("D", 1)
    spread_pass(0, 0, r.MIX)
    each(S, residual, {1: lambda: onward("D", 2)})
    own_z("X")
    onward("C", 1)
    y_wait("S")
    vectors()
    act_forward(5, 6)
    onward("D", 3)
    y_wait("U")
    spread_pass(1, 0, r.RES)
    each(S, feed, {1: lambda: onward("X", 1)})
    act_wait(1)
    act_wait(2)
    onward("C", 2)
    each(4, grad_down, {2: lambda: onward("X", 2)})
    y_wait("D")
    each(S, back_feed, {0: lambda: onward("C", 3), 1: lambda: mid(0, 0), 2: lambda: onward("X", 3), 3: lambda: mid(0, 1)})
    fold_pass(2, S - 1)
    compress()
    mid_c(0)
    each(4, grad_up)
    each(G, lambda i: to_y(2, turn(i)))
    all_sent("U")
    each(S, back_norm, {2: lambda: mid(0, 2)})
    fold_pass(4, S - 1)
    grad_out()
    each(S, back_attend, {2: lambda: mid(1, 0)})
    small_y()
    each(4, grad_proj, {1: lambda: mid(1, 1)})
    mid_c(1)
    proj_y(0)
    mid(1, 2)
    each(S, out_rows)
    proj_y(1)
    mid_c(2)
    fold_pass(5, S - 1)
    each(S, input_rows)
    proj_y(2)
    fold_pass(6, S - 1)
    new_send()
    mid(2, 0)
    cross_c()
    proj_y(3)
    fin(0, keep(r.OD))
    give(3, r.OD, r.od)
    mid(2, 1)
    mid(2, 2)
    fin(1, hold(mineU))
    tier_back(0, mineU, r.TU)
    mid(3, 0)
    small_z()
    each(S, own_out)
    rows_out(5, r.OR.at[1], r.out)
    mid(3, 1)
    fin(2, hold(mineB))
    tier_back(4, mineB, r.TB)
    new_out()
    memories()
    rows_out(4, r.OR.at[0], r.om)
    rows_out(8, r.OR.at[2], r.ocm)
    mid(3, 2)
    fin_c(hold(mineC))
    tier_back(1, mineC, r.TC)
    small_tier()
    each(S, own_input)
    rows_out(6, r.IG, r.ig)
    tier_out(0)
    tier_out(4)
    tier_out(1)
    fin(3, across)
    give(2, r.OA, r.oa)
    small_out()
    drain()

def whole_layer(nb, ht, hd, arrays):
    S, R, M = arrays["seg"].shape
    rw, rd, rs = arrays["w_query"].shape[0], arrays["wd"].shape[0], M // (4 * nb)
    nu = R // 16
    G, Cw, Fw, L = nb // 2, M // 4, nb * rd, 64 * nu
    dma = pltpu.SemaphoreType.DMA
    V = lambda shape, dtype=bf16: pltpu.VMEM(shape, dtype)
    ct = 2
    D4, A4, U4, C4 = (4, rd // 4, M), (4, rw, 4 * Cw), (4, rw, Fw), (4, rw, 3 * Cw)
    ins = arrays
    outs = dict(
        out=((S, R, M), bf16),
        ig=((S, R, M), f32),
        om=((S, R, M), bf16),
        ocm=((S, R, M), bf16),
        od=((rd, M), f32),
        ou=((rw, 4 * Fw), f32),
        oc=((3, rw, M), f32),
        oa=((4, rw, M), f32),
        os=((4, 24, 128), f32),
    )
    scratch = dict(
        WA=V((nb,) + A4),
        WU=V((nb,) + U4),
        WC=V((nb,) + C4),
        WD=V((nb, rd, M)),
        SM=V((nb, 4, 8, 128), f32),
        CTX=V((S, 12 * nu, 16, M)),
        COT=V((S, 4 * nu, 16, M)),
        MK=V((S, 4, L // 12, 128), f32),
        DIST=V((L, 3 * L), f32),
        VV=V((8, max(M, Fw)), f32),
        SMG=V((24, 128), f32),
        Q=V((S, L, Cw)),
        KV=V((S, 3 * L, 2 * Cw)),
        PR=V((S, ht, L, 3 * L), f32),
        MIX=V((4, S, L, Cw)),
        RT=V((S, L, Cw), f32),
        RES=V((4, S, L, Cw)),
        MU=V((S, L, 128), f32),
        NRM=V((S, 4 * nu, 16, M)),
        ACT=V((S, L, Fw)),
        GP=V((S, L, Fw)),
        DNP=V((4, S, L, Cw)),
        DNR=V((3, S, L, Cw)),
        ST=V((4, S, 8, L), f32),
        DR=V((S, L, Cw), f32),
        DB=V((S, L, Cw)),
        DMP=V((4, S, L, Cw)),
        DMR=V((3, S, L, Cw)),
        OP=V((S, 4 * nu, 16, M)),
        OR=V((3, S, nu, 16, M)),
        IR=V((3, S, nu, 16, M)),
        DC=V((S * L // 3, Cw)),
        GD=V((nb,) + D4),
        GU=V((nb,) + U4),
        GC=V((nb, 4, rw, ct * Cw)),
        GB=V((nb, 4, rw, (3 - ct) * Cw)),
        GA=V((nb,) + A4),
        YD=V((G,) + D4),
        YU=V((G,) + U4),
        YC=V((4, rw, ct * Cw)),
        YB=V((G, 4, rw, (3 - ct) * Cw)),
        YA=V((G,) + A4),
        ZD=V((4,) + D4),
        ZU=V((4,) + U4),
        ZC=V((2, 4, 4, rw, ct * Cw)),
        ZB=V((4, 4, rw, (3 - ct) * Cw)),
        ZA=V((4,) + A4),
        YS=V((24, 128), f32),
        ZS=V((G, 24, 128), f32),
        TU=V(U4),
        TC=V((4, rw, ct * Cw)),
        TB=V((4, rw, (3 - ct) * Cw)),
        NEW=V((4, S, L // 3, Cw)),
        IG=V((S, nu, 16, M), f32),
        OD=V((rd, M), f32),
        OU=V((rw, 4 * Fw), f32),
        OC=V((3, rw, M), f32),
        OA=V((4, rw, M), f32),
        MEMV=V((S, R, M)),
        osem=dma((9,)),
        lsem=dma((7,)),
        ts=dma((4,)),
        tr=dma((4,)),
        zs=dma((6,)),
        zr=dma((9, G - 1)),
        ys=dma((6,)),
        yr=dma((6,)),
        acs=dma((3,)),
        acc=dma((3,)),
        acf=dma((3,)),
        acx=dma((7,)),
        es=dma((7,)),
        er=dma((7, S, 2)),
        ns=dma((2,)),
        gys=dma((5,)),
        gyr=dma((5, G)),
        gzs=dma((6,)),
        gzr=dma((6, 3)),
        ss=dma((2,)),
        sr=dma((2,)),
        xs=dma((1,)),
        xr=dma((G,)),
        gts=dma((5,)),
        gtr=dma((5,)),
    )
    names = list(ins) + list(outs) + list(scratch)
    near = dict(gain=VM, bias=VM, bdown=VM, bconv=VM, bup=VM, mask=VM, evicted=SM, slopes=SM)
    return pl.pallas_call(
        functools.partial(layer_kernel, names, (nb, nu, S, ht, hd, M, Cw, rw, rd, rs)),
        out_shape=[jax.ShapeDtypeStruct(s, d) for s, d in outs.values()],
        in_specs=[near.get(n, ANY) for n in ins],
        out_specs=[VM if n == "os" else ANY for n in outs],
        scratch_shapes=list(scratch.values()),
        compiler_params=pltpu.CompilerParams(
            collective_id=9, has_side_effects=True, vmem_limit_bytes=63 * 2**20
        ),
        name="whole_layer",
    )(*ins.values())


def finish_kernel(names, shape, *refs):
    r = Names(names, refs)
    nb, rs, rd, Fw, Cw, heads = shape
    b, t = lax.axis_index("batch"), lax.axis_index("tier")
    moves = [(r.out, r.o_out), (r.ig, r.o_ig), (r.od, r.o_od), (r.ou, r.o_ou), (r.oc, r.o_oc)]
    moves += [(r.oa.at[i], o) for i, o in enumerate((r.o_q, r.o_k, r.o_v, r.o_o))]
    moves += [(r.om, r.o_mem), (r.ocm, r.o_comp)]
    bufs = refs[len(names) :]
    into = [pltpu.make_async_copy(src, buf, r.sem.at[i]) for i, ((src, _), buf) in enumerate(zip(moves, bufs))]
    n = len(moves)
    onto = [pltpu.make_async_copy(buf, dst, r.sem.at[n + i]) for i, ((_, dst), buf) in enumerate(zip(moves, bufs))]
    for cp in into:
        cp.start()
    spot = 4 * b + t
    block, inner = spot // (Cw // rs), lax.rem(spot, Cw // rs)
    half, group = inner // (128 // rs), lax.rem(inner, 128 // rs)
    for i, o in enumerate((r.o_down, r.o_gain, r.o_bias, r.o_conv)):
        row = r.os[block, pl.ds(Fw // 128 + (Cw // 128) * i + half, 1), :]
        turned = pltpu.roll(jnp.broadcast_to(row, (8, 128)), lax.rem(128 - rs * group, 128), 1)
        o[...] = turned[0:1, :rs]
    r.o_up[...] = r.os[t, pl.ds(b, 1), :rd]
    at = Fw // 128 + 4 * (Cw // 128)
    total = r.os[0, at : at + 1]
    for q in range(1, 4):
        total = total + r.os[q, at : at + 1]
    r.o_slopes[...] = total[:, :heads]
    for cp, then in zip(into, onto):
        cp.wait()
        then.start()
    for cp in onto:
        cp.wait()


def finish(nb, heads, arrays):
    S, R, M = arrays["out"].shape
    rw, rd, rs = arrays["oa"].shape[1], arrays["od"].shape[0], M // (4 * nb)
    Cw, Fw = M // 4, nb * rd
    rows, mat, vec = (S, R, M), (rw, M), (1, rs)
    outs = dict(
        o_out=(rows, bf16, ANY),
        o_ig=(rows, f32, ANY),
        o_mem=(rows, bf16, ANY),
        o_comp=(rows, bf16, ANY),
        o_q=(mat, f32, ANY),
        o_k=(mat, f32, ANY),
        o_v=(mat, f32, ANY),
        o_o=(mat, f32, ANY),
        o_ou=((rw, 4 * Fw), f32, ANY),
        o_up=((1, rd), f32, VM),
        o_od=((rd, M), f32, ANY),
        o_down=(vec, f32, VM),
        o_gain=(vec, f32, VM),
        o_bias=(vec, f32, VM),
        o_oc=((3, rw, M), f32, ANY),
        o_conv=(vec, f32, VM),
        o_slopes=((1, heads), f32, VM),
    )
    moved = ("o_out", "o_ig", "o_od", "o_ou", "o_oc", "o_q", "o_k", "o_v", "o_o", "o_mem", "o_comp")
    return pl.pallas_call(
        functools.partial(
            finish_kernel, list(arrays) + list(outs) + ["sem"], (nb, rs, rd, Fw, Cw, heads)
        ),
        out_shape=[jax.ShapeDtypeStruct(s, d) for s, d, _ in outs.values()],
        in_specs=[VM if n == "os" else ANY for n in arrays],
        out_specs=[o[2] for o in outs.values()],
        scratch_shapes=[pltpu.SemaphoreType.DMA((2 * len(moved),))]
        + [pltpu.VMEM(outs[n][0], outs[n][1]) for n in moved],
        compiler_params=pltpu.CompilerParams(vmem_limit_bytes=63 * 2**20),
        name="finish",
    )(*arrays.values())


def per_device_fused(
    nb,
    segment,
    memory,
    compressed,
    evicted,
    window_mask,
    cotangent,
    w_query,
    w_key,
    w_value,
    w_output,
    w_up,
    b_up,
    w_down,
    b_down,
    ln_gain,
    ln_bias,
    w_conv,
    b_conv,
    slopes,
):
    S, R, M = segment.shape
    heads = slopes.shape[0]
    line = lambda v: v.reshape(1, -1)
    names = ("out", "ig", "om", "ocm", "od", "ou", "oc", "oa", "os")
    made = whole_layer(
        nb,
        heads // 4,
        M // heads,
        dict(
            w_query=w_query,
            w_key=w_key,
            w_value=w_value,
            w_output=w_output,
            w_up=w_up,
            w_conv=w_conv,
            wd=w_down,
            comp=compressed,
            seg=segment,
            cot=cotangent,
            mem=memory,
            gain=line(ln_gain),
            bias=line(ln_bias),
            bdown=line(b_down),
            bconv=line(b_conv),
            bup=line(b_up),
            mask=window_mask,
            evicted=evicted,
            slopes=slopes,
        ),
    )
    outs = finish(nb, heads, dict(zip(names, made)))
    flat = (9, 11, 12, 13, 15, 16)
    return tuple(o.reshape(-1) if i in flat else o for i, o in enumerate(outs))


def solution(mesh):
    both = ("batch", "tier")
    rows = P("batch", "tier", None)
    mat, vec = P(both, None), P(both)
    nb = mesh.shape["batch"]

    def body(*args):
        fused = args[6].shape[0] % 16 == 0 and args[12].shape[0] == 128
        return (per_device_fused if fused else per_device)(nb, *args)

    return jax.shard_map(
        body,
        mesh=mesh,
        in_specs=(
            (rows, rows, rows, P("batch"), P("batch", "tier"), rows)
            + (mat, mat, mat, mat, mat, vec, mat, vec, vec, vec)
            + (P(None, both, None), vec, P())
        ),
        out_specs=(
            (rows, rows, rows, rows, mat, mat, mat, mat, mat, vec, mat, vec, vec, vec)
            + (P(None, both, None), vec, P())
        ),
        check_vma=False,
    )
```

```python
import functools
import math

import jax
import jax.numpy as jnp
from jax import lax
from jax.experimental import pallas as pl
from jax.experimental.pallas import tpu as pltpu
from jax.sharding import PartitionSpec as P

norm_eps = 1e-05
MESH = pl.DeviceIdType.MESH
ANY = pl.BlockSpec(memory_space=pl.ANY)
VM = pl.BlockSpec(memory_space=pltpu.VMEM)
SM = pl.BlockSpec(memory_space=pltpu.SMEM)
f32 = jnp.float32
bf16 = jnp.bfloat16


def remote(src, dst, send, recv, device):
    return pltpu.make_async_remote_copy(
        src_ref=src,
        dst_ref=dst,
        send_sem=send,
        recv_sem=recv,
        device_id=device,
        device_id_type=MESH,
    )


def places(groups):
    b, t = lax.axis_index("batch"), lax.axis_index("tier")
    z, y = b // 2, lax.rem(b, 2)
    zs = [lax.rem(z + d, groups) for d in range(groups)]
    zback = [lax.rem(z + groups - d, groups) for d in range(groups)]
    return b, t, z, y, zs, zback


def greet(groups, tiers, columns):
    b, t, z, y, zs, _ = places(groups)
    barrier = pltpu.get_barrier_semaphore()
    peers = []
    if tiers:
        peers += [(b, t ^ d) for d in (1, 2, 3)]
    if columns:
        peers += [(2 * zz + y, t) for zz in zs[1:]] + [(b ^ 1, t)]
    for peer in peers:
        pl.semaphore_signal(barrier, inc=1, device_id=peer, device_id_type=MESH)
    pl.semaphore_wait(barrier, len(peers))


def gather_kernel(groups, nu, *refs):
    (wa, wu, wc, wd, sm, comp, mem, seg, cot, mk) = refs[:10]
    (WA, WU, WC, WD, SM, CTX, COT, MK) = refs[10:18]
    lsem, ts, tr, zsd, zr, ys, yr, acs, acr = refs[18:]
    G = groups
    b, t, z, y, zs, zback = places(G)
    greet(G, True, True)
    ypeer = (b ^ 1, t)
    local, sends = [], []

    def here(src, dst, i):
        cp = pltpu.make_async_copy(src, dst, lsem.at[i])
        cp.start()
        return cp

    kinds = [(sm, SM), (wa, WA), (wu, WU), (wc, WC)]
    own = []
    for k, (src, dst) in enumerate(kinds):
        mine = src if k == 0 else src.at[t]
        own.append(here(mine, dst.at[b, t], k))
        for d in (1, 2, 3):
            piece = src if k == 0 else src.at[t ^ d]
            cp = remote(piece, dst.at[b, t], ts.at[k, d - 1], tr.at[k, d - 1], (b, t ^ d))
            cp.start()
            sends.append(cp)
    own.append(here(wd, WD.at[b], 4))
    pieces = [
        (comp, lambda q: CTX.at[:, pl.ds(nu * q, nu)]),
        (mem.at[:, 0], lambda q: CTX.at[:, 4 * nu + q]),
        (mem.at[:, 1], lambda q: CTX.at[:, 4 * nu + 4 + q]),
        (mem.at[:, 2], lambda q: CTX.at[:, 4 * nu + 8 + q]),
        (seg, lambda q: CTX.at[:, pl.ds(8 * nu + nu * q, nu)]),
        (mk, lambda q: MK.at[:, q]),
        (cot, lambda q: COT.at[:, pl.ds(nu * q, nu)]),
    ]
    for i, (src, at) in enumerate(pieces):
        own.append(here(src, at(t), 5 + i))
        for j, d in enumerate((1, 2)):
            cp = remote(src, at(t), acs.at[i, j], acr.at[i, j], (b, t ^ d))
            cp.start()
            sends.append(cp)
    table = [SM, WA, WU, WD, WC]
    local_of = [0, 1, 2, 4, 3]
    for k, dst in enumerate(table):
        own[local_of[k]].wait()
        if k != 3:
            kk = local_of[k]
            for d in (1, 2, 3):
                remote(dst.at[b, t], dst.at[b, t ^ d], ts.at[kk, d - 1], tr.at[kk, d - 1], (b, t ^ d)).wait_recv()
        for d in range(1, G):
            cp = remote(dst.at[b], dst.at[b], zsd.at[k, d], zr.at[k, d], (2 * zs[d] + y, t))
            cp.start()
            sends.append(cp)
        cp = remote(dst.at[b], dst.at[b], ys.at[k, 0], yr.at[k, 0], ypeer)
        cp.start()
        sends.append(cp)
    for i, (src, at) in enumerate(pieces):
        remote(at(t ^ 2), at(t ^ 2), acs.at[i, 1], acr.at[i, 1], (b, t ^ 2)).wait_recv()
        cp = remote(at(t ^ 2), at(t ^ 2), acs.at[i, 2], acr.at[i, 2], (b, t ^ 1))
        cp.start()
        sends.append(cp)
    for k, dst in enumerate(table):
        for d in range(1, G):
            at = dst.at[2 * zback[d] + y]
            remote(at, at, zsd.at[k, d], zr.at[k, d], ypeer).wait_recv()
            cp = remote(at, at, ys.at[k, d], yr.at[k, d], ypeer)
            cp.start()
            sends.append(cp)
    for k, dst in enumerate(table):
        for d in range(G):
            at = dst.at[2 * zback[d] + (1 - y)]
            remote(at, at, ys.at[k, d], yr.at[k, d], ypeer).wait_recv()
    for i, (src, at) in enumerate(pieces):
        for j, q in ((0, t ^ 1), (2, t ^ 3)):
            remote(at(q), at(q), acs.at[i, j], acr.at[i, j], (b, t ^ 1)).wait_recv()
    for i in range(len(pieces)):
        own[5 + i].wait()
    for cp in sends:
        cp.wait_send()


def gather_all(nb, nu, wa, wu, wc, wd, sm, comp, mem, seg, cot, mk):
    G = nb // 2
    S, _, U, M = comp.shape
    out = [
        jax.ShapeDtypeStruct((nb,) + wa.shape, bf16),
        jax.ShapeDtypeStruct((nb,) + wu.shape, bf16),
        jax.ShapeDtypeStruct((nb,) + wc.shape, bf16),
        jax.ShapeDtypeStruct((nb,) + wd.shape, bf16),
        jax.ShapeDtypeStruct((nb, 4) + sm.shape, f32),
        jax.ShapeDtypeStruct((S, 12 * nu, U, M), bf16),
        jax.ShapeDtypeStruct((S, 4 * nu, U, M), bf16),
        jax.ShapeDtypeStruct((S, 4) + mk.shape[1:], f32),
    ]
    dma = pltpu.SemaphoreType.DMA
    return pl.pallas_call(
        functools.partial(gather_kernel, G, nu),
        out_shape=out,
        in_specs=[ANY] * 10,
        out_specs=[ANY] * 8,
        scratch_shapes=[
            dma((12,)),
            dma((4, 3)),
            dma((4, 3)),
            dma((5, G)),
            dma((5, G)),
            dma((5, G)),
            dma((5, G)),
            dma((7, 3)),
            dma((7, 3)),
        ],
        compiler_params=pltpu.CompilerParams(collective_id=0, has_side_effects=True),
        name="gather_all",
    )(wa, wu, wc, wd, sm, comp, mem, seg, cot, mk)


def spread_kernel(same, x, o, lsem, ss, rs):
    b, t = lax.axis_index("batch"), lax.axis_index("tier")
    greet(1, True, False)
    cps = []
    for d in (1, 2, 3):
        cp = remote(x if same else x.at[t ^ d], o.at[t], ss.at[d - 1], rs.at[d - 1], (b, t ^ d))
        cp.start()
        cps.append(cp)
    mine = pltpu.make_async_copy(x if same else x.at[t], o.at[t], lsem)
    mine.start()
    mine.wait()
    for d in (1, 2, 3):
        remote(o.at[t ^ d], o.at[t ^ d], ss.at[d - 1], rs.at[d - 1], (b, t ^ d)).wait_recv()
    for cp in cps:
        cp.wait_send()


def spread(x, same, cid):
    dma = pltpu.SemaphoreType.DMA
    shape = ((4,) + x.shape) if same else x.shape
    return pl.pallas_call(
        functools.partial(spread_kernel, same),
        out_shape=jax.ShapeDtypeStruct(shape, x.dtype),
        in_specs=[ANY],
        out_specs=ANY,
        scratch_shapes=[dma, dma((3,)), dma((3,))],
        compiler_params=pltpu.CompilerParams(collective_id=cid, has_side_effects=True),
        name="spread_%d" % cid,
    )(x)


def reduce_kernel(groups, *refs):
    GD, GU, GC, GA, SMG = refs[:5]
    OD, OU, OC, OA, OS = refs[5:10]
    YD, YU, YC, YA, YS, ZD, ZU, ZC, ZA, ZS, TU, TC, TA, MU, MC, MA, ys, yr, zsd, zr, ts, tr = refs[10:]
    G = groups
    b, t, z, y, zs, zback = places(G)
    greet(G, True, True)
    ypeer = (b ^ 1, t)
    sends = []
    kinds = [
        (GD, YD, ZD, OD, None, None),
        (GU, YU, ZU, OU, MU, TU),
        (GC, YC, ZC, OC, MC, TC),
        (GA, YA, ZA, OA, MA, TA),
    ]
    for k, (g, yb, *_) in enumerate(kinds):
        for d in range(G):
            zz = zs[(d + 1) % G]
            cp = remote(g.at[2 * zz + (1 - y)], yb.at[zz], ys.at[k, d], yr.at[k, d], ypeer)
            cp.start()
            sends.append(cp)
    cp = remote(SMG, YS, ys.at[4, 0], yr.at[4, 0], ypeer)
    cp.start()
    sends.append(cp)
    for k, (g, yb, zb, o, m, tb) in enumerate(kinds):
        for d in range(G):
            zz = zs[(d + 1) % G]
            at = yb.at[zz]
            remote(at, at, ys.at[k, d], yr.at[k, d], ypeer).wait_recv()

            def add(i, c, yb=yb, zz=zz, g=g):
                yb[zz, i] = (yb[zz, i].astype(f32) + g[2 * zz + y, i].astype(f32)).astype(bf16)
                return c

            lax.fori_loop(0, yb.shape[1], add, 0)
            if d < G - 1:
                cp = remote(at, zb.at[d], zsd.at[k, d], zr.at[k, d], (2 * zz + y, t))
                cp.start()
                sends.append(cp)
    remote(YS, YS, ys.at[4, 0], yr.at[4, 0], ypeer).wait_recv()
    ZS[z] = SMG[...] + YS[...]
    for d in range(G - 1):
        cp = remote(ZS.at[z], ZS.at[z], zsd.at[4, d], zr.at[4, d], (2 * zs[d + 1] + y, t))
        cp.start()
        sends.append(cp)
    for k, (g, yb, zb, o, m, tb) in enumerate(kinds):
        for d in range(G - 1):
            remote(zb.at[d], zb.at[d], zsd.at[k, d], zr.at[k, d], ypeer).wait_recv()

        def total(i, c, k=k, yb=yb, zb=zb, o=o, m=m):
            acc = yb[z, i].astype(f32)
            for d in range(G - 1):
                acc = acc + zb[d, i].astype(f32)
            if k == 0:
                o[i] = acc
            else:
                m[i] = acc.astype(bf16)
            return c

        lax.fori_loop(0, o.shape[0], total, 0)
        if k:
            for d in (1, 2, 3):
                cp = remote(m.at[t ^ d], tb.at[t], ts.at[k - 1, d - 1], tr.at[k - 1, d - 1], (b, t ^ d))
                cp.start()
                sends.append(cp)
    for d in range(G - 1):
        at = ZS.at[zback[d + 1]]
        remote(at, at, zsd.at[4, d], zr.at[4, d], ypeer).wait_recv()
    acc = ZS[0]
    for zz in range(1, G):
        acc = acc + ZS[zz]
    OS[t] = acc
    for d in (1, 2, 3):
        cp = remote(OS.at[t], OS.at[t], ts.at[3, d - 1], tr.at[3, d - 1], (b, t ^ d))
        cp.start()
        sends.append(cp)
    for k, (g, yb, zb, o, m, tb) in enumerate(kinds):
        if k:
            o[t] = m[t].astype(f32)
            for d in (1, 2, 3):
                at = tb.at[t ^ d]
                remote(at, at, ts.at[k - 1, d - 1], tr.at[k - 1, d - 1], (b, t ^ d)).wait_recv()
                o[t ^ d] = tb[t ^ d].astype(f32)
    for d in (1, 2, 3):
        at = OS.at[t ^ d]
        remote(at, at, ts.at[3, d - 1], tr.at[3, d - 1], (b, t ^ d)).wait_recv()
    for cp in sends:
        cp.wait_send()


def reduce_all(nb, gd, gu, gc, ga, sg):
    G = nb // 2
    dma = pltpu.SemaphoreType.DMA
    shapes = [x.shape[1:] for x in (gd, gu, gc, ga)]
    return pl.pallas_call(
        functools.partial(reduce_kernel, G),
        out_shape=[jax.ShapeDtypeStruct(s, f32) for s in shapes]
        + [jax.ShapeDtypeStruct((4,) + sg.shape, f32)],
        in_specs=[VM] * 5,
        out_specs=[VM] * 5,
        scratch_shapes=[pltpu.VMEM((G,) + s, bf16) for s in shapes]
        + [pltpu.VMEM(sg.shape, f32)]
        + [pltpu.VMEM((G - 1,) + s, bf16) for s in shapes]
        + [pltpu.VMEM((G,) + sg.shape, f32)]
        + [pltpu.VMEM(s, bf16) for s in shapes[1:]]
        + [pltpu.VMEM(s, bf16) for s in shapes[1:]]
        + [dma((5, G)), dma((5, G)), dma((5, G)), dma((5, G)), dma((4, 3)), dma((4, 3))],
        compiler_params=pltpu.CompilerParams(
            collective_id=1, has_side_effects=True, vmem_limit_bytes=48 * 2**20
        ),
        name="reduce_all",
    )(gd, gu, gc, ga, sg)


def dot(a, b):
    return jnp.dot(a, b, preferred_element_type=f32)


def dot_tn(a, b):
    return lax.dot_general(a, b, (((0,), (0,)), ((), ())), preferred_element_type=f32)


def dot_nt(a, b):
    return lax.dot_general(a, b, (((1,), (1,)), ((), ())), preferred_element_type=f32)


def per_device(
    nb,
    segment,
    memory,
    compressed,
    evicted,
    window_mask,
    cotangent,
    w_query,
    w_key,
    w_value,
    w_output,
    w_up,
    b_up,
    w_down,
    b_down,
    ln_gain,
    ln_bias,
    w_conv,
    b_conv,
    slopes,
):
    S, R, M = segment.shape
    heads = slopes.shape[0]
    hd = M // heads
    nt = 4
    rw, rd, rs = w_query.shape[0], w_down.shape[0], b_down.shape[0]
    b, t = lax.axis_index("batch"), lax.axis_index("tier")
    Cw, Fw = M // nt, nb * rd
    nu, W = R // 16, R // 3
    seg_len = nt * R
    T = S * seg_len
    ht = heads // nt
    index = 4 * b + t

    wa = jnp.stack([w_query, w_key, w_value, w_output]).reshape(4, rw, nt, Cw)
    wa = wa.transpose(2, 1, 0, 3).reshape(nt, rw, 4 * Cw)
    wu = w_up.reshape(rw, nb, nt, rd).transpose(2, 0, 1, 3).reshape(nt, rw, Fw)
    wc = w_conv.reshape(3, rw, nt, Cw).transpose(2, 1, 0, 3).reshape(nt, rw, 3 * Cw)
    row0 = jnp.concatenate([ln_gain, ln_bias, b_down, b_conv])
    sm = jnp.zeros((8, 128), f32).at[0, : 4 * rs].set(row0.astype(f32)).at[1, :rd].set(b_up.astype(f32))
    mem = memory.reshape(S, W, 3, M).transpose(0, 2, 1, 3)
    mk = jnp.broadcast_to(window_mask.astype(f32)[:, :, None], (S, W, 128))
    WA, WU, WC, WD, SM, CTX, COT, MK = gather_all(
        nb,
        nu,
        wa,
        wu,
        wc,
        w_down,
        sm,
        compressed.reshape(S, nu, 16, M),
        mem,
        segment.reshape(S, nu, 16, M),
        cotangent.reshape(S, nu, 16, M),
        mk,
    )
    WA = WA.reshape(M, 4 * Cw)
    Wqkv, Wo = WA[:, : 3 * Cw], WA[:, 3 * Cw :]
    WU, WC, WD = WU.reshape(M, Fw), WC.reshape(M, 3 * Cw), WD.reshape(Fw, M)
    gain, bias, bdown, bconv = [SM[:, :, 0, i * rs : (i + 1) * rs].reshape(M) for i in range(4)]
    bup = lax.dynamic_index_in_dim(SM, t, 1, False)[:, 1, :rd].reshape(Fw)
    cols = lambda v: lax.dynamic_slice_in_dim(v, t * Cw, Cw, v.ndim - 1)
    ctx = CTX.reshape(S, 3 * seg_len, M)
    cot = COT.reshape(T, M)
    seg = ctx[:, 2 * seg_len :].reshape(T, M)

    kpos = jnp.concatenate(
        [
            jnp.arange(seg_len),
            seg_len + (3 * jnp.arange(seg_len // 3)[None, :] + jnp.arange(3)[:, None]).reshape(-1),
            2 * seg_len + jnp.arange(seg_len),
        ]
    )
    qpos = 2 * seg_len + jnp.arange(seg_len)
    allowed = kpos[None, :] <= qpos[:, None]
    dist = (qpos[:, None] - kpos[None, :]).astype(f32) * (1.0 / (3 * seg_len))
    slope = lax.dynamic_slice_in_dim(slopes, t * ht, ht)
    scale = 1.0 / math.sqrt(hd)
    q = dot(seg, Wqkv[:, :Cw]).astype(bf16).reshape(S, seg_len, ht, hd)
    kv = dot(ctx.reshape(-1, M), Wqkv[:, Cw:]).astype(bf16).reshape(S, 3 * seg_len, 2, ht, hd)
    kk, vv = kv[:, :, 0], kv[:, :, 1]
    raw = jnp.einsum("sqhd,skhd->shqk", q, kk, preferred_element_type=f32)
    scores = jnp.where(allowed, raw * scale - slope[:, None, None] * dist, -1e30)
    high = jnp.max(scores, axis=-1, keepdims=True)
    e = jnp.exp(scores - high)
    probs = e / jnp.sum(e, axis=-1, keepdims=True)
    probs_low = probs.astype(bf16)
    mixed_t = jnp.einsum("shqk,skhd->sqhd", probs_low, vv, preferred_element_type=f32).astype(bf16)
    MIX = spread(mixed_t.reshape(T, Cw), True, 2)
    mixed = MIX.transpose(1, 0, 2).reshape(T, M)
    resid_t = cols(seg).astype(f32) + dot(mixed, Wo)
    RES = spread(resid_t.astype(bf16), True, 3)
    resid = RES.transpose(1, 0, 2).reshape(T, M).astype(f32)
    center = resid - jnp.mean(resid, axis=-1, keepdims=True)
    spread_ = lax.rsqrt(jnp.mean(center * center, axis=-1, keepdims=True) + norm_eps)
    xhat = center * spread_
    normed = (xhat * gain + bias).astype(bf16)
    pre = dot(normed, WU) + bup
    phi = 0.5 * (1.0 + lax.erf(pre * math.sqrt(0.5)))
    act = (pre * phi).astype(bf16)
    slope_act = phi + pre * jnp.exp(-0.5 * pre * pre) * (1.0 / math.sqrt(2 * math.pi))
    place = lambda v: lax.dynamic_update_slice_in_dim(jnp.zeros((T, M), f32), v, t * Cw, 1)
    out_part = dot(act, WD) + place(resid_t + cols(bdown))
    rows = lambda v: v.astype(bf16).reshape(S, nt, R, M).transpose(1, 0, 2, 3)
    output = jnp.sum(spread(rows(out_part), False, 4).astype(f32), axis=0).astype(bf16)
    gdown = dot_tn(act, cot)
    d_act = dot_nt(cot, WD).astype(bf16)
    d_pre = d_act.astype(f32) * slope_act
    gub = jnp.sum(d_pre, axis=0)
    d_pre_low = d_pre.astype(bf16)
    gup = dot_tn(normed, d_pre_low)
    dn_part = dot_nt(d_pre_low, WU)
    stats = jnp.stack([jnp.mean(dn_part * gain, axis=1), jnp.mean(dn_part * gain * xhat, axis=1)])
    stats = lax.psum(stats, "tier")
    cols_of = lambda v: v.astype(bf16).reshape(T, nt, Cw).transpose(1, 0, 2)
    dn = jnp.sum(spread(cols_of(dn_part), False, 5).astype(f32), axis=0)
    xhat_t = cols(xhat)
    ggain, gbias = jnp.sum(dn * xhat_t, axis=0), jnp.sum(dn, axis=0)
    g = dn * cols(gain)
    cot_t = cols(cot).astype(f32)
    gdb = jnp.sum(cot_t, axis=0)
    d_resid = cot_t + (g - stats[0][:, None] - xhat_t * stats[1][:, None]) * spread_
    d_branch = d_resid.astype(bf16)
    gout = dot_tn(mixed, d_branch)
    dm_part = dot_nt(d_branch, Wo)
    dm = jnp.sum(spread(cols_of(dm_part), False, 6).astype(f32), axis=0).astype(bf16)
    dm = dm.reshape(S, seg_len, ht, hd)
    d_probs = jnp.einsum("sqhd,skhd->shqk", dm, vv, preferred_element_type=f32)
    delta = jnp.sum(probs * d_probs, axis=-1, keepdims=True)
    d_scores = probs * (d_probs - delta)
    gslope = -jnp.sum(d_scores * dist, axis=(0, 2, 3))
    d_raw = (d_scores * scale).astype(bf16)
    dq = jnp.einsum("shqk,skhd->sqhd", d_raw, kk, preferred_element_type=f32).astype(bf16)
    dk = jnp.einsum("shqk,sqhd->skhd", d_raw, q, preferred_element_type=f32).astype(bf16)
    dv = jnp.einsum("shqk,sqhd->skhd", probs_low, dm, preferred_element_type=f32).astype(bf16)
    dq, dk, dv = dq.reshape(T, Cw), dk.reshape(S, -1, Cw), dv.reshape(S, -1, Cw)
    flat = ctx.reshape(-1, M)
    gq = dot_tn(seg, dq)
    gk, gv = dot_tn(flat, dk.reshape(-1, Cw)), dot_tn(flat, dv.reshape(-1, Cw))
    own = lambda v: v[:, 2 * seg_len :].reshape(T, Cw)
    ig_part = dot_nt(jnp.concatenate([dq, own(dk), own(dv)], axis=1), Wqkv) + place(d_resid)
    input_grad = jnp.sum(spread(rows(ig_part), False, 7).astype(f32), axis=0)

    nw = seg_len // 3
    win = ctx[:, seg_len : 2 * seg_len].reshape(S, 3, nw, M)
    win = [win[:, k].reshape(S * nw, M) for k in range(3)]
    conv = sum(dot(win[k], WC[:, k * Cw : (k + 1) * Cw]) for k in range(3)) + cols(bconv)
    pooled = sum(cols(win[k]).astype(f32) for k in range(3)) * (1.0 / 3.0)
    mask = MK.reshape(S, nw, 128)[:, :, :1]
    old = (3 * jnp.arange(nw) + 3)[None, :, None] <= evicted[:, None, None]
    live = jnp.where(old, mask, 0.0).reshape(-1, 1)
    d_conv = live * (conv - pooled)
    gcb = jnp.sum(d_conv, axis=0)
    d_low = d_conv.astype(bf16)
    gconv = jnp.concatenate([dot_tn(win[k], d_low) for k in range(3)], axis=1)
    new_t = (mask.reshape(-1, 1) * conv).astype(bf16)
    NEW = spread(new_t, True, 8).reshape(nt, S, nw, Cw).transpose(1, 2, 0, 3).reshape(S, nw, M)
    slot_offset = seg_len - nw
    local_rows = jnp.arange(R, dtype=jnp.int32) + t * R
    padded = jnp.concatenate([jnp.zeros((S, slot_offset, M), bf16), NEW], axis=1)
    slot_rows = lax.dynamic_slice_in_dim(padded, t * R, R, 1)
    written = (local_rows[None, :] >= slot_offset) & (
        3 * (local_rows[None, :] - slot_offset) + 3 <= evicted[:, None]
    )
    new_compressed = jnp.where(written[..., None], slot_rows, compressed)
    new_memory = jnp.where((local_rows[None, :] < evicted[:, None])[..., None], segment, memory)

    low = lambda v, *s: v.astype(bf16).reshape(s)
    gs = lax.dynamic_update_slice_in_dim(jnp.zeros((128,), f32), gslope, t * ht, 0)
    sg = jnp.concatenate([gub, gdb, ggain, gbias, gcb, gs])
    sg = jnp.concatenate([sg, jnp.zeros((24 * 128 - sg.shape[0],), f32)]).reshape(24, 128)
    OD, OU, OC, OA, OS = reduce_all(
        nb,
        low(gdown, nb, 4, rd // 4, M),
        low(gup, nb, 4, rw, Fw),
        low(gconv, nb, 4, rw, 3 * Cw),
        low(jnp.concatenate([gq, gk, gv, gout], axis=1), nb, 4, rw, 4 * Cw),
        sg,
    )
    OA = OA.reshape(nt, rw, 4, Cw).transpose(2, 1, 0, 3).reshape(4, rw, M)
    OU = OU.reshape(nt, rw, nb, rd).transpose(1, 2, 0, 3).reshape(rw, nb * nt * rd)
    OC = OC.reshape(nt, rw, 3, Cw).transpose(2, 1, 0, 3).reshape(3, rw, M)
    OS = OS.reshape(nt, -1)
    vec = lambda o: lax.dynamic_slice_in_dim(OS[:, o : o + Cw].reshape(M), index * rs, rs)
    gub_out = lax.dynamic_slice(OS, (t, b * rd), (1, rd)).reshape(rd)
    gslopes = jnp.sum(OS[:, Fw + 4 * Cw : Fw + 4 * Cw + heads], axis=0)
    return (
        output,
        input_grad,
        new_memory,
        new_compressed,
        OA[0],
        OA[1],
        OA[2],
        OA[3],
        OU,
        gub_out,
        OD.reshape(rd, M),
        vec(Fw),
        vec(Fw + Cw),
        vec(Fw + 2 * Cw),
        OC,
        vec(Fw + 3 * Cw),
        gslopes,
    )


class Names:
    def __init__(self, names, refs):
        for name, ref in zip(names, refs):
            setattr(self, name, ref)


def layer_kernel(names, shape, *refs):
    r = Names(names, refs)
    nb, nu, S, ht, hd, M, Cw, rw, rd, rs = shape
    R = 16 * nu
    Hw = Cw // 2
    G, bq = nb // 2, nb // 4
    L = 16 * 4 * nu
    C3 = 3 * L
    nw = L // 3
    Fw = nb * rd
    scale = 1.0 / math.sqrt(hd)
    b, t, z, y, zs, zback = places(G)
    mate, ends = z ^ 1, (z == 0) | (z == G - 1)
    ypeer = (b ^ 1, t)
    tc = pl.ds(pl.multiple_of(t * Cw, Cw), Cw)
    sends = []

    def got(ref, sem):
        pltpu.make_async_copy(ref, ref, sem).wait()

    def left_all(ref, sem):
        sends.append((ref, sem))

    def each(n, body, between=None):
        def step(i, c):
            body(i)
            for at, then in (between or {}).items():
                pl.when(i == at)(then)
            return c

        lax.fori_loop(0, n, step, 0)

    def ex_send(e, sem, src, dst):
        for d in (1, 2, 3):
            remote(src(t ^ d), dst(d), r.es.at[e], sem, (b, t ^ d)).start()

    def spread_send(e, s, arr):
        at = arr.at[t, s]
        for d in (1, 2):
            remote(at, at, r.es.at[e], r.er.at[e, s, d - 1], (b, t ^ d)).start()

    def spread_pass(e, s, arr):
        at = arr.at[t ^ 2, s]
        got(at, r.er.at[e, s, 1])
        remote(at, at, r.es.at[e], r.er.at[e, s, 0], (b, t ^ 1)).start()

    def spread_wait(e, s, arr):
        @pl.when(s < S - 1)
        def _():
            spread_pass(e, s + 1, arr)

        got(arr.at[0:2, s], r.er.at[e, s, 0])

    folds = {
        2: (lambda q, s: r.DNP.at[q, s], r.DNR),
        4: (lambda q, s: r.DMP.at[q, s], r.DMR),
        5: (lambda q, s: r.OP.at[s, pl.ds(nu * q, nu)], r.OR),
        6: (lambda q, s: r.NRM.at[s, pl.ds(nu * q, nu)], r.IR),
    }

    def fold_send(e, s):
        out, into = folds[e]
        for i, d in enumerate((1, 3)):
            remote(out(t ^ d, s), into.at[i, s], r.es.at[e], r.er.at[e, s, i], (b, t ^ 1)).start()

    def fold_pass(e, s):
        out, into = folds[e]
        at, far = into.at[1, s], out(t ^ 2, s)
        got(at, r.er.at[e, s, 1])
        far[...] = (far[...].astype(f32) + at[...].astype(f32)).astype(bf16)
        remote(far, into.at[2, s], r.es.at[e], r.er.at[e, s, 0], (b, t ^ 2)).start()

    def fold_late(e, s):
        @pl.when(s > 0)
        def _():
            fold_pass(e, s - 1)

    def folded(e, s):
        out, into = folds[e]
        got(into.at[0:2, s], r.er.at[e, s, 0])
        return out(t, s)[...].astype(f32) + into[0, s].astype(f32) + into[2, s].astype(f32)

    def here(src, dst, i):
        cp = pltpu.make_async_copy(src, dst, r.lsem.at[i])
        cp.start()
        return cp

    wide = lambda at, size: pl.ds(pl.multiple_of(at, 128), size)
    mats = (r.w_query, r.w_key, r.w_value, r.w_output)
    whole = {"S": r.SM, "A": r.WA, "U": r.WU, "C": r.WC}
    index = {"S": 0, "A": 1, "U": 2, "C": 3, "H": 7}

    def tiers(n, at):
        return r.WCX.at[at] if n == "H" else whole[n].at[b, at]

    def cuts(n, q):
        if n == "S":
            return [(r.SM.at[b, t], r.SM.at[b, t])]
        if n == "A":
            return [(w.at[:, wide(Cw * q, Cw)], r.WA.at[b, t, :, i * Cw : (i + 1) * Cw]) for i, w in enumerate(mats)]
        if n == "U":
            return [
                (r.w_up.at[:, wide((4 * i + q) * rd, rd)], r.WU.at[b, t, :, i * rd : (i + 1) * rd]) for i in range(nb)
            ]
        half, to = (y, r.WC.at[b]) if n == "C" else (1 - y, r.WCX)
        return [
            (r.w_conv.at[i, :, wide(Cw * q + Hw * half, Hw)], to.at[t, :, i * Hw : (i + 1) * Hw]) for i in range(3)
        ]

    def tier_own(n):
        for src, dst in cuts(n, t):
            here(src, dst, index[n])

    def tier_start(n):
        i = index[n]
        for d in (1, 2, 3):
            for src, dst in cuts(n, t ^ d):
                remote(src, dst, r.ts.at[i], r.tr.at[i], (b, t ^ d)).start()
        left_all(tiers(n, slice(0, 3)), r.ts.at[i])

    def tier_wait(n):
        i = index[n]
        if n != "S":
            got(tiers(n, t), r.lsem.at[i])
        got(tiers(n, slice(0, 3)), r.tr.at[i])

    def if_(cond, body):
        pl.when(cond)(body)

    def at_ends(body):
        return lambda: if_(ends, body)

    def inside(body):
        return lambda: if_(~ends, body)

    def both(*bodies):
        def run():
            for body in bodies:
                body()

        return run

    right, left = (2 * z + 2 + y, t), (2 * z - 2 + y, t)
    parts = {"S": [(r.SM, 0, 0, 4, 0)], "C": [(r.WC, 1, 0, 4, 1)], "X": [(r.WC, 2, 0, 4, 2)]}
    for i, (n, w) in enumerate((("A", r.WA), ("U", r.WU))):
        parts[n] = [(w, 3 + 2 * i + h, h * 2, 2, 3 + i) for h in (0, 1)]
    for i, (n, at) in enumerate((("D", 0), ("E", rd // 2), ("F", rd // 2))):
        parts[n] = [(r.WD, 7 + i, at, rd // 2, 5 + i)]

    def chunk_of(n, part, zz, col=None):
        w, k, at, size, _ = part
        col = ((1 - y) if n in "XF" else y) if col is None else col
        return w.at[2 * zz + col, pl.ds(at, size)]

    def chunks(n, count):
        w, _, at, size, _ = parts[n][0]
        return w.at[0:count, at : at + size * len(parts[n])]

    def hop(part, at, zz, way):
        k = part[1]
        peer, past = (right, z < G - 1) if way == 0 else (left, z > 0)
        return past, remote(at, at, r.zs.at[part[4]], r.zr.at[k, zz - way], peer)

    def own_z(n):
        for part in parts[n]:
            for way in (0, 1):
                past, cp = hop(part, chunk_of(n, part, z), z, way)
                if_(past, cp.start)

    def own_y(n):
        for part in parts[n]:
            at, k = chunk_of(n, part, z), part[4]
            remote(r.WCX if n == "C" else at, at, r.ys.at[k], r.yr.at[k], ypeer).start()

    def arrivals(n, step, js):
        for j in js:
            for part in parts[n]:
                for way in (0, 1):
                    zz = z - j if way == 0 else z + j
                    step(part, j, way, zz, chunk_of(n, part, zz), zz >= 0 if way == 0 else zz < G)

    def onward(n, *js, cross=True):
        def step(part, j, way, zz, at, there):
            k = part[1]

            def body():
                got(at, r.zr.at[k, zz - way])
                if j < G - 1:
                    past, cp = hop(part, at, zz, way)
                    if_(past, cp.start)
                if n not in "CXEF" and cross:
                    remote(at, at, r.ys.at[part[4]], r.yr.at[part[4]], ypeer).start()

            if_(there, body)

        arrivals(n, step, js or range(1, G))

    def over(n, *js):
        def step(part, j, way, zz, at, there):
            if_(there, remote(at, at, r.ys.at[part[4]], r.yr.at[part[4]], ypeer).start)

        arrivals(n, step, js)

    def all_sent(n):
        k = parts[n][0][4]
        if_(ends, lambda: got(chunks(n, 1), r.zs.at[k]))
        if_(~ends, lambda: got(chunks(n, 5), r.zs.at[k]))
        if n not in "XF":
            got(chunks(n, 1 if n in "CE" else G), r.ys.at[k])

    def y_wait(n):
        got(chunks(n, 1 if n in "CE" else G), r.yr.at[parts[n][0][4]])

    def small_start():
        r.SM[b, t] = jnp.zeros((8, 128), f32)
        for q, v in enumerate((r.gain, r.bias, r.bdown, r.bconv, r.bup)):
            r.SM[b, t, q : q + 1, : v.shape[1]] = v[...].astype(f32)
        tier_start("S")

    def memory_rows():
        W = R // 3
        to, frm = (lax.broadcasted_iota(jnp.int32, (R, R), axis) for axis in (0, 1))
        tap = (to >= W).astype(jnp.int32) + (to >= 2 * W).astype(jnp.int32)
        order = (frm == 3 * (to - W * tap) + tap).astype(bf16)
        for s in range(S):
            rows = jnp.dot(order, r.MEMV[s], preferred_element_type=f32).astype(bf16)
            for i in range(3):
                r.CTX[s, 4 * nu + 4 * i + t] = rows[W * i : W * (i + 1)]
            square = lambda axis: lax.broadcasted_iota(jnp.int32, (R // 3, R // 3), axis)
            line = jnp.broadcast_to(r.mask[s : s + 1].astype(f32), (R // 3, R // 3))
            col = jnp.sum(jnp.where(square(0) == square(1), line, 0.0), axis=1, keepdims=True)
            spot = lax.broadcasted_iota(jnp.int32, (R // 3, 128), 0) + (R // 3) * t
            lane = lax.broadcasted_iota(jnp.int32, (R // 3, 128), 1)
            r.MK[s, t] = jnp.where((lane < 64) | (3 * spot + 3 <= r.evicted[s]), col, 0.0)

    def rows_of(src, buf, first):
        at = lambda q: buf.at[:, pl.ds(first + nu * q, nu)]
        parts = [(src.at[:, 16 * i : 16 * i + 16], buf.at[:, first + nu * t + i]) for i in range(nu)]
        return parts, at, True

    def held(at):
        return [(at(t), at(t))], at, False

    def memory_y():
        for i in range(3):
            remote(r.CTX.at[:, 4 * nu + 4 * i + t], r.MEMX.at[:, 4 * i + t], r.ms.at[0], r.ms.at[1], ypeer).start()
        remote(r.MK.at[:, t], r.MKX.at[:, t], r.ms.at[2], r.ms.at[3], ypeer).start()
        left_all(r.MEMX.at[:, 0:3], r.ms.at[0])
        left_all(r.MKX.at[:, 0], r.ms.at[2])

    def memory_come():
        got(r.MEMX.at[:, 0:3], r.ms.at[1])
        got(r.MKX.at[:, 0], r.ms.at[3])

    pieces = [
        rows_of(r.seg, r.CTX, 8 * nu),
        rows_of(r.comp, r.CTX, 0),
        held(lambda q: r.CTX.at[:, 4 * nu + q]),
        held(lambda q: r.CTX.at[:, 4 * nu + 4 + q]),
        held(lambda q: r.CTX.at[:, 4 * nu + 8 + q]),
        rows_of(r.cot, r.COT, 0),
        held(lambda q: r.MK.at[:, q]),
        held(lambda q: r.MEMX.at[:, q]),
        held(lambda q: r.MEMX.at[:, 4 + q]),
        held(lambda q: r.MEMX.at[:, 8 + q]),
        held(lambda q: r.MKX.at[:, q]),
    ]

    group = lambda i: 0 if i < 5 else (1, 2, 3, 3, 3, 4)[i - 5]
    grouped = [(r.CTX, 3 * nu), (r.COT, nu), (r.MK, 1), (r.MEMX, 3), (r.MKX, 1)]

    def act_own():
        for i, (cut, at, far) in enumerate(pieces):
            if far:
                for src, dst in cut:
                    here(src, dst, 4 + group(i))

    def act_start(*which):
        for i in which:
            cut, at, far = pieces[i]
            g = group(i)
            for src, dst in cut:
                remote(src, dst, r.acs.at[g], r.acc.at[g], (b, t ^ 1)).start()
                remote(src, dst, r.acs.at[g], r.acx.at[i], (b, t ^ 2)).start()

    def act_forward(*which):
        for i in which:
            at = pieces[i][1](t ^ 2)
            got(at, r.acx.at[i])
            remote(at, at, r.acs.at[group(i)], r.acf.at[group(i)], (b, t ^ 1)).start()

    def act_wait(g):
        buf, n = grouped[g]
        got(buf.at[:, 0:n], r.acc.at[g])
        got(buf.at[:, 0:n], r.acf.at[g])
        if g < 2:
            got(buf.at[:, 0 : n if g else 2 * nu], r.lsem.at[4 + g])

    def act_sent():
        for g, (buf, n) in enumerate(grouped):
            got(buf.at[:, 0 : 3 * n], r.acs.at[g])

    def table():
        row = lax.broadcasted_iota(jnp.int32, (L, C3), 0) + 2 * L
        col = lax.broadcasted_iota(jnp.int32, (L, C3), 1)
        inner = col - L
        k1 = (inner >= nw).astype(jnp.int32)
        k2 = (inner >= 2 * nw).astype(jnp.int32)
        win = inner - nw * (k1 + k2)
        pos = jnp.where((col >= L) & (col < 2 * L), L + 3 * win + k1 + k2, col)
        r.DIST[...] = jnp.where(pos <= row, (row - pos).astype(f32) * (1.0 / C3), 1e30)
        r.SMG[...] = jnp.zeros_like(r.SMG)

    def seg_rows(s):
        return r.CTX[s, 8 * nu : 12 * nu].reshape(L, M)

    def project(s):
        rows = r.CTX[s].reshape(C3, M)
        kv = jnp.dot(rows, r.WA[:, :, :, Cw : 3 * Cw].reshape(M, 2 * Cw), preferred_element_type=f32)
        r.KV[s] = kv.astype(bf16)
        q = jnp.dot(seg_rows(s), r.WA[:, :, :, :Cw].reshape(M, Cw), preferred_element_type=f32)
        r.Q[s] = q.astype(bf16)


    def attend(s):
        for h in range(ht):
            c = slice(h * hd, (h + 1) * hd)
            raw = dot_nt(r.Q[s, :, c], r.KV[s, :, c])
            scores = raw * scale - r.slopes[t * ht + h] * r.DIST[...]
            e = jnp.exp(scores - jnp.max(scores, axis=1, keepdims=True))
            p = e * (1.0 / jnp.sum(e, axis=1, keepdims=True))
            r.PR[s, h] = p
            v = r.KV[s, :, Cw + h * hd : Cw + (h + 1) * hd]
            r.MIX[t, s, :, c] = jnp.dot(p.astype(bf16), v, preferred_element_type=f32).astype(bf16)
        spread_send(0, s, r.MIX)


    def wo(q):
        return r.WA[bq * q : bq * (q + 1), :, :, 3 * Cw :].reshape(Cw, Cw)

    def residual(s):
        spread_wait(0, s, r.MIX)
        acc = r.CTX[s, 8 * nu : 12 * nu, :, tc].reshape(L, Cw).astype(f32)
        for q in range(4):
            acc = acc + jnp.dot(r.MIX[q, s], wo(q), preferred_element_type=f32)
        r.RT[s] = acc
        r.RES[t, s] = acc.astype(bf16)
        spread_send(1, s, r.RES)

    def vectors():
        lane = lax.broadcasted_iota(jnp.int32, (8, 128), 1)
        for at in range(0, M, 128):
            block = jnp.zeros((8, 128), f32)
            for i in range(128 // rs):
                spot = at // rs + i
                turned = pltpu.roll(r.SM[spot // 4, spot % 4], rs * i, 1)
                block = jnp.where((lane >= rs * i) & (lane < rs * (i + 1)), turned, block)
            r.VV[0:4, at : at + 128] = block[0:4]
        for bb in range(nb):
            r.VV[4:5, bb * rd : (bb + 1) * rd] = r.SM[bb, t, 4:5, :rd]

    def xhat_of(s, q):
        return (r.RES[q, s].astype(f32) - r.MU[s, :, :1]) * r.MU[s, :, 1:2]

    def feed(s):
        spread_wait(1, s, r.RES)
        parts = [r.RES[q, s].astype(f32) for q in range(4)]
        mu = sum(jnp.sum(x, axis=1, keepdims=True) for x in parts) * (1.0 / M)
        var = sum(jnp.sum((x - mu) * (x - mu), axis=1, keepdims=True) for x in parts) * (1.0 / M)
        inv = lax.rsqrt(var + norm_eps)
        lane = lax.broadcasted_iota(jnp.int32, (L, 128), 1)
        r.MU[s] = jnp.where(lane == 0, mu, inv)
        for q in range(4):
            c = slice(q * Cw, (q + 1) * Cw)
            rows = ((parts[q] - mu) * inv) * r.VV[0:1, c] + r.VV[1:2, c]
            r.NRM[s, :, :, c] = rows.astype(bf16).reshape(4 * nu, 16, Cw)
        fb = Fw // 4
        for j in range(4):
            c = slice(j * fb, (j + 1) * fb)
            pre = jnp.dot(r.NRM[s].reshape(L, M), r.WU[:, :, :, c].reshape(M, fb), preferred_element_type=f32) + r.VV[4:5, c]
            phi = 0.5 + 0.5 * lax.erf(pre * math.sqrt(0.5))
            r.ACT[s, :, c] = (pre * phi).astype(bf16)
            r.GP[s, :, c] = (phi + pre * (jnp.exp(-0.5 * pre * pre) * (1.0 / math.sqrt(2 * math.pi)))).astype(bf16)


    def turn(j):
        low = lax.rem(G - j, G)
        inner = jnp.where(z == 1, low, G - 1 - low)
        return jnp.where(z == 0, G - 1 - j, jnp.where(z == G - 1, j, inner))

    grads = {0: (r.GD, r.YD, r.ZD), 1: (r.GU, r.YU, r.ZU), 3: (r.WU, r.YA, r.ZA)}

    def to_y(k, zz):
        g, yb, zb = grads[k]
        remote(g.at[2 * zz + (1 - y)], yb.at[zz], r.gys.at[k], r.gyr.at[k, zz], ypeer).start()

    def plus(into, *others):
        def add(i):
            acc = into[i].astype(f32)
            for o in others:
                acc = acc + o[i].astype(f32)
            into[i] = acc.astype(bf16)

        each(into.shape[0], add)

    def pass_on(i, at, zb, o, sem):
        @pl.when((o != mate) & ~ends)
        def _():
            slot = lax.rem(o, 2)
            got(zb.at[slot], r.gzr.at[sem, slot])
            plus(at, zb.at[slot])

        to = jnp.where(ends, mate, o)
        slot = jnp.where(o == mate, 2, jnp.where(ends, lax.rem(o, 2), 3))
        remote(at, zb.at[slot], r.gzs.at[sem], r.gzr.at[sem, jnp.minimum(slot, 2)], (2 * to + y, t)).start()

    straight = ()

    def mid(k, *steps):
        g, yb, zb = grads[k]
        for i in steps or range(G - 1):
            o = turn(i)
            at = yb.at[o]
            got(at, r.gyr.at[k, o])
            plus(at, g.at[2 * o + y])
            if k in straight:
                remote(at, zb.at[z], r.gzs.at[k], r.gzr.at[k, 2], (2 * o + y, t)).start()
            else:
                pass_on(i, at, zb, o, k)

    def mid_c(*steps):
        for i in steps or range(G - 1):
            o = turn(i)
            for c, col in enumerate((1 - y, y)):
                pass_on(i, r.GC.at[2 * o + col], r.ZC.at[c], o, 4 + c)

    def arrived(zb, sem):
        n = 3 if sem in straight else 2
        got(zb.at[4 - n : 4], r.gzr.at[sem, 2])
        return [zb.at[lax.rem(z + d, G)] for d in range(1, G)] if n == 3 else [zb.at[2], zb.at[3]]

    def summed(at, more, store):
        def total(i):
            acc = at[i].astype(f32)
            for o in more:
                acc = acc + o[i].astype(f32)
            store(i, acc)

        each(4, total)

    def fin(k, store):
        g, yb, zb = grads[k]
        at = yb.at[z]
        got(at, r.gyr.at[k, z])
        summed(at, arrived(zb, k) + [g.at[2 * z + y]], store)

    def cross_c():
        come = arrived(r.ZC.at[0], 4)
        other = r.GC.at[2 * z + 1 - y]

        def store(i, acc):
            other[i] = acc.astype(bf16)

        summed(other, come, store)
        remote(other, r.YC, r.gys.at[4], r.gyr.at[4, 0], ypeer).start()

    def fin_c(store):
        summed(r.GC.at[2 * z + y], arrived(r.ZC.at[1], 5), store)

    def crossed_c():
        got(r.YC, r.gyr.at[4, 0])

    def reduced_sent():
        for k, (g, yb, zb) in grads.items():
            got(g.at[0:G], r.gys.at[k])
            got(g.at[0:3], r.gzs.at[k])
        got(r.YC, r.gys.at[4])
        for sem in (4, 5):
            got(r.GC.at[0:3], r.gzs.at[sem])

    fb = Fw // 4

    def grad_down(i):
        j = turn(i)
        c = pl.ds(pl.multiple_of(j * fb, fb), fb)
        rows = r.ACT[:, :, c].reshape(S * L, fb)
        g = dot_tn(rows, r.COT[...].reshape(S * L, M)).astype(bf16)
        r.GD[pl.ds(j * bq, bq)] = g.reshape(bq, 4, rd // 4, M)
        to_y(0, j)


    def back_feed(s):
        cot = r.COT[s].reshape(L, M)
        for j in range(4):
            c = slice(j * fb, (j + 1) * fb)
            wd = r.WD[bq * j : bq * (j + 1)].reshape(fb, M)
            d_act = dot_nt(cot, wd).astype(bf16).astype(f32)
            d_pre = d_act * r.GP[s, :, c].astype(f32)
            total = jnp.sum(d_pre, axis=0, keepdims=True)
            for i in range(fb // 128):
                at = j * (fb // 128) + i
                r.SMG[at : at + 1] += total[:, 128 * i : 128 * (i + 1)]
            r.GP[s, :, c] = d_pre.astype(bf16)
        m1 = jnp.zeros((L, 1), f32)
        m2 = jnp.zeros((L, 1), f32)
        for q in range(4):
            c = slice(q * Cw, (q + 1) * Cw)
            dn = dot_nt(r.GP[s], r.WU[bq * q : bq * (q + 1)].reshape(Cw, Fw))
            g = dn * r.VV[0:1, c]
            m1 = m1 + jnp.sum(g, axis=1, keepdims=True)
            m2 = m2 + jnp.sum(g * xhat_of(s, q), axis=1, keepdims=True)
            r.DNP[q, s] = dn.astype(bf16)
        lane = lax.broadcasted_iota(jnp.int32, (L, 128), 1)
        both = jnp.where(lane == 0, m1, jnp.where(lane == 1, m2, 0.0)) * (1.0 / M)
        pick = (
            lax.broadcasted_iota(jnp.int32, (8, 128), 0) == lax.broadcasted_iota(jnp.int32, (8, 128), 1)
        ).astype(f32)
        r.ST[t, s] = lax.dot_general(
            pick, both, (((1,), (1,)), ((), ())), precision=lax.Precision.HIGHEST, preferred_element_type=f32
        )
        fold_send(2, s)
        ex_send(3, r.er.at[3, s, 0], lambda q: r.ST.at[t, s], lambda d: r.ST.at[t, s])
        fold_late(2, s)


    def grad_up(i):
        j = turn(i)
        c = pl.ds(pl.multiple_of(j * Cw, Cw), Cw)
        rows = r.NRM[:, :, :, c].reshape(S * L, Cw)
        g = dot_tn(rows, r.GP[...].reshape(S * L, Fw)).astype(bf16)
        r.GU[pl.ds(j * bq, bq)] = g.reshape(bq, 4, rw, Fw)
        to_y(1, j)


    def back_norm(s):
        dn = folded(2, s)
        got(r.ST.at[0:3, s], r.er.at[3, s, 0])
        st = r.ST[0, s] + r.ST[1, s] + r.ST[2, s] + r.ST[3, s]
        side = lax.broadcasted_iota(jnp.int32, (8, 128), 0)
        col_of = lambda i: lax.dot_general(
            st,
            (side == i).astype(f32),
            (((0,), (0,)), ((), ())),
            precision=lax.Precision.HIGHEST,
            preferred_element_type=f32,
        )[:, :1]
        m1, m2 = col_of(0), col_of(1)
        inv = r.MU[s, :, 1:2]
        xhat = (r.RES[t, s].astype(f32) - r.MU[s, :, :1]) * inv
        cot = r.COT[s, :, :, tc].reshape(L, Cw).astype(f32)
        for i, v in enumerate((cot, dn * xhat, dn)):
            total = jnp.sum(v, axis=0, keepdims=True)
            for k in range(Cw // 128):
                at = Fw // 128 + i * (Cw // 128) + k
                r.SMG[at : at + 1] += total[:, 128 * k : 128 * (k + 1)]
        d_resid = cot + (dn * r.VV[0:1, tc] - m1 - xhat * m2) * inv
        r.DR[s] = d_resid
        db = d_resid.astype(bf16)
        r.DB[s] = db
        for q in range(4):
            r.DMP[q, s] = dot_nt(db, wo(q)).astype(bf16)
        fold_send(4, s)
        fold_late(4, s)

    def grad_out():
        for q in range(4):
            g = dot_tn(r.MIX[q].reshape(S * L, Cw), r.DB[...].reshape(S * L, Cw))
            r.GA[bq * q : bq * (q + 1), :, :, 3 * Cw :] = g.astype(bf16).reshape(bq, 4, rw, Cw)
        by_tier(slice(None), slice(3 * Cw, 4 * Cw), r.xs.at[1], r.xr.at[G])

    def by_tier(rows, c, sent, come):
        for d in (1, 2, 3):
            remote(r.GA.at[rows, t ^ d, :, c], r.WU.at[rows, t, :, c], sent, come, (b, t ^ d)).start()
        r.WU[rows, t, :, c] = r.GA[rows, t, :, c]

    def out_rows(s):
        for q in range(4):
            c = slice(q * Cw, (q + 1) * Cw)
            o = jnp.dot(r.ACT[s], r.WD[:, :, c].reshape(Fw, Cw), preferred_element_type=f32)
            mine = (t == q).astype(f32)
            o = o + mine * (r.RT[s] + r.VV[2:3, c])
            r.OP[s, :, :, c] = o.astype(bf16).reshape(4 * nu, 16, Cw)
        fold_send(5, s)
        fold_late(5, s)


    hc = wide(t * Cw + Hw * y, Hw)

    def windows(k, g):
        buf, at = (r.MEMX, 4 * k) if g else (r.CTX, 4 * nu + 4 * k)
        return buf.at[:, at : at + 4]

    def compress():
        sums = jnp.zeros((1, Hw), f32)
        for g in (0, 1):
            conv = r.VV[3:4, hc]
            pooled = 0.0
            for k in range(3):
                wk = r.WC[:, :, :, k * Hw : (k + 1) * Hw].reshape(M, Hw)
                conv = conv + jnp.dot(windows(k, g)[...].reshape(S * nw, M), wk, preferred_element_type=f32)
                pooled = pooled + windows(k, g)[:, :, :, hc].reshape(S * nw, Hw).astype(f32)
            marks = (r.MKX if g else r.MK)[...].reshape(S * nw, 128)
            fresh = (marks[:, :1] * conv).astype(bf16).reshape(S, nw, Hw)
            if g:
                r.NEWX[...] = fresh
            else:
                r.NEW[t, :, :, wide(Hw * y, Hw)] = fresh
            d_conv = marks[:, 64:65] * (conv - pooled * (1.0 / 3.0))
            sums = sums + jnp.sum(d_conv, axis=0, keepdims=True)
            r.DC[g] = d_conv.astype(bf16)
        r.SMG[pl.ds(Fw // 128 + 3 * (Cw // 128) + y, 1)] = sums
        remote(r.NEWX, r.NEW.at[t, :, :, wide(Hw * y, Hw)], r.ns.at[2], r.ns.at[3], ypeer).start()
        left_all(r.NEWX, r.ns.at[2])
        for k in range(3):
            grad = sum(dot_tn(windows(k, g)[...].reshape(S * nw, M), r.DC[g]) for g in (0, 1))
            r.GC[:, :, :, k * Hw : (k + 1) * Hw] = grad.astype(bf16).reshape(nb, 4, rw, Hw)

    slope_row = Fw // 128 + 4 * (Cw // 128)

    def back_attend(s):
        dm = folded(4, s).astype(bf16)
        lane = lax.broadcasted_iota(jnp.int32, (1, 128), 1)
        for h in range(ht):
            c = slice(h * hd, (h + 1) * hd)
            cv = slice(Cw + h * hd, Cw + (h + 1) * hd)
            p = r.PR[s, h]
            dp = dot_nt(dm[:, c], r.KV[s, :, cv])
            delta = jnp.sum(p * dp, axis=1, keepdims=True)
            ds = p * (dp - delta)
            part = jnp.sum(jnp.sum(ds * r.DIST[...], axis=0, keepdims=True), axis=1, keepdims=True)
            r.SMG[slope_row : slope_row + 1] -= jnp.where(lane == t * ht + h, part, 0.0)
            dr = (ds * scale).astype(bf16)
            dq = jnp.dot(dr, r.KV[s, :, c], preferred_element_type=f32).astype(bf16)
            dk = dot_tn(dr, r.Q[s, :, c]).astype(bf16)
            dv = dot_tn(p.astype(bf16), dm[:, c]).astype(bf16)
            r.Q[s, :, c] = dq
            r.KV[s, :, c] = dk
            r.KV[s, :, cv] = dv


    def grad_proj(i):
        j = turn(i)
        c = pl.ds(pl.multiple_of(j * Cw, Cw), Cw)
        gq = jnp.zeros((Cw, Cw), f32)
        gkv = jnp.zeros((Cw, 2 * Cw), f32)
        for s in range(S):
            gq = gq + dot_tn(r.CTX[s, 8 * nu : 12 * nu, :, c].reshape(L, Cw), r.Q[s])
            gkv = gkv + dot_tn(r.CTX[s, :, :, c].reshape(C3, Cw), r.KV[s])
        rows = pl.ds(j * bq, bq)
        r.GA[rows, :, :, :Cw] = gq.astype(bf16).reshape(bq, 4, rw, Cw)
        r.GA[rows, :, :, Cw : 3 * Cw] = gkv.astype(bf16).reshape(bq, 4, rw, 2 * Cw)
        by_tier(rows, slice(0, 3 * Cw), r.xs.at[0], r.xr.at[j])

    def proj_y(*steps):
        for i in steps:
            j = turn(i)
            if i == 0:
                got(r.WU.at[:, 0:3, :, 3 * Cw :], r.xr.at[G])
            got(r.WU.at[pl.ds(j * bq, bq), 0:3, :, : 3 * Cw], r.xr.at[j])
            to_y(3, j)

    def own_out(s):
        r.OR[1, s] = folded(5, s).astype(bf16)

    def input_rows(s):
        x = jnp.concatenate([r.Q[s], r.KV[s, 2 * L :]], axis=1)
        for q in range(4):
            c = slice(q * Cw, (q + 1) * Cw)
            w = r.WA[bq * q : bq * (q + 1), :, :, : 3 * Cw].reshape(Cw, 3 * Cw)
            o = dot_nt(x, w) + (t == q).astype(f32) * r.DR[s]
            r.NRM[s, :, :, c] = o.astype(bf16).reshape(4 * nu, 16, Cw)
        fold_send(6, s)
        fold_late(6, s)


    def keep(o):
        def store(i, acc):
            o[pl.ds(i * (rd // 4), rd // 4)] = acc

        return store

    def across(q, acc):
        for i in range(4):
            r.OA[i, :, wide(q * Cw, Cw)] = acc[:, i * Cw : (i + 1) * Cw]

    def hold(m):
        def store(i, acc):
            m[i] = acc.astype(bf16)

        return store

    def tier_back(k, m, tb):
        for d in (1, 2, 3):
            remote(m.at[t ^ d], tb.at[t], r.gts.at[k], r.gtr.at[k], (b, t ^ d)).start()
        left_all(tb.at[0:3], r.gts.at[k])

    def small_y():
        remote(r.SMG, r.YS, r.ss.at[0], r.sr.at[0], ypeer).start()
        left_all(r.SMG, r.ss.at[0])

    def small_z():
        got(r.YS, r.sr.at[0])
        r.ZS[z] = r.SMG[...] + r.YS[...]
        for d in range(1, G):
            remote(r.ZS.at[z], r.ZS.at[z], r.ss.at[1], r.sr.at[1], (2 * zs[d] + y, t)).start()
        left_all(r.ZS.at[0 : G - 1], r.ss.at[1])

    def small_tier():
        got(r.ZS.at[0 : G - 1], r.sr.at[1])
        acc = r.ZS[0]
        for zz in range(1, G):
            acc = acc + r.ZS[zz]
        r.os[t] = acc
        for d in (1, 2, 3):
            remote(r.os.at[t], r.os.at[t], r.gts.at[3], r.gtr.at[3], (b, t ^ d)).start()
        left_all(r.os.at[0:3], r.gts.at[3])

    def own_input(s):
        r.IG[s] = folded(6, s)

    mineU, mineC = (g.at[2 * z + y] for g in (r.GU, r.GC))
    def give(i, src, dst):
        pltpu.make_async_copy(src, dst, r.osem.at[i]).start()

    def rows_out(i, src, dst):
        for j in range(nu):
            give(i, src.at[:, j], dst.at[:, 16 * j : 16 * j + 16])

    backs = {0: (mineU, r.TU), 1: (mineC, r.TC), 4: (r.YC, r.TB)}

    def lay(k, q, rows):
        if k == 0:
            for i in range(nb):
                r.OU[:, wide((4 * i + q) * rd, rd)] = rows[:, i * rd : (i + 1) * rd].astype(f32)
        else:
            half = y if k == 1 else 1 - y
            for i in range(3):
                r.OC[i, :, wide(q * Cw + Hw * half, Hw)] = rows[:, i * Hw : (i + 1) * Hw].astype(f32)

    def tier_out(k):
        m, tb = backs[k]
        lay(k, t, m[t])
        got(tb.at[0:3], r.gtr.at[k])
        for d in (1, 2, 3):
            lay(k, t ^ d, tb[t ^ d])

    def given():
        for i, (src, dst) in ((0, (r.OU, r.ou)), (1, (r.OC, r.oc)), (2, (r.OA, r.oa)), (3, (r.OD, r.od))):
            pltpu.make_async_copy(src, dst, r.osem.at[i]).wait()
        for i, (src, dst) in ((5, (r.OR.at[1], r.out)), (6, (r.IG, r.ig)), (4, (r.OR.at[0], r.om)), (8, (r.OR.at[2], r.ocm))):
            for j in range(nu):
                pltpu.make_async_copy(src.at[:, j], dst.at[:, 16 * j : 16 * j + 16], r.osem.at[i]).wait()

    def small_out():
        got(r.os.at[0:3], r.gtr.at[3])

    slots = L - nw
    windows_of = [(q, max(R * q - slots, 0), R - max(slots - R * q, 0)) for q in range(4) if slots < R * (q + 1)]

    def new_send():
        got(r.NEWX, r.ns.at[3])
        for q, at, n in windows_of:
            part = r.NEW.at[t, :, at : at + n]
            if_(t != q, remote(part, part, r.ns.at[0], r.ns.at[1], (b, q)).start)

    def new_sent():
        for q, at, n in windows_of:
            if_(t != q, lambda: got(r.NEW.at[0, :, at : at + n], r.ns.at[0]))

    def new_out():
        for q, at, n in windows_of:
            if_(t == q, lambda: got(r.NEW.at[0:3, :, at : at + n], r.ns.at[1]))

    def memories():
        side = lax.broadcasted_iota(jnp.int32, (16, 1), 0)
        for s in range(S):
            for i in range(nu):
                fresh = side + (R * t + 16 * i) < r.evicted[s]
                r.OR[0, s, i] = jnp.where(fresh, r.CTX[s, 8 * nu + nu * t + i], r.MEMV[s, 16 * i : 16 * i + 16])
                r.OR[2, s, i] = r.CTX[s, nu * t + i]
        for q, at, n in windows_of:

            @pl.when(t == q)
            def _(at=at, n=n):
                for i in range((R - n) // 16, nu):
                    w = at + 16 * i - (R - n)
                    for s in range(S):
                        written = 3 * (side + w) + 3 <= r.evicted[s]
                        for p in range(4):
                            c = slice(p * Cw, (p + 1) * Cw)
                            old = r.CTX[s, nu * t + i, :, c]
                            r.OR[2, s, i, :, c] = jnp.where(written, r.NEW[p, s, w : w + 16], old)

    def drain():
        for n in parts:
            if n != "U":
                all_sent(n)
        got(r.GA.at[:, 0:3, :, : 3 * Cw], r.xs.at[0])
        got(r.GA.at[:, 0:3, :, 3 * Cw :], r.xs.at[1])
        for ref, sem in sends:
            got(ref, sem)
        act_sent()
        new_sent()
        reduced_sent()
        for e, ref in enumerate((r.MIX, r.RES, r.DNP, r.ST, r.DMP, r.OR, r.IR)):
            got(ref.at[0:3], r.es.at[e])
        given()

    here(r.wd, r.WD.at[b], 0)
    here(r.mem, r.MEMV, 6)
    for n in "ACHU":
        tier_own(n)
    act_own()
    greet(G, True, True)
    tier_start("A")
    tier_start("H")
    small_start()
    tier_start("U")
    tier_start("C")
    act_start(0, 1)
    got(r.WD.at[b], r.lsem.at[0])
    own_z("D")
    own_z("E")
    own_y("E")
    own_y("D")
    got(r.MEMV, r.lsem.at[6])
    memory_rows()
    act_start(2, 3, 4, 5, 6)
    tier_wait("A")
    own_z("A")
    own_y("A")
    tier_wait("H")
    own_y("C")
    tier_wait("S")
    own_z("S")
    own_y("S")
    table()
    onward("A", 1)
    onward("S", 1)
    onward("A", 2)
    onward("S", 2)
    tier_wait("U")
    own_z("U")
    y_wait("E")
    own_z("F")
    onward("A", 3)
    own_y("U")
    onward("S", 3)
    onward("U", 1)
    act_forward(0, 1, 2, 3, 4)
    act_wait(0)
    y_wait("A")
    each(S, project, {0: lambda: onward("U", 2), 1: lambda: onward("D", 1, cross=False)})
    onward("E", 1)
    tier_wait("C")
    y_wait("C")
    each(S, attend, {1: lambda: onward("U", 3)})
    memory_y()
    over("D", 1)
    onward("F", 1)
    onward("D", 2)
    own_z("C")
    own_z("X")
    spread_pass(0, 0, r.MIX)
    each(S, residual, {1: lambda: onward("E", 2)})
    onward("F", 2)
    onward("D", 3)
    onward("C", 1)
    y_wait("S")
    vectors()
    act_forward(5, 6)
    y_wait("U")
    spread_pass(1, 0, r.RES)
    each(S, feed, {0: lambda: onward("X", 1), 2: lambda: onward("E", 3)})
    memory_come()
    act_start(7, 8, 9, 10)
    onward("F", 3)
    act_wait(1)
    act_wait(2)
    onward("C", 2)
    each(4, grad_down, {2: lambda: onward("X", 2)})
    y_wait("D")
    all_sent("U")
    each(
        S,
        back_feed,
        {
            0: lambda: onward("C", 3),
            1: lambda: mid(0, 0),
            2: both(lambda: onward("X", 3), lambda: act_forward(7, 8, 9, 10)),
            3: at_ends(lambda: mid(0, 1)),
        },
    )
    act_wait(3)
    act_wait(4)
    compress()
    fold_pass(2, S - 1)
    inside(lambda: mid(0, 1))()
    each(S, out_rows)
    mid_c(0)
    each(4, grad_up)
    mid(0, 2)
    fold_pass(5, S - 1)
    each(S, back_norm)
    fold_pass(4, S - 1)
    grad_out()
    mid_c(1)
    each(S, back_attend, {2: lambda: mid(1, 0)})
    mid_c(2)
    small_y()
    new_send()
    each(4, grad_proj, {1: at_ends(lambda: mid(1, 1))})
    inside(lambda: mid(1, 1))()
    at_ends(lambda: mid(1, 2))()
    proj_y(0)
    each(S, input_rows)
    proj_y(1)
    cross_c()
    fold_pass(6, S - 1)
    small_z()
    inside(lambda: mid(1, 2))()
    proj_y(2)
    fin_c(hold(mineC))
    tier_back(1, mineC, r.TC)
    fin(0, keep(r.OD))
    give(3, r.OD, r.od)
    mid(3, 0)
    proj_y(3)
    fin(1, hold(mineU))
    tier_back(0, mineU, r.TU)
    crossed_c()
    tier_back(4, r.YC, r.TB)
    each(S, own_out)
    rows_out(5, r.OR.at[1], r.out)
    new_out()
    memories()
    rows_out(4, r.OR.at[0], r.om)
    rows_out(8, r.OR.at[2], r.ocm)
    mid(3, 1)
    small_tier()
    mid(3, 2)
    each(S, own_input)
    rows_out(6, r.IG, r.ig)
    tier_out(1)
    tier_out(4)
    give(1, r.OC, r.oc)
    tier_out(0)
    give(0, r.OU, r.ou)
    fin(3, across)
    give(2, r.OA, r.oa)
    small_out()
    drain()

def whole_layer(nb, ht, hd, arrays):
    S, R, M = arrays["seg"].shape
    rw, rd, rs = arrays["w_query"].shape[0], arrays["wd"].shape[0], M // (4 * nb)
    nu = R // 16
    G, Cw, Fw, L = nb // 2, M // 4, nb * rd, 64 * nu
    dma = pltpu.SemaphoreType.DMA
    V = lambda shape, dtype=bf16: pltpu.VMEM(shape, dtype)
    D4, A4, U4, C4 = (4, rd // 4, M), (4, rw, 4 * Cw), (4, rw, Fw), (4, rw, 3 * Cw // 2)
    ins = arrays
    outs = dict(
        out=((S, R, M), bf16),
        ig=((S, R, M), f32),
        om=((S, R, M), bf16),
        ocm=((S, R, M), bf16),
        od=((rd, M), f32),
        ou=((rw, 4 * Fw), f32),
        oc=((3, rw, M), f32),
        oa=((4, rw, M), f32),
        os=((4, 24, 128), f32),
    )
    scratch = dict(
        WA=V((nb,) + A4),
        WU=V((nb,) + U4),
        WC=V((nb,) + C4),
        WCX=V(C4),
        MEMX=V((S, 12, 16, M)),
        MKX=V((S, 4, L // 12, 128), f32),
        NEWX=V((S, L // 3, Cw // 2)),
        WD=V((nb, rd, M)),
        SM=V((nb, 4, 8, 128), f32),
        CTX=V((S, 12 * nu, 16, M)),
        COT=V((S, 4 * nu, 16, M)),
        MK=V((S, 4, L // 12, 128), f32),
        DIST=V((L, 3 * L), f32),
        VV=V((8, max(M, Fw)), f32),
        SMG=V((24, 128), f32),
        Q=V((S, L, Cw)),
        KV=V((S, 3 * L, 2 * Cw)),
        PR=V((S, ht, L, 3 * L), f32),
        MIX=V((4, S, L, Cw)),
        RT=V((S, L, Cw), f32),
        RES=V((4, S, L, Cw)),
        MU=V((S, L, 128), f32),
        NRM=V((S, 4 * nu, 16, M)),
        ACT=V((S, L, Fw)),
        GP=V((S, L, Fw)),
        DNP=V((4, S, L, Cw)),
        DNR=V((3, S, L, Cw)),
        ST=V((4, S, 8, L), f32),
        DR=V((S, L, Cw), f32),
        DB=V((S, L, Cw)),
        DMP=V((4, S, L, Cw)),
        DMR=V((3, S, L, Cw)),
        OP=V((S, 4 * nu, 16, M)),
        OR=V((3, S, nu, 16, M)),
        IR=V((3, S, nu, 16, M)),
        DC=V((2, S * L // 3, Cw // 2)),
        GD=V((nb,) + D4),
        GU=V((nb,) + U4),
        GC=V((nb,) + C4),
        GA=V((nb,) + A4),
        YD=V((G,) + D4),
        YU=V((G,) + U4),
        YC=V(C4),
        YA=V((G,) + A4),
        ZD=V((4,) + D4),
        ZU=V((4,) + U4),
        ZC=V((2, 4) + C4),
        ZA=V((4,) + A4),
        YS=V((24, 128), f32),
        ZS=V((G, 24, 128), f32),
        TU=V(U4),
        TC=V(C4),
        TB=V(C4),
        NEW=V((4, S, L // 3, Cw)),
        IG=V((S, nu, 16, M), f32),
        OD=V((rd, M), f32),
        OU=V((rw, 4 * Fw), f32),
        OC=V((3, rw, M), f32),
        OA=V((4, rw, M), f32),
        MEMV=V((S, R, M)),
        osem=dma((9,)),
        lsem=dma((8,)),
        ts=dma((8,)),
        tr=dma((8,)),
        zs=dma((8,)),
        zr=dma((10, G - 1)),
        ys=dma((8,)),
        yr=dma((8,)),
        ms=dma((4,)),
        acs=dma((5,)),
        acc=dma((5,)),
        acf=dma((5,)),
        acx=dma((11,)),
        es=dma((7,)),
        er=dma((7, S, 2)),
        ns=dma((4,)),
        gys=dma((5,)),
        gyr=dma((5, G)),
        gzs=dma((6,)),
        gzr=dma((6, 3)),
        ss=dma((2,)),
        sr=dma((2,)),
        xs=dma((2,)),
        xr=dma((G + 1,)),
        gts=dma((5,)),
        gtr=dma((5,)),
    )
    names = list(ins) + list(outs) + list(scratch)
    near = dict(gain=VM, bias=VM, bdown=VM, bconv=VM, bup=VM, mask=VM, evicted=SM, slopes=SM)
    return pl.pallas_call(
        functools.partial(layer_kernel, names, (nb, nu, S, ht, hd, M, Cw, rw, rd, rs)),
        out_shape=[jax.ShapeDtypeStruct(s, d) for s, d in outs.values()],
        in_specs=[near.get(n, ANY) for n in ins],
        out_specs=[VM if n == "os" else ANY for n in outs],
        scratch_shapes=list(scratch.values()),
        compiler_params=pltpu.CompilerParams(
            collective_id=9, has_side_effects=True, vmem_limit_bytes=63 * 2**20
        ),
        name="whole_layer",
    )(*ins.values())


def finish_kernel(names, shape, *refs):
    r = Names(names, refs)
    nb, rs, rd, Fw, Cw, heads = shape
    b, t = lax.axis_index("batch"), lax.axis_index("tier")
    moves = [(r.out, r.o_out), (r.ig, r.o_ig), (r.od, r.o_od), (r.ou, r.o_ou), (r.oc, r.o_oc)]
    moves += [(r.oa.at[i], o) for i, o in enumerate((r.o_q, r.o_k, r.o_v, r.o_o))]
    moves += [(r.om, r.o_mem), (r.ocm, r.o_comp)]
    bufs = refs[len(names) :]
    into = [pltpu.make_async_copy(src, buf, r.sem.at[i]) for i, ((src, _), buf) in enumerate(zip(moves, bufs))]
    n = len(moves)
    onto = [pltpu.make_async_copy(buf, dst, r.sem.at[n + i]) for i, ((_, dst), buf) in enumerate(zip(moves, bufs))]
    for cp in into:
        cp.start()
    spot = 4 * b + t
    block, inner = spot // (Cw // rs), lax.rem(spot, Cw // rs)
    half, group = inner // (128 // rs), lax.rem(inner, 128 // rs)
    for i, o in enumerate((r.o_down, r.o_gain, r.o_bias, r.o_conv)):
        row = r.os[block, pl.ds(Fw // 128 + (Cw // 128) * i + half, 1), :]
        turned = pltpu.roll(jnp.broadcast_to(row, (8, 128)), lax.rem(128 - rs * group, 128), 1)
        o[...] = turned[0:1, :rs]
    r.o_up[...] = r.os[t, pl.ds(b, 1), :rd]
    at = Fw // 128 + 4 * (Cw // 128)
    total = r.os[0, at : at + 1]
    for q in range(1, 4):
        total = total + r.os[q, at : at + 1]
    r.o_slopes[...] = total[:, :heads]
    for cp, then in zip(into, onto):
        cp.wait()
        then.start()
    for cp in onto:
        cp.wait()


def finish(nb, heads, arrays):
    S, R, M = arrays["out"].shape
    rw, rd, rs = arrays["oa"].shape[1], arrays["od"].shape[0], M // (4 * nb)
    Cw, Fw = M // 4, nb * rd
    rows, mat, vec = (S, R, M), (rw, M), (1, rs)
    outs = dict(
        o_out=(rows, bf16, ANY),
        o_ig=(rows, f32, ANY),
        o_mem=(rows, bf16, ANY),
        o_comp=(rows, bf16, ANY),
        o_q=(mat, f32, ANY),
        o_k=(mat, f32, ANY),
        o_v=(mat, f32, ANY),
        o_o=(mat, f32, ANY),
        o_ou=((rw, 4 * Fw), f32, ANY),
        o_up=((1, rd), f32, VM),
        o_od=((rd, M), f32, ANY),
        o_down=(vec, f32, VM),
        o_gain=(vec, f32, VM),
        o_bias=(vec, f32, VM),
        o_oc=((3, rw, M), f32, ANY),
        o_conv=(vec, f32, VM),
        o_slopes=((1, heads), f32, VM),
    )
    moved = ("o_out", "o_ig", "o_od", "o_ou", "o_oc", "o_q", "o_k", "o_v", "o_o", "o_mem", "o_comp")
    return pl.pallas_call(
        functools.partial(
            finish_kernel, list(arrays) + list(outs) + ["sem"], (nb, rs, rd, Fw, Cw, heads)
        ),
        out_shape=[jax.ShapeDtypeStruct(s, d) for s, d, _ in outs.values()],
        in_specs=[VM if n == "os" else ANY for n in arrays],
        out_specs=[o[2] for o in outs.values()],
        scratch_shapes=[pltpu.SemaphoreType.DMA((2 * len(moved),))]
        + [pltpu.VMEM(outs[n][0], outs[n][1]) for n in moved],
        compiler_params=pltpu.CompilerParams(vmem_limit_bytes=63 * 2**20),
        name="finish",
    )(*arrays.values())


def per_device_fused(
    nb,
    segment,
    memory,
    compressed,
    evicted,
    window_mask,
    cotangent,
    w_query,
    w_key,
    w_value,
    w_output,
    w_up,
    b_up,
    w_down,
    b_down,
    ln_gain,
    ln_bias,
    w_conv,
    b_conv,
    slopes,
):
    S, R, M = segment.shape
    heads = slopes.shape[0]
    line = lambda v: v.reshape(1, -1)
    names = ("out", "ig", "om", "ocm", "od", "ou", "oc", "oa", "os")
    made = whole_layer(
        nb,
        heads // 4,
        M // heads,
        dict(
            w_query=w_query,
            w_key=w_key,
            w_value=w_value,
            w_output=w_output,
            w_up=w_up,
            w_conv=w_conv,
            wd=w_down,
            comp=compressed,
            seg=segment,
            cot=cotangent,
            mem=memory,
            gain=line(ln_gain),
            bias=line(ln_bias),
            bdown=line(b_down),
            bconv=line(b_conv),
            bup=line(b_up),
            mask=window_mask,
            evicted=evicted,
            slopes=slopes,
        ),
    )
    outs = finish(nb, heads, dict(zip(names, made)))
    flat = (9, 11, 12, 13, 15, 16)
    return tuple(o.reshape(-1) if i in flat else o for i, o in enumerate(outs))


def solution(mesh):
    both = ("batch", "tier")
    rows = P("batch", "tier", None)
    mat, vec = P(both, None), P(both)
    nb = mesh.shape["batch"]

    def body(*args):
        fused = args[6].shape[0] % 16 == 0 and args[12].shape[0] == 128
        return (per_device_fused if fused else per_device)(nb, *args)

    return jax.shard_map(
        body,
        mesh=mesh,
        in_specs=(
            (rows, rows, rows, P("batch"), P("batch", "tier"), rows)
            + (mat, mat, mat, mat, mat, vec, mat, vec, vec, vec)
            + (P(None, both, None), vec, P())
        ),
        out_specs=(
            (rows, rows, rows, rows, mat, mat, mat, mat, mat, vec, mat, vec, vec, vec)
            + (P(None, both, None), vec, P())
        ),
        check_vma=False,
    )
```

```python
import functools
import math

import jax
import jax.numpy as jnp
from jax import lax
from jax.experimental import pallas as pl
from jax.experimental.pallas import tpu as pltpu
from jax.sharding import PartitionSpec as P

norm_eps = 1e-05
MESH = pl.DeviceIdType.MESH
ANY = pl.BlockSpec(memory_space=pl.ANY)
VM = pl.BlockSpec(memory_space=pltpu.VMEM)
SM = pl.BlockSpec(memory_space=pltpu.SMEM)
f32 = jnp.float32
bf16 = jnp.bfloat16


def remote(src, dst, send, recv, device):
    return pltpu.make_async_remote_copy(
        src_ref=src,
        dst_ref=dst,
        send_sem=send,
        recv_sem=recv,
        device_id=device,
        device_id_type=MESH,
    )


def places(groups):
    b, t = lax.axis_index("batch"), lax.axis_index("tier")
    z, y = b // 2, lax.rem(b, 2)
    zs = [lax.rem(z + d, groups) for d in range(groups)]
    zback = [lax.rem(z + groups - d, groups) for d in range(groups)]
    return b, t, z, y, zs, zback


def greet(groups, tiers, columns):
    b, t, z, y, zs, _ = places(groups)
    barrier = pltpu.get_barrier_semaphore()
    peers = []
    if tiers:
        peers += [(b, t ^ d) for d in (1, 2, 3)]
    if columns:
        peers += [(2 * zz + y, t) for zz in zs[1:]] + [(b ^ 1, t)]
    for peer in peers:
        pl.semaphore_signal(barrier, inc=1, device_id=peer, device_id_type=MESH)
    pl.semaphore_wait(barrier, len(peers))


def gather_kernel(groups, nu, *refs):
    (wa, wu, wc, wd, sm, comp, mem, seg, cot, mk) = refs[:10]
    (WA, WU, WC, WD, SM, CTX, COT, MK) = refs[10:18]
    lsem, ts, tr, zsd, zr, ys, yr, acs, acr = refs[18:]
    G = groups
    b, t, z, y, zs, zback = places(G)
    greet(G, True, True)
    ypeer = (b ^ 1, t)
    local, sends = [], []

    def here(src, dst, i):
        cp = pltpu.make_async_copy(src, dst, lsem.at[i])
        cp.start()
        return cp

    kinds = [(sm, SM), (wa, WA), (wu, WU), (wc, WC)]
    own = []
    for k, (src, dst) in enumerate(kinds):
        mine = src if k == 0 else src.at[t]
        own.append(here(mine, dst.at[b, t], k))
        for d in (1, 2, 3):
            piece = src if k == 0 else src.at[t ^ d]
            cp = remote(piece, dst.at[b, t], ts.at[k, d - 1], tr.at[k, d - 1], (b, t ^ d))
            cp.start()
            sends.append(cp)
    own.append(here(wd, WD.at[b], 4))
    pieces = [
        (comp, lambda q: CTX.at[:, pl.ds(nu * q, nu)]),
        (mem.at[:, 0], lambda q: CTX.at[:, 4 * nu + q]),
        (mem.at[:, 1], lambda q: CTX.at[:, 4 * nu + 4 + q]),
        (mem.at[:, 2], lambda q: CTX.at[:, 4 * nu + 8 + q]),
        (seg, lambda q: CTX.at[:, pl.ds(8 * nu + nu * q, nu)]),
        (mk, lambda q: MK.at[:, q]),
        (cot, lambda q: COT.at[:, pl.ds(nu * q, nu)]),
    ]
    for i, (src, at) in enumerate(pieces):
        own.append(here(src, at(t), 5 + i))
        for j, d in enumerate((1, 2)):
            cp = remote(src, at(t), acs.at[i, j], acr.at[i, j], (b, t ^ d))
            cp.start()
            sends.append(cp)
    table = [SM, WA, WU, WD, WC]
    local_of = [0, 1, 2, 4, 3]
    for k, dst in enumerate(table):
        own[local_of[k]].wait()
        if k != 3:
            kk = local_of[k]
            for d in (1, 2, 3):
                remote(dst.at[b, t], dst.at[b, t ^ d], ts.at[kk, d - 1], tr.at[kk, d - 1], (b, t ^ d)).wait_recv()
        for d in range(1, G):
            cp = remote(dst.at[b], dst.at[b], zsd.at[k, d], zr.at[k, d], (2 * zs[d] + y, t))
            cp.start()
            sends.append(cp)
        cp = remote(dst.at[b], dst.at[b], ys.at[k, 0], yr.at[k, 0], ypeer)
        cp.start()
        sends.append(cp)
    for i, (src, at) in enumerate(pieces):
        remote(at(t ^ 2), at(t ^ 2), acs.at[i, 1], acr.at[i, 1], (b, t ^ 2)).wait_recv()
        cp = remote(at(t ^ 2), at(t ^ 2), acs.at[i, 2], acr.at[i, 2], (b, t ^ 1))
        cp.start()
        sends.append(cp)
    for k, dst in enumerate(table):
        for d in range(1, G):
            at = dst.at[2 * zback[d] + y]
            remote(at, at, zsd.at[k, d], zr.at[k, d], ypeer).wait_recv()
            cp = remote(at, at, ys.at[k, d], yr.at[k, d], ypeer)
            cp.start()
            sends.append(cp)
    for k, dst in enumerate(table):
        for d in range(G):
            at = dst.at[2 * zback[d] + (1 - y)]
            remote(at, at, ys.at[k, d], yr.at[k, d], ypeer).wait_recv()
    for i, (src, at) in enumerate(pieces):
        for j, q in ((0, t ^ 1), (2, t ^ 3)):
            remote(at(q), at(q), acs.at[i, j], acr.at[i, j], (b, t ^ 1)).wait_recv()
    for i in range(len(pieces)):
        own[5 + i].wait()
    for cp in sends:
        cp.wait_send()


def gather_all(nb, nu, wa, wu, wc, wd, sm, comp, mem, seg, cot, mk):
    G = nb // 2
    S, _, U, M = comp.shape
    out = [
        jax.ShapeDtypeStruct((nb,) + wa.shape, bf16),
        jax.ShapeDtypeStruct((nb,) + wu.shape, bf16),
        jax.ShapeDtypeStruct((nb,) + wc.shape, bf16),
        jax.ShapeDtypeStruct((nb,) + wd.shape, bf16),
        jax.ShapeDtypeStruct((nb, 4) + sm.shape, f32),
        jax.ShapeDtypeStruct((S, 12 * nu, U, M), bf16),
        jax.ShapeDtypeStruct((S, 4 * nu, U, M), bf16),
        jax.ShapeDtypeStruct((S, 4) + mk.shape[1:], f32),
    ]
    dma = pltpu.SemaphoreType.DMA
    return pl.pallas_call(
        functools.partial(gather_kernel, G, nu),
        out_shape=out,
        in_specs=[ANY] * 10,
        out_specs=[ANY] * 8,
        scratch_shapes=[
            dma((12,)),
            dma((4, 3)),
            dma((4, 3)),
            dma((5, G)),
            dma((5, G)),
            dma((5, G)),
            dma((5, G)),
            dma((7, 3)),
            dma((7, 3)),
        ],
        compiler_params=pltpu.CompilerParams(collective_id=0, has_side_effects=True),
        name="gather_all",
    )(wa, wu, wc, wd, sm, comp, mem, seg, cot, mk)


def spread_kernel(same, x, o, lsem, ss, rs):
    b, t = lax.axis_index("batch"), lax.axis_index("tier")
    greet(1, True, False)
    cps = []
    for d in (1, 2, 3):
        cp = remote(x if same else x.at[t ^ d], o.at[t], ss.at[d - 1], rs.at[d - 1], (b, t ^ d))
        cp.start()
        cps.append(cp)
    mine = pltpu.make_async_copy(x if same else x.at[t], o.at[t], lsem)
    mine.start()
    mine.wait()
    for d in (1, 2, 3):
        remote(o.at[t ^ d], o.at[t ^ d], ss.at[d - 1], rs.at[d - 1], (b, t ^ d)).wait_recv()
    for cp in cps:
        cp.wait_send()


def spread(x, same, cid):
    dma = pltpu.SemaphoreType.DMA
    shape = ((4,) + x.shape) if same else x.shape
    return pl.pallas_call(
        functools.partial(spread_kernel, same),
        out_shape=jax.ShapeDtypeStruct(shape, x.dtype),
        in_specs=[ANY],
        out_specs=ANY,
        scratch_shapes=[dma, dma((3,)), dma((3,))],
        compiler_params=pltpu.CompilerParams(collective_id=cid, has_side_effects=True),
        name="spread_%d" % cid,
    )(x)


def reduce_kernel(groups, *refs):
    GD, GU, GC, GA, SMG = refs[:5]
    OD, OU, OC, OA, OS = refs[5:10]
    YD, YU, YC, YA, YS, ZD, ZU, ZC, ZA, ZS, TU, TC, TA, MU, MC, MA, ys, yr, zsd, zr, ts, tr = refs[10:]
    G = groups
    b, t, z, y, zs, zback = places(G)
    greet(G, True, True)
    ypeer = (b ^ 1, t)
    sends = []
    kinds = [
        (GD, YD, ZD, OD, None, None),
        (GU, YU, ZU, OU, MU, TU),
        (GC, YC, ZC, OC, MC, TC),
        (GA, YA, ZA, OA, MA, TA),
    ]
    for k, (g, yb, *_) in enumerate(kinds):
        for d in range(G):
            zz = zs[(d + 1) % G]
            cp = remote(g.at[2 * zz + (1 - y)], yb.at[zz], ys.at[k, d], yr.at[k, d], ypeer)
            cp.start()
            sends.append(cp)
    cp = remote(SMG, YS, ys.at[4, 0], yr.at[4, 0], ypeer)
    cp.start()
    sends.append(cp)
    for k, (g, yb, zb, o, m, tb) in enumerate(kinds):
        for d in range(G):
            zz = zs[(d + 1) % G]
            at = yb.at[zz]
            remote(at, at, ys.at[k, d], yr.at[k, d], ypeer).wait_recv()

            def add(i, c, yb=yb, zz=zz, g=g):
                yb[zz, i] = (yb[zz, i].astype(f32) + g[2 * zz + y, i].astype(f32)).astype(bf16)
                return c

            lax.fori_loop(0, yb.shape[1], add, 0)
            if d < G - 1:
                cp = remote(at, zb.at[d], zsd.at[k, d], zr.at[k, d], (2 * zz + y, t))
                cp.start()
                sends.append(cp)
    remote(YS, YS, ys.at[4, 0], yr.at[4, 0], ypeer).wait_recv()
    ZS[z] = SMG[...] + YS[...]
    for d in range(G - 1):
        cp = remote(ZS.at[z], ZS.at[z], zsd.at[4, d], zr.at[4, d], (2 * zs[d + 1] + y, t))
        cp.start()
        sends.append(cp)
    for k, (g, yb, zb, o, m, tb) in enumerate(kinds):
        for d in range(G - 1):
            remote(zb.at[d], zb.at[d], zsd.at[k, d], zr.at[k, d], ypeer).wait_recv()

        def total(i, c, k=k, yb=yb, zb=zb, o=o, m=m):
            acc = yb[z, i].astype(f32)
            for d in range(G - 1):
                acc = acc + zb[d, i].astype(f32)
            if k == 0:
                o[i] = acc
            else:
                m[i] = acc.astype(bf16)
            return c

        lax.fori_loop(0, o.shape[0], total, 0)
        if k:
            for d in (1, 2, 3):
                cp = remote(m.at[t ^ d], tb.at[t], ts.at[k - 1, d - 1], tr.at[k - 1, d - 1], (b, t ^ d))
                cp.start()
                sends.append(cp)
    for d in range(G - 1):
        at = ZS.at[zback[d + 1]]
        remote(at, at, zsd.at[4, d], zr.at[4, d], ypeer).wait_recv()
    acc = ZS[0]
    for zz in range(1, G):
        acc = acc + ZS[zz]
    OS[t] = acc
    for d in (1, 2, 3):
        cp = remote(OS.at[t], OS.at[t], ts.at[3, d - 1], tr.at[3, d - 1], (b, t ^ d))
        cp.start()
        sends.append(cp)
    for k, (g, yb, zb, o, m, tb) in enumerate(kinds):
        if k:
            o[t] = m[t].astype(f32)
            for d in (1, 2, 3):
                at = tb.at[t ^ d]
                remote(at, at, ts.at[k - 1, d - 1], tr.at[k - 1, d - 1], (b, t ^ d)).wait_recv()
                o[t ^ d] = tb[t ^ d].astype(f32)
    for d in (1, 2, 3):
        at = OS.at[t ^ d]
        remote(at, at, ts.at[3, d - 1], tr.at[3, d - 1], (b, t ^ d)).wait_recv()
    for cp in sends:
        cp.wait_send()


def reduce_all(nb, gd, gu, gc, ga, sg):
    G = nb // 2
    dma = pltpu.SemaphoreType.DMA
    shapes = [x.shape[1:] for x in (gd, gu, gc, ga)]
    return pl.pallas_call(
        functools.partial(reduce_kernel, G),
        out_shape=[jax.ShapeDtypeStruct(s, f32) for s in shapes]
        + [jax.ShapeDtypeStruct((4,) + sg.shape, f32)],
        in_specs=[VM] * 5,
        out_specs=[VM] * 5,
        scratch_shapes=[pltpu.VMEM((G,) + s, bf16) for s in shapes]
        + [pltpu.VMEM(sg.shape, f32)]
        + [pltpu.VMEM((G - 1,) + s, bf16) for s in shapes]
        + [pltpu.VMEM((G,) + sg.shape, f32)]
        + [pltpu.VMEM(s, bf16) for s in shapes[1:]]
        + [pltpu.VMEM(s, bf16) for s in shapes[1:]]
        + [dma((5, G)), dma((5, G)), dma((5, G)), dma((5, G)), dma((4, 3)), dma((4, 3))],
        compiler_params=pltpu.CompilerParams(
            collective_id=1, has_side_effects=True, vmem_limit_bytes=48 * 2**20
        ),
        name="reduce_all",
    )(gd, gu, gc, ga, sg)


def dot(a, b):
    return jnp.dot(a, b, preferred_element_type=f32)


def dot_tn(a, b):
    return lax.dot_general(a, b, (((0,), (0,)), ((), ())), preferred_element_type=f32)


def dot_nt(a, b):
    return lax.dot_general(a, b, (((1,), (1,)), ((), ())), preferred_element_type=f32)


def per_device(
    nb,
    segment,
    memory,
    compressed,
    evicted,
    window_mask,
    cotangent,
    w_query,
    w_key,
    w_value,
    w_output,
    w_up,
    b_up,
    w_down,
    b_down,
    ln_gain,
    ln_bias,
    w_conv,
    b_conv,
    slopes,
):
    S, R, M = segment.shape
    heads = slopes.shape[0]
    hd = M // heads
    nt = 4
    rw, rd, rs = w_query.shape[0], w_down.shape[0], b_down.shape[0]
    b, t = lax.axis_index("batch"), lax.axis_index("tier")
    Cw, Fw = M // nt, nb * rd
    nu, W = R // 16, R // 3
    seg_len = nt * R
    T = S * seg_len
    ht = heads // nt
    index = 4 * b + t

    wa = jnp.stack([w_query, w_key, w_value, w_output]).reshape(4, rw, nt, Cw)
    wa = wa.transpose(2, 1, 0, 3).reshape(nt, rw, 4 * Cw)
    wu = w_up.reshape(rw, nb, nt, rd).transpose(2, 0, 1, 3).reshape(nt, rw, Fw)
    wc = w_conv.reshape(3, rw, nt, Cw).transpose(2, 1, 0, 3).reshape(nt, rw, 3 * Cw)
    row0 = jnp.concatenate([ln_gain, ln_bias, b_down, b_conv])
    sm = jnp.zeros((8, 128), f32).at[0, : 4 * rs].set(row0.astype(f32)).at[1, :rd].set(b_up.astype(f32))
    mem = memory.reshape(S, W, 3, M).transpose(0, 2, 1, 3)
    mk = jnp.broadcast_to(window_mask.astype(f32)[:, :, None], (S, W, 128))
    WA, WU, WC, WD, SM, CTX, COT, MK = gather_all(
        nb,
        nu,
        wa,
        wu,
        wc,
        w_down,
        sm,
        compressed.reshape(S, nu, 16, M),
        mem,
        segment.reshape(S, nu, 16, M),
        cotangent.reshape(S, nu, 16, M),
        mk,
    )
    WA = WA.reshape(M, 4 * Cw)
    Wqkv, Wo = WA[:, : 3 * Cw], WA[:, 3 * Cw :]
    WU, WC, WD = WU.reshape(M, Fw), WC.reshape(M, 3 * Cw), WD.reshape(Fw, M)
    gain, bias, bdown, bconv = [SM[:, :, 0, i * rs : (i + 1) * rs].reshape(M) for i in range(4)]
    bup = lax.dynamic_index_in_dim(SM, t, 1, False)[:, 1, :rd].reshape(Fw)
    cols = lambda v: lax.dynamic_slice_in_dim(v, t * Cw, Cw, v.ndim - 1)
    ctx = CTX.reshape(S, 3 * seg_len, M)
    cot = COT.reshape(T, M)
    seg = ctx[:, 2 * seg_len :].reshape(T, M)

    kpos = jnp.concatenate(
        [
            jnp.arange(seg_len),
            seg_len + (3 * jnp.arange(seg_len // 3)[None, :] + jnp.arange(3)[:, None]).reshape(-1),
            2 * seg_len + jnp.arange(seg_len),
        ]
    )
    qpos = 2 * seg_len + jnp.arange(seg_len)
    allowed = kpos[None, :] <= qpos[:, None]
    dist = (qpos[:, None] - kpos[None, :]).astype(f32) * (1.0 / (3 * seg_len))
    slope = lax.dynamic_slice_in_dim(slopes, t * ht, ht)
    scale = 1.0 / math.sqrt(hd)
    q = dot(seg, Wqkv[:, :Cw]).astype(bf16).reshape(S, seg_len, ht, hd)
    kv = dot(ctx.reshape(-1, M), Wqkv[:, Cw:]).astype(bf16).reshape(S, 3 * seg_len, 2, ht, hd)
    kk, vv = kv[:, :, 0], kv[:, :, 1]
    raw = jnp.einsum("sqhd,skhd->shqk", q, kk, preferred_element_type=f32)
    scores = jnp.where(allowed, raw * scale - slope[:, None, None] * dist, -1e30)
    high = jnp.max(scores, axis=-1, keepdims=True)
    e = jnp.exp(scores - high)
    probs = e / jnp.sum(e, axis=-1, keepdims=True)
    probs_low = probs.astype(bf16)
    mixed_t = jnp.einsum("shqk,skhd->sqhd", probs_low, vv, preferred_element_type=f32).astype(bf16)
    MIX = spread(mixed_t.reshape(T, Cw), True, 2)
    mixed = MIX.transpose(1, 0, 2).reshape(T, M)
    resid_t = cols(seg).astype(f32) + dot(mixed, Wo)
    RES = spread(resid_t.astype(bf16), True, 3)
    resid = RES.transpose(1, 0, 2).reshape(T, M).astype(f32)
    center = resid - jnp.mean(resid, axis=-1, keepdims=True)
    spread_ = lax.rsqrt(jnp.mean(center * center, axis=-1, keepdims=True) + norm_eps)
    xhat = center * spread_
    normed = (xhat * gain + bias).astype(bf16)
    pre = dot(normed, WU) + bup
    phi = 0.5 * (1.0 + lax.erf(pre * math.sqrt(0.5)))
    act = (pre * phi).astype(bf16)
    slope_act = phi + pre * jnp.exp(-0.5 * pre * pre) * (1.0 / math.sqrt(2 * math.pi))
    place = lambda v: lax.dynamic_update_slice_in_dim(jnp.zeros((T, M), f32), v, t * Cw, 1)
    out_part = dot(act, WD) + place(resid_t + cols(bdown))
    rows = lambda v: v.astype(bf16).reshape(S, nt, R, M).transpose(1, 0, 2, 3)
    output = jnp.sum(spread(rows(out_part), False, 4).astype(f32), axis=0).astype(bf16)
    gdown = dot_tn(act, cot)
    d_act = dot_nt(cot, WD).astype(bf16)
    d_pre = d_act.astype(f32) * slope_act
    gub = jnp.sum(d_pre, axis=0)
    d_pre_low = d_pre.astype(bf16)
    gup = dot_tn(normed, d_pre_low)
    dn_part = dot_nt(d_pre_low, WU)
    stats = jnp.stack([jnp.mean(dn_part * gain, axis=1), jnp.mean(dn_part * gain * xhat, axis=1)])
    stats = lax.psum(stats, "tier")
    cols_of = lambda v: v.astype(bf16).reshape(T, nt, Cw).transpose(1, 0, 2)
    dn = jnp.sum(spread(cols_of(dn_part), False, 5).astype(f32), axis=0)
    xhat_t = cols(xhat)
    ggain, gbias = jnp.sum(dn * xhat_t, axis=0), jnp.sum(dn, axis=0)
    g = dn * cols(gain)
    cot_t = cols(cot).astype(f32)
    gdb = jnp.sum(cot_t, axis=0)
    d_resid = cot_t + (g - stats[0][:, None] - xhat_t * stats[1][:, None]) * spread_
    d_branch = d_resid.astype(bf16)
    gout = dot_tn(mixed, d_branch)
    dm_part = dot_nt(d_branch, Wo)
    dm = jnp.sum(spread(cols_of(dm_part), False, 6).astype(f32), axis=0).astype(bf16)
    dm = dm.reshape(S, seg_len, ht, hd)
    d_probs = jnp.einsum("sqhd,skhd->shqk", dm, vv, preferred_element_type=f32)
    delta = jnp.sum(probs * d_probs, axis=-1, keepdims=True)
    d_scores = probs * (d_probs - delta)
    gslope = -jnp.sum(d_scores * dist, axis=(0, 2, 3))
    d_raw = (d_scores * scale).astype(bf16)
    dq = jnp.einsum("shqk,skhd->sqhd", d_raw, kk, preferred_element_type=f32).astype(bf16)
    dk = jnp.einsum("shqk,sqhd->skhd", d_raw, q, preferred_element_type=f32).astype(bf16)
    dv = jnp.einsum("shqk,sqhd->skhd", probs_low, dm, preferred_element_type=f32).astype(bf16)
    dq, dk, dv = dq.reshape(T, Cw), dk.reshape(S, -1, Cw), dv.reshape(S, -1, Cw)
    flat = ctx.reshape(-1, M)
    gq = dot_tn(seg, dq)
    gk, gv = dot_tn(flat, dk.reshape(-1, Cw)), dot_tn(flat, dv.reshape(-1, Cw))
    own = lambda v: v[:, 2 * seg_len :].reshape(T, Cw)
    ig_part = dot_nt(jnp.concatenate([dq, own(dk), own(dv)], axis=1), Wqkv) + place(d_resid)
    input_grad = jnp.sum(spread(rows(ig_part), False, 7).astype(f32), axis=0)

    nw = seg_len // 3
    win = ctx[:, seg_len : 2 * seg_len].reshape(S, 3, nw, M)
    win = [win[:, k].reshape(S * nw, M) for k in range(3)]
    conv = sum(dot(win[k], WC[:, k * Cw : (k + 1) * Cw]) for k in range(3)) + cols(bconv)
    pooled = sum(cols(win[k]).astype(f32) for k in range(3)) * (1.0 / 3.0)
    mask = MK.reshape(S, nw, 128)[:, :, :1]
    old = (3 * jnp.arange(nw) + 3)[None, :, None] <= evicted[:, None, None]
    live = jnp.where(old, mask, 0.0).reshape(-1, 1)
    d_conv = live * (conv - pooled)
    gcb = jnp.sum(d_conv, axis=0)
    d_low = d_conv.astype(bf16)
    gconv = jnp.concatenate([dot_tn(win[k], d_low) for k in range(3)], axis=1)
    new_t = (mask.reshape(-1, 1) * conv).astype(bf16)
    NEW = spread(new_t, True, 8).reshape(nt, S, nw, Cw).transpose(1, 2, 0, 3).reshape(S, nw, M)
    slot_offset = seg_len - nw
    local_rows = jnp.arange(R, dtype=jnp.int32) + t * R
    padded = jnp.concatenate([jnp.zeros((S, slot_offset, M), bf16), NEW], axis=1)
    slot_rows = lax.dynamic_slice_in_dim(padded, t * R, R, 1)
    written = (local_rows[None, :] >= slot_offset) & (
        3 * (local_rows[None, :] - slot_offset) + 3 <= evicted[:, None]
    )
    new_compressed = jnp.where(written[..., None], slot_rows, compressed)
    new_memory = jnp.where((local_rows[None, :] < evicted[:, None])[..., None], segment, memory)

    low = lambda v, *s: v.astype(bf16).reshape(s)
    gs = lax.dynamic_update_slice_in_dim(jnp.zeros((128,), f32), gslope, t * ht, 0)
    sg = jnp.concatenate([gub, gdb, ggain, gbias, gcb, gs])
    sg = jnp.concatenate([sg, jnp.zeros((24 * 128 - sg.shape[0],), f32)]).reshape(24, 128)
    OD, OU, OC, OA, OS = reduce_all(
        nb,
        low(gdown, nb, 4, rd // 4, M),
        low(gup, nb, 4, rw, Fw),
        low(gconv, nb, 4, rw, 3 * Cw),
        low(jnp.concatenate([gq, gk, gv, gout], axis=1), nb, 4, rw, 4 * Cw),
        sg,
    )
    OA = OA.reshape(nt, rw, 4, Cw).transpose(2, 1, 0, 3).reshape(4, rw, M)
    OU = OU.reshape(nt, rw, nb, rd).transpose(1, 2, 0, 3).reshape(rw, nb * nt * rd)
    OC = OC.reshape(nt, rw, 3, Cw).transpose(2, 1, 0, 3).reshape(3, rw, M)
    OS = OS.reshape(nt, -1)
    vec = lambda o: lax.dynamic_slice_in_dim(OS[:, o : o + Cw].reshape(M), index * rs, rs)
    gub_out = lax.dynamic_slice(OS, (t, b * rd), (1, rd)).reshape(rd)
    gslopes = jnp.sum(OS[:, Fw + 4 * Cw : Fw + 4 * Cw + heads], axis=0)
    return (
        output,
        input_grad,
        new_memory,
        new_compressed,
        OA[0],
        OA[1],
        OA[2],
        OA[3],
        OU,
        gub_out,
        OD.reshape(rd, M),
        vec(Fw),
        vec(Fw + Cw),
        vec(Fw + 2 * Cw),
        OC,
        vec(Fw + 3 * Cw),
        gslopes,
    )


class Names:
    def __init__(self, names, refs):
        for name, ref in zip(names, refs):
            setattr(self, name, ref)


def layer_kernel(names, shape, *refs):
    r = Names(names, refs)
    nb, nu, S, ht, hd, M, Cw, rw, rd, rs = shape
    R = 16 * nu
    Hw = Cw // 2
    nd = r.YD.shape[1]
    G, bq = nb // 2, nb // 4
    L = 16 * 4 * nu
    C3 = 3 * L
    nw = L // 3
    Fw = nb * rd
    scale = 1.0 / math.sqrt(hd)
    b, t, z, y, zs, zback = places(G)
    mate, ends = z ^ 1, (z == 0) | (z == G - 1)
    ypeer = (b ^ 1, t)
    tc = pl.ds(pl.multiple_of(t * Cw, Cw), Cw)
    sends = []

    def got(ref, sem):
        pltpu.make_async_copy(ref, ref, sem).wait()

    def left_all(ref, sem):
        sends.append((ref, sem))

    def each(n, body, between=None):
        def step(i, c):
            body(i)
            for at, then in (between or {}).items():
                pl.when(i == at)(then)
            return c

        lax.fori_loop(0, n, step, 0)

    def ex_send(e, sem, src, dst):
        for d in (1, 2, 3):
            remote(src(t ^ d), dst(d), r.es.at[e], sem, (b, t ^ d)).start()

    def spread_send(e, s, arr):
        at = arr.at[t, s]
        for d in (1, 2):
            remote(at, at, r.es.at[e], r.er.at[e, s, d - 1], (b, t ^ d)).start()

    def spread_pass(e, s, arr):
        at = arr.at[t ^ 2, s]
        got(at, r.er.at[e, s, 1])
        remote(at, at, r.es.at[e], r.er.at[e, s, 0], (b, t ^ 1)).start()

    def spread_wait(e, s, arr):
        @pl.when(s < S - 1)
        def _():
            spread_pass(e, s + 1, arr)

        got(arr.at[0:2, s], r.er.at[e, s, 0])

    folds = {
        2: (lambda q, s: r.DNP.at[q, s], r.DNR),
        4: (lambda q, s: r.DMP.at[q, s], r.DMR),
        5: (lambda q, s: r.OP.at[s, pl.ds(nu * q, nu)], r.OR),
        6: (lambda q, s: r.NRM.at[s, pl.ds(nu * q, nu)], r.IR),
    }

    def fold_send(e, s):
        out, into = folds[e]
        for i, d in enumerate((1, 3)):
            remote(out(t ^ d, s), into.at[i, s], r.es.at[e], r.er.at[e, s, i], (b, t ^ 1)).start()

    def fold_pass(e, s):
        out, into = folds[e]
        at, far = into.at[1, s], out(t ^ 2, s)
        got(at, r.er.at[e, s, 1])
        far[...] = (far[...].astype(f32) + at[...].astype(f32)).astype(bf16)
        remote(far, into.at[2, s], r.es.at[e], r.er.at[e, s, 0], (b, t ^ 2)).start()

    def fold_late(e, s):
        @pl.when(s > 0)
        def _():
            fold_pass(e, s - 1)

    def folded(e, s):
        out, into = folds[e]
        got(into.at[0:2, s], r.er.at[e, s, 0])
        return out(t, s)[...].astype(f32) + into[0, s].astype(f32) + into[2, s].astype(f32)

    def here(src, dst, i):
        cp = pltpu.make_async_copy(src, dst, r.lsem.at[i])
        cp.start()
        return cp

    wide = lambda at, size: pl.ds(pl.multiple_of(at, 128), size)
    mats = (r.w_query, r.w_key, r.w_value, r.w_output)
    whole = {"S": r.SM, "A": r.WA, "U": r.WU, "C": r.WC}
    index = {"S": 0, "A": 1, "U": 2, "C": 3, "H": 4}

    def tiers(n, at):
        return r.WCX.at[at] if n == "H" else whole[n].at[b, at]

    def cuts(n, q):
        if n == "S":
            return [(r.SM.at[b, t], r.SM.at[b, t])]
        if n == "A":
            return [(w.at[:, wide(Cw * q, Cw)], r.WA.at[b, t, :, i * Cw : (i + 1) * Cw]) for i, w in enumerate(mats)]
        if n == "U":
            return [
                (r.w_up.at[:, wide((4 * i + q) * rd, rd)], r.WU.at[b, t, :, i * rd : (i + 1) * rd]) for i in range(nb)
            ]
        half, to = (y, r.WC.at[b]) if n == "C" else (1 - y, r.WCX)
        return [
            (r.w_conv.at[i, :, wide(Cw * q + Hw * half, Hw)], to.at[t, :, i * Hw : (i + 1) * Hw]) for i in range(3)
        ]

    def tier_own(n):
        for src, dst in cuts(n, t):
            here(src, dst, index[n])

    def tier_start(n):
        i = index[n]
        for d in (1, 2, 3):
            for src, dst in cuts(n, t ^ d):
                remote(src, dst, r.ts.at[i], r.tr.at[i], (b, t ^ d)).start()
        left_all(tiers(n, slice(0, 3)), r.ts.at[i])

    def tier_wait(n):
        i = index[n]
        if n != "S":
            got(tiers(n, t), r.lsem.at[i])
        got(tiers(n, slice(0, 3)), r.tr.at[i])

    def if_(cond, body):
        pl.when(cond)(body)

    def at_ends(body):
        return lambda: if_(ends, body)

    def inside(body):
        return lambda: if_(~ends, body)

    def both(*bodies):
        def run():
            for body in bodies:
                body()

        return run

    right, left = (2 * z + 2 + y, t), (2 * z - 2 + y, t)
    parts = {"S": [(r.SM, 0, 0, 4, 0)], "C": [(r.WC, 1, 0, 4, 1)], "X": [(r.WC, 2, 0, 4, 2)]}
    for i, (n, w) in enumerate((("A", r.WA), ("U", r.WU))):
        parts[n] = [(w, 3 + 2 * i + h, h * 2, 2, 3 + i) for h in (0, 1)]
    for i, (n, at) in enumerate((("D", 0), ("E", rd // 2), ("F", rd // 2))):
        parts[n] = [(r.WD, 7 + i, at, rd // 2, 5 + i)]

    def chunk_of(n, part, zz, col=None):
        w, k, at, size, _ = part
        col = ((1 - y) if n in "XF" else y) if col is None else col
        return w.at[2 * zz + col, pl.ds(at, size)]

    def chunks(n, count):
        w, _, at, size, _ = parts[n][0]
        return w.at[0:count, at : at + size * len(parts[n])]

    def hop(part, at, zz, way):
        k = part[1]
        peer, past = (right, z < G - 1) if way == 0 else (left, z > 0)
        return past, remote(at, at, r.zs.at[part[4]], r.zr.at[k, zz - way], peer)

    def own_z(n):
        for part in parts[n]:
            for way in (0, 1):
                past, cp = hop(part, chunk_of(n, part, z), z, way)
                if_(past, cp.start)

    def own_y(n):
        for part in parts[n]:
            at, k = chunk_of(n, part, z), part[4]
            remote(r.WCX if n == "C" else at, at, r.ys.at[k], r.yr.at[k], ypeer).start()

    def arrivals(n, step, js):
        for j in js:
            for part in parts[n]:
                for way in (0, 1):
                    zz = z - j if way == 0 else z + j
                    step(part, j, way, zz, chunk_of(n, part, zz), zz >= 0 if way == 0 else zz < G)

    def onward(n, *js, cross=True):
        def step(part, j, way, zz, at, there):
            k = part[1]

            def body():
                got(at, r.zr.at[k, zz - way])
                if j < G - 1:
                    past, cp = hop(part, at, zz, way)
                    if_(past, cp.start)
                if n not in "CXEF" and cross:
                    remote(at, at, r.ys.at[part[4]], r.yr.at[part[4]], ypeer).start()

            if_(there, body)

        arrivals(n, step, js or range(1, G))

    def over(n, *js):
        def step(part, j, way, zz, at, there):
            if_(there, remote(at, at, r.ys.at[part[4]], r.yr.at[part[4]], ypeer).start)

        arrivals(n, step, js)

    def all_sent(n):
        k = parts[n][0][4]
        if_(ends, lambda: got(chunks(n, 1), r.zs.at[k]))
        if_(~ends, lambda: got(chunks(n, 5), r.zs.at[k]))
        if n not in "XF":
            got(chunks(n, 1 if n in "CE" else G), r.ys.at[k])

    def y_wait(n):
        got(chunks(n, 1 if n in "CE" else G), r.yr.at[parts[n][0][4]])

    def small_start():
        r.SM[b, t] = jnp.zeros((8, 128), f32)
        for q, v in enumerate((r.gain, r.bias, r.bdown, r.bconv, r.bup)):
            r.SM[b, t, q : q + 1, : v.shape[1]] = v[...].astype(f32)
        tier_start("S")

    def memory_rows():
        W = R // 3
        to, frm = (lax.broadcasted_iota(jnp.int32, (R, R), axis) for axis in (0, 1))
        tap = (to >= W).astype(jnp.int32) + (to >= 2 * W).astype(jnp.int32)
        order = (frm == 3 * (to - W * tap) + tap).astype(bf16)
        for s in range(S):
            rows = jnp.dot(order, r.MEMV[s], preferred_element_type=f32).astype(bf16)
            for i in range(3):
                r.CTX[s, 4 * nu + 4 * i + t] = rows[W * i : W * (i + 1)]
            square = lambda axis: lax.broadcasted_iota(jnp.int32, (R // 3, R // 3), axis)
            line = jnp.broadcast_to(r.mask[s : s + 1].astype(f32), (R // 3, R // 3))
            col = jnp.sum(jnp.where(square(0) == square(1), line, 0.0), axis=1, keepdims=True)
            spot = lax.broadcasted_iota(jnp.int32, (R // 3, 128), 0) + (R // 3) * t
            lane = lax.broadcasted_iota(jnp.int32, (R // 3, 128), 1)
            r.MK[s, t] = jnp.where((lane < 64) | (3 * spot + 3 <= r.evicted[s]), col, 0.0)

    def rows_of(src, buf, first):
        at = lambda q: buf.at[:, pl.ds(first + nu * q, nu)]
        parts = [(src.at[:, 16 * i : 16 * i + 16], buf.at[:, first + nu * t + i]) for i in range(nu)]
        return parts, at, True

    def held(at):
        return [(at(t), at(t))], at, False

    def memory_y():
        for i in range(3):
            remote(r.CTX.at[:, 4 * nu + 4 * i + t], r.MEMX.at[:, 4 * i + t], r.ms.at[0], r.ms.at[1], ypeer).start()
        remote(r.MK.at[:, t], r.MKX.at[:, t], r.ms.at[2], r.ms.at[3], ypeer).start()
        left_all(r.MEMX.at[:, 0:3], r.ms.at[0])
        left_all(r.MKX.at[:, 0], r.ms.at[2])

    def memory_come():
        got(r.MEMX.at[:, 0:3], r.ms.at[1])
        got(r.MKX.at[:, 0], r.ms.at[3])

    pieces = [
        rows_of(r.seg, r.CTX, 8 * nu),
        rows_of(r.comp, r.CTX, 0),
        held(lambda q: r.CTX.at[:, 4 * nu + q]),
        held(lambda q: r.CTX.at[:, 4 * nu + 4 + q]),
        held(lambda q: r.CTX.at[:, 4 * nu + 8 + q]),
        rows_of(r.cot, r.COT, 0),
        held(lambda q: r.MK.at[:, q]),
        held(lambda q: r.MEMX.at[:, q]),
        held(lambda q: r.MEMX.at[:, 4 + q]),
        held(lambda q: r.MEMX.at[:, 8 + q]),
        held(lambda q: r.MKX.at[:, q]),
    ]

    group = lambda i: 0 if i < 5 else (1, 2, 3, 3, 3, 4)[i - 5]
    grouped = [(r.CTX, 3 * nu), (r.COT, nu), (r.MK, 1), (r.MEMX, 3), (r.MKX, 1)]

    def act_own():
        for i, (cut, at, far) in enumerate(pieces):
            if far:
                for src, dst in cut:
                    here(src, dst, 5 + group(i))

    def act_start(*which):
        for i in which:
            cut, at, far = pieces[i]
            g = group(i)
            for src, dst in cut:
                remote(src, dst, r.acs.at[g], r.acc.at[g], (b, t ^ 1)).start()
                remote(src, dst, r.acs.at[g], r.acx.at[i], (b, t ^ 2)).start()

    def act_forward(*which):
        for i in which:
            at = pieces[i][1](t ^ 2)
            got(at, r.acx.at[i])
            remote(at, at, r.acs.at[group(i)], r.acf.at[group(i)], (b, t ^ 1)).start()

    def act_wait(g):
        buf, n = grouped[g]
        got(buf.at[:, 0:n], r.acc.at[g])
        got(buf.at[:, 0:n], r.acf.at[g])
        if g < 2:
            got(buf.at[:, 0 : n if g else 2 * nu], r.lsem.at[5 + g])

    def act_sent():
        for g, (buf, n) in enumerate(grouped):
            got(buf.at[:, 0 : 3 * n], r.acs.at[g])

    def table():
        row = lax.broadcasted_iota(jnp.int32, (L, C3), 0) + 2 * L
        col = lax.broadcasted_iota(jnp.int32, (L, C3), 1)
        inner = col - L
        k1 = (inner >= nw).astype(jnp.int32)
        k2 = (inner >= 2 * nw).astype(jnp.int32)
        win = inner - nw * (k1 + k2)
        pos = jnp.where((col >= L) & (col < 2 * L), L + 3 * win + k1 + k2, col)
        r.DIST[...] = jnp.where(pos <= row, (row - pos).astype(f32) * (1.0 / C3), 1e30)
        r.SMG[...] = jnp.zeros_like(r.SMG)

    def seg_rows(s):
        return r.CTX[s, 8 * nu : 12 * nu].reshape(L, M)

    def project(s):
        rows = r.CTX[s].reshape(C3, M)
        kv = jnp.dot(rows, r.WA[:, :, :, Cw : 3 * Cw].reshape(M, 2 * Cw), preferred_element_type=f32)
        r.KV[s] = kv.astype(bf16)
        q = jnp.dot(seg_rows(s), r.WA[:, :, :, :Cw].reshape(M, Cw), preferred_element_type=f32)
        r.Q[s] = q.astype(bf16)


    def attend(s):
        for h in range(ht):
            c = slice(h * hd, (h + 1) * hd)
            raw = dot_nt(r.Q[s, :, c], r.KV[s, :, c])
            scores = raw * scale - r.slopes[t * ht + h] * r.DIST[...]
            e = jnp.exp(scores - jnp.max(scores, axis=1, keepdims=True))
            p = e * (1.0 / jnp.sum(e, axis=1, keepdims=True))
            r.PR[s, h] = p
            v = r.KV[s, :, Cw + h * hd : Cw + (h + 1) * hd]
            r.MIX[t, s, :, c] = jnp.dot(p.astype(bf16), v, preferred_element_type=f32).astype(bf16)
        spread_send(0, s, r.MIX)


    def wo(q):
        return r.WA[bq * q : bq * (q + 1), :, :, 3 * Cw :].reshape(Cw, Cw)

    def residual(s):
        spread_wait(0, s, r.MIX)
        acc = r.CTX[s, 8 * nu : 12 * nu, :, tc].reshape(L, Cw).astype(f32)
        for q in range(4):
            acc = acc + jnp.dot(r.MIX[q, s], wo(q), preferred_element_type=f32)
        r.RT[s] = acc
        r.RES[t, s] = acc.astype(bf16)
        spread_send(1, s, r.RES)

    def vectors():
        lane = lax.broadcasted_iota(jnp.int32, (8, 128), 1)
        for at in range(0, M, 128):
            block = jnp.zeros((8, 128), f32)
            for i in range(128 // rs):
                spot = at // rs + i
                turned = pltpu.roll(r.SM[spot // 4, spot % 4], rs * i, 1)
                block = jnp.where((lane >= rs * i) & (lane < rs * (i + 1)), turned, block)
            r.VV[0:4, at : at + 128] = block[0:4]
        for bb in range(nb):
            r.VV[4:5, bb * rd : (bb + 1) * rd] = r.SM[bb, t, 4:5, :rd]

    def xhat_of(s, q):
        return (r.RES[q, s].astype(f32) - r.MU[s, :, :1]) * r.MU[s, :, 1:2]

    def feed(s):
        spread_wait(1, s, r.RES)
        parts = [r.RES[q, s].astype(f32) for q in range(4)]
        mu = sum(jnp.sum(x, axis=1, keepdims=True) for x in parts) * (1.0 / M)
        var = sum(jnp.sum((x - mu) * (x - mu), axis=1, keepdims=True) for x in parts) * (1.0 / M)
        inv = lax.rsqrt(var + norm_eps)
        lane = lax.broadcasted_iota(jnp.int32, (L, 128), 1)
        r.MU[s] = jnp.where(lane == 0, mu, inv)
        for q in range(4):
            c = slice(q * Cw, (q + 1) * Cw)
            rows = ((parts[q] - mu) * inv) * r.VV[0:1, c] + r.VV[1:2, c]
            r.NRM[s, :, :, c] = rows.astype(bf16).reshape(4 * nu, 16, Cw)
        fb = Fw // 4
        for j in range(4):
            c = slice(j * fb, (j + 1) * fb)
            pre = jnp.dot(r.NRM[s].reshape(L, M), r.WU[:, :, :, c].reshape(M, fb), preferred_element_type=f32) + r.VV[4:5, c]
            phi = 0.5 + 0.5 * lax.erf(pre * math.sqrt(0.5))
            r.ACT[s, :, c] = (pre * phi).astype(bf16)
            r.GP[s, :, c] = (phi + pre * (jnp.exp(-0.5 * pre * pre) * (1.0 / math.sqrt(2 * math.pi)))).astype(bf16)


    def turn(j):
        low = lax.rem(G - j, G)
        inner = jnp.where(z == 1, low, G - 1 - low)
        return jnp.where(z == 0, G - 1 - j, jnp.where(z == G - 1, j, inner))

    grads = {0: (r.GD, r.YD, r.ZD), 1: (r.GU, r.YU, r.ZU), 2: (r.GA, r.YO, r.ZO), 3: (r.WU, r.YA, r.ZA)}

    def block(k, b_):
        g = grads[k][0]
        if k == 0:
            return g.at[b_, 0:nd]
        if k == 1:
            return g.at[b_]
        return g.at[b_, :, :, 3 * Cw :] if k == 2 else g.at[b_, :, :, : 3 * Cw]

    def to_y(k, zz):
        g, yb, zb = grads[k]
        remote(block(k, 2 * zz + (1 - y)), yb.at[zz], r.gys.at[k], r.gyr.at[k, zz], ypeer).start()

    def plus(into, *others):
        def add(i):
            acc = into[i].astype(f32)
            for o in others:
                acc = acc + o[i].astype(f32)
            into[i] = acc.astype(bf16)

        each(into.shape[0], add)

    def pass_on(i, at, zb, o, sem):
        @pl.when((o != mate) & ~ends)
        def _():
            slot = lax.rem(o, 2)
            got(zb.at[slot], r.gzr.at[sem, slot])
            plus(at, zb.at[slot])

        to = jnp.where(ends, mate, o)
        slot = jnp.where(o == mate, 2, jnp.where(ends, lax.rem(o, 2), 3))
        remote(at, zb.at[slot], r.gzs.at[sem], r.gzr.at[sem, jnp.minimum(slot, 2)], (2 * to + y, t)).start()

    def mid(k, *steps):
        g, yb, zb = grads[k]
        for i in steps or range(G - 1):
            o = turn(i)
            at = yb.at[o]
            got(at, r.gyr.at[k, o])
            plus(at, block(k, 2 * o + y))
            pass_on(i, at, zb, o, k)

    def part_c(b_):
        return r.GC.at[b_]

    def part_e(b_):
        return r.GD.at[b_, nd:4]

    def along(part, zb, sem, steps):
        for i in steps or range(G - 1):
            o = turn(i)
            for c, col in enumerate((1 - y, y)):
                pass_on(i, part(2 * o + col), zb.at[c], o, sem + c)

    def mid_c(*steps):
        along(part_c, r.ZC, 4, steps)

    def mid_e(*steps):
        along(part_e, r.ZE, 6, steps)

    def arrived(zb, sem):
        got(zb.at[2:4], r.gzr.at[sem, 2])
        return [zb.at[2], zb.at[3]]

    def summed(at, more, store):
        def total(i):
            acc = at[i].astype(f32)
            for o in more:
                acc = acc + o[i].astype(f32)
            store(i, acc)

        each(at.shape[0], total)

    def fin(k, store):
        g, yb, zb = grads[k]
        at = yb.at[z]
        got(at, r.gyr.at[k, z])
        summed(at, arrived(zb, k) + [block(k, 2 * z + y)], store)

    def cross(part, zb, sem, to, i):
        other = part(2 * z + 1 - y)

        def store(j, acc):
            other[j] = acc.astype(bf16)

        summed(other, arrived(zb.at[0], sem), store)
        remote(other, to, r.gys.at[i], r.gyr.at[i, 0], ypeer).start()

    def cross_c():
        cross(part_c, r.ZC, 4, r.YC, 4)

    def cross_e():
        cross(part_e, r.ZE, 6, r.YE, 5)

    def fin_e():
        got(r.YE, r.gyr.at[5, 0])

        def store(j, acc):
            r.OD[pl.ds((nd + j) * (rd // 4), rd // 4)] = acc

        summed(part_e(2 * z + y), arrived(r.ZE.at[1], 7) + [r.YE], store)

    def fin_c(store):
        summed(r.GC.at[2 * z + y], arrived(r.ZC.at[1], 5), store)

    def crossed_c():
        got(r.YC, r.gyr.at[4, 0])

    def reduced_sent():
        for k, (g, yb, zb) in grads.items():
            got(block(k, slice(0, G)), r.gys.at[k])
            got(block(k, slice(0, 3)), r.gzs.at[k])
        got(r.YC, r.gys.at[4])
        got(r.YE, r.gys.at[5])
        for sem in (4, 5):
            got(r.GC.at[0:3], r.gzs.at[sem])
            got(r.GD.at[0:3, nd:4], r.gzs.at[sem + 2])

    fb = Fw // 4

    def grad_down(i):
        j = turn(i)
        c = pl.ds(pl.multiple_of(j * fb, fb), fb)
        rows = r.ACT[:, :, c].reshape(S * L, fb)
        g = dot_tn(rows, r.COT[...].reshape(S * L, M)).astype(bf16)
        r.GD[pl.ds(j * bq, bq)] = g.reshape(bq, 4, rd // 4, M)
        to_y(0, j)


    def back_feed(s):
        cot = r.COT[s].reshape(L, M)
        for j in range(4):
            c = slice(j * fb, (j + 1) * fb)
            wd = r.WD[bq * j : bq * (j + 1)].reshape(fb, M)
            d_act = dot_nt(cot, wd).astype(bf16).astype(f32)
            d_pre = d_act * r.GP[s, :, c].astype(f32)
            total = jnp.sum(d_pre, axis=0, keepdims=True)
            for i in range(fb // 128):
                at = j * (fb // 128) + i
                r.SMG[at : at + 1] += total[:, 128 * i : 128 * (i + 1)]
            r.GP[s, :, c] = d_pre.astype(bf16)
        m1 = jnp.zeros((L, 1), f32)
        m2 = jnp.zeros((L, 1), f32)
        for q in range(4):
            c = slice(q * Cw, (q + 1) * Cw)
            dn = dot_nt(r.GP[s], r.WU[bq * q : bq * (q + 1)].reshape(Cw, Fw))
            g = dn * r.VV[0:1, c]
            m1 = m1 + jnp.sum(g, axis=1, keepdims=True)
            m2 = m2 + jnp.sum(g * xhat_of(s, q), axis=1, keepdims=True)
            r.DNP[q, s] = dn.astype(bf16)
        lane = lax.broadcasted_iota(jnp.int32, (L, 128), 1)
        both = jnp.where(lane == 0, m1, jnp.where(lane == 1, m2, 0.0)) * (1.0 / M)
        pick = (
            lax.broadcasted_iota(jnp.int32, (8, 128), 0) == lax.broadcasted_iota(jnp.int32, (8, 128), 1)
        ).astype(f32)
        r.ST[t, s] = lax.dot_general(
            pick, both, (((1,), (1,)), ((), ())), precision=lax.Precision.HIGHEST, preferred_element_type=f32
        )
        fold_send(2, s)
        ex_send(3, r.er.at[3, s, 0], lambda q: r.ST.at[t, s], lambda d: r.ST.at[t, s])
        fold_late(2, s)


    def grad_up(i):
        j = turn(i)
        c = pl.ds(pl.multiple_of(j * Cw, Cw), Cw)
        rows = r.NRM[:, :, :, c].reshape(S * L, Cw)
        g = dot_tn(rows, r.GP[...].reshape(S * L, Fw)).astype(bf16)
        r.GU[pl.ds(j * bq, bq)] = g.reshape(bq, 4, rw, Fw)
        to_y(1, j)


    def back_norm(s):
        dn = folded(2, s)
        got(r.ST.at[0:3, s], r.er.at[3, s, 0])
        st = r.ST[0, s] + r.ST[1, s] + r.ST[2, s] + r.ST[3, s]
        side = lax.broadcasted_iota(jnp.int32, (8, 128), 0)
        col_of = lambda i: lax.dot_general(
            st,
            (side == i).astype(f32),
            (((0,), (0,)), ((), ())),
            precision=lax.Precision.HIGHEST,
            preferred_element_type=f32,
        )[:, :1]
        m1, m2 = col_of(0), col_of(1)
        inv = r.MU[s, :, 1:2]
        xhat = (r.RES[t, s].astype(f32) - r.MU[s, :, :1]) * inv
        cot = r.COT[s, :, :, tc].reshape(L, Cw).astype(f32)
        for i, v in enumerate((cot, dn * xhat, dn)):
            total = jnp.sum(v, axis=0, keepdims=True)
            for k in range(Cw // 128):
                at = Fw // 128 + i * (Cw // 128) + k
                r.SMG[at : at + 1] += total[:, 128 * k : 128 * (k + 1)]
        d_resid = cot + (dn * r.VV[0:1, tc] - m1 - xhat * m2) * inv
        r.DR[s] = d_resid
        db = d_resid.astype(bf16)
        r.DB[s] = db
        for q in range(4):
            r.DMP[q, s] = dot_nt(db, wo(q)).astype(bf16)
        fold_send(4, s)
        fold_late(4, s)

    def grad_out():
        for q in range(4):
            g = dot_tn(r.MIX[q].reshape(S * L, Cw), r.DB[...].reshape(S * L, Cw))
            r.GA[bq * q : bq * (q + 1), :, :, 3 * Cw :] = g.astype(bf16).reshape(bq, 4, rw, Cw)
        each(G, lambda i: to_y(2, turn(i)))

    def by_tier(rows, c, sent, come):
        for d in (1, 2, 3):
            remote(r.GA.at[rows, t ^ d, :, c], r.WU.at[rows, t, :, c], sent, come, (b, t ^ d)).start()
        r.WU[rows, t, :, c] = r.GA[rows, t, :, c]

    def out_rows(s):
        for q in range(4):
            c = slice(q * Cw, (q + 1) * Cw)
            o = jnp.dot(r.ACT[s], r.WD[:, :, c].reshape(Fw, Cw), preferred_element_type=f32)
            mine = (t == q).astype(f32)
            o = o + mine * (r.RT[s] + r.VV[2:3, c])
            r.OP[s, :, :, c] = o.astype(bf16).reshape(4 * nu, 16, Cw)
        fold_send(5, s)


    hc = wide(t * Cw + Hw * y, Hw)

    def windows(k, g):
        buf, at = (r.MEMX, 4 * k) if g else (r.CTX, 4 * nu + 4 * k)
        return buf.at[:, at : at + 4]

    def compress():
        sums = jnp.zeros((1, Hw), f32)
        for g in (0, 1):
            conv = r.VV[3:4, hc]
            pooled = 0.0
            for k in range(3):
                wk = r.WC[:, :, :, k * Hw : (k + 1) * Hw].reshape(M, Hw)
                conv = conv + jnp.dot(windows(k, g)[...].reshape(S * nw, M), wk, preferred_element_type=f32)
                pooled = pooled + windows(k, g)[:, :, :, hc].reshape(S * nw, Hw).astype(f32)
            marks = (r.MKX if g else r.MK)[...].reshape(S * nw, 128)
            fresh = (marks[:, :1] * conv).astype(bf16).reshape(S, nw, Hw)
            if g:
                r.NEWX[...] = fresh
            else:
                r.NEW[t, :, :, wide(Hw * y, Hw)] = fresh
            d_conv = marks[:, 64:65] * (conv - pooled * (1.0 / 3.0))
            sums = sums + jnp.sum(d_conv, axis=0, keepdims=True)
            r.DC[g] = d_conv.astype(bf16)
        r.SMG[pl.ds(Fw // 128 + 3 * (Cw // 128) + y, 1)] = sums
        remote(r.NEWX, r.NEW.at[t, :, :, wide(Hw * y, Hw)], r.ns.at[2], r.ns.at[3], ypeer).start()
        left_all(r.NEWX, r.ns.at[2])
        for k in range(3):
            grad = sum(dot_tn(windows(k, g)[...].reshape(S * nw, M), r.DC[g]) for g in (0, 1))
            r.GC[:, :, :, k * Hw : (k + 1) * Hw] = grad.astype(bf16).reshape(nb, 4, rw, Hw)

    slope_row = Fw // 128 + 4 * (Cw // 128)

    def back_attend(s):
        dm = folded(4, s).astype(bf16)
        lane = lax.broadcasted_iota(jnp.int32, (1, 128), 1)
        for h in range(ht):
            c = slice(h * hd, (h + 1) * hd)
            cv = slice(Cw + h * hd, Cw + (h + 1) * hd)
            p = r.PR[s, h]
            dp = dot_nt(dm[:, c], r.KV[s, :, cv])
            delta = jnp.sum(p * dp, axis=1, keepdims=True)
            ds = p * (dp - delta)
            part = jnp.sum(jnp.sum(ds * r.DIST[...], axis=0, keepdims=True), axis=1, keepdims=True)
            r.SMG[slope_row : slope_row + 1] -= jnp.where(lane == t * ht + h, part, 0.0)
            dr = (ds * scale).astype(bf16)
            dq = jnp.dot(dr, r.KV[s, :, c], preferred_element_type=f32).astype(bf16)
            dk = dot_tn(dr, r.Q[s, :, c]).astype(bf16)
            dv = dot_tn(p.astype(bf16), dm[:, c]).astype(bf16)
            r.Q[s, :, c] = dq
            r.KV[s, :, c] = dk
            r.KV[s, :, cv] = dv


    def grad_proj(i):
        j = turn(i)
        c = pl.ds(pl.multiple_of(j * Cw, Cw), Cw)
        gq = jnp.zeros((Cw, Cw), f32)
        gkv = jnp.zeros((Cw, 2 * Cw), f32)
        for s in range(S):
            gq = gq + dot_tn(r.CTX[s, 8 * nu : 12 * nu, :, c].reshape(L, Cw), r.Q[s])
            gkv = gkv + dot_tn(r.CTX[s, :, :, c].reshape(C3, Cw), r.KV[s])
        rows = pl.ds(j * bq, bq)
        r.GA[rows, :, :, :Cw] = gq.astype(bf16).reshape(bq, 4, rw, Cw)
        r.GA[rows, :, :, Cw : 3 * Cw] = gkv.astype(bf16).reshape(bq, 4, rw, 2 * Cw)
        by_tier(rows, slice(0, 3 * Cw), r.xs.at[0], r.xr.at[j])

    def proj_y(*steps):
        for i in steps:
            j = turn(i)
            got(r.WU.at[pl.ds(j * bq, bq), 0:3, :, : 3 * Cw], r.xr.at[j])
            to_y(3, j)

    def own_out(s):
        r.OR[1, s] = folded(5, s).astype(bf16)

    def input_rows(s):
        x = jnp.concatenate([r.Q[s], r.KV[s, 2 * L :]], axis=1)
        for q in range(4):
            c = slice(q * Cw, (q + 1) * Cw)
            w = r.WA[bq * q : bq * (q + 1), :, :, : 3 * Cw].reshape(Cw, 3 * Cw)
            o = dot_nt(x, w) + (t == q).astype(f32) * r.DR[s]
            r.NRM[s, :, :, c] = o.astype(bf16).reshape(4 * nu, 16, Cw)
        fold_send(6, s)
        fold_late(6, s)


    def keep(o):
        def store(i, acc):
            o[pl.ds(i * (rd // 4), rd // 4)] = acc

        return store

    def across(q, acc):
        for i in range(3):
            r.OA[i, :, wide(q * Cw, Cw)] = acc[:, i * Cw : (i + 1) * Cw]

    def hold(m):
        def store(i, acc):
            m[i] = acc.astype(bf16)

        return store

    def tier_back(k, m, tb):
        for d in (1, 2, 3):
            remote(m.at[t ^ d], tb.at[t], r.gts.at[k], r.gtr.at[k], (b, t ^ d)).start()
        left_all(tb.at[0:3], r.gts.at[k])

    def small_y():
        remote(r.SMG, r.YS, r.ss.at[0], r.sr.at[0], ypeer).start()
        left_all(r.SMG, r.ss.at[0])

    def small_z():
        got(r.YS, r.sr.at[0])
        r.ZS[z] = r.SMG[...] + r.YS[...]
        for d in range(1, G):
            remote(r.ZS.at[z], r.ZS.at[z], r.ss.at[1], r.sr.at[1], (2 * zs[d] + y, t)).start()
        left_all(r.ZS.at[0 : G - 1], r.ss.at[1])

    def small_tier():
        got(r.ZS.at[0 : G - 1], r.sr.at[1])
        acc = r.ZS[0]
        for zz in range(1, G):
            acc = acc + r.ZS[zz]
        r.os[t] = acc
        for d in (1, 2, 3):
            remote(r.os.at[t], r.os.at[t], r.gts.at[3], r.gtr.at[3], (b, t ^ d)).start()
        left_all(r.os.at[0:3], r.gts.at[3])

    def own_input(s):
        r.IG[s] = folded(6, s)

    mineU, mineC, mineO = r.GU.at[2 * z + y], r.GC.at[2 * z + y], r.GA.at[2 * z + y, :, :, 3 * Cw :]
    def give(i, src, dst):
        pltpu.make_async_copy(src, dst, r.osem.at[i]).start()

    def rows_out(i, src, dst):
        for j in range(nu):
            give(i, src.at[:, j], dst.at[:, 16 * j : 16 * j + 16])

    backs = {0: (mineU, r.TU), 1: (mineC, r.TC), 2: (mineO, r.TO), 4: (r.YC, r.TB)}

    def lay(k, q, rows):
        if k == 0:
            for i in range(nb):
                r.OU[:, wide((4 * i + q) * rd, rd)] = rows[:, i * rd : (i + 1) * rd].astype(f32)
        elif k == 2:
            r.OA[3, :, wide(q * Cw, Cw)] = rows.astype(f32)
        else:
            half = y if k == 1 else 1 - y
            for i in range(3):
                r.OC[i, :, wide(q * Cw + Hw * half, Hw)] = rows[:, i * Hw : (i + 1) * Hw].astype(f32)

    def tier_out(k):
        m, tb = backs[k]
        lay(k, t, m[t])
        got(tb.at[0:3], r.gtr.at[k])
        for d in (1, 2, 3):
            lay(k, t ^ d, tb[t ^ d])

    def given():
        for i, (src, dst) in ((0, (r.OU, r.ou)), (1, (r.OC, r.oc)), (2, (r.OA, r.oa)), (3, (r.OD, r.od))):
            pltpu.make_async_copy(src, dst, r.osem.at[i]).wait()
        for i, (src, dst) in ((5, (r.OR.at[1], r.out)), (6, (r.IG, r.ig)), (4, (r.OR.at[0], r.om)), (8, (r.OR.at[2], r.ocm))):
            for j in range(nu):
                pltpu.make_async_copy(src.at[:, j], dst.at[:, 16 * j : 16 * j + 16], r.osem.at[i]).wait()

    def small_out():
        got(r.os.at[0:3], r.gtr.at[3])

    slots = L - nw
    windows_of = [(q, max(R * q - slots, 0), R - max(slots - R * q, 0)) for q in range(4) if slots < R * (q + 1)]

    def new_send():
        got(r.NEWX, r.ns.at[3])
        for q, at, n in windows_of:
            part = r.NEW.at[t, :, at : at + n]
            if_(t != q, remote(part, part, r.ns.at[0], r.ns.at[1], (b, q)).start)

    def new_sent():
        for q, at, n in windows_of:
            if_(t != q, lambda: got(r.NEW.at[0, :, at : at + n], r.ns.at[0]))

    def new_out():
        for q, at, n in windows_of:
            if_(t == q, lambda: got(r.NEW.at[0:3, :, at : at + n], r.ns.at[1]))

    def memories():
        side = lax.broadcasted_iota(jnp.int32, (16, 1), 0)
        for s in range(S):
            for i in range(nu):
                fresh = side + (R * t + 16 * i) < r.evicted[s]
                r.OR[0, s, i] = jnp.where(fresh, r.CTX[s, 8 * nu + nu * t + i], r.MEMV[s, 16 * i : 16 * i + 16])
                r.OR[2, s, i] = r.CTX[s, nu * t + i]
        for q, at, n in windows_of:

            @pl.when(t == q)
            def _(at=at, n=n):
                for i in range((R - n) // 16, nu):
                    w = at + 16 * i - (R - n)
                    for s in range(S):
                        written = 3 * (side + w) + 3 <= r.evicted[s]
                        for p in range(4):
                            c = slice(p * Cw, (p + 1) * Cw)
                            old = r.CTX[s, nu * t + i, :, c]
                            r.OR[2, s, i, :, c] = jnp.where(written, r.NEW[p, s, w : w + 16], old)

    def drain():
        for n in parts:
            if n != "U":
                all_sent(n)
        got(r.GA.at[:, 0:3, :, : 3 * Cw], r.xs.at[0])
        for ref, sem in sends:
            got(ref, sem)
        act_sent()
        new_sent()
        reduced_sent()
        for e, ref in enumerate((r.MIX, r.RES, r.DNP, r.ST, r.DMP, r.OR, r.IR)):
            got(ref.at[0:3], r.es.at[e])
        given()

    here(r.wd, r.WD.at[b], 0)
    here(r.mem, r.MEMV, 7)
    for n in "ACHU":
        tier_own(n)
    act_own()
    greet(G, True, True)
    tier_start("A")
    tier_start("H")
    small_start()
    tier_start("U")
    tier_start("C")
    act_start(0, 1)
    got(r.WD.at[b], r.lsem.at[0])
    own_z("D")
    own_z("E")
    own_y("E")
    own_y("D")
    got(r.MEMV, r.lsem.at[7])
    memory_rows()
    act_start(2, 3, 4, 5, 6)
    tier_wait("A")
    own_z("A")
    own_y("A")
    tier_wait("H")
    own_y("C")
    tier_wait("S")
    own_z("S")
    own_y("S")
    table()
    onward("A", 1)
    onward("S", 1)
    onward("A", 2)
    onward("S", 2)
    tier_wait("U")
    own_z("U")
    y_wait("E")
    own_z("F")
    onward("A", 3)
    own_y("U")
    onward("S", 3)
    onward("U", 1)
    act_forward(0, 1, 2, 3, 4)
    act_wait(0)
    y_wait("A")
    each(S, project, {0: lambda: onward("U", 2), 1: lambda: onward("D", 1, cross=False)})
    onward("E", 1)
    tier_wait("C")
    y_wait("C")
    each(S, attend, {1: lambda: onward("U", 3)})
    memory_y()
    over("D", 1)
    onward("F", 1)
    onward("D", 2)
    own_z("C")
    own_z("X")
    spread_pass(0, 0, r.MIX)
    each(S, residual, {1: lambda: onward("E", 2)})
    onward("F", 2)
    onward("D", 3)
    onward("C", 1)
    y_wait("S")
    vectors()
    act_forward(5, 6)
    y_wait("U")
    spread_pass(1, 0, r.RES)
    each(S, feed, {0: lambda: onward("X", 1), 2: lambda: onward("E", 3)})
    memory_come()
    act_start(7, 8, 9, 10)
    onward("F", 3)
    act_wait(1)
    act_wait(2)
    each(4, grad_down)
    mid_e(0)
    at_ends(both(lambda: mid_e(1), lambda: mid_e(2)))()
    onward("C", 2)
    onward("X", 2)
    y_wait("D")
    all_sent("U")
    each(
        S,
        back_feed,
        {
            0: lambda: onward("C", 3),
            1: both(inside(lambda: mid_e(1)), lambda: mid(0, 0)),
            2: both(lambda: onward("X", 3), lambda: act_forward(7, 8, 9, 10)),
            3: at_ends(lambda: mid(0, 1)),
        },
    )
    fold_pass(2, S - 1)
    each(2, out_rows)
    inside(both(lambda: mid_e(2), lambda: mid(0, 1)))()
    fold_pass(5, 0)
    fold_pass(5, 1)
    act_wait(3)
    act_wait(4)
    compress()
    mid_c(0)
    each(4, grad_up)
    mid(0, 2)
    each(S, back_norm)
    fold_pass(4, S - 1)
    grad_out()
    each(S - 2, lambda s: out_rows(s + 2))
    cross_e()
    mid_c(1)
    fold_pass(5, 2)
    fold_pass(5, 3)
    each(S, back_attend, {0: lambda: mid(1, 0)})
    mid_c(2)
    small_y()
    each(4, grad_proj, {1: at_ends(lambda: mid(1, 1))})
    inside(lambda: mid(1, 1))()
    at_ends(lambda: mid(1, 2))()
    proj_y(0)
    each(S, input_rows)
    proj_y(1)
    cross_c()
    fold_pass(6, S - 1)
    at_ends(lambda: mid(2, 0, 1))()
    small_z()
    inside(lambda: mid(1, 2))()
    proj_y(2)
    at_ends(both(lambda: mid(2, 2), lambda: mid(3, 0)))()
    inside(lambda: mid(2, 0, 1, 2))()
    fin_c(hold(mineC))
    tier_back(1, mineC, r.TC)
    proj_y(3)
    new_send()
    inside(lambda: mid(3, 0))()
    fin(1, hold(mineU))
    tier_back(0, mineU, r.TU)
    mid(3, 1)
    fin(0, keep(r.OD))
    fin_e()
    give(3, r.OD, r.od)
    fin(2, hold(mineO))
    tier_back(2, mineO, r.TO)
    mid(3, 2)
    crossed_c()
    tier_back(4, r.YC, r.TB)
    small_tier()
    each(S, own_out)
    rows_out(5, r.OR.at[1], r.out)
    new_out()
    memories()
    rows_out(4, r.OR.at[0], r.om)
    rows_out(8, r.OR.at[2], r.ocm)
    each(S, own_input)
    rows_out(6, r.IG, r.ig)
    tier_out(1)
    tier_out(0)
    give(0, r.OU, r.ou)
    tier_out(4)
    tier_out(2)
    give(1, r.OC, r.oc)
    fin(3, across)
    give(2, r.OA, r.oa)
    small_out()
    drain()

def whole_layer(nb, ht, hd, arrays):
    S, R, M = arrays["seg"].shape
    rw, rd, rs = arrays["w_query"].shape[0], arrays["wd"].shape[0], M // (4 * nb)
    nu = R // 16
    G, Cw, Fw, L = nb // 2, M // 4, nb * rd, 64 * nu
    dma = pltpu.SemaphoreType.DMA
    V = lambda shape, dtype=bf16: pltpu.VMEM(shape, dtype)
    nd = 3
    D4, A4, U4, C4 = (4, rd // 4, M), (4, rw, 4 * Cw), (4, rw, Fw), (4, rw, 3 * Cw // 2)
    ins = arrays
    outs = dict(
        out=((S, R, M), bf16),
        ig=((S, R, M), f32),
        om=((S, R, M), bf16),
        ocm=((S, R, M), bf16),
        od=((rd, M), f32),
        ou=((rw, 4 * Fw), f32),
        oc=((3, rw, M), f32),
        oa=((4, rw, M), f32),
        os=((4, 24, 128), f32),
    )
    scratch = dict(
        WA=V((nb,) + A4),
        WU=V((nb,) + U4),
        WC=V((nb,) + C4),
        WCX=V(C4),
        MEMX=V((S, 12, 16, M)),
        MKX=V((S, 4, L // 12, 128), f32),
        NEWX=V((S, L // 3, Cw // 2)),
        WD=V((nb, rd, M)),
        SM=V((nb, 4, 8, 128), f32),
        CTX=V((S, 12 * nu, 16, M)),
        COT=V((S, 4 * nu, 16, M)),
        MK=V((S, 4, L // 12, 128), f32),
        DIST=V((L, 3 * L), f32),
        VV=V((8, max(M, Fw)), f32),
        SMG=V((24, 128), f32),
        Q=V((S, L, Cw)),
        KV=V((S, 3 * L, 2 * Cw)),
        PR=V((S, ht, L, 3 * L), f32),
        MIX=V((4, S, L, Cw)),
        RT=V((S, L, Cw), f32),
        RES=V((4, S, L, Cw)),
        MU=V((S, L, 128), f32),
        NRM=V((S, 4 * nu, 16, M)),
        ACT=V((S, L, Fw)),
        GP=V((S, L, Fw)),
        DNP=V((4, S, L, Cw)),
        DNR=V((3, S, L, Cw)),
        ST=V((4, S, 8, L), f32),
        DR=V((S, L, Cw), f32),
        DB=V((S, L, Cw)),
        DMP=V((4, S, L, Cw)),
        DMR=V((3, S, L, Cw)),
        OP=V((S, 4 * nu, 16, M)),
        OR=V((3, S, nu, 16, M)),
        IR=V((3, S, nu, 16, M)),
        DC=V((2, S * L // 3, Cw // 2)),
        GD=V((nb,) + D4),
        GU=V((nb,) + U4),
        GC=V((nb,) + C4),
        GA=V((nb,) + A4),
        YD=V((G, nd) + D4[1:]),
        YE=V((4 - nd,) + D4[1:]),
        YU=V((G,) + U4),
        YC=V(C4),
        YO=V((G, 4, rw, Cw)),
        YA=V((G, 4, rw, 3 * Cw)),
        ZD=V((4, nd) + D4[1:]),
        ZE=V((2, 4, 4 - nd) + D4[1:]),
        ZU=V((4,) + U4),
        ZC=V((2, 4) + C4),
        ZO=V((4, 4, rw, Cw)),
        ZA=V((4, 4, rw, 3 * Cw)),
        YS=V((24, 128), f32),
        ZS=V((G, 24, 128), f32),
        TU=V(U4),
        TO=V((4, rw, Cw)),
        TC=V(C4),
        TB=V(C4),
        NEW=V((4, S, L // 3, Cw)),
        IG=V((S, nu, 16, M), f32),
        OD=V((rd, M), f32),
        OU=V((rw, 4 * Fw), f32),
        OC=V((3, rw, M), f32),
        OA=V((4, rw, M), f32),
        MEMV=V((S, R, M)),
        osem=dma((9,)),
        lsem=dma((8,)),
        ts=dma((5,)),
        tr=dma((5,)),
        zs=dma((8,)),
        zr=dma((10, G - 1)),
        ys=dma((8,)),
        yr=dma((8,)),
        ms=dma((4,)),
        acs=dma((5,)),
        acc=dma((5,)),
        acf=dma((5,)),
        acx=dma((11,)),
        es=dma((7,)),
        er=dma((7, S, 2)),
        ns=dma((4,)),
        gys=dma((6,)),
        gyr=dma((6, G)),
        gzs=dma((8,)),
        gzr=dma((8, 3)),
        ss=dma((2,)),
        sr=dma((2,)),
        xs=dma((1,)),
        xr=dma((G,)),
        gts=dma((5,)),
        gtr=dma((5,)),
    )
    names = list(ins) + list(outs) + list(scratch)
    near = dict(gain=VM, bias=VM, bdown=VM, bconv=VM, bup=VM, mask=VM, evicted=SM, slopes=SM)
    return pl.pallas_call(
        functools.partial(layer_kernel, names, (nb, nu, S, ht, hd, M, Cw, rw, rd, rs)),
        out_shape=[jax.ShapeDtypeStruct(s, d) for s, d in outs.values()],
        in_specs=[near.get(n, ANY) for n in ins],
        out_specs=[VM if n == "os" else ANY for n in outs],
        scratch_shapes=list(scratch.values()),
        compiler_params=pltpu.CompilerParams(
            collective_id=9, has_side_effects=True, vmem_limit_bytes=63 * 2**20
        ),
        name="whole_layer",
    )(*ins.values())


def finish_kernel(names, shape, *refs):
    r = Names(names, refs)
    nb, rs, rd, Fw, Cw, heads = shape
    b, t = lax.axis_index("batch"), lax.axis_index("tier")
    squares = (r.o_q, r.o_k, r.o_v, r.o_o)
    moves = [(r.out, r.o_out), (r.ig, r.o_ig), (r.od, r.o_od), (r.ou, r.o_ou), (r.oc, r.o_oc), (r.om, r.o_mem), (r.ocm, r.o_comp)]
    n = len(moves)
    bufs = refs[len(names) :]
    small = pltpu.make_async_copy(r.os, r.osv, r.sem.at[n])
    small.start()
    into = [pltpu.make_async_copy(src, buf, r.sem.at[i]) for i, ((src, _), buf) in enumerate(zip(moves, bufs))]
    into.append(pltpu.make_async_copy(r.oa, bufs[n], r.sem.at[n + 1]))
    onto = [
        [pltpu.make_async_copy(buf, dst, r.sem.at[n + 2 + i])] for i, ((_, dst), buf) in enumerate(zip(moves, bufs))
    ]
    onto.append([pltpu.make_async_copy(bufs[n].at[i], o, r.sem.at[2 * n + 2 + i]) for i, o in enumerate(squares)])
    for cp in into:
        cp.start()
    small.wait()
    spot = 4 * b + t
    block, inner = spot // (Cw // rs), lax.rem(spot, Cw // rs)
    half, group = inner // (128 // rs), lax.rem(inner, 128 // rs)
    for i, o in enumerate((r.o_down, r.o_gain, r.o_bias, r.o_conv)):
        row = r.osv[block, pl.ds(Fw // 128 + (Cw // 128) * i + half, 1), :]
        turned = pltpu.roll(jnp.broadcast_to(row, (8, 128)), lax.rem(128 - rs * group, 128), 1)
        o[...] = turned[0:1, :rs]
    r.o_up[...] = r.osv[t, pl.ds(b, 1), :rd]
    at = Fw // 128 + 4 * (Cw // 128)
    total = r.osv[0, at : at + 1]
    for q in range(1, 4):
        total = total + r.osv[q, at : at + 1]
    r.o_slopes[...] = total[:, :heads]
    for cp, then in zip(into, onto):
        cp.wait()
        for c in then:
            c.start()
    for then in onto:
        for c in then:
            c.wait()


def finish(nb, heads, arrays):
    S, R, M = arrays["out"].shape
    rw, rd, rs = arrays["oa"].shape[1], arrays["od"].shape[0], M // (4 * nb)
    Cw, Fw = M // 4, nb * rd
    rows, mat, vec = (S, R, M), (rw, M), (1, rs)
    outs = dict(
        o_out=(rows, bf16, ANY),
        o_ig=(rows, f32, ANY),
        o_mem=(rows, bf16, ANY),
        o_comp=(rows, bf16, ANY),
        o_q=(mat, f32, ANY),
        o_k=(mat, f32, ANY),
        o_v=(mat, f32, ANY),
        o_o=(mat, f32, ANY),
        o_ou=((rw, 4 * Fw), f32, ANY),
        o_up=((1, rd), f32, VM),
        o_od=((rd, M), f32, ANY),
        o_down=(vec, f32, VM),
        o_gain=(vec, f32, VM),
        o_bias=(vec, f32, VM),
        o_oc=((3, rw, M), f32, ANY),
        o_conv=(vec, f32, VM),
        o_slopes=((1, heads), f32, VM),
    )
    moved = ("out", "ig", "od", "ou", "oc", "om", "ocm", "oa")
    n = len(moved) - 1
    return pl.pallas_call(
        functools.partial(
            finish_kernel, list(arrays) + list(outs) + ["sem", "osv"], (nb, rs, rd, Fw, Cw, heads)
        ),
        out_shape=[jax.ShapeDtypeStruct(s, d) for s, d, _ in outs.values()],
        in_specs=[ANY] * len(arrays),
        out_specs=[o[2] for o in outs.values()],
        scratch_shapes=[pltpu.SemaphoreType.DMA((2 * n + 6,)), pltpu.VMEM(arrays["os"].shape, f32)]
        + [pltpu.VMEM(arrays[i].shape, arrays[i].dtype) for i in moved],
        compiler_params=pltpu.CompilerParams(vmem_limit_bytes=63 * 2**20),
        name="finish",
    )(*arrays.values())


def per_device_fused(
    nb,
    segment,
    memory,
    compressed,
    evicted,
    window_mask,
    cotangent,
    w_query,
    w_key,
    w_value,
    w_output,
    w_up,
    b_up,
    w_down,
    b_down,
    ln_gain,
    ln_bias,
    w_conv,
    b_conv,
    slopes,
):
    S, R, M = segment.shape
    heads = slopes.shape[0]
    line = lambda v: v.reshape(1, -1)
    names = ("out", "ig", "om", "ocm", "od", "ou", "oc", "oa", "os")
    made = whole_layer(
        nb,
        heads // 4,
        M // heads,
        dict(
            w_query=w_query,
            w_key=w_key,
            w_value=w_value,
            w_output=w_output,
            w_up=w_up,
            w_conv=w_conv,
            wd=w_down,
            comp=compressed,
            seg=segment,
            cot=cotangent,
            mem=memory,
            gain=line(ln_gain),
            bias=line(ln_bias),
            bdown=line(b_down),
            bconv=line(b_conv),
            bup=line(b_up),
            mask=window_mask,
            evicted=evicted,
            slopes=slopes,
        ),
    )
    outs = finish(nb, heads, dict(zip(names, made)))
    flat = (9, 11, 12, 13, 15, 16)
    return tuple(o.reshape(-1) if i in flat else o for i, o in enumerate(outs))


def solution(mesh):
    both = ("batch", "tier")
    rows = P("batch", "tier", None)
    mat, vec = P(both, None), P(both)
    nb = mesh.shape["batch"]

    def body(*args):
        fused = args[6].shape[0] % 16 == 0 and args[12].shape[0] == 128
        return (per_device_fused if fused else per_device)(nb, *args)

    return jax.shard_map(
        body,
        mesh=mesh,
        in_specs=(
            (rows, rows, rows, P("batch"), P("batch", "tier"), rows)
            + (mat, mat, mat, mat, mat, vec, mat, vec, vec, vec)
            + (P(None, both, None), vec, P())
        ),
        out_specs=(
            (rows, rows, rows, rows, mat, mat, mat, mat, mat, vec, mat, vec, vec, vec)
            + (P(None, both, None), vec, P())
        ),
        check_vma=False,
    )
```

```python
import functools
import math

import jax
import jax.numpy as jnp
from jax import lax
from jax.experimental import pallas as pl
from jax.experimental.pallas import tpu as pltpu
from jax.sharding import PartitionSpec as P

norm_eps = 1e-05
MESH = pl.DeviceIdType.MESH
ANY = pl.BlockSpec(memory_space=pl.ANY)
VM = pl.BlockSpec(memory_space=pltpu.VMEM)
SM = pl.BlockSpec(memory_space=pltpu.SMEM)
f32 = jnp.float32
bf16 = jnp.bfloat16


def remote(src, dst, send, recv, device):
    return pltpu.make_async_remote_copy(
        src_ref=src,
        dst_ref=dst,
        send_sem=send,
        recv_sem=recv,
        device_id=device,
        device_id_type=MESH,
    )


def places(groups):
    b, t = lax.axis_index("batch"), lax.axis_index("tier")
    z, y = b // 2, lax.rem(b, 2)
    zs = [lax.rem(z + d, groups) for d in range(groups)]
    zback = [lax.rem(z + groups - d, groups) for d in range(groups)]
    return b, t, z, y, zs, zback


def greet(groups, tiers, columns):
    b, t, z, y, zs, _ = places(groups)
    barrier = pltpu.get_barrier_semaphore()
    peers = []
    if tiers:
        peers += [(b, t ^ d) for d in (1, 2, 3)]
    if columns:
        peers += [(2 * zz + y, t) for zz in zs[1:]] + [(b ^ 1, t)]
    for peer in peers:
        pl.semaphore_signal(barrier, inc=1, device_id=peer, device_id_type=MESH)
    pl.semaphore_wait(barrier, len(peers))


def gather_kernel(groups, nu, *refs):
    (wa, wu, wc, wd, sm, comp, mem, seg, cot, mk) = refs[:10]
    (WA, WU, WC, WD, SM, CTX, COT, MK) = refs[10:18]
    lsem, ts, tr, zsd, zr, ys, yr, acs, acr = refs[18:]
    G = groups
    b, t, z, y, zs, zback = places(G)
    greet(G, True, True)
    ypeer = (b ^ 1, t)
    local, sends = [], []

    def here(src, dst, i):
        cp = pltpu.make_async_copy(src, dst, lsem.at[i])
        cp.start()
        return cp

    kinds = [(sm, SM), (wa, WA), (wu, WU), (wc, WC)]
    own = []
    for k, (src, dst) in enumerate(kinds):
        mine = src if k == 0 else src.at[t]
        own.append(here(mine, dst.at[b, t], k))
        for d in (1, 2, 3):
            piece = src if k == 0 else src.at[t ^ d]
            cp = remote(piece, dst.at[b, t], ts.at[k, d - 1], tr.at[k, d - 1], (b, t ^ d))
            cp.start()
            sends.append(cp)
    own.append(here(wd, WD.at[b], 4))
    pieces = [
        (comp, lambda q: CTX.at[:, pl.ds(nu * q, nu)]),
        (mem.at[:, 0], lambda q: CTX.at[:, 4 * nu + q]),
        (mem.at[:, 1], lambda q: CTX.at[:, 4 * nu + 4 + q]),
        (mem.at[:, 2], lambda q: CTX.at[:, 4 * nu + 8 + q]),
        (seg, lambda q: CTX.at[:, pl.ds(8 * nu + nu * q, nu)]),
        (mk, lambda q: MK.at[:, q]),
        (cot, lambda q: COT.at[:, pl.ds(nu * q, nu)]),
    ]
    for i, (src, at) in enumerate(pieces):
        own.append(here(src, at(t), 5 + i))
        for j, d in enumerate((1, 2)):
            cp = remote(src, at(t), acs.at[i, j], acr.at[i, j], (b, t ^ d))
            cp.start()
            sends.append(cp)
    table = [SM, WA, WU, WD, WC]
    local_of = [0, 1, 2, 4, 3]
    for k, dst in enumerate(table):
        own[local_of[k]].wait()
        if k != 3:
            kk = local_of[k]
            for d in (1, 2, 3):
                remote(dst.at[b, t], dst.at[b, t ^ d], ts.at[kk, d - 1], tr.at[kk, d - 1], (b, t ^ d)).wait_recv()
        for d in range(1, G):
            cp = remote(dst.at[b], dst.at[b], zsd.at[k, d], zr.at[k, d], (2 * zs[d] + y, t))
            cp.start()
            sends.append(cp)
        cp = remote(dst.at[b], dst.at[b], ys.at[k, 0], yr.at[k, 0], ypeer)
        cp.start()
        sends.append(cp)
    for i, (src, at) in enumerate(pieces):
        remote(at(t ^ 2), at(t ^ 2), acs.at[i, 1], acr.at[i, 1], (b, t ^ 2)).wait_recv()
        cp = remote(at(t ^ 2), at(t ^ 2), acs.at[i, 2], acr.at[i, 2], (b, t ^ 1))
        cp.start()
        sends.append(cp)
    for k, dst in enumerate(table):
        for d in range(1, G):
            at = dst.at[2 * zback[d] + y]
            remote(at, at, zsd.at[k, d], zr.at[k, d], ypeer).wait_recv()
            cp = remote(at, at, ys.at[k, d], yr.at[k, d], ypeer)
            cp.start()
            sends.append(cp)
    for k, dst in enumerate(table):
        for d in range(G):
            at = dst.at[2 * zback[d] + (1 - y)]
            remote(at, at, ys.at[k, d], yr.at[k, d], ypeer).wait_recv()
    for i, (src, at) in enumerate(pieces):
        for j, q in ((0, t ^ 1), (2, t ^ 3)):
            remote(at(q), at(q), acs.at[i, j], acr.at[i, j], (b, t ^ 1)).wait_recv()
    for i in range(len(pieces)):
        own[5 + i].wait()
    for cp in sends:
        cp.wait_send()


def gather_all(nb, nu, wa, wu, wc, wd, sm, comp, mem, seg, cot, mk):
    G = nb // 2
    S, _, U, M = comp.shape
    out = [
        jax.ShapeDtypeStruct((nb,) + wa.shape, bf16),
        jax.ShapeDtypeStruct((nb,) + wu.shape, bf16),
        jax.ShapeDtypeStruct((nb,) + wc.shape, bf16),
        jax.ShapeDtypeStruct((nb,) + wd.shape, bf16),
        jax.ShapeDtypeStruct((nb, 4) + sm.shape, f32),
        jax.ShapeDtypeStruct((S, 12 * nu, U, M), bf16),
        jax.ShapeDtypeStruct((S, 4 * nu, U, M), bf16),
        jax.ShapeDtypeStruct((S, 4) + mk.shape[1:], f32),
    ]
    dma = pltpu.SemaphoreType.DMA
    return pl.pallas_call(
        functools.partial(gather_kernel, G, nu),
        out_shape=out,
        in_specs=[ANY] * 10,
        out_specs=[ANY] * 8,
        scratch_shapes=[
            dma((12,)),
            dma((4, 3)),
            dma((4, 3)),
            dma((5, G)),
            dma((5, G)),
            dma((5, G)),
            dma((5, G)),
            dma((7, 3)),
            dma((7, 3)),
        ],
        compiler_params=pltpu.CompilerParams(collective_id=0, has_side_effects=True),
        name="gather_all",
    )(wa, wu, wc, wd, sm, comp, mem, seg, cot, mk)


def spread_kernel(same, x, o, lsem, ss, rs):
    b, t = lax.axis_index("batch"), lax.axis_index("tier")
    greet(1, True, False)
    cps = []
    for d in (1, 2, 3):
        cp = remote(x if same else x.at[t ^ d], o.at[t], ss.at[d - 1], rs.at[d - 1], (b, t ^ d))
        cp.start()
        cps.append(cp)
    mine = pltpu.make_async_copy(x if same else x.at[t], o.at[t], lsem)
    mine.start()
    mine.wait()
    for d in (1, 2, 3):
        remote(o.at[t ^ d], o.at[t ^ d], ss.at[d - 1], rs.at[d - 1], (b, t ^ d)).wait_recv()
    for cp in cps:
        cp.wait_send()


def spread(x, same, cid):
    dma = pltpu.SemaphoreType.DMA
    shape = ((4,) + x.shape) if same else x.shape
    return pl.pallas_call(
        functools.partial(spread_kernel, same),
        out_shape=jax.ShapeDtypeStruct(shape, x.dtype),
        in_specs=[ANY],
        out_specs=ANY,
        scratch_shapes=[dma, dma((3,)), dma((3,))],
        compiler_params=pltpu.CompilerParams(collective_id=cid, has_side_effects=True),
        name="spread_%d" % cid,
    )(x)


def reduce_kernel(groups, *refs):
    GD, GU, GC, GA, SMG = refs[:5]
    OD, OU, OC, OA, OS = refs[5:10]
    YD, YU, YC, YA, YS, ZD, ZU, ZC, ZA, ZS, TU, TC, TA, MU, MC, MA, ys, yr, zsd, zr, ts, tr = refs[10:]
    G = groups
    b, t, z, y, zs, zback = places(G)
    greet(G, True, True)
    ypeer = (b ^ 1, t)
    sends = []
    kinds = [
        (GD, YD, ZD, OD, None, None),
        (GU, YU, ZU, OU, MU, TU),
        (GC, YC, ZC, OC, MC, TC),
        (GA, YA, ZA, OA, MA, TA),
    ]
    for k, (g, yb, *_) in enumerate(kinds):
        for d in range(G):
            zz = zs[(d + 1) % G]
            cp = remote(g.at[2 * zz + (1 - y)], yb.at[zz], ys.at[k, d], yr.at[k, d], ypeer)
            cp.start()
            sends.append(cp)
    cp = remote(SMG, YS, ys.at[4, 0], yr.at[4, 0], ypeer)
    cp.start()
    sends.append(cp)
    for k, (g, yb, zb, o, m, tb) in enumerate(kinds):
        for d in range(G):
            zz = zs[(d + 1) % G]
            at = yb.at[zz]
            remote(at, at, ys.at[k, d], yr.at[k, d], ypeer).wait_recv()

            def add(i, c, yb=yb, zz=zz, g=g):
                yb[zz, i] = (yb[zz, i].astype(f32) + g[2 * zz + y, i].astype(f32)).astype(bf16)
                return c

            lax.fori_loop(0, yb.shape[1], add, 0)
            if d < G - 1:
                cp = remote(at, zb.at[d], zsd.at[k, d], zr.at[k, d], (2 * zz + y, t))
                cp.start()
                sends.append(cp)
    remote(YS, YS, ys.at[4, 0], yr.at[4, 0], ypeer).wait_recv()
    ZS[z] = SMG[...] + YS[...]
    for d in range(G - 1):
        cp = remote(ZS.at[z], ZS.at[z], zsd.at[4, d], zr.at[4, d], (2 * zs[d + 1] + y, t))
        cp.start()
        sends.append(cp)
    for k, (g, yb, zb, o, m, tb) in enumerate(kinds):
        for d in range(G - 1):
            remote(zb.at[d], zb.at[d], zsd.at[k, d], zr.at[k, d], ypeer).wait_recv()

        def total(i, c, k=k, yb=yb, zb=zb, o=o, m=m):
            acc = yb[z, i].astype(f32)
            for d in range(G - 1):
                acc = acc + zb[d, i].astype(f32)
            if k == 0:
                o[i] = acc
            else:
                m[i] = acc.astype(bf16)
            return c

        lax.fori_loop(0, o.shape[0], total, 0)
        if k:
            for d in (1, 2, 3):
                cp = remote(m.at[t ^ d], tb.at[t], ts.at[k - 1, d - 1], tr.at[k - 1, d - 1], (b, t ^ d))
                cp.start()
                sends.append(cp)
    for d in range(G - 1):
        at = ZS.at[zback[d + 1]]
        remote(at, at, zsd.at[4, d], zr.at[4, d], ypeer).wait_recv()
    acc = ZS[0]
    for zz in range(1, G):
        acc = acc + ZS[zz]
    OS[t] = acc
    for d in (1, 2, 3):
        cp = remote(OS.at[t], OS.at[t], ts.at[3, d - 1], tr.at[3, d - 1], (b, t ^ d))
        cp.start()
        sends.append(cp)
    for k, (g, yb, zb, o, m, tb) in enumerate(kinds):
        if k:
            o[t] = m[t].astype(f32)
            for d in (1, 2, 3):
                at = tb.at[t ^ d]
                remote(at, at, ts.at[k - 1, d - 1], tr.at[k - 1, d - 1], (b, t ^ d)).wait_recv()
                o[t ^ d] = tb[t ^ d].astype(f32)
    for d in (1, 2, 3):
        at = OS.at[t ^ d]
        remote(at, at, ts.at[3, d - 1], tr.at[3, d - 1], (b, t ^ d)).wait_recv()
    for cp in sends:
        cp.wait_send()


def reduce_all(nb, gd, gu, gc, ga, sg):
    G = nb // 2
    dma = pltpu.SemaphoreType.DMA
    shapes = [x.shape[1:] for x in (gd, gu, gc, ga)]
    return pl.pallas_call(
        functools.partial(reduce_kernel, G),
        out_shape=[jax.ShapeDtypeStruct(s, f32) for s in shapes]
        + [jax.ShapeDtypeStruct((4,) + sg.shape, f32)],
        in_specs=[VM] * 5,
        out_specs=[VM] * 5,
        scratch_shapes=[pltpu.VMEM((G,) + s, bf16) for s in shapes]
        + [pltpu.VMEM(sg.shape, f32)]
        + [pltpu.VMEM((G - 1,) + s, bf16) for s in shapes]
        + [pltpu.VMEM((G,) + sg.shape, f32)]
        + [pltpu.VMEM(s, bf16) for s in shapes[1:]]
        + [pltpu.VMEM(s, bf16) for s in shapes[1:]]
        + [dma((5, G)), dma((5, G)), dma((5, G)), dma((5, G)), dma((4, 3)), dma((4, 3))],
        compiler_params=pltpu.CompilerParams(
            collective_id=1, has_side_effects=True, vmem_limit_bytes=48 * 2**20
        ),
        name="reduce_all",
    )(gd, gu, gc, ga, sg)


def dot(a, b):
    return jnp.dot(a, b, preferred_element_type=f32)


def dot_tn(a, b):
    return lax.dot_general(a, b, (((0,), (0,)), ((), ())), preferred_element_type=f32)


def dot_nt(a, b):
    return lax.dot_general(a, b, (((1,), (1,)), ((), ())), preferred_element_type=f32)


def per_device(
    nb,
    segment,
    memory,
    compressed,
    evicted,
    window_mask,
    cotangent,
    w_query,
    w_key,
    w_value,
    w_output,
    w_up,
    b_up,
    w_down,
    b_down,
    ln_gain,
    ln_bias,
    w_conv,
    b_conv,
    slopes,
):
    S, R, M = segment.shape
    heads = slopes.shape[0]
    hd = M // heads
    nt = 4
    rw, rd, rs = w_query.shape[0], w_down.shape[0], b_down.shape[0]
    b, t = lax.axis_index("batch"), lax.axis_index("tier")
    Cw, Fw = M // nt, nb * rd
    nu, W = R // 16, R // 3
    seg_len = nt * R
    T = S * seg_len
    ht = heads // nt
    index = 4 * b + t

    wa = jnp.stack([w_query, w_key, w_value, w_output]).reshape(4, rw, nt, Cw)
    wa = wa.transpose(2, 1, 0, 3).reshape(nt, rw, 4 * Cw)
    wu = w_up.reshape(rw, nb, nt, rd).transpose(2, 0, 1, 3).reshape(nt, rw, Fw)
    wc = w_conv.reshape(3, rw, nt, Cw).transpose(2, 1, 0, 3).reshape(nt, rw, 3 * Cw)
    row0 = jnp.concatenate([ln_gain, ln_bias, b_down, b_conv])
    sm = jnp.zeros((8, 128), f32).at[0, : 4 * rs].set(row0.astype(f32)).at[1, :rd].set(b_up.astype(f32))
    mem = memory.reshape(S, W, 3, M).transpose(0, 2, 1, 3)
    mk = jnp.broadcast_to(window_mask.astype(f32)[:, :, None], (S, W, 128))
    WA, WU, WC, WD, SM, CTX, COT, MK = gather_all(
        nb,
        nu,
        wa,
        wu,
        wc,
        w_down,
        sm,
        compressed.reshape(S, nu, 16, M),
        mem,
        segment.reshape(S, nu, 16, M),
        cotangent.reshape(S, nu, 16, M),
        mk,
    )
    WA = WA.reshape(M, 4 * Cw)
    Wqkv, Wo = WA[:, : 3 * Cw], WA[:, 3 * Cw :]
    WU, WC, WD = WU.reshape(M, Fw), WC.reshape(M, 3 * Cw), WD.reshape(Fw, M)
    gain, bias, bdown, bconv = [SM[:, :, 0, i * rs : (i + 1) * rs].reshape(M) for i in range(4)]
    bup = lax.dynamic_index_in_dim(SM, t, 1, False)[:, 1, :rd].reshape(Fw)
    cols = lambda v: lax.dynamic_slice_in_dim(v, t * Cw, Cw, v.ndim - 1)
    ctx = CTX.reshape(S, 3 * seg_len, M)
    cot = COT.reshape(T, M)
    seg = ctx[:, 2 * seg_len :].reshape(T, M)

    kpos = jnp.concatenate(
        [
            jnp.arange(seg_len),
            seg_len + (3 * jnp.arange(seg_len // 3)[None, :] + jnp.arange(3)[:, None]).reshape(-1),
            2 * seg_len + jnp.arange(seg_len),
        ]
    )
    qpos = 2 * seg_len + jnp.arange(seg_len)
    allowed = kpos[None, :] <= qpos[:, None]
    dist = (qpos[:, None] - kpos[None, :]).astype(f32) * (1.0 / (3 * seg_len))
    slope = lax.dynamic_slice_in_dim(slopes, t * ht, ht)
    scale = 1.0 / math.sqrt(hd)
    q = dot(seg, Wqkv[:, :Cw]).astype(bf16).reshape(S, seg_len, ht, hd)
    kv = dot(ctx.reshape(-1, M), Wqkv[:, Cw:]).astype(bf16).reshape(S, 3 * seg_len, 2, ht, hd)
    kk, vv = kv[:, :, 0], kv[:, :, 1]
    raw = jnp.einsum("sqhd,skhd->shqk", q, kk, preferred_element_type=f32)
    scores = jnp.where(allowed, raw * scale - slope[:, None, None] * dist, -1e30)
    high = jnp.max(scores, axis=-1, keepdims=True)
    e = jnp.exp(scores - high)
    probs = e / jnp.sum(e, axis=-1, keepdims=True)
    probs_low = probs.astype(bf16)
    mixed_t = jnp.einsum("shqk,skhd->sqhd", probs_low, vv, preferred_element_type=f32).astype(bf16)
    MIX = spread(mixed_t.reshape(T, Cw), True, 2)
    mixed = MIX.transpose(1, 0, 2).reshape(T, M)
    resid_t = cols(seg).astype(f32) + dot(mixed, Wo)
    RES = spread(resid_t.astype(bf16), True, 3)
    resid = RES.transpose(1, 0, 2).reshape(T, M).astype(f32)
    center = resid - jnp.mean(resid, axis=-1, keepdims=True)
    spread_ = lax.rsqrt(jnp.mean(center * center, axis=-1, keepdims=True) + norm_eps)
    xhat = center * spread_
    normed = (xhat * gain + bias).astype(bf16)
    pre = dot(normed, WU) + bup
    phi = 0.5 * (1.0 + lax.erf(pre * math.sqrt(0.5)))
    act = (pre * phi).astype(bf16)
    slope_act = phi + pre * jnp.exp(-0.5 * pre * pre) * (1.0 / math.sqrt(2 * math.pi))
    place = lambda v: lax.dynamic_update_slice_in_dim(jnp.zeros((T, M), f32), v, t * Cw, 1)
    out_part = dot(act, WD) + place(resid_t + cols(bdown))
    rows = lambda v: v.astype(bf16).reshape(S, nt, R, M).transpose(1, 0, 2, 3)
    output = jnp.sum(spread(rows(out_part), False, 4).astype(f32), axis=0).astype(bf16)
    gdown = dot_tn(act, cot)
    d_act = dot_nt(cot, WD).astype(bf16)
    d_pre = d_act.astype(f32) * slope_act
    gub = jnp.sum(d_pre, axis=0)
    d_pre_low = d_pre.astype(bf16)
    gup = dot_tn(normed, d_pre_low)
    dn_part = dot_nt(d_pre_low, WU)
    stats = jnp.stack([jnp.mean(dn_part * gain, axis=1), jnp.mean(dn_part * gain * xhat, axis=1)])
    stats = lax.psum(stats, "tier")
    cols_of = lambda v: v.astype(bf16).reshape(T, nt, Cw).transpose(1, 0, 2)
    dn = jnp.sum(spread(cols_of(dn_part), False, 5).astype(f32), axis=0)
    xhat_t = cols(xhat)
    ggain, gbias = jnp.sum(dn * xhat_t, axis=0), jnp.sum(dn, axis=0)
    g = dn * cols(gain)
    cot_t = cols(cot).astype(f32)
    gdb = jnp.sum(cot_t, axis=0)
    d_resid = cot_t + (g - stats[0][:, None] - xhat_t * stats[1][:, None]) * spread_
    d_branch = d_resid.astype(bf16)
    gout = dot_tn(mixed, d_branch)
    dm_part = dot_nt(d_branch, Wo)
    dm = jnp.sum(spread(cols_of(dm_part), False, 6).astype(f32), axis=0).astype(bf16)
    dm = dm.reshape(S, seg_len, ht, hd)
    d_probs = jnp.einsum("sqhd,skhd->shqk", dm, vv, preferred_element_type=f32)
    delta = jnp.sum(probs * d_probs, axis=-1, keepdims=True)
    d_scores = probs * (d_probs - delta)
    gslope = -jnp.sum(d_scores * dist, axis=(0, 2, 3))
    d_raw = (d_scores * scale).astype(bf16)
    dq = jnp.einsum("shqk,skhd->sqhd", d_raw, kk, preferred_element_type=f32).astype(bf16)
    dk = jnp.einsum("shqk,sqhd->skhd", d_raw, q, preferred_element_type=f32).astype(bf16)
    dv = jnp.einsum("shqk,sqhd->skhd", probs_low, dm, preferred_element_type=f32).astype(bf16)
    dq, dk, dv = dq.reshape(T, Cw), dk.reshape(S, -1, Cw), dv.reshape(S, -1, Cw)
    flat = ctx.reshape(-1, M)
    gq = dot_tn(seg, dq)
    gk, gv = dot_tn(flat, dk.reshape(-1, Cw)), dot_tn(flat, dv.reshape(-1, Cw))
    own = lambda v: v[:, 2 * seg_len :].reshape(T, Cw)
    ig_part = dot_nt(jnp.concatenate([dq, own(dk), own(dv)], axis=1), Wqkv) + place(d_resid)
    input_grad = jnp.sum(spread(rows(ig_part), False, 7).astype(f32), axis=0)

    nw = seg_len // 3
    win = ctx[:, seg_len : 2 * seg_len].reshape(S, 3, nw, M)
    win = [win[:, k].reshape(S * nw, M) for k in range(3)]
    conv = sum(dot(win[k], WC[:, k * Cw : (k + 1) * Cw]) for k in range(3)) + cols(bconv)
    pooled = sum(cols(win[k]).astype(f32) for k in range(3)) * (1.0 / 3.0)
    mask = MK.reshape(S, nw, 128)[:, :, :1]
    old = (3 * jnp.arange(nw) + 3)[None, :, None] <= evicted[:, None, None]
    live = jnp.where(old, mask, 0.0).reshape(-1, 1)
    d_conv = live * (conv - pooled)
    gcb = jnp.sum(d_conv, axis=0)
    d_low = d_conv.astype(bf16)
    gconv = jnp.concatenate([dot_tn(win[k], d_low) for k in range(3)], axis=1)
    new_t = (mask.reshape(-1, 1) * conv).astype(bf16)
    NEW = spread(new_t, True, 8).reshape(nt, S, nw, Cw).transpose(1, 2, 0, 3).reshape(S, nw, M)
    slot_offset = seg_len - nw
    local_rows = jnp.arange(R, dtype=jnp.int32) + t * R
    padded = jnp.concatenate([jnp.zeros((S, slot_offset, M), bf16), NEW], axis=1)
    slot_rows = lax.dynamic_slice_in_dim(padded, t * R, R, 1)
    written = (local_rows[None, :] >= slot_offset) & (
        3 * (local_rows[None, :] - slot_offset) + 3 <= evicted[:, None]
    )
    new_compressed = jnp.where(written[..., None], slot_rows, compressed)
    new_memory = jnp.where((local_rows[None, :] < evicted[:, None])[..., None], segment, memory)

    low = lambda v, *s: v.astype(bf16).reshape(s)
    gs = lax.dynamic_update_slice_in_dim(jnp.zeros((128,), f32), gslope, t * ht, 0)
    sg = jnp.concatenate([gub, gdb, ggain, gbias, gcb, gs])
    sg = jnp.concatenate([sg, jnp.zeros((24 * 128 - sg.shape[0],), f32)]).reshape(24, 128)
    OD, OU, OC, OA, OS = reduce_all(
        nb,
        low(gdown, nb, 4, rd // 4, M),
        low(gup, nb, 4, rw, Fw),
        low(gconv, nb, 4, rw, 3 * Cw),
        low(jnp.concatenate([gq, gk, gv, gout], axis=1), nb, 4, rw, 4 * Cw),
        sg,
    )
    OA = OA.reshape(nt, rw, 4, Cw).transpose(2, 1, 0, 3).reshape(4, rw, M)
    OU = OU.reshape(nt, rw, nb, rd).transpose(1, 2, 0, 3).reshape(rw, nb * nt * rd)
    OC = OC.reshape(nt, rw, 3, Cw).transpose(2, 1, 0, 3).reshape(3, rw, M)
    OS = OS.reshape(nt, -1)
    vec = lambda o: lax.dynamic_slice_in_dim(OS[:, o : o + Cw].reshape(M), index * rs, rs)
    gub_out = lax.dynamic_slice(OS, (t, b * rd), (1, rd)).reshape(rd)
    gslopes = jnp.sum(OS[:, Fw + 4 * Cw : Fw + 4 * Cw + heads], axis=0)
    return (
        output,
        input_grad,
        new_memory,
        new_compressed,
        OA[0],
        OA[1],
        OA[2],
        OA[3],
        OU,
        gub_out,
        OD.reshape(rd, M),
        vec(Fw),
        vec(Fw + Cw),
        vec(Fw + 2 * Cw),
        OC,
        vec(Fw + 3 * Cw),
        gslopes,
    )


class Names:
    def __init__(self, names, refs):
        for name, ref in zip(names, refs):
            setattr(self, name, ref)


def layer_kernel(names, shape, *refs):
    r = Names(names, refs)
    nb, nu, S, ht, hd, M, Cw, rw, rd, rs = shape
    R = 16 * nu
    Hw = Cw // 2
    nd = r.YD.shape[1]
    G, bq = nb // 2, nb // 4
    L = 16 * 4 * nu
    C3 = 3 * L
    nw = L // 3
    Fw = nb * rd
    scale = 1.0 / math.sqrt(hd)
    b, t, z, y, zs, zback = places(G)
    mate, ends = z ^ 1, (z == 0) | (z == G - 1)
    ypeer = (b ^ 1, t)
    tc = pl.ds(pl.multiple_of(t * Cw, Cw), Cw)
    sends = []

    def got(ref, sem):
        pltpu.make_async_copy(ref, ref, sem).wait()

    def left_all(ref, sem):
        sends.append((ref, sem))

    def each(n, body, between=None):
        def step(i, c):
            body(i)
            for at, then in (between or {}).items():
                pl.when(i == at)(then)
            return c

        lax.fori_loop(0, n, step, 0)

    def ex_send(e, sem, src, dst):
        for d in (1, 2, 3):
            remote(src(t ^ d), dst(d), r.es.at[e], sem, (b, t ^ d)).start()

    def spread_send(e, s, arr):
        at = arr.at[t, s]
        for d in (1, 2):
            remote(at, at, r.es.at[e], r.er.at[e, s, d - 1], (b, t ^ d)).start()

    def spread_pass(e, s, arr):
        at = arr.at[t ^ 2, s]
        got(at, r.er.at[e, s, 1])
        remote(at, at, r.es.at[e], r.er.at[e, s, 0], (b, t ^ 1)).start()

    def spread_wait(e, s, arr):
        @pl.when(s < S - 1)
        def _():
            spread_pass(e, s + 1, arr)

        got(arr.at[0:2, s], r.er.at[e, s, 0])

    folds = {
        2: (lambda q, s: r.DNP.at[q, s], r.DNR),
        4: (lambda q, s: r.DMP.at[q, s], r.DMR),
        5: (lambda q, s: r.OP.at[s, pl.ds(nu * q, nu)], r.OR),
        6: (lambda q, s: r.NRM.at[s, pl.ds(nu * q, nu)], r.IR),
    }

    def fold_send(e, s):
        out, into = folds[e]
        for i, d in enumerate((1, 3)):
            remote(out(t ^ d, s), into.at[i, s], r.es.at[e], r.er.at[e, s, i], (b, t ^ 1)).start()

    def fold_pass(e, s):
        out, into = folds[e]
        at, far = into.at[1, s], out(t ^ 2, s)
        got(at, r.er.at[e, s, 1])
        far[...] = (far[...].astype(f32) + at[...].astype(f32)).astype(bf16)
        remote(far, into.at[2, s], r.es.at[e], r.er.at[e, s, 0], (b, t ^ 2)).start()

    def fold_late(e, s):
        @pl.when(s > 0)
        def _():
            fold_pass(e, s - 1)

    def folded(e, s):
        out, into = folds[e]
        got(into.at[0:2, s], r.er.at[e, s, 0])
        return out(t, s)[...].astype(f32) + into[0, s].astype(f32) + into[2, s].astype(f32)

    def here(src, dst, i):
        cp = pltpu.make_async_copy(src, dst, r.lsem.at[i])
        cp.start()
        return cp

    wide = lambda at, size: pl.ds(pl.multiple_of(at, 128), size)
    mats = (r.w_query, r.w_key, r.w_value, r.w_output)
    whole = {"S": r.SM, "A": r.WA, "U": r.WU, "C": r.WC}
    index = {"S": 0, "A": 1, "U": 2, "C": 3, "H": 4}

    def tiers(n, at):
        return r.WCX.at[at] if n == "H" else whole[n].at[b, at]

    def cuts(n, q):
        if n == "S":
            return [(r.SM.at[b, t], r.SM.at[b, t])]
        if n == "A":
            return [(w.at[:, wide(Cw * q, Cw)], r.WA.at[b, t, :, i * Cw : (i + 1) * Cw]) for i, w in enumerate(mats)]
        if n == "U":
            return [
                (r.w_up.at[:, wide((4 * i + q) * rd, rd)], r.WU.at[b, t, :, i * rd : (i + 1) * rd]) for i in range(nb)
            ]
        half, to = (y, r.WC.at[b]) if n == "C" else (1 - y, r.WCX)
        return [
            (r.w_conv.at[i, :, wide(Cw * q + Hw * half, Hw)], to.at[t, :, i * Hw : (i + 1) * Hw]) for i in range(3)
        ]

    def tier_own(n):
        for src, dst in cuts(n, t):
            here(src, dst, index[n])

    def tier_start(n):
        i = index[n]
        for d in (1, 2, 3):
            for src, dst in cuts(n, t ^ d):
                remote(src, dst, r.ts.at[i], r.tr.at[i], (b, t ^ d)).start()
        left_all(tiers(n, slice(0, 3)), r.ts.at[i])

    def tier_wait(n):
        i = index[n]
        if n != "S":
            got(tiers(n, t), r.lsem.at[i])
        got(tiers(n, slice(0, 3)), r.tr.at[i])

    def if_(cond, body):
        pl.when(cond)(body)

    def at_ends(body):
        return lambda: if_(ends, body)

    def inside(body):
        return lambda: if_(~ends, body)

    def both(*bodies):
        def run():
            for body in bodies:
                body()

        return run

    right, left = (2 * z + 2 + y, t), (2 * z - 2 + y, t)
    parts = {"S": [(r.SM, 0, 0, 4, 0)], "C": [(r.WC, 1, 0, 4, 1)], "X": [(r.WC, 2, 0, 4, 2)]}
    for i, (n, w) in enumerate((("A", r.WA), ("U", r.WU))):
        parts[n] = [(w, 3 + 2 * i + h, h * 2, 2, 3 + i) for h in (0, 1)]
    first = rd // 4
    rest = (rd - first) // 2
    parts["D"] = [(r.WD, 7, 0, first, 5)]
    for i, n in enumerate("EF"):
        parts[n] = [(r.WD, 8 + 2 * i + h, first + h * rest, rest, 6 + i) for h in (0, 1)]

    def chunk_of(n, part, zz, col=None):
        w, k, at, size, _ = part
        col = ((1 - y) if n in "XF" else y) if col is None else col
        return w.at[2 * zz + col, pl.ds(at, size)]

    def chunks(n, count):
        w, _, at, size, _ = parts[n][0]
        return w.at[0:count, at : at + size * len(parts[n])]

    def hop(part, at, zz, way):
        k = part[1]
        peer, past = (right, z < G - 1) if way == 0 else (left, z > 0)
        return past, remote(at, at, r.zs.at[part[4]], r.zr.at[k, zz - way], peer)

    def own_z(n):
        for part in parts[n]:
            for way in (0, 1):
                past, cp = hop(part, chunk_of(n, part, z), z, way)
                if_(past, cp.start)

    def own_y(n):
        for part in parts[n]:
            at, k = chunk_of(n, part, z), part[4]
            remote(r.WCX if n == "C" else at, at, r.ys.at[k], r.yr.at[k], ypeer).start()

    def arrivals(n, step, js):
        for j in js:
            for part in parts[n]:
                for way in (0, 1):
                    zz = z - j if way == 0 else z + j
                    step(part, j, way, zz, chunk_of(n, part, zz), zz >= 0 if way == 0 else zz < G)

    def onward(n, *js, cross=True):
        def step(part, j, way, zz, at, there):
            k = part[1]

            def body():
                got(at, r.zr.at[k, zz - way])
                if j < G - 1:
                    past, cp = hop(part, at, zz, way)
                    if_(past, cp.start)
                if n not in "CXEF" and cross:
                    remote(at, at, r.ys.at[part[4]], r.yr.at[part[4]], ypeer).start()

            if_(there, body)

        arrivals(n, step, js or range(1, G))

    def over(n, *js):
        def step(part, j, way, zz, at, there):
            if_(there, remote(at, at, r.ys.at[part[4]], r.yr.at[part[4]], ypeer).start)

        arrivals(n, step, js)

    def all_sent(n):
        k = parts[n][0][4]
        if_(ends, lambda: got(chunks(n, 1), r.zs.at[k]))
        if_(~ends, lambda: got(chunks(n, 5), r.zs.at[k]))
        if n not in "XF":
            got(chunks(n, 1 if n in "CE" else G), r.ys.at[k])

    def y_wait(n):
        got(chunks(n, 1 if n in "CE" else G), r.yr.at[parts[n][0][4]])

    def small_start():
        r.SM[b, t] = jnp.zeros((8, 128), f32)
        for q, v in enumerate((r.gain, r.bias, r.bdown, r.bconv, r.bup)):
            r.SM[b, t, q : q + 1, : v.shape[1]] = v[...].astype(f32)
        tier_start("S")

    def memory_rows():
        W = R // 3
        to, frm = (lax.broadcasted_iota(jnp.int32, (R, R), axis) for axis in (0, 1))
        tap = (to >= W).astype(jnp.int32) + (to >= 2 * W).astype(jnp.int32)
        order = (frm == 3 * (to - W * tap) + tap).astype(bf16)
        for s in range(S):
            rows = jnp.dot(order, r.MEMV[s], preferred_element_type=f32).astype(bf16)
            for i in range(3):
                r.CTX[s, 4 * nu + 4 * i + t] = rows[W * i : W * (i + 1)]
            square = lambda axis: lax.broadcasted_iota(jnp.int32, (R // 3, R // 3), axis)
            line = jnp.broadcast_to(r.mask[s : s + 1].astype(f32), (R // 3, R // 3))
            col = jnp.sum(jnp.where(square(0) == square(1), line, 0.0), axis=1, keepdims=True)
            spot = lax.broadcasted_iota(jnp.int32, (R // 3, 128), 0) + (R // 3) * t
            lane = lax.broadcasted_iota(jnp.int32, (R // 3, 128), 1)
            r.MK[s, t] = jnp.where((lane < 64) | (3 * spot + 3 <= r.evicted[s]), col, 0.0)

    def rows_of(src, buf, first):
        at = lambda q: buf.at[:, pl.ds(first + nu * q, nu)]
        parts = [(src.at[:, 16 * i : 16 * i + 16], buf.at[:, first + nu * t + i]) for i in range(nu)]
        return parts, at, True

    def held(at):
        return [(at(t), at(t))], at, False

    def memory_y():
        for i in range(3):
            remote(r.CTX.at[:, 4 * nu + 4 * i + t], r.MEMX.at[:, 4 * i + t], r.ms.at[0], r.ms.at[1], ypeer).start()
        remote(r.MK.at[:, t], r.MKX.at[:, t], r.ms.at[2], r.ms.at[3], ypeer).start()
        left_all(r.MEMX.at[:, 0:3], r.ms.at[0])
        left_all(r.MKX.at[:, 0], r.ms.at[2])

    def memory_come():
        got(r.MEMX.at[:, 0:3], r.ms.at[1])
        got(r.MKX.at[:, 0], r.ms.at[3])

    pieces = [
        rows_of(r.seg, r.CTX, 8 * nu),
        rows_of(r.comp, r.CTX, 0),
        held(lambda q: r.CTX.at[:, 4 * nu + q]),
        held(lambda q: r.CTX.at[:, 4 * nu + 4 + q]),
        held(lambda q: r.CTX.at[:, 4 * nu + 8 + q]),
        rows_of(r.cot, r.COT, 0),
        held(lambda q: r.MK.at[:, q]),
        held(lambda q: r.MEMX.at[:, q]),
        held(lambda q: r.MEMX.at[:, 4 + q]),
        held(lambda q: r.MEMX.at[:, 8 + q]),
        held(lambda q: r.MKX.at[:, q]),
    ]

    group = lambda i: 0 if i < 5 else (1, 2, 3, 3, 3, 4)[i - 5]
    grouped = [(r.CTX, 3 * nu), (r.COT, nu), (r.MK, 1), (r.MEMX, 3), (r.MKX, 1)]

    def act_own():
        for i, (cut, at, far) in enumerate(pieces):
            if far:
                for src, dst in cut:
                    here(src, dst, 5 + group(i))

    def act_start(*which):
        for i in which:
            cut, at, far = pieces[i]
            g = group(i)
            for src, dst in cut:
                remote(src, dst, r.acs.at[g], r.acc.at[g], (b, t ^ 1)).start()
                remote(src, dst, r.acs.at[g], r.acx.at[i], (b, t ^ 2)).start()

    def act_forward(*which):
        for i in which:
            at = pieces[i][1](t ^ 2)
            got(at, r.acx.at[i])
            remote(at, at, r.acs.at[group(i)], r.acf.at[group(i)], (b, t ^ 1)).start()

    def act_wait(g):
        buf, n = grouped[g]
        got(buf.at[:, 0:n], r.acc.at[g])
        got(buf.at[:, 0:n], r.acf.at[g])
        if g < 2:
            got(buf.at[:, 0 : n if g else 2 * nu], r.lsem.at[5 + g])

    def act_sent():
        for g, (buf, n) in enumerate(grouped):
            got(buf.at[:, 0 : 3 * n], r.acs.at[g])

    def table():
        row = lax.broadcasted_iota(jnp.int32, (L, C3), 0) + 2 * L
        col = lax.broadcasted_iota(jnp.int32, (L, C3), 1)
        inner = col - L
        k1 = (inner >= nw).astype(jnp.int32)
        k2 = (inner >= 2 * nw).astype(jnp.int32)
        win = inner - nw * (k1 + k2)
        pos = jnp.where((col >= L) & (col < 2 * L), L + 3 * win + k1 + k2, col)
        r.DIST[...] = jnp.where(pos <= row, (row - pos).astype(f32) * (1.0 / C3), 1e30)
        r.SMG[...] = jnp.zeros_like(r.SMG)

    def seg_rows(s):
        return r.CTX[s, 8 * nu : 12 * nu].reshape(L, M)

    def project(s):
        rows = r.CTX[s].reshape(C3, M)
        kv = jnp.dot(rows, r.WA[:, :, :, Cw : 3 * Cw].reshape(M, 2 * Cw), preferred_element_type=f32)
        r.KV[s] = kv.astype(bf16)
        q = jnp.dot(seg_rows(s), r.WA[:, :, :, :Cw].reshape(M, Cw), preferred_element_type=f32)
        r.Q[s] = q.astype(bf16)


    def attend(s):
        for h in range(ht):
            c = slice(h * hd, (h + 1) * hd)
            raw = dot_nt(r.Q[s, :, c], r.KV[s, :, c])
            scores = raw * scale - r.slopes[t * ht + h] * r.DIST[...]
            e = jnp.exp(scores - jnp.max(scores, axis=1, keepdims=True))
            p = e * (1.0 / jnp.sum(e, axis=1, keepdims=True))
            r.PR[s, h] = p
            v = r.KV[s, :, Cw + h * hd : Cw + (h + 1) * hd]
            r.MIX[t, s, :, c] = jnp.dot(p.astype(bf16), v, preferred_element_type=f32).astype(bf16)
        spread_send(0, s, r.MIX)


    def wo(q):
        return r.WA[bq * q : bq * (q + 1), :, :, 3 * Cw :].reshape(Cw, Cw)

    def residual(s):
        spread_wait(0, s, r.MIX)
        acc = r.CTX[s, 8 * nu : 12 * nu, :, tc].reshape(L, Cw).astype(f32)
        for q in range(4):
            acc = acc + jnp.dot(r.MIX[q, s], wo(q), preferred_element_type=f32)
        r.RT[s] = acc
        r.RES[t, s] = acc.astype(bf16)
        spread_send(1, s, r.RES)

    def vectors():
        lane = lax.broadcasted_iota(jnp.int32, (8, 128), 1)
        for at in range(0, M, 128):
            block = jnp.zeros((8, 128), f32)
            for i in range(128 // rs):
                spot = at // rs + i
                turned = pltpu.roll(r.SM[spot // 4, spot % 4], rs * i, 1)
                block = jnp.where((lane >= rs * i) & (lane < rs * (i + 1)), turned, block)
            r.VV[0:4, at : at + 128] = block[0:4]
        for bb in range(nb):
            r.VV[4:5, bb * rd : (bb + 1) * rd] = r.SM[bb, t, 4:5, :rd]

    def xhat_of(s, q):
        return (r.RES[q, s].astype(f32) - r.MU[s, :, :1]) * r.MU[s, :, 1:2]

    def feed(s):
        spread_wait(1, s, r.RES)
        parts = [r.RES[q, s].astype(f32) for q in range(4)]
        mu = sum(jnp.sum(x, axis=1, keepdims=True) for x in parts) * (1.0 / M)
        var = sum(jnp.sum((x - mu) * (x - mu), axis=1, keepdims=True) for x in parts) * (1.0 / M)
        inv = lax.rsqrt(var + norm_eps)
        lane = lax.broadcasted_iota(jnp.int32, (L, 128), 1)
        r.MU[s] = jnp.where(lane == 0, mu, inv)
        for q in range(4):
            c = slice(q * Cw, (q + 1) * Cw)
            rows = ((parts[q] - mu) * inv) * r.VV[0:1, c] + r.VV[1:2, c]
            r.NRM[s, :, :, c] = rows.astype(bf16).reshape(4 * nu, 16, Cw)
        fb = Fw // 4
        for j in range(4):
            c = slice(j * fb, (j + 1) * fb)
            pre = jnp.dot(r.NRM[s].reshape(L, M), r.WU[:, :, :, c].reshape(M, fb), preferred_element_type=f32) + r.VV[4:5, c]
            phi = 0.5 + 0.5 * lax.erf(pre * math.sqrt(0.5))
            r.ACT[s, :, c] = (pre * phi).astype(bf16)
            r.GP[s, :, c] = (phi + pre * (jnp.exp(-0.5 * pre * pre) * (1.0 / math.sqrt(2 * math.pi)))).astype(bf16)


    def turn(j):
        low = lax.rem(G - j, G)
        inner = jnp.where(z == 1, low, G - 1 - low)
        return jnp.where(z == 0, G - 1 - j, jnp.where(z == G - 1, j, inner))

    grads = {0: (r.GD, r.YD, r.ZD), 1: (r.GU, r.YU, r.ZU), 2: (r.GA, r.YO, r.ZO), 3: (r.WU, r.YA, r.ZA)}

    def block(k, b_):
        g = grads[k][0]
        if k == 0:
            return g.at[b_, 0:nd]
        if k == 1:
            return g.at[b_]
        return g.at[b_, :, :, 3 * Cw :] if k == 2 else g.at[b_, :, :, : 3 * Cw]

    def to_y(k, zz):
        g, yb, zb = grads[k]
        remote(block(k, 2 * zz + (1 - y)), yb.at[zz], r.gys.at[k], r.gyr.at[k, zz], ypeer).start()

    def plus(into, *others):
        def add(i):
            acc = into[i].astype(f32)
            for o in others:
                acc = acc + o[i].astype(f32)
            into[i] = acc.astype(bf16)

        each(into.shape[0], add)

    def pass_on(i, at, zb, o, sem):
        @pl.when((o != mate) & ~ends)
        def _():
            slot = lax.rem(o, 2)
            got(zb.at[slot], r.gzr.at[sem, slot])
            plus(at, zb.at[slot])

        to = jnp.where(ends, mate, o)
        slot = jnp.where(o == mate, 2, jnp.where(ends, lax.rem(o, 2), 3))
        remote(at, zb.at[slot], r.gzs.at[sem], r.gzr.at[sem, jnp.minimum(slot, 2)], (2 * to + y, t)).start()

    def mid(k, *steps):
        g, yb, zb = grads[k]
        for i in steps or range(G - 1):
            o = turn(i)
            at = yb.at[o]
            got(at, r.gyr.at[k, o])
            plus(at, block(k, 2 * o + y))
            pass_on(i, at, zb, o, k)

    def part_c(b_):
        return r.GC.at[b_]

    def part_e(b_):
        return r.GD.at[b_, nd:4]

    def along(part, zb, sem, steps):
        for i in steps or range(G - 1):
            o = turn(i)
            for c, col in enumerate((1 - y, y)):
                pass_on(i, part(2 * o + col), zb.at[c], o, sem + c)

    def mid_c(*steps):
        along(part_c, r.ZC, 4, steps)

    def mid_e(*steps):
        along(part_e, r.ZE, 6, steps)

    def arrived(zb, sem):
        got(zb.at[2:4], r.gzr.at[sem, 2])
        return [zb.at[2], zb.at[3]]

    def summed(at, more, store):
        def total(i):
            acc = at[i].astype(f32)
            for o in more:
                acc = acc + o[i].astype(f32)
            store(i, acc)

        each(at.shape[0], total)

    def fin(k, store):
        g, yb, zb = grads[k]
        at = yb.at[z]
        got(at, r.gyr.at[k, z])
        summed(at, arrived(zb, k) + [block(k, 2 * z + y)], store)

    def cross(part, zb, sem, to, i):
        other = part(2 * z + 1 - y)

        def store(j, acc):
            other[j] = acc.astype(bf16)

        summed(other, arrived(zb.at[0], sem), store)
        remote(other, to, r.gys.at[i], r.gyr.at[i, 0], ypeer).start()

    def cross_c():
        cross(part_c, r.ZC, 4, r.YC, 4)

    def cross_e():
        cross(part_e, r.ZE, 6, r.YE, 5)

    def fin_e():
        got(r.YE, r.gyr.at[5, 0])

        def store(j, acc):
            r.OD[pl.ds((nd + j) * (rd // 4), rd // 4)] = acc

        summed(part_e(2 * z + y), arrived(r.ZE.at[1], 7) + [r.YE], store)

    def fin_c(store):
        summed(r.GC.at[2 * z + y], arrived(r.ZC.at[1], 5), store)

    def crossed_c():
        got(r.YC, r.gyr.at[4, 0])

    def reduced_sent():
        for k, (g, yb, zb) in grads.items():
            got(block(k, slice(0, G)), r.gys.at[k])
            got(block(k, slice(0, 3)), r.gzs.at[k])
        got(r.YC, r.gys.at[4])
        got(r.YE, r.gys.at[5])
        for sem in (4, 5):
            got(r.GC.at[0:3], r.gzs.at[sem])
            got(r.GD.at[0:3, nd:4], r.gzs.at[sem + 2])

    fb = Fw // 4

    def grad_down(i):
        j = turn(i)
        c = pl.ds(pl.multiple_of(j * fb, fb), fb)
        rows = r.ACT[:, :, c].reshape(S * L, fb)
        g = dot_tn(rows, r.COT[...].reshape(S * L, M)).astype(bf16)
        r.GD[pl.ds(j * bq, bq)] = g.reshape(bq, 4, rd // 4, M)
        to_y(0, j)


    def back_feed(s):
        cot = r.COT[s].reshape(L, M)
        for j in range(4):
            c = slice(j * fb, (j + 1) * fb)
            wd = r.WD[bq * j : bq * (j + 1)].reshape(fb, M)
            d_act = dot_nt(cot, wd).astype(bf16).astype(f32)
            d_pre = d_act * r.GP[s, :, c].astype(f32)
            total = jnp.sum(d_pre, axis=0, keepdims=True)
            for i in range(fb // 128):
                at = j * (fb // 128) + i
                r.SMG[at : at + 1] += total[:, 128 * i : 128 * (i + 1)]
            r.GP[s, :, c] = d_pre.astype(bf16)
        m1 = jnp.zeros((L, 1), f32)
        m2 = jnp.zeros((L, 1), f32)
        for q in range(4):
            c = slice(q * Cw, (q + 1) * Cw)
            dn = dot_nt(r.GP[s], r.WU[bq * q : bq * (q + 1)].reshape(Cw, Fw))
            g = dn * r.VV[0:1, c]
            m1 = m1 + jnp.sum(g, axis=1, keepdims=True)
            m2 = m2 + jnp.sum(g * xhat_of(s, q), axis=1, keepdims=True)
            r.DNP[q, s] = dn.astype(bf16)
        lane = lax.broadcasted_iota(jnp.int32, (L, 128), 1)
        both = jnp.where(lane == 0, m1, jnp.where(lane == 1, m2, 0.0)) * (1.0 / M)
        pick = (
            lax.broadcasted_iota(jnp.int32, (8, 128), 0) == lax.broadcasted_iota(jnp.int32, (8, 128), 1)
        ).astype(f32)
        r.ST[t, s] = lax.dot_general(
            pick, both, (((1,), (1,)), ((), ())), precision=lax.Precision.HIGHEST, preferred_element_type=f32
        )
        fold_send(2, s)
        ex_send(3, r.er.at[3, s, 0], lambda q: r.ST.at[t, s], lambda d: r.ST.at[t, s])
        fold_late(2, s)


    def grad_up(i):
        j = turn(i)
        c = pl.ds(pl.multiple_of(j * Cw, Cw), Cw)
        rows = r.NRM[:, :, :, c].reshape(S * L, Cw)
        g = dot_tn(rows, r.GP[...].reshape(S * L, Fw)).astype(bf16)
        r.GU[pl.ds(j * bq, bq)] = g.reshape(bq, 4, rw, Fw)
        to_y(1, j)


    def back_norm(s):
        dn = folded(2, s)
        got(r.ST.at[0:3, s], r.er.at[3, s, 0])
        st = r.ST[0, s] + r.ST[1, s] + r.ST[2, s] + r.ST[3, s]
        side = lax.broadcasted_iota(jnp.int32, (8, 128), 0)
        col_of = lambda i: lax.dot_general(
            st,
            (side == i).astype(f32),
            (((0,), (0,)), ((), ())),
            precision=lax.Precision.HIGHEST,
            preferred_element_type=f32,
        )[:, :1]
        m1, m2 = col_of(0), col_of(1)
        inv = r.MU[s, :, 1:2]
        xhat = (r.RES[t, s].astype(f32) - r.MU[s, :, :1]) * inv
        cot = r.COT[s, :, :, tc].reshape(L, Cw).astype(f32)
        for i, v in enumerate((cot, dn * xhat, dn)):
            total = jnp.sum(v, axis=0, keepdims=True)
            for k in range(Cw // 128):
                at = Fw // 128 + i * (Cw // 128) + k
                r.SMG[at : at + 1] += total[:, 128 * k : 128 * (k + 1)]
        d_resid = cot + (dn * r.VV[0:1, tc] - m1 - xhat * m2) * inv
        r.DR[s] = d_resid
        db = d_resid.astype(bf16)
        r.DB[s] = db
        for q in range(4):
            r.DMP[q, s] = dot_nt(db, wo(q)).astype(bf16)
        fold_send(4, s)
        fold_late(4, s)

    def grad_out():
        for q in range(4):
            g = dot_tn(r.MIX[q].reshape(S * L, Cw), r.DB[...].reshape(S * L, Cw))
            r.GA[bq * q : bq * (q + 1), :, :, 3 * Cw :] = g.astype(bf16).reshape(bq, 4, rw, Cw)
        each(G, lambda i: to_y(2, turn(i)))

    def by_tier(rows, c, sent, come):
        for d in (1, 2, 3):
            remote(r.GA.at[rows, t ^ d, :, c], r.WU.at[rows, t, :, c], sent, come, (b, t ^ d)).start()
        r.WU[rows, t, :, c] = r.GA[rows, t, :, c]

    def out_rows(s):
        for q in range(4):
            c = slice(q * Cw, (q + 1) * Cw)
            o = jnp.dot(r.ACT[s], r.WD[:, :, c].reshape(Fw, Cw), preferred_element_type=f32)
            mine = (t == q).astype(f32)
            o = o + mine * (r.RT[s] + r.VV[2:3, c])
            r.OP[s, :, :, c] = o.astype(bf16).reshape(4 * nu, 16, Cw)
        fold_send(5, s)


    hc = wide(t * Cw + Hw * y, Hw)

    def windows(k, g):
        buf, at = (r.MEMX, 4 * k) if g else (r.CTX, 4 * nu + 4 * k)
        return buf.at[:, at : at + 4]

    def compress():
        sums = jnp.zeros((1, Hw), f32)
        for g in (0, 1):
            conv = r.VV[3:4, hc]
            pooled = 0.0
            for k in range(3):
                wk = r.WC[:, :, :, k * Hw : (k + 1) * Hw].reshape(M, Hw)
                conv = conv + jnp.dot(windows(k, g)[...].reshape(S * nw, M), wk, preferred_element_type=f32)
                pooled = pooled + windows(k, g)[:, :, :, hc].reshape(S * nw, Hw).astype(f32)
            marks = (r.MKX if g else r.MK)[...].reshape(S * nw, 128)
            fresh = (marks[:, :1] * conv).astype(bf16).reshape(S, nw, Hw)
            if g:
                r.NEWX[...] = fresh
            else:
                r.NEW[t, :, :, wide(Hw * y, Hw)] = fresh
            d_conv = marks[:, 64:65] * (conv - pooled * (1.0 / 3.0))
            sums = sums + jnp.sum(d_conv, axis=0, keepdims=True)
            r.DC[g] = d_conv.astype(bf16)
        r.SMG[pl.ds(Fw // 128 + 3 * (Cw // 128) + y, 1)] = sums
        remote(r.NEWX, r.NEW.at[t, :, :, wide(Hw * y, Hw)], r.ns.at[2], r.ns.at[3], ypeer).start()
        left_all(r.NEWX, r.ns.at[2])
        for k in range(3):
            grad = sum(dot_tn(windows(k, g)[...].reshape(S * nw, M), r.DC[g]) for g in (0, 1))
            r.GC[:, :, :, k * Hw : (k + 1) * Hw] = grad.astype(bf16).reshape(nb, 4, rw, Hw)

    slope_row = Fw // 128 + 4 * (Cw // 128)

    def back_attend(s):
        dm = folded(4, s).astype(bf16)
        lane = lax.broadcasted_iota(jnp.int32, (1, 128), 1)
        for h in range(ht):
            c = slice(h * hd, (h + 1) * hd)
            cv = slice(Cw + h * hd, Cw + (h + 1) * hd)
            p = r.PR[s, h]
            dp = dot_nt(dm[:, c], r.KV[s, :, cv])
            delta = jnp.sum(p * dp, axis=1, keepdims=True)
            ds = p * (dp - delta)
            part = jnp.sum(jnp.sum(ds * r.DIST[...], axis=0, keepdims=True), axis=1, keepdims=True)
            r.SMG[slope_row : slope_row + 1] -= jnp.where(lane == t * ht + h, part, 0.0)
            dr = (ds * scale).astype(bf16)
            dq = jnp.dot(dr, r.KV[s, :, c], preferred_element_type=f32).astype(bf16)
            dk = dot_tn(dr, r.Q[s, :, c]).astype(bf16)
            dv = dot_tn(p.astype(bf16), dm[:, c]).astype(bf16)
            r.Q[s, :, c] = dq
            r.KV[s, :, c] = dk
            r.KV[s, :, cv] = dv


    def grad_proj(i):
        j = turn(i)
        c = pl.ds(pl.multiple_of(j * Cw, Cw), Cw)
        gq = jnp.zeros((Cw, Cw), f32)
        gkv = jnp.zeros((Cw, 2 * Cw), f32)
        for s in range(S):
            gq = gq + dot_tn(r.CTX[s, 8 * nu : 12 * nu, :, c].reshape(L, Cw), r.Q[s])
            gkv = gkv + dot_tn(r.CTX[s, :, :, c].reshape(C3, Cw), r.KV[s])
        rows = pl.ds(j * bq, bq)
        r.GA[rows, :, :, :Cw] = gq.astype(bf16).reshape(bq, 4, rw, Cw)
        r.GA[rows, :, :, Cw : 3 * Cw] = gkv.astype(bf16).reshape(bq, 4, rw, 2 * Cw)
        by_tier(rows, slice(0, 3 * Cw), r.xs.at[0], r.xr.at[j])

    def proj_y(*steps):
        for i in steps:
            j = turn(i)
            got(r.WU.at[pl.ds(j * bq, bq), 0:3, :, : 3 * Cw], r.xr.at[j])
            to_y(3, j)

    def own_out(s):
        r.OR[1, s] = folded(5, s).astype(bf16)

    def input_rows(s):
        x = jnp.concatenate([r.Q[s], r.KV[s, 2 * L :]], axis=1)
        for q in range(4):
            c = slice(q * Cw, (q + 1) * Cw)
            w = r.WA[bq * q : bq * (q + 1), :, :, : 3 * Cw].reshape(Cw, 3 * Cw)
            o = dot_nt(x, w) + (t == q).astype(f32) * r.DR[s]
            r.NRM[s, :, :, c] = o.astype(bf16).reshape(4 * nu, 16, Cw)
        fold_send(6, s)
        fold_late(6, s)


    def keep(o):
        def store(i, acc):
            o[pl.ds(i * (rd // 4), rd // 4)] = acc

        return store

    def across(q, acc):
        for i in range(3):
            r.OA[i, :, wide(q * Cw, Cw)] = acc[:, i * Cw : (i + 1) * Cw]

    def hold(m):
        def store(i, acc):
            m[i] = acc.astype(bf16)

        return store

    def tier_back(k, m, tb):
        for d in (1, 2, 3):
            remote(m.at[t ^ d], tb.at[t], r.gts.at[k], r.gtr.at[k], (b, t ^ d)).start()
        left_all(tb.at[0:3], r.gts.at[k])

    def small_y():
        remote(r.SMG, r.YS, r.ss.at[0], r.sr.at[0], ypeer).start()
        left_all(r.SMG, r.ss.at[0])

    def small_z():
        got(r.YS, r.sr.at[0])
        r.ZS[z] = r.SMG[...] + r.YS[...]
        for d in range(1, G):
            remote(r.ZS.at[z], r.ZS.at[z], r.ss.at[1], r.sr.at[1], (2 * zs[d] + y, t)).start()
        left_all(r.ZS.at[0 : G - 1], r.ss.at[1])

    def small_tier():
        got(r.ZS.at[0 : G - 1], r.sr.at[1])
        acc = r.ZS[0]
        for zz in range(1, G):
            acc = acc + r.ZS[zz]
        r.os[t] = acc
        for d in (1, 2, 3):
            remote(r.os.at[t], r.os.at[t], r.gts.at[3], r.gtr.at[3], (b, t ^ d)).start()
        left_all(r.os.at[0:3], r.gts.at[3])

    def own_input(s):
        r.IG[s] = folded(6, s)

    mineU, mineC, mineO = r.GU.at[2 * z + y], r.GC.at[2 * z + y], r.GA.at[2 * z + y, :, :, 3 * Cw :]
    def give(i, src, dst):
        pltpu.make_async_copy(src, dst, r.osem.at[i]).start()

    def rows_out(i, src, dst):
        for j in range(nu):
            give(i, src.at[:, j], dst.at[:, 16 * j : 16 * j + 16])

    backs = {0: (mineU, r.TU), 1: (mineC, r.TC), 2: (mineO, r.TO), 4: (r.YC, r.TB)}

    def lay(k, q, rows):
        if k == 0:
            for i in range(nb):
                r.OU[:, wide((4 * i + q) * rd, rd)] = rows[:, i * rd : (i + 1) * rd].astype(f32)
        elif k == 2:
            r.OA[3, :, wide(q * Cw, Cw)] = rows.astype(f32)
        else:
            half = y if k == 1 else 1 - y
            for i in range(3):
                r.OC[i, :, wide(q * Cw + Hw * half, Hw)] = rows[:, i * Hw : (i + 1) * Hw].astype(f32)

    def tier_out(k):
        m, tb = backs[k]
        lay(k, t, m[t])
        got(tb.at[0:3], r.gtr.at[k])
        for d in (1, 2, 3):
            lay(k, t ^ d, tb[t ^ d])

    def given():
        for i, (src, dst) in ((0, (r.OU, r.ou)), (1, (r.OC, r.oc)), (2, (r.OA, r.oa)), (3, (r.OD, r.od))):
            pltpu.make_async_copy(src, dst, r.osem.at[i]).wait()
        for i, (src, dst) in ((5, (r.OR.at[1], r.out)), (6, (r.IG, r.ig)), (4, (r.OR.at[0], r.om)), (8, (r.OR.at[2], r.ocm))):
            for j in range(nu):
                pltpu.make_async_copy(src.at[:, j], dst.at[:, 16 * j : 16 * j + 16], r.osem.at[i]).wait()

    def small_out():
        got(r.os.at[0:3], r.gtr.at[3])

    slots = L - nw
    windows_of = [(q, max(R * q - slots, 0), R - max(slots - R * q, 0)) for q in range(4) if slots < R * (q + 1)]

    def new_send():
        got(r.NEWX, r.ns.at[3])
        for q, at, n in windows_of:
            part = r.NEW.at[t, :, at : at + n]
            if_(t != q, remote(part, part, r.ns.at[0], r.ns.at[1], (b, q)).start)

    def new_sent():
        for q, at, n in windows_of:
            if_(t != q, lambda: got(r.NEW.at[0, :, at : at + n], r.ns.at[0]))

    def new_out():
        for q, at, n in windows_of:
            if_(t == q, lambda: got(r.NEW.at[0:3, :, at : at + n], r.ns.at[1]))

    def memories():
        side = lax.broadcasted_iota(jnp.int32, (16, 1), 0)
        for s in range(S):
            for i in range(nu):
                fresh = side + (R * t + 16 * i) < r.evicted[s]
                r.OR[0, s, i] = jnp.where(fresh, r.CTX[s, 8 * nu + nu * t + i], r.MEMV[s, 16 * i : 16 * i + 16])
                r.OR[2, s, i] = r.CTX[s, nu * t + i]
        for q, at, n in windows_of:

            @pl.when(t == q)
            def _(at=at, n=n):
                for i in range((R - n) // 16, nu):
                    w = at + 16 * i - (R - n)
                    for s in range(S):
                        written = 3 * (side + w) + 3 <= r.evicted[s]
                        for p in range(4):
                            c = slice(p * Cw, (p + 1) * Cw)
                            old = r.CTX[s, nu * t + i, :, c]
                            r.OR[2, s, i, :, c] = jnp.where(written, r.NEW[p, s, w : w + 16], old)

    def drain():
        for n in parts:
            if n != "U":
                all_sent(n)
        got(r.GA.at[:, 0:3, :, : 3 * Cw], r.xs.at[0])
        for ref, sem in sends:
            got(ref, sem)
        act_sent()
        new_sent()
        reduced_sent()
        for e, ref in enumerate((r.MIX, r.RES, r.DNP, r.ST, r.DMP, r.OR, r.IR)):
            got(ref.at[0:3], r.es.at[e])
        given()

    here(r.wd, r.WD.at[b], 0)
    here(r.mem, r.MEMV, 7)
    for n in "ACHU":
        tier_own(n)
    act_own()
    greet(G, True, True)
    tier_start("A")
    tier_start("H")
    small_start()
    tier_start("U")
    tier_start("C")
    act_start(0, 1)
    got(r.WD.at[b], r.lsem.at[0])
    own_z("D")
    own_z("E")
    own_y("E")
    own_y("D")
    got(r.MEMV, r.lsem.at[7])
    memory_rows()
    act_start(2, 3, 4, 5, 6)
    tier_wait("A")
    own_z("A")
    own_y("A")
    tier_wait("H")
    own_y("C")
    tier_wait("S")
    own_z("S")
    own_y("S")
    table()
    onward("A", 1)
    onward("S", 1)
    onward("A", 2)
    onward("S", 2)
    tier_wait("U")
    own_z("U")
    y_wait("E")
    own_z("F")
    onward("A", 3)
    own_y("U")
    onward("S", 3)
    onward("U", 1)
    act_forward(0, 1, 2, 3, 4)
    act_wait(0)
    y_wait("A")
    each(S, project, {0: lambda: onward("U", 2), 1: lambda: onward("D", 1, cross=False)})
    inside(lambda: onward("E", 1))()
    inside(lambda: onward("F", 1))()
    tier_wait("C")
    y_wait("C")
    each(S, attend)
    onward("U", 3)
    memory_y()
    over("D", 1)
    onward("D", 2)
    own_z("C")
    own_z("X")
    spread_pass(0, 0, r.MIX)
    each(S, residual)
    inside(lambda: onward("E", 2))()
    inside(lambda: onward("F", 2))()
    y_wait("S")
    vectors()
    act_forward(5, 6)
    onward("D", 3)
    y_wait("U")
    spread_pass(1, 0, r.RES)
    each(S, feed, {0: inside(lambda: onward("C", 1)), 1: inside(lambda: onward("E", 3)), 2: inside(lambda: onward("X", 1))})
    memory_come()
    act_start(7, 8, 9, 10)
    act_wait(1)
    act_wait(2)
    each(4, grad_down)
    mid_e(0)
    at_ends(both(lambda: mid_e(1), lambda: mid_e(2)))()
    inside(lambda: onward("F", 3))()
    inside(lambda: onward("C", 2))()
    inside(lambda: onward("X", 2))()
    at_ends(both(lambda: onward("E"), lambda: onward("F")))()
    y_wait("D")
    all_sent("U")
    each(
        S,
        back_feed,
        {
            0: inside(lambda: onward("C", 3)),
            1: both(inside(lambda: mid_e(1)), lambda: mid(0, 0)),
            2: both(inside(lambda: onward("X", 3)), lambda: act_forward(7, 8, 9, 10)),
            3: at_ends(lambda: mid(0, 1)),
        },
    )
    fold_pass(2, S - 1)
    each(2, out_rows)
    inside(both(lambda: mid_e(2), lambda: mid(0, 1)))()
    fold_pass(5, 0)
    fold_pass(5, 1)
    act_wait(3)
    act_wait(4)
    at_ends(both(lambda: onward("C"), lambda: onward("X")))()
    compress()
    mid_c(0)
    each(4, grad_up)
    mid(0, 2)
    each(S, back_norm)
    fold_pass(4, S - 1)
    grad_out()
    each(S - 2, lambda s: out_rows(s + 2))
    cross_e()
    mid_c(1)
    fold_pass(5, 2)
    fold_pass(5, 3)
    each(S, back_attend, {0: lambda: mid(1, 0)})
    mid_c(2)
    small_y()
    each(4, grad_proj, {1: at_ends(lambda: mid(1, 1))})
    inside(lambda: mid(1, 1))()
    at_ends(lambda: mid(1, 2))()
    proj_y(0)
    each(S, input_rows)
    proj_y(1)
    cross_c()
    fold_pass(6, S - 1)
    at_ends(lambda: mid(2, 0, 1))()
    inside(lambda: mid(1, 2))()
    proj_y(2)
    at_ends(both(lambda: mid(2, 2), lambda: mid(3, 0)))()
    inside(lambda: mid(2, 0, 1, 2))()
    small_z()
    fin_c(hold(mineC))
    tier_back(1, mineC, r.TC)
    proj_y(3)
    new_send()
    inside(lambda: mid(3, 0))()
    fin(1, hold(mineU))
    tier_back(0, mineU, r.TU)
    mid(3, 1)
    fin(0, keep(r.OD))
    fin_e()
    give(3, r.OD, r.od)
    fin(2, hold(mineO))
    tier_back(2, mineO, r.TO)
    mid(3, 2)
    crossed_c()
    tier_back(4, r.YC, r.TB)
    small_tier()
    each(S, own_out)
    rows_out(5, r.OR.at[1], r.out)
    new_out()
    memories()
    rows_out(4, r.OR.at[0], r.om)
    rows_out(8, r.OR.at[2], r.ocm)
    each(S, own_input)
    rows_out(6, r.IG, r.ig)
    tier_out(1)
    tier_out(0)
    give(0, r.OU, r.ou)
    tier_out(4)
    tier_out(2)
    give(1, r.OC, r.oc)
    fin(3, across)
    give(2, r.OA, r.oa)
    small_out()
    drain()

def whole_layer(nb, ht, hd, arrays):
    S, R, M = arrays["seg"].shape
    rw, rd, rs = arrays["w_query"].shape[0], arrays["wd"].shape[0], M // (4 * nb)
    nu = R // 16
    G, Cw, Fw, L = nb // 2, M // 4, nb * rd, 64 * nu
    dma = pltpu.SemaphoreType.DMA
    V = lambda shape, dtype=bf16: pltpu.VMEM(shape, dtype)
    nd = 3
    D4, A4, U4, C4 = (4, rd // 4, M), (4, rw, 4 * Cw), (4, rw, Fw), (4, rw, 3 * Cw // 2)
    ins = arrays
    outs = dict(
        out=((S, R, M), bf16),
        ig=((S, R, M), f32),
        om=((S, R, M), bf16),
        ocm=((S, R, M), bf16),
        od=((rd, M), f32),
        ou=((rw, 4 * Fw), f32),
        oc=((3, rw, M), f32),
        oa=((4, rw, M), f32),
        os=((4, 24, 128), f32),
    )
    scratch = dict(
        WA=V((nb,) + A4),
        WU=V((nb,) + U4),
        WC=V((nb,) + C4),
        WCX=V(C4),
        MEMX=V((S, 12, 16, M)),
        MKX=V((S, 4, L // 12, 128), f32),
        NEWX=V((S, L // 3, Cw // 2)),
        WD=V((nb, rd, M)),
        SM=V((nb, 4, 8, 128), f32),
        CTX=V((S, 12 * nu, 16, M)),
        COT=V((S, 4 * nu, 16, M)),
        MK=V((S, 4, L // 12, 128), f32),
        DIST=V((L, 3 * L), f32),
        VV=V((8, max(M, Fw)), f32),
        SMG=V((24, 128), f32),
        Q=V((S, L, Cw)),
        KV=V((S, 3 * L, 2 * Cw)),
        PR=V((S, ht, L, 3 * L), f32),
        MIX=V((4, S, L, Cw)),
        RT=V((S, L, Cw), f32),
        RES=V((4, S, L, Cw)),
        MU=V((S, L, 128), f32),
        NRM=V((S, 4 * nu, 16, M)),
        ACT=V((S, L, Fw)),
        GP=V((S, L, Fw)),
        DNP=V((4, S, L, Cw)),
        DNR=V((3, S, L, Cw)),
        ST=V((4, S, 8, L), f32),
        DR=V((S, L, Cw), f32),
        DB=V((S, L, Cw)),
        DMP=V((4, S, L, Cw)),
        DMR=V((3, S, L, Cw)),
        OP=V((S, 4 * nu, 16, M)),
        OR=V((3, S, nu, 16, M)),
        IR=V((3, S, nu, 16, M)),
        DC=V((2, S * L // 3, Cw // 2)),
        GD=V((nb,) + D4),
        GU=V((nb,) + U4),
        GC=V((nb,) + C4),
        GA=V((nb,) + A4),
        YD=V((G, nd) + D4[1:]),
        YE=V((4 - nd,) + D4[1:]),
        YU=V((G,) + U4),
        YC=V(C4),
        YO=V((G, 4, rw, Cw)),
        YA=V((G, 4, rw, 3 * Cw)),
        ZD=V((4, nd) + D4[1:]),
        ZE=V((2, 4, 4 - nd) + D4[1:]),
        ZU=V((4,) + U4),
        ZC=V((2, 4) + C4),
        ZO=V((4, 4, rw, Cw)),
        ZA=V((4, 4, rw, 3 * Cw)),
        YS=V((24, 128), f32),
        ZS=V((G, 24, 128), f32),
        TU=V(U4),
        TO=V((4, rw, Cw)),
        TC=V(C4),
        TB=V(C4),
        NEW=V((4, S, L // 3, Cw)),
        IG=V((S, nu, 16, M), f32),
        OD=V((rd, M), f32),
        OU=V((rw, 4 * Fw), f32),
        OC=V((3, rw, M), f32),
        OA=V((4, rw, M), f32),
        MEMV=V((S, R, M)),
        osem=dma((9,)),
        lsem=dma((8,)),
        ts=dma((5,)),
        tr=dma((5,)),
        zs=dma((8,)),
        zr=dma((12, G - 1)),
        ys=dma((8,)),
        yr=dma((8,)),
        ms=dma((4,)),
        acs=dma((5,)),
        acc=dma((5,)),
        acf=dma((5,)),
        acx=dma((11,)),
        es=dma((7,)),
        er=dma((7, S, 2)),
        ns=dma((4,)),
        gys=dma((6,)),
        gyr=dma((6, G)),
        gzs=dma((8,)),
        gzr=dma((8, 3)),
        ss=dma((2,)),
        sr=dma((2,)),
        xs=dma((1,)),
        xr=dma((G,)),
        gts=dma((5,)),
        gtr=dma((5,)),
    )
    names = list(ins) + list(outs) + list(scratch)
    near = dict(gain=VM, bias=VM, bdown=VM, bconv=VM, bup=VM, mask=VM, evicted=SM, slopes=SM)
    return pl.pallas_call(
        functools.partial(layer_kernel, names, (nb, nu, S, ht, hd, M, Cw, rw, rd, rs)),
        out_shape=[jax.ShapeDtypeStruct(s, d) for s, d in outs.values()],
        in_specs=[near.get(n, ANY) for n in ins],
        out_specs=[VM if n == "os" else ANY for n in outs],
        scratch_shapes=list(scratch.values()),
        compiler_params=pltpu.CompilerParams(
            collective_id=9, has_side_effects=True, vmem_limit_bytes=63 * 2**20
        ),
        name="whole_layer",
    )(*ins.values())


def finish_kernel(names, shape, *refs):
    r = Names(names, refs)
    nb, rs, rd, Fw, Cw, heads = shape
    b, t = lax.axis_index("batch"), lax.axis_index("tier")
    squares = (r.o_q, r.o_k, r.o_v, r.o_o)
    moves = [(r.out, r.o_out), (r.ig, r.o_ig), (r.od, r.o_od), (r.ou, r.o_ou), (r.oc, r.o_oc), (r.om, r.o_mem), (r.ocm, r.o_comp)]
    n = len(moves)
    bufs = refs[len(names) :]
    small = pltpu.make_async_copy(r.os, r.osv, r.sem.at[n])
    small.start()
    into = [pltpu.make_async_copy(src, buf, r.sem.at[i]) for i, ((src, _), buf) in enumerate(zip(moves, bufs))]
    into.append(pltpu.make_async_copy(r.oa, bufs[n], r.sem.at[n + 1]))
    onto = [
        [pltpu.make_async_copy(buf, dst, r.sem.at[n + 2 + i])] for i, ((_, dst), buf) in enumerate(zip(moves, bufs))
    ]
    onto.append([pltpu.make_async_copy(bufs[n].at[i], o, r.sem.at[2 * n + 2 + i]) for i, o in enumerate(squares)])
    for cp in into:
        cp.start()
    small.wait()
    spot = 4 * b + t
    block, inner = spot // (Cw // rs), lax.rem(spot, Cw // rs)
    half, group = inner // (128 // rs), lax.rem(inner, 128 // rs)
    for i, o in enumerate((r.o_down, r.o_gain, r.o_bias, r.o_conv)):
        row = r.osv[block, pl.ds(Fw // 128 + (Cw // 128) * i + half, 1), :]
        turned = pltpu.roll(jnp.broadcast_to(row, (8, 128)), lax.rem(128 - rs * group, 128), 1)
        o[...] = turned[0:1, :rs]
    r.o_up[...] = r.osv[t, pl.ds(b, 1), :rd]
    at = Fw // 128 + 4 * (Cw // 128)
    total = r.osv[0, at : at + 1]
    for q in range(1, 4):
        total = total + r.osv[q, at : at + 1]
    r.o_slopes[...] = total[:, :heads]
    for cp, then in zip(into, onto):
        cp.wait()
        for c in then:
            c.start()
    for then in onto:
        for c in then:
            c.wait()


def finish(nb, heads, arrays):
    S, R, M = arrays["out"].shape
    rw, rd, rs = arrays["oa"].shape[1], arrays["od"].shape[0], M // (4 * nb)
    Cw, Fw = M // 4, nb * rd
    rows, mat, vec = (S, R, M), (rw, M), (1, rs)
    outs = dict(
        o_out=(rows, bf16, ANY),
        o_ig=(rows, f32, ANY),
        o_mem=(rows, bf16, ANY),
        o_comp=(rows, bf16, ANY),
        o_q=(mat, f32, ANY),
        o_k=(mat, f32, ANY),
        o_v=(mat, f32, ANY),
        o_o=(mat, f32, ANY),
        o_ou=((rw, 4 * Fw), f32, ANY),
        o_up=((1, rd), f32, VM),
        o_od=((rd, M), f32, ANY),
        o_down=(vec, f32, VM),
        o_gain=(vec, f32, VM),
        o_bias=(vec, f32, VM),
        o_oc=((3, rw, M), f32, ANY),
        o_conv=(vec, f32, VM),
        o_slopes=((1, heads), f32, VM),
    )
    moved = ("out", "ig", "od", "ou", "oc", "om", "ocm", "oa")
    n = len(moved) - 1
    return pl.pallas_call(
        functools.partial(
            finish_kernel, list(arrays) + list(outs) + ["sem", "osv"], (nb, rs, rd, Fw, Cw, heads)
        ),
        out_shape=[jax.ShapeDtypeStruct(s, d) for s, d, _ in outs.values()],
        in_specs=[ANY] * len(arrays),
        out_specs=[o[2] for o in outs.values()],
        scratch_shapes=[pltpu.SemaphoreType.DMA((2 * n + 6,)), pltpu.VMEM(arrays["os"].shape, f32)]
        + [pltpu.VMEM(arrays[i].shape, arrays[i].dtype) for i in moved],
        compiler_params=pltpu.CompilerParams(vmem_limit_bytes=63 * 2**20),
        name="finish",
    )(*arrays.values())


def per_device_fused(
    nb,
    segment,
    memory,
    compressed,
    evicted,
    window_mask,
    cotangent,
    w_query,
    w_key,
    w_value,
    w_output,
    w_up,
    b_up,
    w_down,
    b_down,
    ln_gain,
    ln_bias,
    w_conv,
    b_conv,
    slopes,
):
    S, R, M = segment.shape
    heads = slopes.shape[0]
    line = lambda v: v.reshape(1, -1)
    names = ("out", "ig", "om", "ocm", "od", "ou", "oc", "oa", "os")
    made = whole_layer(
        nb,
        heads // 4,
        M // heads,
        dict(
            w_query=w_query,
            w_key=w_key,
            w_value=w_value,
            w_output=w_output,
            w_up=w_up,
            w_conv=w_conv,
            wd=w_down,
            comp=compressed,
            seg=segment,
            cot=cotangent,
            mem=memory,
            gain=line(ln_gain),
            bias=line(ln_bias),
            bdown=line(b_down),
            bconv=line(b_conv),
            bup=line(b_up),
            mask=window_mask,
            evicted=evicted,
            slopes=slopes,
        ),
    )
    outs = finish(nb, heads, dict(zip(names, made)))
    flat = (9, 11, 12, 13, 15, 16)
    return tuple(o.reshape(-1) if i in flat else o for i, o in enumerate(outs))


def solution(mesh):
    both = ("batch", "tier")
    rows = P("batch", "tier", None)
    mat, vec = P(both, None), P(both)
    nb = mesh.shape["batch"]

    def body(*args):
        fused = args[6].shape[0] % 16 == 0 and args[12].shape[0] == 128
        return (per_device_fused if fused else per_device)(nb, *args)

    return jax.shard_map(
        body,
        mesh=mesh,
        in_specs=(
            (rows, rows, rows, P("batch"), P("batch", "tier"), rows)
            + (mat, mat, mat, mat, mat, vec, mat, vec, vec, vec)
            + (P(None, both, None), vec, P())
        ),
        out_specs=(
            (rows, rows, rows, rows, mat, mat, mat, mat, mat, vec, mat, vec, vec, vec)
            + (P(None, both, None), vec, P())
        ),
        check_vma=False,
    )
```

```python
import functools
import math

import jax
import jax.numpy as jnp
from jax import lax
from jax.experimental import pallas as pl
from jax.experimental.pallas import tpu as pltpu
from jax.sharding import PartitionSpec as P

norm_eps = 1e-05
MESH = pl.DeviceIdType.MESH
ANY = pl.BlockSpec(memory_space=pl.ANY)
VM = pl.BlockSpec(memory_space=pltpu.VMEM)
SM = pl.BlockSpec(memory_space=pltpu.SMEM)
f32 = jnp.float32
bf16 = jnp.bfloat16


def remote(src, dst, send, recv, device):
    return pltpu.make_async_remote_copy(
        src_ref=src,
        dst_ref=dst,
        send_sem=send,
        recv_sem=recv,
        device_id=device,
        device_id_type=MESH,
    )


def places(groups):
    b, t = lax.axis_index("batch"), lax.axis_index("tier")
    z, y = b // 2, lax.rem(b, 2)
    zs = [lax.rem(z + d, groups) for d in range(groups)]
    zback = [lax.rem(z + groups - d, groups) for d in range(groups)]
    return b, t, z, y, zs, zback


def greet(groups, tiers, columns):
    b, t, z, y, zs, _ = places(groups)
    barrier = pltpu.get_barrier_semaphore()
    peers = []
    if tiers:
        peers += [(b, t ^ d) for d in (1, 2, 3)]
    if columns:
        peers += [(2 * zz + y, t) for zz in zs[1:]] + [(b ^ 1, t)]
    for peer in peers:
        pl.semaphore_signal(barrier, inc=1, device_id=peer, device_id_type=MESH)
    pl.semaphore_wait(barrier, len(peers))


def gather_kernel(groups, nu, *refs):
    (wa, wu, wc, wd, sm, comp, mem, seg, cot, mk) = refs[:10]
    (WA, WU, WC, WD, SM, CTX, COT, MK) = refs[10:18]
    lsem, ts, tr, zsd, zr, ys, yr, acs, acr = refs[18:]
    G = groups
    b, t, z, y, zs, zback = places(G)
    greet(G, True, True)
    ypeer = (b ^ 1, t)
    local, sends = [], []

    def here(src, dst, i):
        cp = pltpu.make_async_copy(src, dst, lsem.at[i])
        cp.start()
        return cp

    kinds = [(sm, SM), (wa, WA), (wu, WU), (wc, WC)]
    own = []
    for k, (src, dst) in enumerate(kinds):
        mine = src if k == 0 else src.at[t]
        own.append(here(mine, dst.at[b, t], k))
        for d in (1, 2, 3):
            piece = src if k == 0 else src.at[t ^ d]
            cp = remote(piece, dst.at[b, t], ts.at[k, d - 1], tr.at[k, d - 1], (b, t ^ d))
            cp.start()
            sends.append(cp)
    own.append(here(wd, WD.at[b], 4))
    pieces = [
        (comp, lambda q: CTX.at[:, pl.ds(nu * q, nu)]),
        (mem.at[:, 0], lambda q: CTX.at[:, 4 * nu + q]),
        (mem.at[:, 1], lambda q: CTX.at[:, 4 * nu + 4 + q]),
        (mem.at[:, 2], lambda q: CTX.at[:, 4 * nu + 8 + q]),
        (seg, lambda q: CTX.at[:, pl.ds(8 * nu + nu * q, nu)]),
        (mk, lambda q: MK.at[:, q]),
        (cot, lambda q: COT.at[:, pl.ds(nu * q, nu)]),
    ]
    for i, (src, at) in enumerate(pieces):
        own.append(here(src, at(t), 5 + i))
        for j, d in enumerate((1, 2)):
            cp = remote(src, at(t), acs.at[i, j], acr.at[i, j], (b, t ^ d))
            cp.start()
            sends.append(cp)
    table = [SM, WA, WU, WD, WC]
    local_of = [0, 1, 2, 4, 3]
    for k, dst in enumerate(table):
        own[local_of[k]].wait()
        if k != 3:
            kk = local_of[k]
            for d in (1, 2, 3):
                remote(dst.at[b, t], dst.at[b, t ^ d], ts.at[kk, d - 1], tr.at[kk, d - 1], (b, t ^ d)).wait_recv()
        for d in range(1, G):
            cp = remote(dst.at[b], dst.at[b], zsd.at[k, d], zr.at[k, d], (2 * zs[d] + y, t))
            cp.start()
            sends.append(cp)
        cp = remote(dst.at[b], dst.at[b], ys.at[k, 0], yr.at[k, 0], ypeer)
        cp.start()
        sends.append(cp)
    for i, (src, at) in enumerate(pieces):
        remote(at(t ^ 2), at(t ^ 2), acs.at[i, 1], acr.at[i, 1], (b, t ^ 2)).wait_recv()
        cp = remote(at(t ^ 2), at(t ^ 2), acs.at[i, 2], acr.at[i, 2], (b, t ^ 1))
        cp.start()
        sends.append(cp)
    for k, dst in enumerate(table):
        for d in range(1, G):
            at = dst.at[2 * zback[d] + y]
            remote(at, at, zsd.at[k, d], zr.at[k, d], ypeer).wait_recv()
            cp = remote(at, at, ys.at[k, d], yr.at[k, d], ypeer)
            cp.start()
            sends.append(cp)
    for k, dst in enumerate(table):
        for d in range(G):
            at = dst.at[2 * zback[d] + (1 - y)]
            remote(at, at, ys.at[k, d], yr.at[k, d], ypeer).wait_recv()
    for i, (src, at) in enumerate(pieces):
        for j, q in ((0, t ^ 1), (2, t ^ 3)):
            remote(at(q), at(q), acs.at[i, j], acr.at[i, j], (b, t ^ 1)).wait_recv()
    for i in range(len(pieces)):
        own[5 + i].wait()
    for cp in sends:
        cp.wait_send()


def gather_all(nb, nu, wa, wu, wc, wd, sm, comp, mem, seg, cot, mk):
    G = nb // 2
    S, _, U, M = comp.shape
    out = [
        jax.ShapeDtypeStruct((nb,) + wa.shape, bf16),
        jax.ShapeDtypeStruct((nb,) + wu.shape, bf16),
        jax.ShapeDtypeStruct((nb,) + wc.shape, bf16),
        jax.ShapeDtypeStruct((nb,) + wd.shape, bf16),
        jax.ShapeDtypeStruct((nb, 4) + sm.shape, f32),
        jax.ShapeDtypeStruct((S, 12 * nu, U, M), bf16),
        jax.ShapeDtypeStruct((S, 4 * nu, U, M), bf16),
        jax.ShapeDtypeStruct((S, 4) + mk.shape[1:], f32),
    ]
    dma = pltpu.SemaphoreType.DMA
    return pl.pallas_call(
        functools.partial(gather_kernel, G, nu),
        out_shape=out,
        in_specs=[ANY] * 10,
        out_specs=[ANY] * 8,
        scratch_shapes=[
            dma((12,)),
            dma((4, 3)),
            dma((4, 3)),
            dma((5, G)),
            dma((5, G)),
            dma((5, G)),
            dma((5, G)),
            dma((7, 3)),
            dma((7, 3)),
        ],
        compiler_params=pltpu.CompilerParams(collective_id=0, has_side_effects=True),
        name="gather_all",
    )(wa, wu, wc, wd, sm, comp, mem, seg, cot, mk)


def spread_kernel(same, x, o, lsem, ss, rs):
    b, t = lax.axis_index("batch"), lax.axis_index("tier")
    greet(1, True, False)
    cps = []
    for d in (1, 2, 3):
        cp = remote(x if same else x.at[t ^ d], o.at[t], ss.at[d - 1], rs.at[d - 1], (b, t ^ d))
        cp.start()
        cps.append(cp)
    mine = pltpu.make_async_copy(x if same else x.at[t], o.at[t], lsem)
    mine.start()
    mine.wait()
    for d in (1, 2, 3):
        remote(o.at[t ^ d], o.at[t ^ d], ss.at[d - 1], rs.at[d - 1], (b, t ^ d)).wait_recv()
    for cp in cps:
        cp.wait_send()


def spread(x, same, cid):
    dma = pltpu.SemaphoreType.DMA
    shape = ((4,) + x.shape) if same else x.shape
    return pl.pallas_call(
        functools.partial(spread_kernel, same),
        out_shape=jax.ShapeDtypeStruct(shape, x.dtype),
        in_specs=[ANY],
        out_specs=ANY,
        scratch_shapes=[dma, dma((3,)), dma((3,))],
        compiler_params=pltpu.CompilerParams(collective_id=cid, has_side_effects=True),
        name="spread_%d" % cid,
    )(x)


def reduce_kernel(groups, *refs):
    GD, GU, GC, GA, SMG = refs[:5]
    OD, OU, OC, OA, OS = refs[5:10]
    YD, YU, YC, YA, YS, ZD, ZU, ZC, ZA, ZS, TU, TC, TA, MU, MC, MA, ys, yr, zsd, zr, ts, tr = refs[10:]
    G = groups
    b, t, z, y, zs, zback = places(G)
    greet(G, True, True)
    ypeer = (b ^ 1, t)
    sends = []
    kinds = [
        (GD, YD, ZD, OD, None, None),
        (GU, YU, ZU, OU, MU, TU),
        (GC, YC, ZC, OC, MC, TC),
        (GA, YA, ZA, OA, MA, TA),
    ]
    for k, (g, yb, *_) in enumerate(kinds):
        for d in range(G):
            zz = zs[(d + 1) % G]
            cp = remote(g.at[2 * zz + (1 - y)], yb.at[zz], ys.at[k, d], yr.at[k, d], ypeer)
            cp.start()
            sends.append(cp)
    cp = remote(SMG, YS, ys.at[4, 0], yr.at[4, 0], ypeer)
    cp.start()
    sends.append(cp)
    for k, (g, yb, zb, o, m, tb) in enumerate(kinds):
        for d in range(G):
            zz = zs[(d + 1) % G]
            at = yb.at[zz]
            remote(at, at, ys.at[k, d], yr.at[k, d], ypeer).wait_recv()

            def add(i, c, yb=yb, zz=zz, g=g):
                yb[zz, i] = (yb[zz, i].astype(f32) + g[2 * zz + y, i].astype(f32)).astype(bf16)
                return c

            lax.fori_loop(0, yb.shape[1], add, 0)
            if d < G - 1:
                cp = remote(at, zb.at[d], zsd.at[k, d], zr.at[k, d], (2 * zz + y, t))
                cp.start()
                sends.append(cp)
    remote(YS, YS, ys.at[4, 0], yr.at[4, 0], ypeer).wait_recv()
    ZS[z] = SMG[...] + YS[...]
    for d in range(G - 1):
        cp = remote(ZS.at[z], ZS.at[z], zsd.at[4, d], zr.at[4, d], (2 * zs[d + 1] + y, t))
        cp.start()
        sends.append(cp)
    for k, (g, yb, zb, o, m, tb) in enumerate(kinds):
        for d in range(G - 1):
            remote(zb.at[d], zb.at[d], zsd.at[k, d], zr.at[k, d], ypeer).wait_recv()

        def total(i, c, k=k, yb=yb, zb=zb, o=o, m=m):
            acc = yb[z, i].astype(f32)
            for d in range(G - 1):
                acc = acc + zb[d, i].astype(f32)
            if k == 0:
                o[i] = acc
            else:
                m[i] = acc.astype(bf16)
            return c

        lax.fori_loop(0, o.shape[0], total, 0)
        if k:
            for d in (1, 2, 3):
                cp = remote(m.at[t ^ d], tb.at[t], ts.at[k - 1, d - 1], tr.at[k - 1, d - 1], (b, t ^ d))
                cp.start()
                sends.append(cp)
    for d in range(G - 1):
        at = ZS.at[zback[d + 1]]
        remote(at, at, zsd.at[4, d], zr.at[4, d], ypeer).wait_recv()
    acc = ZS[0]
    for zz in range(1, G):
        acc = acc + ZS[zz]
    OS[t] = acc
    for d in (1, 2, 3):
        cp = remote(OS.at[t], OS.at[t], ts.at[3, d - 1], tr.at[3, d - 1], (b, t ^ d))
        cp.start()
        sends.append(cp)
    for k, (g, yb, zb, o, m, tb) in enumerate(kinds):
        if k:
            o[t] = m[t].astype(f32)
            for d in (1, 2, 3):
                at = tb.at[t ^ d]
                remote(at, at, ts.at[k - 1, d - 1], tr.at[k - 1, d - 1], (b, t ^ d)).wait_recv()
                o[t ^ d] = tb[t ^ d].astype(f32)
    for d in (1, 2, 3):
        at = OS.at[t ^ d]
        remote(at, at, ts.at[3, d - 1], tr.at[3, d - 1], (b, t ^ d)).wait_recv()
    for cp in sends:
        cp.wait_send()


def reduce_all(nb, gd, gu, gc, ga, sg):
    G = nb // 2
    dma = pltpu.SemaphoreType.DMA
    shapes = [x.shape[1:] for x in (gd, gu, gc, ga)]
    return pl.pallas_call(
        functools.partial(reduce_kernel, G),
        out_shape=[jax.ShapeDtypeStruct(s, f32) for s in shapes]
        + [jax.ShapeDtypeStruct((4,) + sg.shape, f32)],
        in_specs=[VM] * 5,
        out_specs=[VM] * 5,
        scratch_shapes=[pltpu.VMEM((G,) + s, bf16) for s in shapes]
        + [pltpu.VMEM(sg.shape, f32)]
        + [pltpu.VMEM((G - 1,) + s, bf16) for s in shapes]
        + [pltpu.VMEM((G,) + sg.shape, f32)]
        + [pltpu.VMEM(s, bf16) for s in shapes[1:]]
        + [pltpu.VMEM(s, bf16) for s in shapes[1:]]
        + [dma((5, G)), dma((5, G)), dma((5, G)), dma((5, G)), dma((4, 3)), dma((4, 3))],
        compiler_params=pltpu.CompilerParams(
            collective_id=1, has_side_effects=True, vmem_limit_bytes=48 * 2**20
        ),
        name="reduce_all",
    )(gd, gu, gc, ga, sg)


def dot(a, b):
    return jnp.dot(a, b, preferred_element_type=f32)


def dot_tn(a, b):
    return lax.dot_general(a, b, (((0,), (0,)), ((), ())), preferred_element_type=f32)


def dot_nt(a, b):
    return lax.dot_general(a, b, (((1,), (1,)), ((), ())), preferred_element_type=f32)


def per_device(
    nb,
    segment,
    memory,
    compressed,
    evicted,
    window_mask,
    cotangent,
    w_query,
    w_key,
    w_value,
    w_output,
    w_up,
    b_up,
    w_down,
    b_down,
    ln_gain,
    ln_bias,
    w_conv,
    b_conv,
    slopes,
):
    S, R, M = segment.shape
    heads = slopes.shape[0]
    hd = M // heads
    nt = 4
    rw, rd, rs = w_query.shape[0], w_down.shape[0], b_down.shape[0]
    b, t = lax.axis_index("batch"), lax.axis_index("tier")
    Cw, Fw = M // nt, nb * rd
    nu, W = R // 16, R // 3
    seg_len = nt * R
    T = S * seg_len
    ht = heads // nt
    index = 4 * b + t

    wa = jnp.stack([w_query, w_key, w_value, w_output]).reshape(4, rw, nt, Cw)
    wa = wa.transpose(2, 1, 0, 3).reshape(nt, rw, 4 * Cw)
    wu = w_up.reshape(rw, nb, nt, rd).transpose(2, 0, 1, 3).reshape(nt, rw, Fw)
    wc = w_conv.reshape(3, rw, nt, Cw).transpose(2, 1, 0, 3).reshape(nt, rw, 3 * Cw)
    row0 = jnp.concatenate([ln_gain, ln_bias, b_down, b_conv])
    sm = jnp.zeros((8, 128), f32).at[0, : 4 * rs].set(row0.astype(f32)).at[1, :rd].set(b_up.astype(f32))
    mem = memory.reshape(S, W, 3, M).transpose(0, 2, 1, 3)
    mk = jnp.broadcast_to(window_mask.astype(f32)[:, :, None], (S, W, 128))
    WA, WU, WC, WD, SM, CTX, COT, MK = gather_all(
        nb,
        nu,
        wa,
        wu,
        wc,
        w_down,
        sm,
        compressed.reshape(S, nu, 16, M),
        mem,
        segment.reshape(S, nu, 16, M),
        cotangent.reshape(S, nu, 16, M),
        mk,
    )
    WA = WA.reshape(M, 4 * Cw)
    Wqkv, Wo = WA[:, : 3 * Cw], WA[:, 3 * Cw :]
    WU, WC, WD = WU.reshape(M, Fw), WC.reshape(M, 3 * Cw), WD.reshape(Fw, M)
    gain, bias, bdown, bconv = [SM[:, :, 0, i * rs : (i + 1) * rs].reshape(M) for i in range(4)]
    bup = lax.dynamic_index_in_dim(SM, t, 1, False)[:, 1, :rd].reshape(Fw)
    cols = lambda v: lax.dynamic_slice_in_dim(v, t * Cw, Cw, v.ndim - 1)
    ctx = CTX.reshape(S, 3 * seg_len, M)
    cot = COT.reshape(T, M)
    seg = ctx[:, 2 * seg_len :].reshape(T, M)

    kpos = jnp.concatenate(
        [
            jnp.arange(seg_len),
            seg_len + (3 * jnp.arange(seg_len // 3)[None, :] + jnp.arange(3)[:, None]).reshape(-1),
            2 * seg_len + jnp.arange(seg_len),
        ]
    )
    qpos = 2 * seg_len + jnp.arange(seg_len)
    allowed = kpos[None, :] <= qpos[:, None]
    dist = (qpos[:, None] - kpos[None, :]).astype(f32) * (1.0 / (3 * seg_len))
    slope = lax.dynamic_slice_in_dim(slopes, t * ht, ht)
    scale = 1.0 / math.sqrt(hd)
    q = dot(seg, Wqkv[:, :Cw]).astype(bf16).reshape(S, seg_len, ht, hd)
    kv = dot(ctx.reshape(-1, M), Wqkv[:, Cw:]).astype(bf16).reshape(S, 3 * seg_len, 2, ht, hd)
    kk, vv = kv[:, :, 0], kv[:, :, 1]
    raw = jnp.einsum("sqhd,skhd->shqk", q, kk, preferred_element_type=f32)
    scores = jnp.where(allowed, raw * scale - slope[:, None, None] * dist, -1e30)
    high = jnp.max(scores, axis=-1, keepdims=True)
    e = jnp.exp(scores - high)
    probs = e / jnp.sum(e, axis=-1, keepdims=True)
    probs_low = probs.astype(bf16)
    mixed_t = jnp.einsum("shqk,skhd->sqhd", probs_low, vv, preferred_element_type=f32).astype(bf16)
    MIX = spread(mixed_t.reshape(T, Cw), True, 2)
    mixed = MIX.transpose(1, 0, 2).reshape(T, M)
    resid_t = cols(seg).astype(f32) + dot(mixed, Wo)
    RES = spread(resid_t.astype(bf16), True, 3)
    resid = RES.transpose(1, 0, 2).reshape(T, M).astype(f32)
    center = resid - jnp.mean(resid, axis=-1, keepdims=True)
    spread_ = lax.rsqrt(jnp.mean(center * center, axis=-1, keepdims=True) + norm_eps)
    xhat = center * spread_
    normed = (xhat * gain + bias).astype(bf16)
    pre = dot(normed, WU) + bup
    phi = 0.5 * (1.0 + lax.erf(pre * math.sqrt(0.5)))
    act = (pre * phi).astype(bf16)
    slope_act = phi + pre * jnp.exp(-0.5 * pre * pre) * (1.0 / math.sqrt(2 * math.pi))
    place = lambda v: lax.dynamic_update_slice_in_dim(jnp.zeros((T, M), f32), v, t * Cw, 1)
    out_part = dot(act, WD) + place(resid_t + cols(bdown))
    rows = lambda v: v.astype(bf16).reshape(S, nt, R, M).transpose(1, 0, 2, 3)
    output = jnp.sum(spread(rows(out_part), False, 4).astype(f32), axis=0).astype(bf16)
    gdown = dot_tn(act, cot)
    d_act = dot_nt(cot, WD).astype(bf16)
    d_pre = d_act.astype(f32) * slope_act
    gub = jnp.sum(d_pre, axis=0)
    d_pre_low = d_pre.astype(bf16)
    gup = dot_tn(normed, d_pre_low)
    dn_part = dot_nt(d_pre_low, WU)
    stats = jnp.stack([jnp.mean(dn_part * gain, axis=1), jnp.mean(dn_part * gain * xhat, axis=1)])
    stats = lax.psum(stats, "tier")
    cols_of = lambda v: v.astype(bf16).reshape(T, nt, Cw).transpose(1, 0, 2)
    dn = jnp.sum(spread(cols_of(dn_part), False, 5).astype(f32), axis=0)
    xhat_t = cols(xhat)
    ggain, gbias = jnp.sum(dn * xhat_t, axis=0), jnp.sum(dn, axis=0)
    g = dn * cols(gain)
    cot_t = cols(cot).astype(f32)
    gdb = jnp.sum(cot_t, axis=0)
    d_resid = cot_t + (g - stats[0][:, None] - xhat_t * stats[1][:, None]) * spread_
    d_branch = d_resid.astype(bf16)
    gout = dot_tn(mixed, d_branch)
    dm_part = dot_nt(d_branch, Wo)
    dm = jnp.sum(spread(cols_of(dm_part), False, 6).astype(f32), axis=0).astype(bf16)
    dm = dm.reshape(S, seg_len, ht, hd)
    d_probs = jnp.einsum("sqhd,skhd->shqk", dm, vv, preferred_element_type=f32)
    delta = jnp.sum(probs * d_probs, axis=-1, keepdims=True)
    d_scores = probs * (d_probs - delta)
    gslope = -jnp.sum(d_scores * dist, axis=(0, 2, 3))
    d_raw = (d_scores * scale).astype(bf16)
    dq = jnp.einsum("shqk,skhd->sqhd", d_raw, kk, preferred_element_type=f32).astype(bf16)
    dk = jnp.einsum("shqk,sqhd->skhd", d_raw, q, preferred_element_type=f32).astype(bf16)
    dv = jnp.einsum("shqk,sqhd->skhd", probs_low, dm, preferred_element_type=f32).astype(bf16)
    dq, dk, dv = dq.reshape(T, Cw), dk.reshape(S, -1, Cw), dv.reshape(S, -1, Cw)
    flat = ctx.reshape(-1, M)
    gq = dot_tn(seg, dq)
    gk, gv = dot_tn(flat, dk.reshape(-1, Cw)), dot_tn(flat, dv.reshape(-1, Cw))
    own = lambda v: v[:, 2 * seg_len :].reshape(T, Cw)
    ig_part = dot_nt(jnp.concatenate([dq, own(dk), own(dv)], axis=1), Wqkv) + place(d_resid)
    input_grad = jnp.sum(spread(rows(ig_part), False, 7).astype(f32), axis=0)

    nw = seg_len // 3
    win = ctx[:, seg_len : 2 * seg_len].reshape(S, 3, nw, M)
    win = [win[:, k].reshape(S * nw, M) for k in range(3)]
    conv = sum(dot(win[k], WC[:, k * Cw : (k + 1) * Cw]) for k in range(3)) + cols(bconv)
    pooled = sum(cols(win[k]).astype(f32) for k in range(3)) * (1.0 / 3.0)
    mask = MK.reshape(S, nw, 128)[:, :, :1]
    old = (3 * jnp.arange(nw) + 3)[None, :, None] <= evicted[:, None, None]
    live = jnp.where(old, mask, 0.0).reshape(-1, 1)
    d_conv = live * (conv - pooled)
    gcb = jnp.sum(d_conv, axis=0)
    d_low = d_conv.astype(bf16)
    gconv = jnp.concatenate([dot_tn(win[k], d_low) for k in range(3)], axis=1)
    new_t = (mask.reshape(-1, 1) * conv).astype(bf16)
    NEW = spread(new_t, True, 8).reshape(nt, S, nw, Cw).transpose(1, 2, 0, 3).reshape(S, nw, M)
    slot_offset = seg_len - nw
    local_rows = jnp.arange(R, dtype=jnp.int32) + t * R
    padded = jnp.concatenate([jnp.zeros((S, slot_offset, M), bf16), NEW], axis=1)
    slot_rows = lax.dynamic_slice_in_dim(padded, t * R, R, 1)
    written = (local_rows[None, :] >= slot_offset) & (
        3 * (local_rows[None, :] - slot_offset) + 3 <= evicted[:, None]
    )
    new_compressed = jnp.where(written[..., None], slot_rows, compressed)
    new_memory = jnp.where((local_rows[None, :] < evicted[:, None])[..., None], segment, memory)

    low = lambda v, *s: v.astype(bf16).reshape(s)
    gs = lax.dynamic_update_slice_in_dim(jnp.zeros((128,), f32), gslope, t * ht, 0)
    sg = jnp.concatenate([gub, gdb, ggain, gbias, gcb, gs])
    sg = jnp.concatenate([sg, jnp.zeros((24 * 128 - sg.shape[0],), f32)]).reshape(24, 128)
    OD, OU, OC, OA, OS = reduce_all(
        nb,
        low(gdown, nb, 4, rd // 4, M),
        low(gup, nb, 4, rw, Fw),
        low(gconv, nb, 4, rw, 3 * Cw),
        low(jnp.concatenate([gq, gk, gv, gout], axis=1), nb, 4, rw, 4 * Cw),
        sg,
    )
    OA = OA.reshape(nt, rw, 4, Cw).transpose(2, 1, 0, 3).reshape(4, rw, M)
    OU = OU.reshape(nt, rw, nb, rd).transpose(1, 2, 0, 3).reshape(rw, nb * nt * rd)
    OC = OC.reshape(nt, rw, 3, Cw).transpose(2, 1, 0, 3).reshape(3, rw, M)
    OS = OS.reshape(nt, -1)
    vec = lambda o: lax.dynamic_slice_in_dim(OS[:, o : o + Cw].reshape(M), index * rs, rs)
    gub_out = lax.dynamic_slice(OS, (t, b * rd), (1, rd)).reshape(rd)
    gslopes = jnp.sum(OS[:, Fw + 4 * Cw : Fw + 4 * Cw + heads], axis=0)
    return (
        output,
        input_grad,
        new_memory,
        new_compressed,
        OA[0],
        OA[1],
        OA[2],
        OA[3],
        OU,
        gub_out,
        OD.reshape(rd, M),
        vec(Fw),
        vec(Fw + Cw),
        vec(Fw + 2 * Cw),
        OC,
        vec(Fw + 3 * Cw),
        gslopes,
    )


class Names:
    def __init__(self, names, refs):
        for name, ref in zip(names, refs):
            setattr(self, name, ref)


def layer_kernel(names, shape, *refs):
    r = Names(names, refs)
    nb, nu, S, ht, hd, M, Cw, rw, rd, rs = shape
    R = 16 * nu
    Hw = Cw // 2
    nd = r.YD.shape[1]
    G, bq = nb // 2, nb // 4
    L = 16 * 4 * nu
    C3 = 3 * L
    nw = L // 3
    Fw = nb * rd
    scale = 1.0 / math.sqrt(hd)
    b, t, z, y, zs, zback = places(G)
    mate, ends = z ^ 1, (z == 0) | (z == G - 1)
    ypeer = (b ^ 1, t)
    tc = pl.ds(pl.multiple_of(t * Cw, Cw), Cw)
    sends = []

    def got(ref, sem):
        pltpu.make_async_copy(ref, ref, sem).wait()

    def left_all(ref, sem):
        sends.append((ref, sem))

    def each(n, body, between=None):
        def step(i, c):
            body(i)
            for at, then in (between or {}).items():
                pl.when(i == at)(then)
            return c

        lax.fori_loop(0, n, step, 0)

    def ex_send(e, sem, src, dst):
        for d in (1, 2, 3):
            remote(src(t ^ d), dst(d), r.es.at[e], sem, (b, t ^ d)).start()

    def spread_send(e, s, arr):
        at = arr.at[t, s]
        for d in (1, 2):
            remote(at, at, r.es.at[e], r.er.at[e, s, d - 1], (b, t ^ d)).start()

    def spread_pass(e, s, arr):
        at = arr.at[t ^ 2, s]
        got(at, r.er.at[e, s, 1])
        remote(at, at, r.es.at[e], r.er.at[e, s, 0], (b, t ^ 1)).start()

    def spread_wait(e, s, arr):
        @pl.when(s < S - 1)
        def _():
            spread_pass(e, s + 1, arr)

        got(arr.at[0:2, s], r.er.at[e, s, 0])

    folds = {
        2: (lambda q, s: r.DNP.at[q, s], r.DNR),
        4: (lambda q, s: r.DMP.at[q, s], r.DMR),
        5: (lambda q, s: r.OP.at[s, pl.ds(nu * q, nu)], r.OR),
        6: (lambda q, s: r.NRM.at[s, pl.ds(nu * q, nu)], r.IR),
    }

    def fold_send(e, s):
        out, into = folds[e]
        for i, d in enumerate((1, 3)):
            remote(out(t ^ d, s), into.at[i, s], r.es.at[e], r.er.at[e, s, i], (b, t ^ 1)).start()

    def fold_pass(e, s):
        out, into = folds[e]
        at, far = into.at[1, s], out(t ^ 2, s)
        got(at, r.er.at[e, s, 1])
        far[...] = (far[...].astype(f32) + at[...].astype(f32)).astype(bf16)
        remote(far, into.at[2, s], r.es.at[e], r.er.at[e, s, 0], (b, t ^ 2)).start()

    def fold_late(e, s):
        @pl.when(s > 0)
        def _():
            fold_pass(e, s - 1)

    def folded(e, s):
        out, into = folds[e]
        got(into.at[0:2, s], r.er.at[e, s, 0])
        return out(t, s)[...].astype(f32) + into[0, s].astype(f32) + into[2, s].astype(f32)

    def here(src, dst, i):
        cp = pltpu.make_async_copy(src, dst, r.lsem.at[i])
        cp.start()
        return cp

    wide = lambda at, size: pl.ds(pl.multiple_of(at, 128), size)
    mats = (r.w_query, r.w_key, r.w_value, r.w_output)
    whole = {"S": r.SM, "A": r.WA, "U": r.WU, "C": r.WC}
    index = {"S": 0, "A": 1, "U": 2, "C": 3, "H": 4}

    def tiers(n, at):
        return r.WCX.at[at] if n == "H" else whole[n].at[b, at]

    def cuts(n, q):
        if n == "S":
            return [(r.SM.at[b, t], r.SM.at[b, t])]
        if n == "A":
            return [(w.at[:, wide(Cw * q, Cw)], r.WA.at[b, t, :, i * Cw : (i + 1) * Cw]) for i, w in enumerate(mats)]
        if n == "U":
            return [
                (r.w_up.at[:, wide((4 * i + q) * rd, rd)], r.WU.at[b, t, :, i * rd : (i + 1) * rd]) for i in range(nb)
            ]
        half, to = (y, r.WC.at[b]) if n == "C" else (1 - y, r.WCX)
        return [
            (r.w_conv.at[i, :, wide(Cw * q + Hw * half, Hw)], to.at[t, :, i * Hw : (i + 1) * Hw]) for i in range(3)
        ]

    def tier_own(n):
        for src, dst in cuts(n, t):
            here(src, dst, index[n])

    def tier_start(n):
        i = index[n]
        for d in (1, 2, 3):
            for src, dst in cuts(n, t ^ d):
                remote(src, dst, r.ts.at[i], r.tr.at[i], (b, t ^ d)).start()
        left_all(tiers(n, slice(0, 3)), r.ts.at[i])

    def tier_wait(n):
        i = index[n]
        if n != "S":
            got(tiers(n, t), r.lsem.at[i])
        got(tiers(n, slice(0, 3)), r.tr.at[i])

    def if_(cond, body):
        pl.when(cond)(body)

    def at_ends(body):
        return lambda: if_(ends, body)

    def inside(body):
        return lambda: if_(~ends, body)

    def both(*bodies):
        def run():
            for body in bodies:
                body()

        return run

    right, left = (2 * z + 2 + y, t), (2 * z - 2 + y, t)
    parts = {"S": [(r.SM, 0, 0, 4, 0)], "C": [(r.WC, 1, 0, 4, 1)], "X": [(r.WC, 2, 0, 4, 2)]}
    for i, (n, w) in enumerate((("A", r.WA), ("U", r.WU))):
        parts[n] = [(w, 3 + 2 * i + h, h * 2, 2, 3 + i) for h in (0, 1)]
    first = rd // 4
    rest = (rd - first) // 2
    parts["D"] = [(r.WD, 7, 0, first, 5)]
    for i, n in enumerate("EF"):
        parts[n] = [(r.WD, 8 + 2 * i + h, first + h * rest, rest, 6 + i) for h in (0, 1)]

    def chunk_of(n, part, zz, col=None):
        w, k, at, size, _ = part
        col = ((1 - y) if n in "XF" else y) if col is None else col
        return w.at[2 * zz + col, pl.ds(at, size)]

    def chunks(n, count):
        w, _, at, size, _ = parts[n][0]
        return w.at[0:count, at : at + size * len(parts[n])]

    def hop(part, at, zz, way):
        k = part[1]
        peer, past = (right, z < G - 1) if way == 0 else (left, z > 0)
        return past, remote(at, at, r.zs.at[part[4]], r.zr.at[k, zz - way], peer)

    def own_z(n):
        for part in parts[n]:
            for way in (0, 1):
                past, cp = hop(part, chunk_of(n, part, z), z, way)
                if_(past, cp.start)

    def own_y(n):
        for part in parts[n]:
            at, k = chunk_of(n, part, z), part[4]
            remote(r.WCX if n == "C" else at, at, r.ys.at[k], r.yr.at[k], ypeer).start()

    def arrivals(n, step, js):
        for j in js:
            for part in parts[n]:
                for way in (0, 1):
                    zz = z - j if way == 0 else z + j
                    step(part, j, way, zz, chunk_of(n, part, zz), zz >= 0 if way == 0 else zz < G)

    def onward(n, *js, cross=True):
        def step(part, j, way, zz, at, there):
            k = part[1]

            def body():
                got(at, r.zr.at[k, zz - way])
                if j < G - 1:
                    past, cp = hop(part, at, zz, way)
                    if_(past, cp.start)
                if n not in "CXEF" and cross:
                    remote(at, at, r.ys.at[part[4]], r.yr.at[part[4]], ypeer).start()

            if_(there, body)

        arrivals(n, step, js or range(1, G))

    def over(n, *js):
        def step(part, j, way, zz, at, there):
            if_(there, remote(at, at, r.ys.at[part[4]], r.yr.at[part[4]], ypeer).start)

        arrivals(n, step, js)

    def all_sent(n):
        k = parts[n][0][4]
        if_(ends, lambda: got(chunks(n, 1), r.zs.at[k]))
        if_(~ends, lambda: got(chunks(n, 5), r.zs.at[k]))
        if n not in "XF":
            got(chunks(n, 1 if n in "CE" else G), r.ys.at[k])

    def y_wait(n):
        got(chunks(n, 1 if n in "CE" else G), r.yr.at[parts[n][0][4]])

    def small_start():
        r.SM[b, t] = jnp.zeros((8, 128), f32)
        for q, v in enumerate((r.gain, r.bias, r.bdown, r.bconv, r.bup)):
            r.SM[b, t, q : q + 1, : v.shape[1]] = v[...].astype(f32)
        tier_start("S")

    def memory_rows():
        W = R // 3
        to, frm = (lax.broadcasted_iota(jnp.int32, (R, R), axis) for axis in (0, 1))
        tap = (to >= W).astype(jnp.int32) + (to >= 2 * W).astype(jnp.int32)
        order = (frm == 3 * (to - W * tap) + tap).astype(bf16)
        for s in range(S):
            rows = jnp.dot(order, r.MEMV[s], preferred_element_type=f32).astype(bf16)
            for i in range(3):
                r.CTX[s, 4 * nu + 4 * i + t] = rows[W * i : W * (i + 1)]
            square = lambda axis: lax.broadcasted_iota(jnp.int32, (R // 3, R // 3), axis)
            line = jnp.broadcast_to(r.mask[s : s + 1].astype(f32), (R // 3, R // 3))
            col = jnp.sum(jnp.where(square(0) == square(1), line, 0.0), axis=1, keepdims=True)
            spot = lax.broadcasted_iota(jnp.int32, (R // 3, 128), 0) + (R // 3) * t
            lane = lax.broadcasted_iota(jnp.int32, (R // 3, 128), 1)
            r.MK[s, t] = jnp.where((lane < 64) | (3 * spot + 3 <= r.evicted[s]), col, 0.0)

    def rows_of(src, buf, first):
        at = lambda q: buf.at[:, pl.ds(first + nu * q, nu)]
        parts = [(src.at[:, 16 * i : 16 * i + 16], buf.at[:, first + nu * t + i]) for i in range(nu)]
        return parts, at, True

    def held(at):
        return [(at(t), at(t))], at, False

    def memory_y():
        for i in range(3):
            remote(r.CTX.at[:, 4 * nu + 4 * i + t], r.MEMX.at[:, 4 * i + t], r.ms.at[0], r.ms.at[1], ypeer).start()
        remote(r.MK.at[:, t], r.MKX.at[:, t], r.ms.at[2], r.ms.at[3], ypeer).start()
        left_all(r.MEMX.at[:, 0:3], r.ms.at[0])
        left_all(r.MKX.at[:, 0], r.ms.at[2])

    def memory_come():
        got(r.MEMX.at[:, 0:3], r.ms.at[1])
        got(r.MKX.at[:, 0], r.ms.at[3])

    pieces = [
        rows_of(r.seg, r.CTX, 8 * nu),
        rows_of(r.comp, r.CTX, 0),
        held(lambda q: r.CTX.at[:, 4 * nu + q]),
        held(lambda q: r.CTX.at[:, 4 * nu + 4 + q]),
        held(lambda q: r.CTX.at[:, 4 * nu + 8 + q]),
        rows_of(r.cot, r.COT, 0),
        held(lambda q: r.MK.at[:, q]),
        held(lambda q: r.MEMX.at[:, q]),
        held(lambda q: r.MEMX.at[:, 4 + q]),
        held(lambda q: r.MEMX.at[:, 8 + q]),
        held(lambda q: r.MKX.at[:, q]),
    ]

    group = lambda i: 0 if i < 5 else (1, 2, 3, 3, 3, 4)[i - 5]
    grouped = [(r.CTX, 3 * nu), (r.COT, nu), (r.MK, 1), (r.MEMX, 3), (r.MKX, 1)]

    def act_own():
        for i, (cut, at, far) in enumerate(pieces):
            if far:
                for src, dst in cut:
                    here(src, dst, 5 + group(i))

    def act_start(*which):
        for i in which:
            cut, at, far = pieces[i]
            g = group(i)
            for src, dst in cut:
                remote(src, dst, r.acs.at[g], r.acc.at[g], (b, t ^ 1)).start()
                remote(src, dst, r.acs.at[g], r.acx.at[i], (b, t ^ 2)).start()

    def act_forward(*which):
        for i in which:
            at = pieces[i][1](t ^ 2)
            got(at, r.acx.at[i])
            remote(at, at, r.acs.at[group(i)], r.acf.at[group(i)], (b, t ^ 1)).start()

    def act_wait(g):
        buf, n = grouped[g]
        got(buf.at[:, 0:n], r.acc.at[g])
        got(buf.at[:, 0:n], r.acf.at[g])
        if g < 2:
            got(buf.at[:, 0 : n if g else 2 * nu], r.lsem.at[5 + g])

    def act_sent():
        for g, (buf, n) in enumerate(grouped):
            got(buf.at[:, 0 : 3 * n], r.acs.at[g])

    def table():
        row = lax.broadcasted_iota(jnp.int32, (L, C3), 0) + 2 * L
        col = lax.broadcasted_iota(jnp.int32, (L, C3), 1)
        inner = col - L
        k1 = (inner >= nw).astype(jnp.int32)
        k2 = (inner >= 2 * nw).astype(jnp.int32)
        win = inner - nw * (k1 + k2)
        pos = jnp.where((col >= L) & (col < 2 * L), L + 3 * win + k1 + k2, col)
        r.DIST[...] = jnp.where(pos <= row, (row - pos).astype(f32) * (1.0 / C3), 1e30)
        r.SMG[...] = jnp.zeros_like(r.SMG)

    def seg_rows(s):
        return r.CTX[s, 8 * nu : 12 * nu].reshape(L, M)

    def project(s):
        rows = r.CTX[s].reshape(C3, M)
        kv = jnp.dot(rows, r.WA[:, :, :, Cw : 3 * Cw].reshape(M, 2 * Cw), preferred_element_type=f32)
        r.KV[s] = kv.astype(bf16)
        q = jnp.dot(seg_rows(s), r.WA[:, :, :, :Cw].reshape(M, Cw), preferred_element_type=f32)
        r.Q[s] = q.astype(bf16)


    def attend(s):
        for h in range(ht):
            c = slice(h * hd, (h + 1) * hd)
            raw = dot_nt(r.Q[s, :, c], r.KV[s, :, c])
            scores = raw * scale - r.slopes[t * ht + h] * r.DIST[...]
            e = jnp.exp(scores - jnp.max(scores, axis=1, keepdims=True))
            p = e * (1.0 / jnp.sum(e, axis=1, keepdims=True))
            r.PR[s, h] = p
            v = r.KV[s, :, Cw + h * hd : Cw + (h + 1) * hd]
            r.MIX[t, s, :, c] = jnp.dot(p.astype(bf16), v, preferred_element_type=f32).astype(bf16)
        spread_send(0, s, r.MIX)


    def wo(q):
        return r.WA[bq * q : bq * (q + 1), :, :, 3 * Cw :].reshape(Cw, Cw)

    def residual(s):
        spread_wait(0, s, r.MIX)
        acc = r.CTX[s, 8 * nu : 12 * nu, :, tc].reshape(L, Cw).astype(f32)
        for q in range(4):
            acc = acc + jnp.dot(r.MIX[q, s], wo(q), preferred_element_type=f32)
        r.RT[s] = acc
        r.RES[t, s] = acc.astype(bf16)
        spread_send(1, s, r.RES)

    def vectors():
        lane = lax.broadcasted_iota(jnp.int32, (8, 128), 1)
        for at in range(0, M, 128):
            block = jnp.zeros((8, 128), f32)
            for i in range(128 // rs):
                spot = at // rs + i
                turned = pltpu.roll(r.SM[spot // 4, spot % 4], rs * i, 1)
                block = jnp.where((lane >= rs * i) & (lane < rs * (i + 1)), turned, block)
            r.VV[0:4, at : at + 128] = block[0:4]
        for bb in range(nb):
            r.VV[4:5, bb * rd : (bb + 1) * rd] = r.SM[bb, t, 4:5, :rd]

    def xhat_of(s, q):
        return (r.RES[q, s].astype(f32) - r.MU[s, :, :1]) * r.MU[s, :, 1:2]

    def feed(s):
        spread_wait(1, s, r.RES)
        parts = [r.RES[q, s].astype(f32) for q in range(4)]
        mu = sum(jnp.sum(x, axis=1, keepdims=True) for x in parts) * (1.0 / M)
        var = sum(jnp.sum((x - mu) * (x - mu), axis=1, keepdims=True) for x in parts) * (1.0 / M)
        inv = lax.rsqrt(var + norm_eps)
        lane = lax.broadcasted_iota(jnp.int32, (L, 128), 1)
        r.MU[s] = jnp.where(lane == 0, mu, inv)
        for q in range(4):
            c = slice(q * Cw, (q + 1) * Cw)
            rows = ((parts[q] - mu) * inv) * r.VV[0:1, c] + r.VV[1:2, c]
            r.NRM[s, :, :, c] = rows.astype(bf16).reshape(4 * nu, 16, Cw)
        fb = Fw // 4
        for j in range(4):
            c = slice(j * fb, (j + 1) * fb)
            pre = jnp.dot(r.NRM[s].reshape(L, M), r.WU[:, :, :, c].reshape(M, fb), preferred_element_type=f32) + r.VV[4:5, c]
            phi = 0.5 + 0.5 * lax.erf(pre * math.sqrt(0.5))
            r.ACT[s, :, c] = (pre * phi).astype(bf16)
            r.GP[s, :, c] = (phi + pre * (jnp.exp(-0.5 * pre * pre) * (1.0 / math.sqrt(2 * math.pi)))).astype(bf16)


    def turn(j):
        low = lax.rem(G - j, G)
        inner = jnp.where(z == 1, low, G - 1 - low)
        return jnp.where(z == 0, G - 1 - j, jnp.where(z == G - 1, j, inner))

    grads = {0: (r.GD, r.YD, r.ZD), 1: (r.GU, r.YU, r.ZU), 2: (r.GA, r.YO, r.ZO), 3: (r.WU, r.YA, r.ZA)}

    def block(k, b_):
        g = grads[k][0]
        if k == 0:
            return g.at[b_, 0:nd]
        if k == 1:
            return g.at[b_]
        return g.at[b_, :, :, 3 * Cw :] if k == 2 else g.at[b_, :, :, : 3 * Cw]

    def to_y(k, zz):
        g, yb, zb = grads[k]
        remote(block(k, 2 * zz + (1 - y)), yb.at[zz], r.gys.at[k], r.gyr.at[k, zz], ypeer).start()

    def plus(into, *others):
        def add(i):
            acc = into[i].astype(f32)
            for o in others:
                acc = acc + o[i].astype(f32)
            into[i] = acc.astype(bf16)

        each(into.shape[0], add)

    def pass_on(i, at, zb, o, sem):
        @pl.when((o != mate) & ~ends)
        def _():
            slot = lax.rem(o, 2)
            got(zb.at[slot], r.gzr.at[sem, slot])
            plus(at, zb.at[slot])

        to = jnp.where(ends, mate, o)
        slot = jnp.where(o == mate, 2, jnp.where(ends, lax.rem(o, 2), 3))
        remote(at, zb.at[slot], r.gzs.at[sem], r.gzr.at[sem, jnp.minimum(slot, 2)], (2 * to + y, t)).start()

    def mid(k, *steps):
        g, yb, zb = grads[k]
        for i in steps or range(G - 1):
            o = turn(i)
            at = yb.at[o]
            got(at, r.gyr.at[k, o])
            plus(at, block(k, 2 * o + y))
            pass_on(i, at, zb, o, k)

    def part_c(b_):
        return r.GC.at[b_]

    def part_e(b_):
        return r.GD.at[b_, nd:4]

    def along(part, zb, sem, steps):
        for i in steps or range(G - 1):
            o = turn(i)
            for c, col in enumerate((1 - y, y)):
                pass_on(i, part(2 * o + col), zb.at[c], o, sem + c)

    def mid_c(*steps):
        along(part_c, r.ZC, 4, steps)

    def mid_e(*steps):
        along(part_e, r.ZE, 6, steps)

    def arrived(zb, sem):
        got(zb.at[2:4], r.gzr.at[sem, 2])
        return [zb.at[2], zb.at[3]]

    def summed(at, more, store):
        def total(i):
            acc = at[i].astype(f32)
            for o in more:
                acc = acc + o[i].astype(f32)
            store(i, acc)

        each(at.shape[0], total)

    def fin(k, store):
        g, yb, zb = grads[k]
        at = yb.at[z]
        got(at, r.gyr.at[k, z])
        summed(at, arrived(zb, k) + [block(k, 2 * z + y)], store)

    def cross(part, zb, sem, to, i):
        other = part(2 * z + 1 - y)

        def store(j, acc):
            other[j] = acc.astype(bf16)

        summed(other, arrived(zb.at[0], sem), store)
        remote(other, to, r.gys.at[i], r.gyr.at[i, 0], ypeer).start()

    def cross_c():
        cross(part_c, r.ZC, 4, r.YC, 4)

    def cross_e():
        cross(part_e, r.ZE, 6, r.YE, 5)

    def fin_e():
        got(r.YE, r.gyr.at[5, 0])

        def store(j, acc):
            r.OD[pl.ds((nd + j) * (rd // 4), rd // 4)] = acc

        summed(part_e(2 * z + y), arrived(r.ZE.at[1], 7) + [r.YE], store)

    def fin_c(store):
        summed(r.GC.at[2 * z + y], arrived(r.ZC.at[1], 5), store)

    def crossed_c():
        got(r.YC, r.gyr.at[4, 0])

    def reduced_sent():
        for k, (g, yb, zb) in grads.items():
            got(block(k, slice(0, G)), r.gys.at[k])
            got(block(k, slice(0, 3)), r.gzs.at[k])
        got(r.YC, r.gys.at[4])
        got(r.YE, r.gys.at[5])
        for sem in (4, 5):
            got(r.GC.at[0:3], r.gzs.at[sem])
            got(r.GD.at[0:3, nd:4], r.gzs.at[sem + 2])

    fb = Fw // 4

    def grad_down(i):
        j = turn(i)
        c = pl.ds(pl.multiple_of(j * fb, fb), fb)
        rows = r.ACT[:, :, c].reshape(S * L, fb)
        g = dot_tn(rows, r.COT[...].reshape(S * L, M)).astype(bf16)
        r.GD[pl.ds(j * bq, bq)] = g.reshape(bq, 4, rd // 4, M)
        to_y(0, j)


    def back_feed(s):
        cot = r.COT[s].reshape(L, M)
        for j in range(4):
            c = slice(j * fb, (j + 1) * fb)
            wd = r.WD[bq * j : bq * (j + 1)].reshape(fb, M)
            d_act = dot_nt(cot, wd).astype(bf16).astype(f32)
            d_pre = d_act * r.GP[s, :, c].astype(f32)
            total = jnp.sum(d_pre, axis=0, keepdims=True)
            for i in range(fb // 128):
                at = j * (fb // 128) + i
                r.SMG[at : at + 1] += total[:, 128 * i : 128 * (i + 1)]
            r.GP[s, :, c] = d_pre.astype(bf16)
        m1 = jnp.zeros((L, 1), f32)
        m2 = jnp.zeros((L, 1), f32)
        for q in range(4):
            c = slice(q * Cw, (q + 1) * Cw)
            dn = dot_nt(r.GP[s], r.WU[bq * q : bq * (q + 1)].reshape(Cw, Fw))
            g = dn * r.VV[0:1, c]
            m1 = m1 + jnp.sum(g, axis=1, keepdims=True)
            m2 = m2 + jnp.sum(g * xhat_of(s, q), axis=1, keepdims=True)
            r.DNP[q, s] = dn.astype(bf16)
        lane = lax.broadcasted_iota(jnp.int32, (L, 128), 1)
        both = jnp.where(lane == 0, m1, jnp.where(lane == 1, m2, 0.0)) * (1.0 / M)
        pick = (
            lax.broadcasted_iota(jnp.int32, (8, 128), 0) == lax.broadcasted_iota(jnp.int32, (8, 128), 1)
        ).astype(f32)
        r.ST[t, s] = lax.dot_general(
            pick, both, (((1,), (1,)), ((), ())), precision=lax.Precision.HIGHEST, preferred_element_type=f32
        )
        fold_send(2, s)
        ex_send(3, r.er.at[3, s, 0], lambda q: r.ST.at[t, s], lambda d: r.ST.at[t, s])
        fold_late(2, s)


    def grad_up(i):
        j = turn(i)
        c = pl.ds(pl.multiple_of(j * Cw, Cw), Cw)
        rows = r.NRM[:, :, :, c].reshape(S * L, Cw)
        g = dot_tn(rows, r.GP[...].reshape(S * L, Fw)).astype(bf16)
        r.GU[pl.ds(j * bq, bq)] = g.reshape(bq, 4, rw, Fw)
        to_y(1, j)


    def back_norm(s):
        dn = folded(2, s)
        got(r.ST.at[0:3, s], r.er.at[3, s, 0])
        st = r.ST[0, s] + r.ST[1, s] + r.ST[2, s] + r.ST[3, s]
        side = lax.broadcasted_iota(jnp.int32, (8, 128), 0)
        col_of = lambda i: lax.dot_general(
            st,
            (side == i).astype(f32),
            (((0,), (0,)), ((), ())),
            precision=lax.Precision.HIGHEST,
            preferred_element_type=f32,
        )[:, :1]
        m1, m2 = col_of(0), col_of(1)
        inv = r.MU[s, :, 1:2]
        xhat = (r.RES[t, s].astype(f32) - r.MU[s, :, :1]) * inv
        cot = r.COT[s, :, :, tc].reshape(L, Cw).astype(f32)
        for i, v in enumerate((cot, dn * xhat, dn)):
            total = jnp.sum(v, axis=0, keepdims=True)
            for k in range(Cw // 128):
                at = Fw // 128 + i * (Cw // 128) + k
                r.SMG[at : at + 1] += total[:, 128 * k : 128 * (k + 1)]
        d_resid = cot + (dn * r.VV[0:1, tc] - m1 - xhat * m2) * inv
        r.DR[s] = d_resid
        db = d_resid.astype(bf16)
        r.DB[s] = db
        for q in range(4):
            r.DMP[q, s] = dot_nt(db, wo(q)).astype(bf16)
        fold_send(4, s)
        fold_late(4, s)

    def grad_out():
        for q in range(4):
            g = dot_tn(r.MIX[q].reshape(S * L, Cw), r.DB[...].reshape(S * L, Cw))
            r.GA[bq * q : bq * (q + 1), :, :, 3 * Cw :] = g.astype(bf16).reshape(bq, 4, rw, Cw)
        each(G, lambda i: to_y(2, turn(i)))

    def by_tier(rows, c, sent, come):
        for d in (1, 2, 3):
            remote(r.GA.at[rows, t ^ d, :, c], r.WU.at[rows, t, :, c], sent, come, (b, t ^ d)).start()
        r.WU[rows, t, :, c] = r.GA[rows, t, :, c]

    def out_rows(s):
        for q in range(4):
            c = slice(q * Cw, (q + 1) * Cw)
            o = jnp.dot(r.ACT[s], r.WD[:, :, c].reshape(Fw, Cw), preferred_element_type=f32)
            mine = (t == q).astype(f32)
            o = o + mine * (r.RT[s] + r.VV[2:3, c])
            r.OP[s, :, :, c] = o.astype(bf16).reshape(4 * nu, 16, Cw)
        fold_send(5, s)


    hc = wide(t * Cw + Hw * y, Hw)

    def windows(k, g):
        buf, at = (r.MEMX, 4 * k) if g else (r.CTX, 4 * nu + 4 * k)
        return buf.at[:, at : at + 4]

    def compress():
        sums = jnp.zeros((1, Hw), f32)
        for g in (0, 1):
            conv = r.VV[3:4, hc]
            pooled = 0.0
            for k in range(3):
                wk = r.WC[:, :, :, k * Hw : (k + 1) * Hw].reshape(M, Hw)
                conv = conv + jnp.dot(windows(k, g)[...].reshape(S * nw, M), wk, preferred_element_type=f32)
                pooled = pooled + windows(k, g)[:, :, :, hc].reshape(S * nw, Hw).astype(f32)
            marks = (r.MKX if g else r.MK)[...].reshape(S * nw, 128)
            fresh = (marks[:, :1] * conv).astype(bf16).reshape(S, nw, Hw)
            if g:
                r.NEWX[...] = fresh
            else:
                r.NEW[t, :, :, wide(Hw * y, Hw)] = fresh
            d_conv = marks[:, 64:65] * (conv - pooled * (1.0 / 3.0))
            sums = sums + jnp.sum(d_conv, axis=0, keepdims=True)
            r.DC[g] = d_conv.astype(bf16)
        r.SMG[pl.ds(Fw // 128 + 3 * (Cw // 128) + y, 1)] = sums
        remote(r.NEWX, r.NEW.at[t, :, :, wide(Hw * y, Hw)], r.ns.at[2], r.ns.at[3], ypeer).start()
        left_all(r.NEWX, r.ns.at[2])
        for k in range(3):
            grad = sum(dot_tn(windows(k, g)[...].reshape(S * nw, M), r.DC[g]) for g in (0, 1))
            r.GC[:, :, :, k * Hw : (k + 1) * Hw] = grad.astype(bf16).reshape(nb, 4, rw, Hw)

    slope_row = Fw // 128 + 4 * (Cw // 128)

    def back_attend(s):
        dm = folded(4, s).astype(bf16)
        lane = lax.broadcasted_iota(jnp.int32, (1, 128), 1)
        for h in range(ht):
            c = slice(h * hd, (h + 1) * hd)
            cv = slice(Cw + h * hd, Cw + (h + 1) * hd)
            p = r.PR[s, h]
            dp = dot_nt(dm[:, c], r.KV[s, :, cv])
            delta = jnp.sum(p * dp, axis=1, keepdims=True)
            ds = p * (dp - delta)
            part = jnp.sum(jnp.sum(ds * r.DIST[...], axis=0, keepdims=True), axis=1, keepdims=True)
            r.SMG[slope_row : slope_row + 1] -= jnp.where(lane == t * ht + h, part, 0.0)
            dr = (ds * scale).astype(bf16)
            dq = jnp.dot(dr, r.KV[s, :, c], preferred_element_type=f32).astype(bf16)
            dk = dot_tn(dr, r.Q[s, :, c]).astype(bf16)
            dv = dot_tn(p.astype(bf16), dm[:, c]).astype(bf16)
            r.Q[s, :, c] = dq
            r.KV[s, :, c] = dk
            r.KV[s, :, cv] = dv


    def grad_proj(i):
        j = turn(i)
        c = pl.ds(pl.multiple_of(j * Cw, Cw), Cw)
        gq = jnp.zeros((Cw, Cw), f32)
        gkv = jnp.zeros((Cw, 2 * Cw), f32)
        for s in range(S):
            gq = gq + dot_tn(r.CTX[s, 8 * nu : 12 * nu, :, c].reshape(L, Cw), r.Q[s])
            gkv = gkv + dot_tn(r.CTX[s, :, :, c].reshape(C3, Cw), r.KV[s])
        rows = pl.ds(j * bq, bq)
        r.GA[rows, :, :, :Cw] = gq.astype(bf16).reshape(bq, 4, rw, Cw)
        r.GA[rows, :, :, Cw : 3 * Cw] = gkv.astype(bf16).reshape(bq, 4, rw, 2 * Cw)
        by_tier(rows, slice(0, 3 * Cw), r.xs.at[0], r.xr.at[j])

    def proj_y(*steps):
        for i in steps:
            j = turn(i)
            got(r.WU.at[pl.ds(j * bq, bq), 0:3, :, : 3 * Cw], r.xr.at[j])
            to_y(3, j)

    def own_out(s):
        r.OR[1, s] = folded(5, s).astype(bf16)

    def input_rows(s):
        x = jnp.concatenate([r.Q[s], r.KV[s, 2 * L :]], axis=1)
        for q in range(4):
            c = slice(q * Cw, (q + 1) * Cw)
            w = r.WA[bq * q : bq * (q + 1), :, :, : 3 * Cw].reshape(Cw, 3 * Cw)
            o = dot_nt(x, w) + (t == q).astype(f32) * r.DR[s]
            r.NRM[s, :, :, c] = o.astype(bf16).reshape(4 * nu, 16, Cw)
        fold_send(6, s)
        fold_late(6, s)


    def keep(o):
        def store(i, acc):
            o[pl.ds(i * (rd // 4), rd // 4)] = acc

        return store

    def across(q, acc):
        for i in range(3):
            r.OA[i, :, wide(q * Cw, Cw)] = acc[:, i * Cw : (i + 1) * Cw]

    def hold(m):
        def store(i, acc):
            m[i] = acc.astype(bf16)

        return store

    def tier_back(k, m, tb):
        for d in (1, 2, 3):
            remote(m.at[t ^ d], tb.at[t], r.gts.at[k], r.gtr.at[k], (b, t ^ d)).start()
        left_all(tb.at[0:3], r.gts.at[k])

    def small_y():
        remote(r.SMG, r.YS, r.ss.at[0], r.sr.at[0], ypeer).start()
        left_all(r.SMG, r.ss.at[0])

    def small_z():
        got(r.YS, r.sr.at[0])
        r.ZS[z] = r.SMG[...] + r.YS[...]
        for d in range(1, G):
            remote(r.ZS.at[z], r.ZS.at[z], r.ss.at[1], r.sr.at[1], (2 * zs[d] + y, t)).start()
        left_all(r.ZS.at[0 : G - 1], r.ss.at[1])

    def small_tier():
        got(r.ZS.at[0 : G - 1], r.sr.at[1])
        acc = r.ZS[0]
        for zz in range(1, G):
            acc = acc + r.ZS[zz]
        r.OS[t] = acc
        for d in (1, 2, 3):
            remote(r.OS.at[t], r.OS.at[t], r.gts.at[3], r.gtr.at[3], (b, t ^ d)).start()
        left_all(r.OS.at[0:3], r.gts.at[3])

    def own_input(s):
        r.IG[s] = folded(6, s)

    mineU, mineC, mineO = r.GU.at[2 * z + y], r.GC.at[2 * z + y], r.GA.at[2 * z + y, :, :, 3 * Cw :]
    def give(i, src, dst):
        pltpu.make_async_copy(src, dst, r.osem.at[i]).start()

    def rows_out(i, src, dst):
        for j in range(nu):
            give(i, src.at[:, j], dst.at[:, 16 * j : 16 * j + 16])

    backs = {0: (mineU, r.TU), 1: (mineC, r.TC), 2: (mineO, r.TO), 4: (r.YC, r.TB)}

    def lay(k, q, rows):
        if k == 0:
            for i in range(nb):
                r.OU[:, wide((4 * i + q) * rd, rd)] = rows[:, i * rd : (i + 1) * rd].astype(f32)
        elif k == 2:
            r.OA[3, :, wide(q * Cw, Cw)] = rows.astype(f32)
        else:
            half = y if k == 1 else 1 - y
            for i in range(3):
                r.OC[i, :, wide(q * Cw + Hw * half, Hw)] = rows[:, i * Hw : (i + 1) * Hw].astype(f32)

    def tier_out(k):
        m, tb = backs[k]
        lay(k, t, m[t])
        got(tb.at[0:3], r.gtr.at[k])
        for d in (1, 2, 3):
            lay(k, t ^ d, tb[t ^ d])

    def given():
        for i, (src, dst) in ((0, (r.OU, r.ou)), (1, (r.OC, r.oc)), (2, (r.OA, r.oa)), (3, (r.OD, r.od)), (7, (r.OS, r.os))):
            pltpu.make_async_copy(src, dst, r.osem.at[i]).wait()
        for i, (src, dst) in ((5, (r.OR.at[1], r.out)), (6, (r.IG, r.ig)), (4, (r.OR.at[0], r.om)), (8, (r.OR.at[2], r.ocm))):
            for j in range(nu):
                pltpu.make_async_copy(src.at[:, j], dst.at[:, 16 * j : 16 * j + 16], r.osem.at[i]).wait()

    def small_out():
        got(r.OS.at[0:3], r.gtr.at[3])
        give(7, r.OS, r.os)

    slots = L - nw
    windows_of = [(q, max(R * q - slots, 0), R - max(slots - R * q, 0)) for q in range(4) if slots < R * (q + 1)]

    def new_send():
        got(r.NEWX, r.ns.at[3])
        for q, at, n in windows_of:
            part = r.NEW.at[t, :, at : at + n]
            if_(t != q, remote(part, part, r.ns.at[0], r.ns.at[1], (b, q)).start)

    def new_sent():
        for q, at, n in windows_of:
            if_(t != q, lambda: got(r.NEW.at[0, :, at : at + n], r.ns.at[0]))

    def new_out():
        for q, at, n in windows_of:
            if_(t == q, lambda: got(r.NEW.at[0:3, :, at : at + n], r.ns.at[1]))

    def memories():
        side = lax.broadcasted_iota(jnp.int32, (16, 1), 0)
        for s in range(S):
            for i in range(nu):
                fresh = side + (R * t + 16 * i) < r.evicted[s]
                r.OR[0, s, i] = jnp.where(fresh, r.CTX[s, 8 * nu + nu * t + i], r.MEMV[s, 16 * i : 16 * i + 16])
                r.OR[2, s, i] = r.CTX[s, nu * t + i]
        for q, at, n in windows_of:

            @pl.when(t == q)
            def _(at=at, n=n):
                for i in range((R - n) // 16, nu):
                    w = at + 16 * i - (R - n)
                    for s in range(S):
                        written = 3 * (side + w) + 3 <= r.evicted[s]
                        for p in range(4):
                            c = slice(p * Cw, (p + 1) * Cw)
                            old = r.CTX[s, nu * t + i, :, c]
                            r.OR[2, s, i, :, c] = jnp.where(written, r.NEW[p, s, w : w + 16], old)

    def drain():
        for n in parts:
            if n != "U":
                all_sent(n)
        got(r.GA.at[:, 0:3, :, : 3 * Cw], r.xs.at[0])
        for ref, sem in sends:
            got(ref, sem)
        act_sent()
        new_sent()
        for e, ref in enumerate((r.MIX, r.RES, r.DNP, r.ST, r.DMP, r.OR, r.IR)):
            got(ref.at[0:3], r.es.at[e])

    here(r.wd, r.WD.at[b], 0)
    here(r.mem, r.MEMV, 7)
    for n in "ACHU":
        tier_own(n)
    act_own()
    greet(G, True, True)
    tier_start("A")
    tier_start("H")
    small_start()
    tier_start("U")
    tier_start("C")
    act_start(0, 1)
    got(r.WD.at[b], r.lsem.at[0])
    own_z("D")
    own_z("E")
    own_y("E")
    own_y("D")
    got(r.MEMV, r.lsem.at[7])
    memory_rows()
    act_start(2, 3, 4, 5, 6)
    tier_wait("A")
    own_z("A")
    own_y("A")
    tier_wait("H")
    own_y("C")
    tier_wait("S")
    own_z("S")
    own_y("S")
    table()
    onward("A", 1)
    onward("S", 1)
    onward("A", 2)
    onward("S", 2)
    tier_wait("U")
    own_z("U")
    y_wait("E")
    own_z("F")
    onward("A", 3)
    own_y("U")
    onward("S", 3)
    onward("U", 1)
    act_forward(0, 1, 2, 3, 4)
    act_wait(0)
    y_wait("A")
    each(S, project, {0: lambda: onward("U", 2), 1: lambda: onward("D", 1, cross=False)})
    inside(lambda: onward("E", 1))()
    inside(lambda: onward("F", 1))()
    tier_wait("C")
    y_wait("C")
    each(S, attend)
    onward("U", 3)
    memory_y()
    over("D", 1)
    onward("D", 2)
    own_z("C")
    own_z("X")
    spread_pass(0, 0, r.MIX)
    each(S, residual)
    inside(lambda: onward("E", 2))()
    inside(lambda: onward("F", 2))()
    y_wait("S")
    vectors()
    act_forward(5, 6)
    onward("D", 3)
    y_wait("U")
    spread_pass(1, 0, r.RES)
    each(S, feed, {0: inside(lambda: onward("C", 1)), 1: inside(lambda: onward("E", 3)), 2: inside(lambda: onward("X", 1))})
    memory_come()
    act_start(7, 8, 9, 10)
    act_wait(1)
    act_wait(2)
    each(4, grad_down)
    mid_e(0)
    at_ends(both(lambda: mid_e(1), lambda: mid_e(2)))()
    inside(lambda: onward("F", 3))()
    inside(lambda: onward("C", 2))()
    inside(lambda: onward("X", 2))()
    at_ends(both(lambda: onward("E"), lambda: onward("F")))()
    y_wait("D")
    all_sent("U")
    each(
        S,
        back_feed,
        {
            0: inside(lambda: onward("C", 3)),
            1: both(inside(lambda: mid_e(1)), lambda: mid(0, 0)),
            2: both(inside(lambda: onward("X", 3)), lambda: act_forward(7, 8, 9, 10)),
            3: at_ends(lambda: mid(0, 1)),
        },
    )
    fold_pass(2, S - 1)
    each(2, out_rows)
    each(4, grad_up)
    fold_pass(5, 0)
    fold_pass(5, 1)
    inside(both(lambda: mid_e(2), lambda: mid(0, 1)))()
    at_ends(lambda: mid(0, 2))()
    act_wait(3)
    act_wait(4)
    at_ends(both(lambda: onward("C"), lambda: onward("X")))()
    compress()
    inside(lambda: mid(0, 2))()
    mid_c(0)
    at_ends(lambda: mid_c(1))()
    each(S, back_norm)
    fold_pass(4, S - 1)
    grad_out()
    each(S - 2, lambda s: out_rows(s + 2))
    cross_e()
    inside(lambda: mid_c(1))()
    fold_pass(5, 2)
    fold_pass(5, 3)
    mid(1, 0)
    at_ends(lambda: mid_c(2))()
    each(S, back_attend)
    inside(lambda: mid_c(2))()
    small_y()
    each(4, grad_proj, {1: at_ends(lambda: mid(1, 1))})
    inside(lambda: mid(1, 1))()
    at_ends(lambda: mid(1, 2))()
    proj_y(0)
    each(S, input_rows)
    proj_y(1)
    cross_c()
    fold_pass(6, S - 1)
    at_ends(lambda: mid(2, 0, 1))()
    inside(lambda: mid(1, 2))()
    proj_y(2)
    at_ends(both(lambda: mid(2, 2), lambda: mid(3, 0)))()
    inside(lambda: mid(2, 0, 1, 2))()
    small_z()
    fin_c(hold(mineC))
    tier_back(1, mineC, r.TC)
    proj_y(3)
    new_send()
    inside(lambda: mid(3, 0))()
    fin(1, hold(mineU))
    tier_back(0, mineU, r.TU)
    mid(3, 1)
    crossed_c()
    tier_back(4, r.YC, r.TB)
    fin(0, keep(r.OD))
    fin_e()
    give(3, r.OD, r.od)
    fin(2, hold(mineO))
    tier_back(2, mineO, r.TO)
    mid(3, 2)
    small_tier()
    each(S, own_out)
    rows_out(5, r.OR.at[1], r.out)
    new_out()
    memories()
    rows_out(4, r.OR.at[0], r.om)
    rows_out(8, r.OR.at[2], r.ocm)
    each(S, own_input)
    rows_out(6, r.IG, r.ig)
    tier_out(1)
    tier_out(0)
    give(0, r.OU, r.ou)
    tier_out(4)
    tier_out(2)
    give(1, r.OC, r.oc)
    small_out()
    drain()
    fin(3, across)
    give(2, r.OA, r.oa)
    reduced_sent()
    given()

def whole_layer(nb, ht, hd, arrays):
    S, R, M = arrays["seg"].shape
    rw, rd, rs = arrays["w_query"].shape[0], arrays["wd"].shape[0], M // (4 * nb)
    nu = R // 16
    G, Cw, Fw, L = nb // 2, M // 4, nb * rd, 64 * nu
    dma = pltpu.SemaphoreType.DMA
    V = lambda shape, dtype=bf16: pltpu.VMEM(shape, dtype)
    nd = 3
    D4, A4, U4, C4 = (4, rd // 4, M), (4, rw, 4 * Cw), (4, rw, Fw), (4, rw, 3 * Cw // 2)
    ins = arrays
    outs = dict(
        out=((S, R, M), bf16),
        ig=((S, R, M), f32),
        om=((S, R, M), bf16),
        ocm=((S, R, M), bf16),
        od=((rd, M), f32),
        ou=((rw, 4 * Fw), f32),
        oc=((3, rw, M), f32),
        oa=((4, rw, M), f32),
        os=((4, 24, 128), f32),
    )
    scratch = dict(
        WA=V((nb,) + A4),
        WU=V((nb,) + U4),
        WC=V((nb,) + C4),
        WCX=V(C4),
        MEMX=V((S, 12, 16, M)),
        MKX=V((S, 4, L // 12, 128), f32),
        NEWX=V((S, L // 3, Cw // 2)),
        WD=V((nb, rd, M)),
        SM=V((nb, 4, 8, 128), f32),
        CTX=V((S, 12 * nu, 16, M)),
        COT=V((S, 4 * nu, 16, M)),
        MK=V((S, 4, L // 12, 128), f32),
        DIST=V((L, 3 * L), f32),
        VV=V((8, max(M, Fw)), f32),
        SMG=V((24, 128), f32),
        Q=V((S, L, Cw)),
        KV=V((S, 3 * L, 2 * Cw)),
        PR=V((S, ht, L, 3 * L), f32),
        MIX=V((4, S, L, Cw)),
        RT=V((S, L, Cw), f32),
        RES=V((4, S, L, Cw)),
        MU=V((S, L, 128), f32),
        NRM=V((S, 4 * nu, 16, M)),
        ACT=V((S, L, Fw)),
        GP=V((S, L, Fw)),
        DNP=V((4, S, L, Cw)),
        DNR=V((3, S, L, Cw)),
        ST=V((4, S, 8, L), f32),
        DR=V((S, L, Cw), f32),
        DB=V((S, L, Cw)),
        DMP=V((4, S, L, Cw)),
        DMR=V((3, S, L, Cw)),
        OP=V((S, 4 * nu, 16, M)),
        OR=V((3, S, nu, 16, M)),
        IR=V((3, S, nu, 16, M)),
        DC=V((2, S * L // 3, Cw // 2)),
        GD=V((nb,) + D4),
        GU=V((nb,) + U4),
        GC=V((nb,) + C4),
        GA=V((nb,) + A4),
        YD=V((G, nd) + D4[1:]),
        YE=V((4 - nd,) + D4[1:]),
        YU=V((G,) + U4),
        YC=V(C4),
        YO=V((G, 4, rw, Cw)),
        YA=V((G, 4, rw, 3 * Cw)),
        ZD=V((4, nd) + D4[1:]),
        ZE=V((2, 4, 4 - nd) + D4[1:]),
        ZU=V((4,) + U4),
        ZC=V((2, 4) + C4),
        ZO=V((4, 4, rw, Cw)),
        ZA=V((4, 4, rw, 3 * Cw)),
        YS=V((24, 128), f32),
        ZS=V((G, 24, 128), f32),
        TU=V(U4),
        TO=V((4, rw, Cw)),
        TC=V(C4),
        TB=V(C4),
        NEW=V((4, S, L // 3, Cw)),
        IG=V((S, nu, 16, M), f32),
        OD=V((rd, M), f32),
        OU=V((rw, 4 * Fw), f32),
        OC=V((3, rw, M), f32),
        OA=V((4, rw, M), f32),
        OS=V((4, 24, 128), f32),
        MEMV=V((S, R, M)),
        osem=dma((9,)),
        lsem=dma((8,)),
        ts=dma((5,)),
        tr=dma((5,)),
        zs=dma((8,)),
        zr=dma((12, G - 1)),
        ys=dma((8,)),
        yr=dma((8,)),
        ms=dma((4,)),
        acs=dma((5,)),
        acc=dma((5,)),
        acf=dma((5,)),
        acx=dma((11,)),
        es=dma((7,)),
        er=dma((7, S, 2)),
        ns=dma((4,)),
        gys=dma((6,)),
        gyr=dma((6, G)),
        gzs=dma((8,)),
        gzr=dma((8, 3)),
        ss=dma((2,)),
        sr=dma((2,)),
        xs=dma((1,)),
        xr=dma((G,)),
        gts=dma((5,)),
        gtr=dma((5,)),
    )
    names = list(ins) + list(outs) + list(scratch)
    near = dict(gain=VM, bias=VM, bdown=VM, bconv=VM, bup=VM, mask=VM, evicted=SM, slopes=SM)
    return pl.pallas_call(
        functools.partial(layer_kernel, names, (nb, nu, S, ht, hd, M, Cw, rw, rd, rs)),
        out_shape=[jax.ShapeDtypeStruct(s, d) for s, d in outs.values()],
        in_specs=[near.get(n, ANY) for n in ins],
        out_specs=[ANY] * len(outs),
        scratch_shapes=list(scratch.values()),
        compiler_params=pltpu.CompilerParams(
            collective_id=9, has_side_effects=True, vmem_limit_bytes=63 * 2**20
        ),
        name="whole_layer",
    )(*ins.values())


def finish_kernel(names, shape, *refs):
    r = Names(names, refs)
    nb, rs, rd, Fw, Cw, heads = shape
    b, t = lax.axis_index("batch"), lax.axis_index("tier")
    squares = (r.o_q, r.o_k, r.o_v, r.o_o)
    moves = [(r.out, r.o_out), (r.ig, r.o_ig), (r.od, r.o_od), (r.ou, r.o_ou), (r.oc, r.o_oc), (r.om, r.o_mem), (r.ocm, r.o_comp)]
    n = len(moves)
    bufs = refs[len(names) :]
    small = pltpu.make_async_copy(r.os, r.osv, r.sem.at[n])
    small.start()
    into = [pltpu.make_async_copy(src, buf, r.sem.at[i]) for i, ((src, _), buf) in enumerate(zip(moves, bufs))]
    into.append(pltpu.make_async_copy(r.oa, bufs[n], r.sem.at[n + 1]))
    onto = [
        [pltpu.make_async_copy(buf, dst, r.sem.at[n + 2 + i])] for i, ((_, dst), buf) in enumerate(zip(moves, bufs))
    ]
    onto.append([pltpu.make_async_copy(bufs[n].at[i], o, r.sem.at[2 * n + 2 + i]) for i, o in enumerate(squares)])
    for cp in into:
        cp.start()
    small.wait()
    spot = 4 * b + t
    block, inner = spot // (Cw // rs), lax.rem(spot, Cw // rs)
    half, group = inner // (128 // rs), lax.rem(inner, 128 // rs)
    for i in range(4):
        row = r.osv[block, pl.ds(Fw // 128 + (Cw // 128) * i + half, 1), :]
        turned = pltpu.roll(jnp.broadcast_to(row, (8, 128)), lax.rem(128 - rs * group, 128), 1)
        r.vecs[i : i + 1, :] = turned[0:1, :rs]
    r.ups[...] = r.osv[t, pl.ds(b, 1), :rd]
    at = Fw // 128 + 4 * (Cw // 128)
    total = r.osv[0, at : at + 1]
    for q in range(1, 4):
        total = total + r.osv[q, at : at + 1]
    r.slope[...] = total[:, :heads]
    lines = [(r.vecs.at[i : i + 1], o) for i, o in enumerate((r.o_down, r.o_gain, r.o_bias, r.o_conv))]
    lines += [(r.ups, r.o_up), (r.slope, r.o_slopes)]
    onto.append([pltpu.make_async_copy(src, dst, r.sem.at[2 * n + 6 + i]) for i, (src, dst) in enumerate(lines)])
    for c in onto[-1]:
        c.start()
    for cp, then in zip(into, onto):
        cp.wait()
        for c in then:
            c.start()
    for then in onto:
        for c in then:
            c.wait()


def finish(nb, heads, arrays):
    S, R, M = arrays["out"].shape
    rw, rd, rs = arrays["oa"].shape[1], arrays["od"].shape[0], M // (4 * nb)
    Cw, Fw = M // 4, nb * rd
    rows, mat, vec = (S, R, M), (rw, M), (1, rs)
    outs = dict(
        o_out=(rows, bf16, ANY),
        o_ig=(rows, f32, ANY),
        o_mem=(rows, bf16, ANY),
        o_comp=(rows, bf16, ANY),
        o_q=(mat, f32, ANY),
        o_k=(mat, f32, ANY),
        o_v=(mat, f32, ANY),
        o_o=(mat, f32, ANY),
        o_ou=((rw, 4 * Fw), f32, ANY),
        o_up=((1, rd), f32, ANY),
        o_od=((rd, M), f32, ANY),
        o_down=(vec, f32, ANY),
        o_gain=(vec, f32, ANY),
        o_bias=(vec, f32, ANY),
        o_oc=((3, rw, M), f32, ANY),
        o_conv=(vec, f32, ANY),
        o_slopes=((1, heads), f32, ANY),
    )
    moved = ("out", "ig", "od", "ou", "oc", "om", "ocm", "oa")
    n = len(moved) - 1
    return pl.pallas_call(
        functools.partial(
            finish_kernel, list(arrays) + list(outs) + ["sem", "osv", "vecs", "ups", "slope"], (nb, rs, rd, Fw, Cw, heads)
        ),
        out_shape=[jax.ShapeDtypeStruct(s, d) for s, d, _ in outs.values()],
        in_specs=[ANY] * len(arrays),
        out_specs=[o[2] for o in outs.values()],
        scratch_shapes=[
            pltpu.SemaphoreType.DMA((2 * n + 12,)),
            pltpu.VMEM(arrays["os"].shape, f32),
            pltpu.VMEM((4, rs), f32),
            pltpu.VMEM((1, rd), f32),
            pltpu.VMEM((1, heads), f32),
        ]
        + [pltpu.VMEM(arrays[i].shape, arrays[i].dtype) for i in moved],
        compiler_params=pltpu.CompilerParams(vmem_limit_bytes=63 * 2**20),
        name="finish",
    )(*arrays.values())


def per_device_fused(
    nb,
    segment,
    memory,
    compressed,
    evicted,
    window_mask,
    cotangent,
    w_query,
    w_key,
    w_value,
    w_output,
    w_up,
    b_up,
    w_down,
    b_down,
    ln_gain,
    ln_bias,
    w_conv,
    b_conv,
    slopes,
):
    S, R, M = segment.shape
    heads = slopes.shape[0]
    line = lambda v: v.reshape(1, -1)
    names = ("out", "ig", "om", "ocm", "od", "ou", "oc", "oa", "os")
    made = whole_layer(
        nb,
        heads // 4,
        M // heads,
        dict(
            w_query=w_query,
            w_key=w_key,
            w_value=w_value,
            w_output=w_output,
            w_up=w_up,
            w_conv=w_conv,
            wd=w_down,
            comp=compressed,
            seg=segment,
            cot=cotangent,
            mem=memory,
            gain=line(ln_gain),
            bias=line(ln_bias),
            bdown=line(b_down),
            bconv=line(b_conv),
            bup=line(b_up),
            mask=window_mask,
            evicted=evicted,
            slopes=slopes,
        ),
    )
    outs = finish(nb, heads, dict(zip(names, made)))
    flat = (9, 11, 12, 13, 15, 16)
    return tuple(o.reshape(-1) if i in flat else o for i, o in enumerate(outs))


def solution(mesh):
    both = ("batch", "tier")
    rows = P("batch", "tier", None)
    mat, vec = P(both, None), P(both)
    nb = mesh.shape["batch"]

    def body(*args):
        fused = args[6].shape[0] % 16 == 0 and args[12].shape[0] == 128
        return (per_device_fused if fused else per_device)(nb, *args)

    return jax.shard_map(
        body,
        mesh=mesh,
        in_specs=(
            (rows, rows, rows, P("batch"), P("batch", "tier"), rows)
            + (mat, mat, mat, mat, mat, vec, mat, vec, vec, vec)
            + (P(None, both, None), vec, P())
        ),
        out_specs=(
            (rows, rows, rows, rows, mat, mat, mat, mat, mat, vec, mat, vec, vec, vec)
            + (P(None, both, None), vec, P())
        ),
        check_vma=False,
    )
```

```python
import functools
import math

import jax
import jax.numpy as jnp
from jax import lax
from jax.experimental import pallas as pl
from jax.experimental.pallas import tpu as pltpu
from jax.sharding import PartitionSpec as P

norm_eps = 1e-05
MESH = pl.DeviceIdType.MESH
ANY = pl.BlockSpec(memory_space=pl.ANY)
VM = pl.BlockSpec(memory_space=pltpu.VMEM)
SM = pl.BlockSpec(memory_space=pltpu.SMEM)
f32 = jnp.float32
bf16 = jnp.bfloat16


def remote(src, dst, send, recv, device):
    return pltpu.make_async_remote_copy(
        src_ref=src,
        dst_ref=dst,
        send_sem=send,
        recv_sem=recv,
        device_id=device,
        device_id_type=MESH,
    )


def places(groups):
    b, t = lax.axis_index("batch"), lax.axis_index("tier")
    z, y = b // 2, lax.rem(b, 2)
    zs = [lax.rem(z + d, groups) for d in range(groups)]
    zback = [lax.rem(z + groups - d, groups) for d in range(groups)]
    return b, t, z, y, zs, zback


def greet(groups, tiers, columns):
    b, t, z, y, zs, _ = places(groups)
    barrier = pltpu.get_barrier_semaphore()
    peers = []
    if tiers:
        peers += [(b, t ^ d) for d in (1, 2, 3)]
    if columns:
        peers += [(2 * zz + y, t) for zz in zs[1:]] + [(b ^ 1, t)]
    for peer in peers:
        pl.semaphore_signal(barrier, inc=1, device_id=peer, device_id_type=MESH)
    pl.semaphore_wait(barrier, len(peers))


def gather_kernel(groups, nu, *refs):
    (wa, wu, wc, wd, sm, comp, mem, seg, cot, mk) = refs[:10]
    (WA, WU, WC, WD, SM, CTX, COT, MK) = refs[10:18]
    lsem, ts, tr, zsd, zr, ys, yr, acs, acr = refs[18:]
    G = groups
    b, t, z, y, zs, zback = places(G)
    greet(G, True, True)
    ypeer = (b ^ 1, t)
    local, sends = [], []

    def here(src, dst, i):
        cp = pltpu.make_async_copy(src, dst, lsem.at[i])
        cp.start()
        return cp

    kinds = [(sm, SM), (wa, WA), (wu, WU), (wc, WC)]
    own = []
    for k, (src, dst) in enumerate(kinds):
        mine = src if k == 0 else src.at[t]
        own.append(here(mine, dst.at[b, t], k))
        for d in (1, 2, 3):
            piece = src if k == 0 else src.at[t ^ d]
            cp = remote(piece, dst.at[b, t], ts.at[k, d - 1], tr.at[k, d - 1], (b, t ^ d))
            cp.start()
            sends.append(cp)
    own.append(here(wd, WD.at[b], 4))
    pieces = [
        (comp, lambda q: CTX.at[:, pl.ds(nu * q, nu)]),
        (mem.at[:, 0], lambda q: CTX.at[:, 4 * nu + q]),
        (mem.at[:, 1], lambda q: CTX.at[:, 4 * nu + 4 + q]),
        (mem.at[:, 2], lambda q: CTX.at[:, 4 * nu + 8 + q]),
        (seg, lambda q: CTX.at[:, pl.ds(8 * nu + nu * q, nu)]),
        (mk, lambda q: MK.at[:, q]),
        (cot, lambda q: COT.at[:, pl.ds(nu * q, nu)]),
    ]
    for i, (src, at) in enumerate(pieces):
        own.append(here(src, at(t), 5 + i))
        for j, d in enumerate((1, 2)):
            cp = remote(src, at(t), acs.at[i, j], acr.at[i, j], (b, t ^ d))
            cp.start()
            sends.append(cp)
    table = [SM, WA, WU, WD, WC]
    local_of = [0, 1, 2, 4, 3]
    for k, dst in enumerate(table):
        own[local_of[k]].wait()
        if k != 3:
            kk = local_of[k]
            for d in (1, 2, 3):
                remote(dst.at[b, t], dst.at[b, t ^ d], ts.at[kk, d - 1], tr.at[kk, d - 1], (b, t ^ d)).wait_recv()
        for d in range(1, G):
            cp = remote(dst.at[b], dst.at[b], zsd.at[k, d], zr.at[k, d], (2 * zs[d] + y, t))
            cp.start()
            sends.append(cp)
        cp = remote(dst.at[b], dst.at[b], ys.at[k, 0], yr.at[k, 0], ypeer)
        cp.start()
        sends.append(cp)
    for i, (src, at) in enumerate(pieces):
        remote(at(t ^ 2), at(t ^ 2), acs.at[i, 1], acr.at[i, 1], (b, t ^ 2)).wait_recv()
        cp = remote(at(t ^ 2), at(t ^ 2), acs.at[i, 2], acr.at[i, 2], (b, t ^ 1))
        cp.start()
        sends.append(cp)
    for k, dst in enumerate(table):
        for d in range(1, G):
            at = dst.at[2 * zback[d] + y]
            remote(at, at, zsd.at[k, d], zr.at[k, d], ypeer).wait_recv()
            cp = remote(at, at, ys.at[k, d], yr.at[k, d], ypeer)
            cp.start()
            sends.append(cp)
    for k, dst in enumerate(table):
        for d in range(G):
            at = dst.at[2 * zback[d] + (1 - y)]
            remote(at, at, ys.at[k, d], yr.at[k, d], ypeer).wait_recv()
    for i, (src, at) in enumerate(pieces):
        for j, q in ((0, t ^ 1), (2, t ^ 3)):
            remote(at(q), at(q), acs.at[i, j], acr.at[i, j], (b, t ^ 1)).wait_recv()
    for i in range(len(pieces)):
        own[5 + i].wait()
    for cp in sends:
        cp.wait_send()


def gather_all(nb, nu, wa, wu, wc, wd, sm, comp, mem, seg, cot, mk):
    G = nb // 2
    S, _, U, M = comp.shape
    out = [
        jax.ShapeDtypeStruct((nb,) + wa.shape, bf16),
        jax.ShapeDtypeStruct((nb,) + wu.shape, bf16),
        jax.ShapeDtypeStruct((nb,) + wc.shape, bf16),
        jax.ShapeDtypeStruct((nb,) + wd.shape, bf16),
        jax.ShapeDtypeStruct((nb, 4) + sm.shape, f32),
        jax.ShapeDtypeStruct((S, 12 * nu, U, M), bf16),
        jax.ShapeDtypeStruct((S, 4 * nu, U, M), bf16),
        jax.ShapeDtypeStruct((S, 4) + mk.shape[1:], f32),
    ]
    dma = pltpu.SemaphoreType.DMA
    return pl.pallas_call(
        functools.partial(gather_kernel, G, nu),
        out_shape=out,
        in_specs=[ANY] * 10,
        out_specs=[ANY] * 8,
        scratch_shapes=[
            dma((12,)),
            dma((4, 3)),
            dma((4, 3)),
            dma((5, G)),
            dma((5, G)),
            dma((5, G)),
            dma((5, G)),
            dma((7, 3)),
            dma((7, 3)),
        ],
        compiler_params=pltpu.CompilerParams(collective_id=0, has_side_effects=True),
        name="gather_all",
    )(wa, wu, wc, wd, sm, comp, mem, seg, cot, mk)


def spread_kernel(same, x, o, lsem, ss, rs):
    b, t = lax.axis_index("batch"), lax.axis_index("tier")
    greet(1, True, False)
    cps = []
    for d in (1, 2, 3):
        cp = remote(x if same else x.at[t ^ d], o.at[t], ss.at[d - 1], rs.at[d - 1], (b, t ^ d))
        cp.start()
        cps.append(cp)
    mine = pltpu.make_async_copy(x if same else x.at[t], o.at[t], lsem)
    mine.start()
    mine.wait()
    for d in (1, 2, 3):
        remote(o.at[t ^ d], o.at[t ^ d], ss.at[d - 1], rs.at[d - 1], (b, t ^ d)).wait_recv()
    for cp in cps:
        cp.wait_send()


def spread(x, same, cid):
    dma = pltpu.SemaphoreType.DMA
    shape = ((4,) + x.shape) if same else x.shape
    return pl.pallas_call(
        functools.partial(spread_kernel, same),
        out_shape=jax.ShapeDtypeStruct(shape, x.dtype),
        in_specs=[ANY],
        out_specs=ANY,
        scratch_shapes=[dma, dma((3,)), dma((3,))],
        compiler_params=pltpu.CompilerParams(collective_id=cid, has_side_effects=True),
        name="spread_%d" % cid,
    )(x)


def reduce_kernel(groups, *refs):
    GD, GU, GC, GA, SMG = refs[:5]
    OD, OU, OC, OA, OS = refs[5:10]
    YD, YU, YC, YA, YS, ZD, ZU, ZC, ZA, ZS, TU, TC, TA, MU, MC, MA, ys, yr, zsd, zr, ts, tr = refs[10:]
    G = groups
    b, t, z, y, zs, zback = places(G)
    greet(G, True, True)
    ypeer = (b ^ 1, t)
    sends = []
    kinds = [
        (GD, YD, ZD, OD, None, None),
        (GU, YU, ZU, OU, MU, TU),
        (GC, YC, ZC, OC, MC, TC),
        (GA, YA, ZA, OA, MA, TA),
    ]
    for k, (g, yb, *_) in enumerate(kinds):
        for d in range(G):
            zz = zs[(d + 1) % G]
            cp = remote(g.at[2 * zz + (1 - y)], yb.at[zz], ys.at[k, d], yr.at[k, d], ypeer)
            cp.start()
            sends.append(cp)
    cp = remote(SMG, YS, ys.at[4, 0], yr.at[4, 0], ypeer)
    cp.start()
    sends.append(cp)
    for k, (g, yb, zb, o, m, tb) in enumerate(kinds):
        for d in range(G):
            zz = zs[(d + 1) % G]
            at = yb.at[zz]
            remote(at, at, ys.at[k, d], yr.at[k, d], ypeer).wait_recv()

            def add(i, c, yb=yb, zz=zz, g=g):
                yb[zz, i] = (yb[zz, i].astype(f32) + g[2 * zz + y, i].astype(f32)).astype(bf16)
                return c

            lax.fori_loop(0, yb.shape[1], add, 0)
            if d < G - 1:
                cp = remote(at, zb.at[d], zsd.at[k, d], zr.at[k, d], (2 * zz + y, t))
                cp.start()
                sends.append(cp)
    remote(YS, YS, ys.at[4, 0], yr.at[4, 0], ypeer).wait_recv()
    ZS[z] = SMG[...] + YS[...]
    for d in range(G - 1):
        cp = remote(ZS.at[z], ZS.at[z], zsd.at[4, d], zr.at[4, d], (2 * zs[d + 1] + y, t))
        cp.start()
        sends.append(cp)
    for k, (g, yb, zb, o, m, tb) in enumerate(kinds):
        for d in range(G - 1):
            remote(zb.at[d], zb.at[d], zsd.at[k, d], zr.at[k, d], ypeer).wait_recv()

        def total(i, c, k=k, yb=yb, zb=zb, o=o, m=m):
            acc = yb[z, i].astype(f32)
            for d in range(G - 1):
                acc = acc + zb[d, i].astype(f32)
            if k == 0:
                o[i] = acc
            else:
                m[i] = acc.astype(bf16)
            return c

        lax.fori_loop(0, o.shape[0], total, 0)
        if k:
            for d in (1, 2, 3):
                cp = remote(m.at[t ^ d], tb.at[t], ts.at[k - 1, d - 1], tr.at[k - 1, d - 1], (b, t ^ d))
                cp.start()
                sends.append(cp)
    for d in range(G - 1):
        at = ZS.at[zback[d + 1]]
        remote(at, at, zsd.at[4, d], zr.at[4, d], ypeer).wait_recv()
    acc = ZS[0]
    for zz in range(1, G):
        acc = acc + ZS[zz]
    OS[t] = acc
    for d in (1, 2, 3):
        cp = remote(OS.at[t], OS.at[t], ts.at[3, d - 1], tr.at[3, d - 1], (b, t ^ d))
        cp.start()
        sends.append(cp)
    for k, (g, yb, zb, o, m, tb) in enumerate(kinds):
        if k:
            o[t] = m[t].astype(f32)
            for d in (1, 2, 3):
                at = tb.at[t ^ d]
                remote(at, at, ts.at[k - 1, d - 1], tr.at[k - 1, d - 1], (b, t ^ d)).wait_recv()
                o[t ^ d] = tb[t ^ d].astype(f32)
    for d in (1, 2, 3):
        at = OS.at[t ^ d]
        remote(at, at, ts.at[3, d - 1], tr.at[3, d - 1], (b, t ^ d)).wait_recv()
    for cp in sends:
        cp.wait_send()


def reduce_all(nb, gd, gu, gc, ga, sg):
    G = nb // 2
    dma = pltpu.SemaphoreType.DMA
    shapes = [x.shape[1:] for x in (gd, gu, gc, ga)]
    return pl.pallas_call(
        functools.partial(reduce_kernel, G),
        out_shape=[jax.ShapeDtypeStruct(s, f32) for s in shapes]
        + [jax.ShapeDtypeStruct((4,) + sg.shape, f32)],
        in_specs=[VM] * 5,
        out_specs=[VM] * 5,
        scratch_shapes=[pltpu.VMEM((G,) + s, bf16) for s in shapes]
        + [pltpu.VMEM(sg.shape, f32)]
        + [pltpu.VMEM((G - 1,) + s, bf16) for s in shapes]
        + [pltpu.VMEM((G,) + sg.shape, f32)]
        + [pltpu.VMEM(s, bf16) for s in shapes[1:]]
        + [pltpu.VMEM(s, bf16) for s in shapes[1:]]
        + [dma((5, G)), dma((5, G)), dma((5, G)), dma((5, G)), dma((4, 3)), dma((4, 3))],
        compiler_params=pltpu.CompilerParams(
            collective_id=1, has_side_effects=True, vmem_limit_bytes=48 * 2**20
        ),
        name="reduce_all",
    )(gd, gu, gc, ga, sg)


def dot(a, b):
    return jnp.dot(a, b, preferred_element_type=f32)


def dot_tn(a, b):
    return lax.dot_general(a, b, (((0,), (0,)), ((), ())), preferred_element_type=f32)


def dot_nt(a, b):
    return lax.dot_general(a, b, (((1,), (1,)), ((), ())), preferred_element_type=f32)


def per_device(
    nb,
    segment,
    memory,
    compressed,
    evicted,
    window_mask,
    cotangent,
    w_query,
    w_key,
    w_value,
    w_output,
    w_up,
    b_up,
    w_down,
    b_down,
    ln_gain,
    ln_bias,
    w_conv,
    b_conv,
    slopes,
):
    S, R, M = segment.shape
    heads = slopes.shape[0]
    hd = M // heads
    nt = 4
    rw, rd, rs = w_query.shape[0], w_down.shape[0], b_down.shape[0]
    b, t = lax.axis_index("batch"), lax.axis_index("tier")
    Cw, Fw = M // nt, nb * rd
    nu, W = R // 16, R // 3
    seg_len = nt * R
    T = S * seg_len
    ht = heads // nt
    index = 4 * b + t

    wa = jnp.stack([w_query, w_key, w_value, w_output]).reshape(4, rw, nt, Cw)
    wa = wa.transpose(2, 1, 0, 3).reshape(nt, rw, 4 * Cw)
    wu = w_up.reshape(rw, nb, nt, rd).transpose(2, 0, 1, 3).reshape(nt, rw, Fw)
    wc = w_conv.reshape(3, rw, nt, Cw).transpose(2, 1, 0, 3).reshape(nt, rw, 3 * Cw)
    row0 = jnp.concatenate([ln_gain, ln_bias, b_down, b_conv])
    sm = jnp.zeros((8, 128), f32).at[0, : 4 * rs].set(row0.astype(f32)).at[1, :rd].set(b_up.astype(f32))
    mem = memory.reshape(S, W, 3, M).transpose(0, 2, 1, 3)
    mk = jnp.broadcast_to(window_mask.astype(f32)[:, :, None], (S, W, 128))
    WA, WU, WC, WD, SM, CTX, COT, MK = gather_all(
        nb,
        nu,
        wa,
        wu,
        wc,
        w_down,
        sm,
        compressed.reshape(S, nu, 16, M),
        mem,
        segment.reshape(S, nu, 16, M),
        cotangent.reshape(S, nu, 16, M),
        mk,
    )
    WA = WA.reshape(M, 4 * Cw)
    Wqkv, Wo = WA[:, : 3 * Cw], WA[:, 3 * Cw :]
    WU, WC, WD = WU.reshape(M, Fw), WC.reshape(M, 3 * Cw), WD.reshape(Fw, M)
    gain, bias, bdown, bconv = [SM[:, :, 0, i * rs : (i + 1) * rs].reshape(M) for i in range(4)]
    bup = lax.dynamic_index_in_dim(SM, t, 1, False)[:, 1, :rd].reshape(Fw)
    cols = lambda v: lax.dynamic_slice_in_dim(v, t * Cw, Cw, v.ndim - 1)
    ctx = CTX.reshape(S, 3 * seg_len, M)
    cot = COT.reshape(T, M)
    seg = ctx[:, 2 * seg_len :].reshape(T, M)

    kpos = jnp.concatenate(
        [
            jnp.arange(seg_len),
            seg_len + (3 * jnp.arange(seg_len // 3)[None, :] + jnp.arange(3)[:, None]).reshape(-1),
            2 * seg_len + jnp.arange(seg_len),
        ]
    )
    qpos = 2 * seg_len + jnp.arange(seg_len)
    allowed = kpos[None, :] <= qpos[:, None]
    dist = (qpos[:, None] - kpos[None, :]).astype(f32) * (1.0 / (3 * seg_len))
    slope = lax.dynamic_slice_in_dim(slopes, t * ht, ht)
    scale = 1.0 / math.sqrt(hd)
    q = dot(seg, Wqkv[:, :Cw]).astype(bf16).reshape(S, seg_len, ht, hd)
    kv = dot(ctx.reshape(-1, M), Wqkv[:, Cw:]).astype(bf16).reshape(S, 3 * seg_len, 2, ht, hd)
    kk, vv = kv[:, :, 0], kv[:, :, 1]
    raw = jnp.einsum("sqhd,skhd->shqk", q, kk, preferred_element_type=f32)
    scores = jnp.where(allowed, raw * scale - slope[:, None, None] * dist, -1e30)
    high = jnp.max(scores, axis=-1, keepdims=True)
    e = jnp.exp(scores - high)
    probs = e / jnp.sum(e, axis=-1, keepdims=True)
    probs_low = probs.astype(bf16)
    mixed_t = jnp.einsum("shqk,skhd->sqhd", probs_low, vv, preferred_element_type=f32).astype(bf16)
    MIX = spread(mixed_t.reshape(T, Cw), True, 2)
    mixed = MIX.transpose(1, 0, 2).reshape(T, M)
    resid_t = cols(seg).astype(f32) + dot(mixed, Wo)
    RES = spread(resid_t.astype(bf16), True, 3)
    resid = RES.transpose(1, 0, 2).reshape(T, M).astype(f32)
    center = resid - jnp.mean(resid, axis=-1, keepdims=True)
    spread_ = lax.rsqrt(jnp.mean(center * center, axis=-1, keepdims=True) + norm_eps)
    xhat = center * spread_
    normed = (xhat * gain + bias).astype(bf16)
    pre = dot(normed, WU) + bup
    phi = 0.5 * (1.0 + lax.erf(pre * math.sqrt(0.5)))
    act = (pre * phi).astype(bf16)
    slope_act = phi + pre * jnp.exp(-0.5 * pre * pre) * (1.0 / math.sqrt(2 * math.pi))
    place = lambda v: lax.dynamic_update_slice_in_dim(jnp.zeros((T, M), f32), v, t * Cw, 1)
    out_part = dot(act, WD) + place(resid_t + cols(bdown))
    rows = lambda v: v.astype(bf16).reshape(S, nt, R, M).transpose(1, 0, 2, 3)
    output = jnp.sum(spread(rows(out_part), False, 4).astype(f32), axis=0).astype(bf16)
    gdown = dot_tn(act, cot)
    d_act = dot_nt(cot, WD).astype(bf16)
    d_pre = d_act.astype(f32) * slope_act
    gub = jnp.sum(d_pre, axis=0)
    d_pre_low = d_pre.astype(bf16)
    gup = dot_tn(normed, d_pre_low)
    dn_part = dot_nt(d_pre_low, WU)
    stats = jnp.stack([jnp.mean(dn_part * gain, axis=1), jnp.mean(dn_part * gain * xhat, axis=1)])
    stats = lax.psum(stats, "tier")
    cols_of = lambda v: v.astype(bf16).reshape(T, nt, Cw).transpose(1, 0, 2)
    dn = jnp.sum(spread(cols_of(dn_part), False, 5).astype(f32), axis=0)
    xhat_t = cols(xhat)
    ggain, gbias = jnp.sum(dn * xhat_t, axis=0), jnp.sum(dn, axis=0)
    g = dn * cols(gain)
    cot_t = cols(cot).astype(f32)
    gdb = jnp.sum(cot_t, axis=0)
    d_resid = cot_t + (g - stats[0][:, None] - xhat_t * stats[1][:, None]) * spread_
    d_branch = d_resid.astype(bf16)
    gout = dot_tn(mixed, d_branch)
    dm_part = dot_nt(d_branch, Wo)
    dm = jnp.sum(spread(cols_of(dm_part), False, 6).astype(f32), axis=0).astype(bf16)
    dm = dm.reshape(S, seg_len, ht, hd)
    d_probs = jnp.einsum("sqhd,skhd->shqk", dm, vv, preferred_element_type=f32)
    delta = jnp.sum(probs * d_probs, axis=-1, keepdims=True)
    d_scores = probs * (d_probs - delta)
    gslope = -jnp.sum(d_scores * dist, axis=(0, 2, 3))
    d_raw = (d_scores * scale).astype(bf16)
    dq = jnp.einsum("shqk,skhd->sqhd", d_raw, kk, preferred_element_type=f32).astype(bf16)
    dk = jnp.einsum("shqk,sqhd->skhd", d_raw, q, preferred_element_type=f32).astype(bf16)
    dv = jnp.einsum("shqk,sqhd->skhd", probs_low, dm, preferred_element_type=f32).astype(bf16)
    dq, dk, dv = dq.reshape(T, Cw), dk.reshape(S, -1, Cw), dv.reshape(S, -1, Cw)
    flat = ctx.reshape(-1, M)
    gq = dot_tn(seg, dq)
    gk, gv = dot_tn(flat, dk.reshape(-1, Cw)), dot_tn(flat, dv.reshape(-1, Cw))
    own = lambda v: v[:, 2 * seg_len :].reshape(T, Cw)
    ig_part = dot_nt(jnp.concatenate([dq, own(dk), own(dv)], axis=1), Wqkv) + place(d_resid)
    input_grad = jnp.sum(spread(rows(ig_part), False, 7).astype(f32), axis=0)

    nw = seg_len // 3
    win = ctx[:, seg_len : 2 * seg_len].reshape(S, 3, nw, M)
    win = [win[:, k].reshape(S * nw, M) for k in range(3)]
    conv = sum(dot(win[k], WC[:, k * Cw : (k + 1) * Cw]) for k in range(3)) + cols(bconv)
    pooled = sum(cols(win[k]).astype(f32) for k in range(3)) * (1.0 / 3.0)
    mask = MK.reshape(S, nw, 128)[:, :, :1]
    old = (3 * jnp.arange(nw) + 3)[None, :, None] <= evicted[:, None, None]
    live = jnp.where(old, mask, 0.0).reshape(-1, 1)
    d_conv = live * (conv - pooled)
    gcb = jnp.sum(d_conv, axis=0)
    d_low = d_conv.astype(bf16)
    gconv = jnp.concatenate([dot_tn(win[k], d_low) for k in range(3)], axis=1)
    new_t = (mask.reshape(-1, 1) * conv).astype(bf16)
    NEW = spread(new_t, True, 8).reshape(nt, S, nw, Cw).transpose(1, 2, 0, 3).reshape(S, nw, M)
    slot_offset = seg_len - nw
    local_rows = jnp.arange(R, dtype=jnp.int32) + t * R
    padded = jnp.concatenate([jnp.zeros((S, slot_offset, M), bf16), NEW], axis=1)
    slot_rows = lax.dynamic_slice_in_dim(padded, t * R, R, 1)
    written = (local_rows[None, :] >= slot_offset) & (
        3 * (local_rows[None, :] - slot_offset) + 3 <= evicted[:, None]
    )
    new_compressed = jnp.where(written[..., None], slot_rows, compressed)
    new_memory = jnp.where((local_rows[None, :] < evicted[:, None])[..., None], segment, memory)

    low = lambda v, *s: v.astype(bf16).reshape(s)
    gs = lax.dynamic_update_slice_in_dim(jnp.zeros((128,), f32), gslope, t * ht, 0)
    sg = jnp.concatenate([gub, gdb, ggain, gbias, gcb, gs])
    sg = jnp.concatenate([sg, jnp.zeros((24 * 128 - sg.shape[0],), f32)]).reshape(24, 128)
    OD, OU, OC, OA, OS = reduce_all(
        nb,
        low(gdown, nb, 4, rd // 4, M),
        low(gup, nb, 4, rw, Fw),
        low(gconv, nb, 4, rw, 3 * Cw),
        low(jnp.concatenate([gq, gk, gv, gout], axis=1), nb, 4, rw, 4 * Cw),
        sg,
    )
    OA = OA.reshape(nt, rw, 4, Cw).transpose(2, 1, 0, 3).reshape(4, rw, M)
    OU = OU.reshape(nt, rw, nb, rd).transpose(1, 2, 0, 3).reshape(rw, nb * nt * rd)
    OC = OC.reshape(nt, rw, 3, Cw).transpose(2, 1, 0, 3).reshape(3, rw, M)
    OS = OS.reshape(nt, -1)
    vec = lambda o: lax.dynamic_slice_in_dim(OS[:, o : o + Cw].reshape(M), index * rs, rs)
    gub_out = lax.dynamic_slice(OS, (t, b * rd), (1, rd)).reshape(rd)
    gslopes = jnp.sum(OS[:, Fw + 4 * Cw : Fw + 4 * Cw + heads], axis=0)
    return (
        output,
        input_grad,
        new_memory,
        new_compressed,
        OA[0],
        OA[1],
        OA[2],
        OA[3],
        OU,
        gub_out,
        OD.reshape(rd, M),
        vec(Fw),
        vec(Fw + Cw),
        vec(Fw + 2 * Cw),
        OC,
        vec(Fw + 3 * Cw),
        gslopes,
    )


class Names:
    def __init__(self, names, refs):
        for name, ref in zip(names, refs):
            setattr(self, name, ref)


def layer_kernel(names, shape, *refs):
    r = Names(names, refs)
    nb, nu, S, ht, hd, M, Cw, rw, rd, rs = shape
    R = 16 * nu
    Hw = Cw // 2
    nd = r.YD.shape[1]
    G, bq = nb // 2, nb // 4
    L = 16 * 4 * nu
    C3 = 3 * L
    nw = L // 3
    Fw = nb * rd
    scale = 1.0 / math.sqrt(hd)
    b, t, z, y, zs, zback = places(G)
    mate, ends = z ^ 1, (z == 0) | (z == G - 1)
    ypeer = (b ^ 1, t)
    tc = pl.ds(pl.multiple_of(t * Cw, Cw), Cw)
    sends = []

    def got(ref, sem):
        pltpu.make_async_copy(ref, ref, sem).wait()

    def left_all(ref, sem):
        sends.append((ref, sem))

    def each(n, body, between=None):
        def step(i, c):
            body(i)
            for at, then in (between or {}).items():
                pl.when(i == at)(then)
            return c

        lax.fori_loop(0, n, step, 0)

    def ex_send(e, sem, src, dst):
        for d in (1, 2, 3):
            remote(src(t ^ d), dst(d), r.es.at[e], sem, (b, t ^ d)).start()

    def spread_send(e, s, arr):
        at = arr.at[t, s]
        for d in (1, 2):
            remote(at, at, r.es.at[e], r.er.at[e, s, d - 1], (b, t ^ d)).start()

    def spread_pass(e, s, arr):
        at = arr.at[t ^ 2, s]
        got(at, r.er.at[e, s, 1])
        remote(at, at, r.es.at[e], r.er.at[e, s, 0], (b, t ^ 1)).start()

    def spread_wait(e, s, arr):
        @pl.when(s < S - 1)
        def _():
            spread_pass(e, s + 1, arr)

        got(arr.at[0:2, s], r.er.at[e, s, 0])

    folds = {
        2: (lambda q, s: r.DNP.at[q, s], r.DNR),
        4: (lambda q, s: r.DMP.at[q, s], r.DMR),
        5: (lambda q, s: r.OP.at[s, pl.ds(nu * q, nu)], r.OR),
        6: (lambda q, s: r.NRM.at[s, pl.ds(nu * q, nu)], r.IR),
    }

    def fold_send(e, s):
        out, into = folds[e]
        for i, d in enumerate((1, 3)):
            remote(out(t ^ d, s), into.at[i, s], r.es.at[e], r.er.at[e, s, i], (b, t ^ 1)).start()

    def fold_pass(e, s):
        out, into = folds[e]
        at, far = into.at[1, s], out(t ^ 2, s)
        got(at, r.er.at[e, s, 1])
        far[...] = (far[...].astype(f32) + at[...].astype(f32)).astype(bf16)
        remote(far, into.at[2, s], r.es.at[e], r.er.at[e, s, 0], (b, t ^ 2)).start()

    def fold_late(e, s):
        @pl.when(s > 0)
        def _():
            fold_pass(e, s - 1)

    def folded(e, s):
        out, into = folds[e]
        got(into.at[0:2, s], r.er.at[e, s, 0])
        return out(t, s)[...].astype(f32) + into[0, s].astype(f32) + into[2, s].astype(f32)

    def here(src, dst, i):
        cp = pltpu.make_async_copy(src, dst, r.lsem.at[i])
        cp.start()
        return cp

    wide = lambda at, size: pl.ds(pl.multiple_of(at, 128), size)
    mats = (r.w_query, r.w_key, r.w_value, r.w_output)
    whole = {"S": r.SM, "A": r.WA, "U": r.WU, "C": r.WC}
    index = {"S": 0, "A": 1, "U": 2, "C": 3, "H": 4}

    def tiers(n, at):
        return r.WCX.at[at] if n == "H" else whole[n].at[b, at]

    def cuts(n, q):
        if n == "S":
            return [(r.SM.at[b, t], r.SM.at[b, t])]
        if n == "A":
            return [(w.at[:, wide(Cw * q, Cw)], r.WA.at[b, t, :, i * Cw : (i + 1) * Cw]) for i, w in enumerate(mats)]
        if n == "U":
            return [
                (r.w_up.at[:, wide((4 * i + q) * rd, rd)], r.WU.at[b, t, :, i * rd : (i + 1) * rd]) for i in range(nb)
            ]
        half, to = (y, r.WC.at[b]) if n == "C" else (1 - y, r.WCX)
        return [
            (r.w_conv.at[i, :, wide(Cw * q + Hw * half, Hw)], to.at[t, :, i * Hw : (i + 1) * Hw]) for i in range(3)
        ]

    def tier_own(n):
        for src, dst in cuts(n, t):
            here(src, dst, index[n])

    def tier_start(n):
        i = index[n]
        for d in (1, 2, 3):
            for src, dst in cuts(n, t ^ d):
                remote(src, dst, r.ts.at[i], r.tr.at[i], (b, t ^ d)).start()
        left_all(tiers(n, slice(0, 3)), r.ts.at[i])

    def tier_wait(n):
        i = index[n]
        if n != "S":
            got(tiers(n, t), r.lsem.at[i])
        got(tiers(n, slice(0, 3)), r.tr.at[i])

    def if_(cond, body):
        pl.when(cond)(body)

    def at_ends(body):
        return lambda: if_(ends, body)

    def inside(body):
        return lambda: if_(~ends, body)

    def both(*bodies):
        def run():
            for body in bodies:
                body()

        return run

    right, left = (2 * z + 2 + y, t), (2 * z - 2 + y, t)
    parts = {"S": [(r.SM, 0, t, 1, 0)], "C": [(r.WC, 1, 0, 4, 1)], "X": [(r.WC, 2, 0, 4, 2)]}
    for i, (n, w) in enumerate((("A", r.WA), ("U", r.WU))):
        parts[n] = [(w, 3 + 2 * i + h, h * 2, 2, 3 + i) for h in (0, 1)]
    first = rd // 4
    rest = (rd - first) // 2
    parts["D"] = [(r.WD, 7, 0, first, 5)]
    for i, n in enumerate("EF"):
        parts[n] = [(r.WD, 8 + 2 * i + h, first + h * rest, rest, 6 + i) for h in (0, 1)]

    def chunk_of(n, part, zz, col=None):
        w, k, at, size, _ = part
        col = ((1 - y) if n in "XF" else y) if col is None else col
        return w.at[2 * zz + col, pl.ds(at, size)]

    def chunks(n, count):
        w, _, at, size, _ = parts[n][0]
        return w.at[0:count, pl.ds(at, size * len(parts[n]))]

    def hop(part, at, zz, way):
        k = part[1]
        peer, past = (right, z < G - 1) if way == 0 else (left, z > 0)
        return past, remote(at, at, r.zs.at[part[4]], r.zr.at[k, zz - way], peer)

    def own_z(n):
        for part in parts[n]:
            for way in (0, 1):
                past, cp = hop(part, chunk_of(n, part, z), z, way)
                if_(past, cp.start)

    def own_y(n):
        for part in parts[n]:
            at, k = chunk_of(n, part, z), part[4]
            remote(r.WCX if n == "C" else at, at, r.ys.at[k], r.yr.at[k], ypeer).start()

    def arrivals(n, step, js):
        for j in js:
            for part in parts[n]:
                for way in (0, 1):
                    zz = z - j if way == 0 else z + j
                    step(part, j, way, zz, chunk_of(n, part, zz), zz >= 0 if way == 0 else zz < G)

    def onward(n, *js, cross=True):
        def step(part, j, way, zz, at, there):
            k = part[1]

            def body():
                got(at, r.zr.at[k, zz - way])
                if j < G - 1:
                    past, cp = hop(part, at, zz, way)
                    if_(past, cp.start)
                if n not in "CXEF" and cross:
                    remote(at, at, r.ys.at[part[4]], r.yr.at[part[4]], ypeer).start()

            if_(there, body)

        arrivals(n, step, js or range(1, G))

    def over(n, *js):
        def step(part, j, way, zz, at, there):
            if_(there, remote(at, at, r.ys.at[part[4]], r.yr.at[part[4]], ypeer).start)

        arrivals(n, step, js)

    def all_sent(n):
        k = parts[n][0][4]
        if_(ends, lambda: got(chunks(n, 1), r.zs.at[k]))
        if_(~ends, lambda: got(chunks(n, 5), r.zs.at[k]))
        if n not in "XF":
            got(chunks(n, 1 if n in "CE" else G), r.ys.at[k])

    def y_wait(n):
        got(chunks(n, 1 if n in "CE" else G), r.yr.at[parts[n][0][4]])

    def small_start():
        r.SM[b, t] = jnp.zeros((8, 128), f32)
        for q, v in enumerate((r.gain, r.bias, r.bdown, r.bconv, r.bup)):
            r.SM[b, t, q : q + 1, : v.shape[1]] = v[...].astype(f32)

    def small_spread():
        for d in (1, 2, 3):
            remote(r.SM.at[:, t], r.SM.at[:, t], r.ts.at[0], r.tr.at[0], (b, t ^ d)).start()
        left_all(r.SM.at[:, 0:3], r.ts.at[0])

    def small_come():
        got(r.SM.at[:, 0:3], r.tr.at[0])

    def memory_rows():
        W = R // 3
        to, frm = (lax.broadcasted_iota(jnp.int32, (R, R), axis) for axis in (0, 1))
        tap = (to >= W).astype(jnp.int32) + (to >= 2 * W).astype(jnp.int32)
        order = (frm == 3 * (to - W * tap) + tap).astype(bf16)
        for s in range(S):
            rows = jnp.dot(order, r.MEMV[s], preferred_element_type=f32).astype(bf16)
            for i in range(3):
                r.CTX[s, 4 * nu + 4 * i + t] = rows[W * i : W * (i + 1)]
            square = lambda axis: lax.broadcasted_iota(jnp.int32, (R // 3, R // 3), axis)
            line = jnp.broadcast_to(r.mask[s : s + 1].astype(f32), (R // 3, R // 3))
            col = jnp.sum(jnp.where(square(0) == square(1), line, 0.0), axis=1, keepdims=True)
            spot = lax.broadcasted_iota(jnp.int32, (R // 3, 128), 0) + (R // 3) * t
            lane = lax.broadcasted_iota(jnp.int32, (R // 3, 128), 1)
            r.MK[s, t] = jnp.where((lane < 64) | (3 * spot + 3 <= r.evicted[s]), col, 0.0)

    def rows_of(src, buf, first):
        at = lambda q: buf.at[:, pl.ds(first + nu * q, nu)]
        parts = [(src.at[:, 16 * i : 16 * i + 16], buf.at[:, first + nu * t + i]) for i in range(nu)]
        return parts, at, True

    def held(at):
        return [(at(t), at(t))], at, False

    def memory_y():
        for i in range(3):
            remote(r.CTX.at[:, 4 * nu + 4 * i + t], r.MEMX.at[:, 4 * i + t], r.ms.at[0], r.ms.at[1], ypeer).start()
        remote(r.MK.at[:, t], r.MKX.at[:, t], r.ms.at[2], r.ms.at[3], ypeer).start()
        left_all(r.MEMX.at[:, 0:3], r.ms.at[0])
        left_all(r.MKX.at[:, 0], r.ms.at[2])

    def memory_come():
        got(r.MEMX.at[:, 0:3], r.ms.at[1])
        got(r.MKX.at[:, 0], r.ms.at[3])

    pieces = [
        rows_of(r.seg, r.CTX, 8 * nu),
        rows_of(r.comp, r.CTX, 0),
        held(lambda q: r.CTX.at[:, 4 * nu + q]),
        held(lambda q: r.CTX.at[:, 4 * nu + 4 + q]),
        held(lambda q: r.CTX.at[:, 4 * nu + 8 + q]),
        rows_of(r.cot, r.COT, 0),
        held(lambda q: r.MK.at[:, q]),
        held(lambda q: r.MEMX.at[:, q]),
        held(lambda q: r.MEMX.at[:, 4 + q]),
        held(lambda q: r.MEMX.at[:, 8 + q]),
        held(lambda q: r.MKX.at[:, q]),
    ]

    group = lambda i: 0 if i < 5 else (1, 2, 3, 3, 3, 4)[i - 5]
    grouped = [(r.CTX, 3 * nu), (r.COT, nu), (r.MK, 1), (r.MEMX, 3), (r.MKX, 1)]

    def act_own():
        for i, (cut, at, far) in enumerate(pieces):
            if far:
                for src, dst in cut:
                    here(src, dst, 5 + group(i))

    def act_start(*which):
        for i in which:
            cut, at, far = pieces[i]
            g = group(i)
            for src, dst in cut:
                remote(src, dst, r.acs.at[g], r.acc.at[g], (b, t ^ 1)).start()
                remote(src, dst, r.acs.at[g], r.acx.at[i], (b, t ^ 2)).start()

    def act_forward(*which):
        for i in which:
            at = pieces[i][1](t ^ 2)
            got(at, r.acx.at[i])
            remote(at, at, r.acs.at[group(i)], r.acf.at[group(i)], (b, t ^ 1)).start()

    def act_wait(g):
        buf, n = grouped[g]
        got(buf.at[:, 0:n], r.acc.at[g])
        got(buf.at[:, 0:n], r.acf.at[g])
        if g < 2:
            got(buf.at[:, 0 : n if g else 2 * nu], r.lsem.at[5 + g])

    def act_sent():
        for g, (buf, n) in enumerate(grouped):
            got(buf.at[:, 0 : 3 * n], r.acs.at[g])

    def table():
        row = lax.broadcasted_iota(jnp.int32, (L, C3), 0) + 2 * L
        col = lax.broadcasted_iota(jnp.int32, (L, C3), 1)
        inner = col - L
        k1 = (inner >= nw).astype(jnp.int32)
        k2 = (inner >= 2 * nw).astype(jnp.int32)
        win = inner - nw * (k1 + k2)
        pos = jnp.where((col >= L) & (col < 2 * L), L + 3 * win + k1 + k2, col)
        r.DIST[...] = jnp.where(pos <= row, (row - pos).astype(f32) * (1.0 / C3), 1e30)
        r.SMG[...] = jnp.zeros_like(r.SMG)

    def seg_rows(s):
        return r.CTX[s, 8 * nu : 12 * nu].reshape(L, M)

    def project(s):
        rows = r.CTX[s].reshape(C3, M)
        kv = jnp.dot(rows, r.WA[:, :, :, Cw : 3 * Cw].reshape(M, 2 * Cw), preferred_element_type=f32)
        r.KV[s] = kv.astype(bf16)
        q = jnp.dot(seg_rows(s), r.WA[:, :, :, :Cw].reshape(M, Cw), preferred_element_type=f32)
        r.Q[s] = q.astype(bf16)


    def attend(s):
        for h in range(ht):
            c = slice(h * hd, (h + 1) * hd)
            raw = dot_nt(r.Q[s, :, c], r.KV[s, :, c])
            scores = raw * scale - r.slopes[t * ht + h] * r.DIST[...]
            e = jnp.exp(scores - jnp.max(scores, axis=1, keepdims=True))
            p = e * (1.0 / jnp.sum(e, axis=1, keepdims=True))
            r.PR[s, h] = p
            v = r.KV[s, :, Cw + h * hd : Cw + (h + 1) * hd]
            r.MIX[t, s, :, c] = jnp.dot(p.astype(bf16), v, preferred_element_type=f32).astype(bf16)
        spread_send(0, s, r.MIX)


    def wo(q):
        return r.WA[bq * q : bq * (q + 1), :, :, 3 * Cw :].reshape(Cw, Cw)

    def residual(s):
        spread_wait(0, s, r.MIX)
        acc = r.CTX[s, 8 * nu : 12 * nu, :, tc].reshape(L, Cw).astype(f32)
        for q in range(4):
            acc = acc + jnp.dot(r.MIX[q, s], wo(q), preferred_element_type=f32)
        r.RT[s] = acc
        r.RES[t, s] = acc.astype(bf16)
        spread_send(1, s, r.RES)

    def vectors():
        lane = lax.broadcasted_iota(jnp.int32, (8, 128), 1)
        for at in range(0, M, 128):
            block = jnp.zeros((8, 128), f32)
            for i in range(128 // rs):
                spot = at // rs + i
                turned = pltpu.roll(r.SM[spot // 4, spot % 4], rs * i, 1)
                block = jnp.where((lane >= rs * i) & (lane < rs * (i + 1)), turned, block)
            r.VV[0:4, at : at + 128] = block[0:4]
        for bb in range(nb):
            r.VV[4:5, bb * rd : (bb + 1) * rd] = r.SM[bb, t, 4:5, :rd]

    def xhat_of(s, q):
        return (r.RES[q, s].astype(f32) - r.MU[s, :, :1]) * r.MU[s, :, 1:2]

    def feed(s):
        spread_wait(1, s, r.RES)
        parts = [r.RES[q, s].astype(f32) for q in range(4)]
        mu = sum(jnp.sum(x, axis=1, keepdims=True) for x in parts) * (1.0 / M)
        var = sum(jnp.sum((x - mu) * (x - mu), axis=1, keepdims=True) for x in parts) * (1.0 / M)
        inv = lax.rsqrt(var + norm_eps)
        lane = lax.broadcasted_iota(jnp.int32, (L, 128), 1)
        r.MU[s] = jnp.where(lane == 0, mu, inv)
        for q in range(4):
            c = slice(q * Cw, (q + 1) * Cw)
            rows = ((parts[q] - mu) * inv) * r.VV[0:1, c] + r.VV[1:2, c]
            r.NRM[s, :, :, c] = rows.astype(bf16).reshape(4 * nu, 16, Cw)
        fb = Fw // 4
        for j in range(4):
            c = slice(j * fb, (j + 1) * fb)
            pre = jnp.dot(r.NRM[s].reshape(L, M), r.WU[:, :, :, c].reshape(M, fb), preferred_element_type=f32) + r.VV[4:5, c]
            phi = 0.5 + 0.5 * lax.erf(pre * math.sqrt(0.5))
            r.ACT[s, :, c] = (pre * phi).astype(bf16)
            r.GP[s, :, c] = (phi + pre * (jnp.exp(-0.5 * pre * pre) * (1.0 / math.sqrt(2 * math.pi)))).astype(bf16)


    def turn(j):
        low = lax.rem(G - j, G)
        inner = jnp.where(z == 1, low, G - 1 - low)
        return jnp.where(z == 0, G - 1 - j, jnp.where(z == G - 1, j, inner))

    grads = {0: (r.GD, r.YD, r.ZD), 1: (r.GU, r.YU, r.ZU), 2: (r.GA, r.YO, r.ZO), 3: (r.WU, r.YA, r.ZA)}

    def block(k, b_):
        g = grads[k][0]
        if k == 0:
            return g.at[b_, 0:nd]
        if k == 1:
            return g.at[b_]
        return g.at[b_, :, :, 3 * Cw :] if k == 2 else g.at[b_, :, :, : 3 * Cw]

    def to_y(k, zz):
        g, yb, zb = grads[k]
        remote(block(k, 2 * zz + (1 - y)), yb.at[zz], r.gys.at[k], r.gyr.at[k, zz], ypeer).start()

    def plus(into, *others):
        def add(i):
            acc = into[i].astype(f32)
            for o in others:
                acc = acc + o[i].astype(f32)
            into[i] = acc.astype(bf16)

        each(into.shape[0], add)

    def pass_on(i, at, zb, o, sem):
        @pl.when((o != mate) & ~ends)
        def _():
            slot = lax.rem(o, 2)
            got(zb.at[slot], r.gzr.at[sem, slot])
            plus(at, zb.at[slot])

        to = jnp.where(ends, mate, o)
        slot = jnp.where(o == mate, 2, jnp.where(ends, lax.rem(o, 2), 3))
        remote(at, zb.at[slot], r.gzs.at[sem], r.gzr.at[sem, jnp.minimum(slot, 2)], (2 * to + y, t)).start()

    def mid(k, *steps):
        g, yb, zb = grads[k]
        for i in steps or range(G - 1):
            o = turn(i)
            at = yb.at[o]
            got(at, r.gyr.at[k, o])
            plus(at, block(k, 2 * o + y))
            pass_on(i, at, zb, o, k)

    def part_c(b_):
        return r.GC.at[b_]

    def part_e(b_):
        return r.GD.at[b_, nd:4]

    def along(part, zb, sem, steps):
        for i in steps or range(G - 1):
            o = turn(i)
            for c, col in enumerate((1 - y, y)):
                pass_on(i, part(2 * o + col), zb.at[c], o, sem + c)

    def mid_c(*steps):
        along(part_c, r.ZC, 4, steps)

    def mid_e(*steps):
        along(part_e, r.ZE, 6, steps)

    def arrived(zb, sem):
        got(zb.at[2:4], r.gzr.at[sem, 2])
        return [zb.at[2], zb.at[3]]

    def summed(at, more, store):
        def total(i):
            acc = at[i].astype(f32)
            for o in more:
                acc = acc + o[i].astype(f32)
            store(i, acc)

        each(at.shape[0], total)

    def fin(k, store):
        g, yb, zb = grads[k]
        at = yb.at[z]
        got(at, r.gyr.at[k, z])
        summed(at, arrived(zb, k) + [block(k, 2 * z + y)], store)

    def cross(part, zb, sem, to, i):
        other = part(2 * z + 1 - y)

        def store(j, acc):
            other[j] = acc.astype(bf16)

        summed(other, arrived(zb.at[0], sem), store)
        remote(other, to, r.gys.at[i], r.gyr.at[i, 0], ypeer).start()

    def cross_c():
        cross(part_c, r.ZC, 4, r.YC, 4)

    def cross_e():
        cross(part_e, r.ZE, 6, r.YE, 5)

    def fin_e():
        got(r.YE, r.gyr.at[5, 0])

        def store(j, acc):
            r.OD[pl.ds((nd + j) * (rd // 4), rd // 4)] = acc

        summed(part_e(2 * z + y), arrived(r.ZE.at[1], 7) + [r.YE], store)

    def fin_c(store):
        summed(r.GC.at[2 * z + y], arrived(r.ZC.at[1], 5), store)

    def crossed_c():
        got(r.YC, r.gyr.at[4, 0])

    def reduced_sent():
        for k, (g, yb, zb) in grads.items():
            got(block(k, slice(0, G)), r.gys.at[k])
            got(block(k, slice(0, 3)), r.gzs.at[k])
        got(r.YC, r.gys.at[4])
        got(r.YE, r.gys.at[5])
        for sem in (4, 5):
            got(r.GC.at[0:3], r.gzs.at[sem])
            got(r.GD.at[0:3, nd:4], r.gzs.at[sem + 2])

    fb = Fw // 4

    def grad_down(i):
        j = turn(i)
        c = pl.ds(pl.multiple_of(j * fb, fb), fb)
        rows = r.ACT[:, :, c].reshape(S * L, fb)
        g = dot_tn(rows, r.COT[...].reshape(S * L, M)).astype(bf16)
        r.GD[pl.ds(j * bq, bq)] = g.reshape(bq, 4, rd // 4, M)
        to_y(0, j)


    def back_feed(s):
        cot = r.COT[s].reshape(L, M)
        for j in range(4):
            c = slice(j * fb, (j + 1) * fb)
            wd = r.WD[bq * j : bq * (j + 1)].reshape(fb, M)
            d_act = dot_nt(cot, wd).astype(bf16).astype(f32)
            d_pre = d_act * r.GP[s, :, c].astype(f32)
            total = jnp.sum(d_pre, axis=0, keepdims=True)
            for i in range(fb // 128):
                at = j * (fb // 128) + i
                r.SMG[at : at + 1] += total[:, 128 * i : 128 * (i + 1)]
            r.GP[s, :, c] = d_pre.astype(bf16)
        m1 = jnp.zeros((L, 1), f32)
        m2 = jnp.zeros((L, 1), f32)
        for q in range(4):
            c = slice(q * Cw, (q + 1) * Cw)
            dn = dot_nt(r.GP[s], r.WU[bq * q : bq * (q + 1)].reshape(Cw, Fw))
            g = dn * r.VV[0:1, c]
            m1 = m1 + jnp.sum(g, axis=1, keepdims=True)
            m2 = m2 + jnp.sum(g * xhat_of(s, q), axis=1, keepdims=True)
            r.DNP[q, s] = dn.astype(bf16)
        lane = lax.broadcasted_iota(jnp.int32, (L, 128), 1)
        both = jnp.where(lane == 0, m1, jnp.where(lane == 1, m2, 0.0)) * (1.0 / M)
        pick = (
            lax.broadcasted_iota(jnp.int32, (8, 128), 0) == lax.broadcasted_iota(jnp.int32, (8, 128), 1)
        ).astype(f32)
        r.ST[t, s] = lax.dot_general(
            pick, both, (((1,), (1,)), ((), ())), precision=lax.Precision.HIGHEST, preferred_element_type=f32
        )
        fold_send(2, s)
        ex_send(3, r.er.at[3, s, 0], lambda q: r.ST.at[t, s], lambda d: r.ST.at[t, s])
        fold_late(2, s)


    def grad_up(i):
        j = turn(i)
        c = pl.ds(pl.multiple_of(j * Cw, Cw), Cw)
        rows = r.NRM[:, :, :, c].reshape(S * L, Cw)
        g = dot_tn(rows, r.GP[...].reshape(S * L, Fw)).astype(bf16)
        r.GU[pl.ds(j * bq, bq)] = g.reshape(bq, 4, rw, Fw)
        to_y(1, j)


    def back_norm(s):
        dn = folded(2, s)
        got(r.ST.at[0:3, s], r.er.at[3, s, 0])
        st = r.ST[0, s] + r.ST[1, s] + r.ST[2, s] + r.ST[3, s]
        side = lax.broadcasted_iota(jnp.int32, (8, 128), 0)
        col_of = lambda i: lax.dot_general(
            st,
            (side == i).astype(f32),
            (((0,), (0,)), ((), ())),
            precision=lax.Precision.HIGHEST,
            preferred_element_type=f32,
        )[:, :1]
        m1, m2 = col_of(0), col_of(1)
        inv = r.MU[s, :, 1:2]
        xhat = (r.RES[t, s].astype(f32) - r.MU[s, :, :1]) * inv
        cot = r.COT[s, :, :, tc].reshape(L, Cw).astype(f32)
        for i, v in enumerate((cot, dn * xhat, dn)):
            total = jnp.sum(v, axis=0, keepdims=True)
            for k in range(Cw // 128):
                at = Fw // 128 + i * (Cw // 128) + k
                r.SMG[at : at + 1] += total[:, 128 * k : 128 * (k + 1)]
        d_resid = cot + (dn * r.VV[0:1, tc] - m1 - xhat * m2) * inv
        r.DR[s] = d_resid
        db = d_resid.astype(bf16)
        r.DB[s] = db
        for q in range(4):
            r.DMP[q, s] = dot_nt(db, wo(q)).astype(bf16)
        fold_send(4, s)
        fold_late(4, s)

    def grad_out():
        for q in range(4):
            g = dot_tn(r.MIX[q].reshape(S * L, Cw), r.DB[...].reshape(S * L, Cw))
            r.GA[bq * q : bq * (q + 1), :, :, 3 * Cw :] = g.astype(bf16).reshape(bq, 4, rw, Cw)
        each(G, lambda i: to_y(2, turn(i)))

    def by_tier(rows, c, sent, come):
        for d in (1, 2, 3):
            remote(r.GA.at[rows, t ^ d, :, c], r.WU.at[rows, t, :, c], sent, come, (b, t ^ d)).start()
        r.WU[rows, t, :, c] = r.GA[rows, t, :, c]

    def out_rows(s):
        for q in range(4):
            c = slice(q * Cw, (q + 1) * Cw)
            o = jnp.dot(r.ACT[s], r.WD[:, :, c].reshape(Fw, Cw), preferred_element_type=f32)
            mine = (t == q).astype(f32)
            o = o + mine * (r.RT[s] + r.VV[2:3, c])
            r.OP[s, :, :, c] = o.astype(bf16).reshape(4 * nu, 16, Cw)
        fold_send(5, s)


    hc = wide(t * Cw + Hw * y, Hw)

    def windows(k, g):
        buf, at = (r.MEMX, 4 * k) if g else (r.CTX, 4 * nu + 4 * k)
        return buf.at[:, at : at + 4]

    def compress():
        sums = jnp.zeros((1, Hw), f32)
        for g in (0, 1):
            conv = r.VV[3:4, hc]
            pooled = 0.0
            for k in range(3):
                wk = r.WC[:, :, :, k * Hw : (k + 1) * Hw].reshape(M, Hw)
                conv = conv + jnp.dot(windows(k, g)[...].reshape(S * nw, M), wk, preferred_element_type=f32)
                pooled = pooled + windows(k, g)[:, :, :, hc].reshape(S * nw, Hw).astype(f32)
            marks = (r.MKX if g else r.MK)[...].reshape(S * nw, 128)
            fresh = (marks[:, :1] * conv).astype(bf16).reshape(S, nw, Hw)
            if g:
                r.NEWX[...] = fresh
            else:
                r.NEW[t, :, :, wide(Hw * y, Hw)] = fresh
            d_conv = marks[:, 64:65] * (conv - pooled * (1.0 / 3.0))
            sums = sums + jnp.sum(d_conv, axis=0, keepdims=True)
            r.DC[g] = d_conv.astype(bf16)
        r.SMG[pl.ds(Fw // 128 + 3 * (Cw // 128) + y, 1)] = sums
        remote(r.NEWX, r.NEW.at[t, :, :, wide(Hw * y, Hw)], r.ns.at[2], r.ns.at[3], ypeer).start()
        left_all(r.NEWX, r.ns.at[2])
        for k in range(3):
            grad = sum(dot_tn(windows(k, g)[...].reshape(S * nw, M), r.DC[g]) for g in (0, 1))
            r.GC[:, :, :, k * Hw : (k + 1) * Hw] = grad.astype(bf16).reshape(nb, 4, rw, Hw)

    slope_row = Fw // 128 + 4 * (Cw // 128)

    def back_attend(s):
        dm = folded(4, s).astype(bf16)
        lane = lax.broadcasted_iota(jnp.int32, (1, 128), 1)
        for h in range(ht):
            c = slice(h * hd, (h + 1) * hd)
            cv = slice(Cw + h * hd, Cw + (h + 1) * hd)
            p = r.PR[s, h]
            dp = dot_nt(dm[:, c], r.KV[s, :, cv])
            delta = jnp.sum(p * dp, axis=1, keepdims=True)
            ds = p * (dp - delta)
            part = jnp.sum(jnp.sum(ds * r.DIST[...], axis=0, keepdims=True), axis=1, keepdims=True)
            r.SMG[slope_row : slope_row + 1] -= jnp.where(lane == t * ht + h, part, 0.0)
            dr = (ds * scale).astype(bf16)
            dq = jnp.dot(dr, r.KV[s, :, c], preferred_element_type=f32).astype(bf16)
            dk = dot_tn(dr, r.Q[s, :, c]).astype(bf16)
            dv = dot_tn(p.astype(bf16), dm[:, c]).astype(bf16)
            r.Q[s, :, c] = dq
            r.KV[s, :, c] = dk
            r.KV[s, :, cv] = dv


    def grad_proj(i):
        j = turn(i)
        c = pl.ds(pl.multiple_of(j * Cw, Cw), Cw)
        gq = jnp.zeros((Cw, Cw), f32)
        gkv = jnp.zeros((Cw, 2 * Cw), f32)
        for s in range(S):
            gq = gq + dot_tn(r.CTX[s, 8 * nu : 12 * nu, :, c].reshape(L, Cw), r.Q[s])
            gkv = gkv + dot_tn(r.CTX[s, :, :, c].reshape(C3, Cw), r.KV[s])
        rows = pl.ds(j * bq, bq)
        r.GA[rows, :, :, :Cw] = gq.astype(bf16).reshape(bq, 4, rw, Cw)
        r.GA[rows, :, :, Cw : 3 * Cw] = gkv.astype(bf16).reshape(bq, 4, rw, 2 * Cw)
        by_tier(rows, slice(0, 3 * Cw), r.xs.at[0], r.xr.at[j])

    def proj_y(*steps):
        for i in steps:
            j = turn(i)
            got(r.WU.at[pl.ds(j * bq, bq), 0:3, :, : 3 * Cw], r.xr.at[j])
            to_y(3, j)

    def own_out(s):
        r.OR[1, s] = folded(5, s).astype(bf16)

    def input_rows(s):
        x = jnp.concatenate([r.Q[s], r.KV[s, 2 * L :]], axis=1)
        for q in range(4):
            c = slice(q * Cw, (q + 1) * Cw)
            w = r.WA[bq * q : bq * (q + 1), :, :, : 3 * Cw].reshape(Cw, 3 * Cw)
            o = dot_nt(x, w) + (t == q).astype(f32) * r.DR[s]
            r.NRM[s, :, :, c] = o.astype(bf16).reshape(4 * nu, 16, Cw)
        fold_send(6, s)
        fold_late(6, s)


    def keep(o):
        def store(i, acc):
            o[pl.ds(i * (rd // 4), rd // 4)] = acc

        return store

    def across(q, acc):
        for i in range(3):
            r.OA[i, :, wide(q * Cw, Cw)] = acc[:, i * Cw : (i + 1) * Cw]

    def hold(m):
        def store(i, acc):
            m[i] = acc.astype(bf16)

        return store

    def tier_back(k, m, tb):
        for d in (1, 2, 3):
            remote(m.at[t ^ d], tb.at[t], r.gts.at[k], r.gtr.at[k], (b, t ^ d)).start()
        left_all(tb.at[0:3], r.gts.at[k])

    def small_y():
        remote(r.SMG, r.YS, r.ss.at[0], r.sr.at[0], ypeer).start()
        left_all(r.SMG, r.ss.at[0])

    def small_z():
        got(r.YS, r.sr.at[0])
        r.ZS[z] = r.SMG[...] + r.YS[...]
        for d in range(1, G):
            remote(r.ZS.at[z], r.ZS.at[z], r.ss.at[1], r.sr.at[1], (2 * zs[d] + y, t)).start()
        left_all(r.ZS.at[0 : G - 1], r.ss.at[1])

    def small_tier():
        got(r.ZS.at[0 : G - 1], r.sr.at[1])
        acc = r.ZS[0]
        for zz in range(1, G):
            acc = acc + r.ZS[zz]
        r.OS[t] = acc
        for d in (1, 2, 3):
            remote(r.OS.at[t], r.OS.at[t], r.gts.at[3], r.gtr.at[3], (b, t ^ d)).start()
        left_all(r.OS.at[0:3], r.gts.at[3])

    def own_input(s):
        r.IG[s] = folded(6, s)

    mineU, mineC, mineO = r.GU.at[2 * z + y], r.GC.at[2 * z + y], r.GA.at[2 * z + y, :, :, 3 * Cw :]
    def give(i, src, dst):
        pltpu.make_async_copy(src, dst, r.osem.at[i]).start()

    def rows_out(i, src, dst):
        for j in range(nu):
            give(i, src.at[:, j], dst.at[:, 16 * j : 16 * j + 16])

    backs = {0: (mineU, r.TU), 1: (mineC, r.TC), 2: (mineO, r.TO), 4: (r.YC, r.TB)}

    def lay(k, q, rows):
        if k == 0:
            for i in range(nb):
                r.OU[:, wide((4 * i + q) * rd, rd)] = rows[:, i * rd : (i + 1) * rd].astype(f32)
        elif k == 2:
            r.OA[3, :, wide(q * Cw, Cw)] = rows.astype(f32)
        else:
            half = y if k == 1 else 1 - y
            for i in range(3):
                r.OC[i, :, wide(q * Cw + Hw * half, Hw)] = rows[:, i * Hw : (i + 1) * Hw].astype(f32)

    def tier_out(k):
        m, tb = backs[k]
        lay(k, t, m[t])
        got(tb.at[0:3], r.gtr.at[k])
        for d in (1, 2, 3):
            lay(k, t ^ d, tb[t ^ d])

    def given():
        for i, (src, dst) in ((0, (r.OU, r.ou)), (1, (r.OC, r.oc)), (2, (r.OA, r.oa)), (3, (r.OD, r.od)), (7, (r.OS, r.os))):
            pltpu.make_async_copy(src, dst, r.osem.at[i]).wait()
        for i, (src, dst) in ((5, (r.OR.at[1], r.out)), (6, (r.IG, r.ig)), (4, (r.OR.at[0], r.om)), (8, (r.OR.at[2], r.ocm))):
            for j in range(nu):
                pltpu.make_async_copy(src.at[:, j], dst.at[:, 16 * j : 16 * j + 16], r.osem.at[i]).wait()

    def small_out():
        got(r.OS.at[0:3], r.gtr.at[3])
        give(7, r.OS, r.os)

    slots = L - nw
    windows_of = [(q, max(R * q - slots, 0), R - max(slots - R * q, 0)) for q in range(4) if slots < R * (q + 1)]

    def new_send():
        got(r.NEWX, r.ns.at[3])
        for q, at, n in windows_of:
            part = r.NEW.at[t, :, at : at + n]
            if_(t != q, remote(part, part, r.ns.at[0], r.ns.at[1], (b, q)).start)

    def new_sent():
        for q, at, n in windows_of:
            if_(t != q, lambda: got(r.NEW.at[0, :, at : at + n], r.ns.at[0]))

    def new_out():
        for q, at, n in windows_of:
            if_(t == q, lambda: got(r.NEW.at[0:3, :, at : at + n], r.ns.at[1]))

    def memories():
        side = lax.broadcasted_iota(jnp.int32, (16, 1), 0)
        for s in range(S):
            for i in range(nu):
                fresh = side + (R * t + 16 * i) < r.evicted[s]
                r.OR[0, s, i] = jnp.where(fresh, r.CTX[s, 8 * nu + nu * t + i], r.MEMV[s, 16 * i : 16 * i + 16])
                r.OR[2, s, i] = r.CTX[s, nu * t + i]
        for q, at, n in windows_of:

            @pl.when(t == q)
            def _(at=at, n=n):
                for i in range((R - n) // 16, nu):
                    w = at + 16 * i - (R - n)
                    for s in range(S):
                        written = 3 * (side + w) + 3 <= r.evicted[s]
                        for p in range(4):
                            c = slice(p * Cw, (p + 1) * Cw)
                            old = r.CTX[s, nu * t + i, :, c]
                            r.OR[2, s, i, :, c] = jnp.where(written, r.NEW[p, s, w : w + 16], old)

    def drain():
        for n in parts:
            if n != "U":
                all_sent(n)
        got(r.GA.at[:, 0:3, :, : 3 * Cw], r.xs.at[0])
        for ref, sem in sends:
            got(ref, sem)
        act_sent()
        new_sent()
        for e, ref in enumerate((r.MIX, r.RES, r.DNP, r.ST, r.DMP, r.OR, r.IR)):
            got(ref.at[0:3], r.es.at[e])

    here(r.wd, r.WD.at[b], 0)
    here(r.mem, r.MEMV, 7)
    for n in "ACHU":
        tier_own(n)
    act_own()
    greet(G, True, True)
    tier_start("A")
    tier_start("H")
    small_start()
    tier_start("U")
    act_start(0, 1)
    got(r.WD.at[b], r.lsem.at[0])
    own_z("D")
    own_z("E")
    own_y("E")
    own_y("D")
    got(r.MEMV, r.lsem.at[7])
    memory_rows()
    act_start(2, 3, 4)
    tier_start("C")
    act_start(5, 6)
    tier_wait("A")
    own_z("A")
    own_y("A")
    tier_wait("H")
    own_y("C")
    own_z("S")
    own_y("S")
    table()
    onward("A", 1)
    onward("S", 1)
    onward("A", 2)
    onward("S", 2)
    tier_wait("U")
    own_z("U")
    y_wait("E")
    own_z("F")
    onward("A", 3)
    own_y("U")
    onward("S", 3)
    onward("U", 1)
    act_forward(0, 1, 2, 3, 4)
    act_wait(0)
    y_wait("A")
    each(S, project, {0: inside(lambda: onward("U", 2)), 1: inside(lambda: onward("D", 1, cross=False))})
    at_ends(both(lambda: onward("U", 2), lambda: onward("D", 1, cross=False)))()
    inside(lambda: onward("E", 1))()
    inside(lambda: onward("F", 1))()
    tier_wait("C")
    y_wait("C")
    y_wait("S")
    small_spread()
    each(S, attend)
    onward("U", 3)
    memory_y()
    over("D", 1)
    onward("D", 2)
    own_z("C")
    own_z("X")
    spread_pass(0, 0, r.MIX)
    each(S, residual)
    inside(lambda: onward("E", 2))()
    inside(lambda: onward("F", 2))()
    small_come()
    vectors()
    act_forward(5, 6)
    onward("D", 3)
    y_wait("U")
    spread_pass(1, 0, r.RES)
    each(S, feed, {0: inside(lambda: onward("C", 1)), 1: inside(lambda: onward("E", 3)), 2: inside(lambda: onward("X", 1))})
    memory_come()
    act_start(7, 8, 9, 10)
    act_wait(1)
    act_wait(2)
    each(
        4,
        grad_down,
        {0: lambda: mid_e(0), 1: at_ends(lambda: mid_e(1)), 2: at_ends(lambda: mid_e(2))},
    )
    inside(lambda: onward("F", 3))()
    inside(lambda: onward("C", 2))()
    inside(lambda: onward("X", 2))()
    at_ends(both(lambda: onward("E"), lambda: onward("F")))()
    y_wait("D")
    all_sent("U")
    each(
        S,
        back_feed,
        {
            0: inside(lambda: onward("C", 3)),
            1: both(inside(lambda: mid_e(1)), lambda: mid(0, 0)),
            2: both(inside(lambda: onward("X", 3)), lambda: act_forward(7, 8, 9, 10)),
            3: at_ends(lambda: mid(0, 1)),
        },
    )
    fold_pass(2, S - 1)
    each(2, out_rows)
    each(4, grad_up)
    fold_pass(5, 0)
    fold_pass(5, 1)
    inside(both(lambda: mid_e(2), lambda: mid(0, 1)))()
    at_ends(lambda: mid(0, 2))()
    act_wait(3)
    act_wait(4)
    at_ends(both(lambda: onward("C"), lambda: onward("X")))()
    compress()
    inside(lambda: mid(0, 2))()
    mid_c(0)
    at_ends(lambda: mid_c(1))()
    each(S, back_norm)
    fold_pass(4, S - 1)
    grad_out()
    each(S - 2, lambda s: out_rows(s + 2))
    cross_e()
    inside(lambda: mid_c(1))()
    fold_pass(5, 2)
    fold_pass(5, 3)
    mid(1, 0)
    at_ends(lambda: mid_c(2))()
    each(S, back_attend)
    inside(lambda: mid_c(2))()
    small_y()
    each(4, grad_proj, {1: at_ends(lambda: mid(1, 1))})
    inside(lambda: mid(1, 1))()
    at_ends(lambda: mid(1, 2))()
    proj_y(0)
    each(S, input_rows)
    proj_y(1)
    cross_c()
    fold_pass(6, S - 1)
    at_ends(lambda: mid(2, 0, 1))()
    inside(lambda: mid(1, 2))()
    proj_y(2)
    at_ends(both(lambda: mid(2, 2), lambda: mid(3, 0)))()
    inside(lambda: mid(2, 0, 1, 2))()
    small_z()
    fin_c(hold(mineC))
    tier_back(1, mineC, r.TC)
    proj_y(3)
    new_send()
    inside(lambda: mid(3, 0))()
    fin(1, hold(mineU))
    tier_back(0, mineU, r.TU)
    mid(3, 1)
    crossed_c()
    tier_back(4, r.YC, r.TB)
    fin(0, keep(r.OD))
    fin_e()
    give(3, r.OD, r.od)
    fin(2, hold(mineO))
    tier_back(2, mineO, r.TO)
    mid(3, 2)
    small_tier()
    each(S, own_out)
    rows_out(5, r.OR.at[1], r.out)
    new_out()
    memories()
    rows_out(4, r.OR.at[0], r.om)
    rows_out(8, r.OR.at[2], r.ocm)
    each(S, own_input)
    rows_out(6, r.IG, r.ig)
    tier_out(1)
    tier_out(0)
    give(0, r.OU, r.ou)
    tier_out(4)
    tier_out(2)
    give(1, r.OC, r.oc)
    small_out()
    drain()
    fin(3, across)
    give(2, r.OA, r.oa)
    reduced_sent()
    given()

def whole_layer(nb, ht, hd, arrays):
    S, R, M = arrays["seg"].shape
    rw, rd, rs = arrays["w_query"].shape[0], arrays["wd"].shape[0], M // (4 * nb)
    nu = R // 16
    G, Cw, Fw, L = nb // 2, M // 4, nb * rd, 64 * nu
    dma = pltpu.SemaphoreType.DMA
    V = lambda shape, dtype=bf16: pltpu.VMEM(shape, dtype)
    nd = 3
    D4, A4, U4, C4 = (4, rd // 4, M), (4, rw, 4 * Cw), (4, rw, Fw), (4, rw, 3 * Cw // 2)
    ins = arrays
    outs = dict(
        out=((S, R, M), bf16),
        ig=((S, R, M), f32),
        om=((S, R, M), bf16),
        ocm=((S, R, M), bf16),
        od=((rd, M), f32),
        ou=((rw, 4 * Fw), f32),
        oc=((3, rw, M), f32),
        oa=((4, rw, M), f32),
        os=((4, 24, 128), f32),
    )
    scratch = dict(
        WA=V((nb,) + A4),
        WU=V((nb,) + U4),
        WC=V((nb,) + C4),
        WCX=V(C4),
        MEMX=V((S, 12, 16, M)),
        MKX=V((S, 4, L // 12, 128), f32),
        NEWX=V((S, L // 3, Cw // 2)),
        WD=V((nb, rd, M)),
        SM=V((nb, 4, 8, 128), f32),
        CTX=V((S, 12 * nu, 16, M)),
        COT=V((S, 4 * nu, 16, M)),
        MK=V((S, 4, L // 12, 128), f32),
        DIST=V((L, 3 * L), f32),
        VV=V((8, max(M, Fw)), f32),
        SMG=V((24, 128), f32),
        Q=V((S, L, Cw)),
        KV=V((S, 3 * L, 2 * Cw)),
        PR=V((S, ht, L, 3 * L), f32),
        MIX=V((4, S, L, Cw)),
        RT=V((S, L, Cw), f32),
        RES=V((4, S, L, Cw)),
        MU=V((S, L, 128), f32),
        NRM=V((S, 4 * nu, 16, M)),
        ACT=V((S, L, Fw)),
        GP=V((S, L, Fw)),
        DNP=V((4, S, L, Cw)),
        DNR=V((3, S, L, Cw)),
        ST=V((4, S, 8, L), f32),
        DR=V((S, L, Cw), f32),
        DB=V((S, L, Cw)),
        DMP=V((4, S, L, Cw)),
        DMR=V((3, S, L, Cw)),
        OP=V((S, 4 * nu, 16, M)),
        OR=V((3, S, nu, 16, M)),
        IR=V((3, S, nu, 16, M)),
        DC=V((2, S * L // 3, Cw // 2)),
        GD=V((nb,) + D4),
        GU=V((nb,) + U4),
        GC=V((nb,) + C4),
        GA=V((nb,) + A4),
        YD=V((G, nd) + D4[1:]),
        YE=V((4 - nd,) + D4[1:]),
        YU=V((G,) + U4),
        YC=V(C4),
        YO=V((G, 4, rw, Cw)),
        YA=V((G, 4, rw, 3 * Cw)),
        ZD=V((4, nd) + D4[1:]),
        ZE=V((2, 4, 4 - nd) + D4[1:]),
        ZU=V((4,) + U4),
        ZC=V((2, 4) + C4),
        ZO=V((4, 4, rw, Cw)),
        ZA=V((4, 4, rw, 3 * Cw)),
        YS=V((24, 128), f32),
        ZS=V((G, 24, 128), f32),
        TU=V(U4),
        TO=V((4, rw, Cw)),
        TC=V(C4),
        TB=V(C4),
        NEW=V((4, S, L // 3, Cw)),
        IG=V((S, nu, 16, M), f32),
        OD=V((rd, M), f32),
        OU=V((rw, 4 * Fw), f32),
        OC=V((3, rw, M), f32),
        OA=V((4, rw, M), f32),
        OS=V((4, 24, 128), f32),
        MEMV=V((S, R, M)),
        osem=dma((9,)),
        lsem=dma((8,)),
        ts=dma((5,)),
        tr=dma((5,)),
        zs=dma((8,)),
        zr=dma((12, G - 1)),
        ys=dma((8,)),
        yr=dma((8,)),
        ms=dma((4,)),
        acs=dma((5,)),
        acc=dma((5,)),
        acf=dma((5,)),
        acx=dma((11,)),
        es=dma((7,)),
        er=dma((7, S, 2)),
        ns=dma((4,)),
        gys=dma((6,)),
        gyr=dma((6, G)),
        gzs=dma((8,)),
        gzr=dma((8, 3)),
        ss=dma((2,)),
        sr=dma((2,)),
        xs=dma((1,)),
        xr=dma((G,)),
        gts=dma((5,)),
        gtr=dma((5,)),
    )
    names = list(ins) + list(outs) + list(scratch)
    near = dict(gain=VM, bias=VM, bdown=VM, bconv=VM, bup=VM, mask=VM, evicted=SM, slopes=SM)
    return pl.pallas_call(
        functools.partial(layer_kernel, names, (nb, nu, S, ht, hd, M, Cw, rw, rd, rs)),
        out_shape=[jax.ShapeDtypeStruct(s, d) for s, d in outs.values()],
        in_specs=[near.get(n, ANY) for n in ins],
        out_specs=[ANY] * len(outs),
        scratch_shapes=list(scratch.values()),
        compiler_params=pltpu.CompilerParams(
            collective_id=9, has_side_effects=True, vmem_limit_bytes=63 * 2**20
        ),
        name="whole_layer",
    )(*ins.values())


def finish_kernel(names, shape, *refs):
    r = Names(names, refs)
    nb, rs, rd, Fw, Cw, heads = shape
    b, t = lax.axis_index("batch"), lax.axis_index("tier")
    squares = (r.o_q, r.o_k, r.o_v, r.o_o)
    moves = [(r.out, r.o_out), (r.ig, r.o_ig), (r.od, r.o_od), (r.ou, r.o_ou), (r.oc, r.o_oc), (r.om, r.o_mem), (r.ocm, r.o_comp)]
    n = len(moves)
    bufs = refs[len(names) :]
    small = pltpu.make_async_copy(r.os, r.osv, r.sem.at[n])
    small.start()
    into = [pltpu.make_async_copy(src, buf, r.sem.at[i]) for i, ((src, _), buf) in enumerate(zip(moves, bufs))]
    into.append(pltpu.make_async_copy(r.oa, bufs[n], r.sem.at[n + 1]))
    onto = [
        [pltpu.make_async_copy(buf, dst, r.sem.at[n + 2 + i])] for i, ((_, dst), buf) in enumerate(zip(moves, bufs))
    ]
    onto.append([pltpu.make_async_copy(bufs[n].at[i], o, r.sem.at[2 * n + 2 + i]) for i, o in enumerate(squares)])
    for cp in into:
        cp.start()
    small.wait()
    spot = 4 * b + t
    block, inner = spot // (Cw // rs), lax.rem(spot, Cw // rs)
    half, group = inner // (128 // rs), lax.rem(inner, 128 // rs)
    for i in range(4):
        row = r.osv[block, pl.ds(Fw // 128 + (Cw // 128) * i + half, 1), :]
        turned = pltpu.roll(jnp.broadcast_to(row, (8, 128)), lax.rem(128 - rs * group, 128), 1)
        r.vecs[i : i + 1, :] = turned[0:1, :rs]
    r.ups[...] = r.osv[t, pl.ds(b, 1), :rd]
    at = Fw // 128 + 4 * (Cw // 128)
    total = r.osv[0, at : at + 1]
    for q in range(1, 4):
        total = total + r.osv[q, at : at + 1]
    r.slope[...] = total[:, :heads]
    lines = [(r.vecs.at[i : i + 1], o) for i, o in enumerate((r.o_down, r.o_gain, r.o_bias, r.o_conv))]
    lines += [(r.ups, r.o_up), (r.slope, r.o_slopes)]
    onto.append([pltpu.make_async_copy(src, dst, r.sem.at[2 * n + 6 + i]) for i, (src, dst) in enumerate(lines)])
    for c in onto[-1]:
        c.start()
    for cp, then in zip(into, onto):
        cp.wait()
        for c in then:
            c.start()
    for then in onto:
        for c in then:
            c.wait()


def finish(nb, heads, arrays):
    S, R, M = arrays["out"].shape
    rw, rd, rs = arrays["oa"].shape[1], arrays["od"].shape[0], M // (4 * nb)
    Cw, Fw = M // 4, nb * rd
    rows, mat, vec = (S, R, M), (rw, M), (1, rs)
    outs = dict(
        o_out=(rows, bf16, ANY),
        o_ig=(rows, f32, ANY),
        o_mem=(rows, bf16, ANY),
        o_comp=(rows, bf16, ANY),
        o_q=(mat, f32, ANY),
        o_k=(mat, f32, ANY),
        o_v=(mat, f32, ANY),
        o_o=(mat, f32, ANY),
        o_ou=((rw, 4 * Fw), f32, ANY),
        o_up=((1, rd), f32, ANY),
        o_od=((rd, M), f32, ANY),
        o_down=(vec, f32, ANY),
        o_gain=(vec, f32, ANY),
        o_bias=(vec, f32, ANY),
        o_oc=((3, rw, M), f32, ANY),
        o_conv=(vec, f32, ANY),
        o_slopes=((1, heads), f32, ANY),
    )
    moved = ("out", "ig", "od", "ou", "oc", "om", "ocm", "oa")
    n = len(moved) - 1
    return pl.pallas_call(
        functools.partial(
            finish_kernel, list(arrays) + list(outs) + ["sem", "osv", "vecs", "ups", "slope"], (nb, rs, rd, Fw, Cw, heads)
        ),
        out_shape=[jax.ShapeDtypeStruct(s, d) for s, d, _ in outs.values()],
        in_specs=[ANY] * len(arrays),
        out_specs=[o[2] for o in outs.values()],
        scratch_shapes=[
            pltpu.SemaphoreType.DMA((2 * n + 12,)),
            pltpu.VMEM(arrays["os"].shape, f32),
            pltpu.VMEM((4, rs), f32),
            pltpu.VMEM((1, rd), f32),
            pltpu.VMEM((1, heads), f32),
        ]
        + [pltpu.VMEM(arrays[i].shape, arrays[i].dtype) for i in moved],
        compiler_params=pltpu.CompilerParams(vmem_limit_bytes=63 * 2**20),
        name="finish",
    )(*arrays.values())


def per_device_fused(
    nb,
    segment,
    memory,
    compressed,
    evicted,
    window_mask,
    cotangent,
    w_query,
    w_key,
    w_value,
    w_output,
    w_up,
    b_up,
    w_down,
    b_down,
    ln_gain,
    ln_bias,
    w_conv,
    b_conv,
    slopes,
):
    S, R, M = segment.shape
    heads = slopes.shape[0]
    line = lambda v: v.reshape(1, -1)
    names = ("out", "ig", "om", "ocm", "od", "ou", "oc", "oa", "os")
    made = whole_layer(
        nb,
        heads // 4,
        M // heads,
        dict(
            w_query=w_query,
            w_key=w_key,
            w_value=w_value,
            w_output=w_output,
            w_up=w_up,
            w_conv=w_conv,
            wd=w_down,
            comp=compressed,
            seg=segment,
            cot=cotangent,
            mem=memory,
            gain=line(ln_gain),
            bias=line(ln_bias),
            bdown=line(b_down),
            bconv=line(b_conv),
            bup=line(b_up),
            mask=window_mask,
            evicted=evicted,
            slopes=slopes,
        ),
    )
    outs = finish(nb, heads, dict(zip(names, made)))
    flat = (9, 11, 12, 13, 15, 16)
    return tuple(o.reshape(-1) if i in flat else o for i, o in enumerate(outs))


def solution(mesh):
    both = ("batch", "tier")
    rows = P("batch", "tier", None)
    mat, vec = P(both, None), P(both)
    nb = mesh.shape["batch"]

    def body(*args):
        fused = args[6].shape[0] % 16 == 0 and args[12].shape[0] == 128
        return (per_device_fused if fused else per_device)(nb, *args)

    return jax.shard_map(
        body,
        mesh=mesh,
        in_specs=(
            (rows, rows, rows, P("batch"), P("batch", "tier"), rows)
            + (mat, mat, mat, mat, mat, vec, mat, vec, vec, vec)
            + (P(None, both, None), vec, P())
        ),
        out_specs=(
            (rows, rows, rows, rows, mat, mat, mat, mat, mat, vec, mat, vec, vec, vec)
            + (P(None, both, None), vec, P())
        ),
        check_vma=False,
    )
```
